32 devices in a mesh: head: 2 (over core), seq: 16 (over z, y, x).
Axes of the slice: x: 2, y: 2, z: 4, core: 2. Of those that a mesh axis runs over, the one named last changes fastest.
Arguments:
- query_matrix: bfloat16 [32, 2048, 128], P(None, ('seq', 'head')), may hold values from -6 to 6
- key_matrix: bfloat16 [8, 2048, 128], P(None, ('seq', 'head')), may hold values from -6 to 6
- value_matrix: bfloat16 [8, 2048, 128], P(None, ('seq', 'head')), may hold values from -6 to 6
- output_gradient: bfloat16 [32, 2048, 128], P(None, ('seq', 'head')), may hold values from -6 to 6
- query_head_spans: int32 [32], replicated, may hold values from 64 to 256, as said below
- slab_offset: int32 [1], replicated, may hold values from 0 to 8191
Outputs:
- attn_out: bfloat16 [32, 2048, 128], P(None, ('seq', 'head'))
- query_grad: bfloat16 [32, 2048, 128], P(None, ('seq', 'head'))
- key_grad: bfloat16 [8, 2048, 128], P(None, ('seq', 'head'))
- value_grad: bfloat16 [8, 2048, 128], P(None, ('seq', 'head'))
The draws below stay inside these ranges and needn't reach their ends.
Inputs may be any that keep to these rules, and one draw needn't show every extreme that they name: `query_head_spans`: every span is a multiple of 64; some head has the span 4 * 64 and some head the span 64.
All inputs are finite; a program needn't handle non-finite values.
Results may differ from the reference program's by a relative error of at most 0.019.
Values may be sent and summed in bfloat16 or wider, within the bound.
No kernel may reach another device: no remote copies, remote signals or barrier semaphores. Data moves between devices by JAX's collectives and lax.ppermute only.
A program may use at most 64 MiB of HBM per device.

```python
import jax
import jax.numpy as jnp
from jax import lax

QUERY_HEADS = 32
KEY_VALUE_HEADS = 8
HEAD_WIDTH = 128
TOK_SEQ = 128
LEVELS = 4
SPAN_UNIT = 64
REACH = 2
SEGMENT = 512
SLAB_TOKENS = 2048
N_SEQ = 16


def shared_rows(key):
    query_shape = (QUERY_HEADS, SLAB_TOKENS, HEAD_WIDTH)
    key_array_shape = (KEY_VALUE_HEADS, SLAB_TOKENS, HEAD_WIDTH)
    query_base = jnp.clip(jax.random.normal(jax.random.fold_in(key, 11), query_shape, jnp.float32), -6.0, 6.0)
    key_start_index = jnp.clip(jax.random.normal(jax.random.fold_in(key, 12), key_array_shape, jnp.float32), -6.0, 6.0)
    return (query_base, key_start_index)


def draw_query_matrix(key, part):
    return shared_rows(key)[0].astype(jnp.bfloat16)


def draw_key_matrix(key, part):
    return shared_rows(key)[1].astype(jnp.bfloat16)


def draw_query_head_spans(key, part):
    levels = jax.random.randint(jax.random.fold_in(key, 21), (QUERY_HEADS,), 1, LEVELS + 1)
    longest = jax.random.randint(jax.random.fold_in(key, 22), (), 0, QUERY_HEADS)
    shortest = (longest + jax.random.randint(jax.random.fold_in(key, 23), (), 1, QUERY_HEADS)) % QUERY_HEADS
    levels = levels.at[longest].set(LEVELS).at[shortest].set(1)
    return (levels * SPAN_UNIT).astype(jnp.int32)


def block_levels(rng, shape, pieces, smallest, high):
    level, own = 1.0, jax.random.fold_in(rng, 6)
    for dim, shards_of in pieces:
        draws = jnp.exp(jax.random.uniform(jax.random.fold_in(own, dim), (shards_of,), jnp.float32, smallest / len(pieces), high / len(pieces)))
        level = level * jnp.repeat(draws, shape[dim] // shards_of).reshape([-1 if axis == dim else 1 for axis in range(len(shape))])
    return level


def bell_draw(key, extent, width, reach, shards=(), kind=jnp.bfloat16):
    result = width * jax.random.normal(key, extent, jnp.float32)
    if shards:
        result = result * block_levels(key, extent, shards, -0.22, 0.18)
    return jnp.clip(result, -reach, reach).astype(kind)


def setup_inputs(seed: int = 0) -> dict:
    key_list = jax.random.split(jax.random.key(seed), 7)
    query_matrix = draw_query_matrix(jax.random.fold_in(key_list[6], 71), 0)
    key_matrix = draw_key_matrix(jax.random.fold_in(key_list[6], 71), 0)
    value_matrix = bell_draw(key_list[2], (KEY_VALUE_HEADS, SLAB_TOKENS, HEAD_WIDTH), 1.0, 6.0, ((1, 32),))
    output_gradient = bell_draw(key_list[3], (QUERY_HEADS, SLAB_TOKENS, HEAD_WIDTH), 1.0, 6.0, ((1, 32),))
    query_head_spans = draw_query_head_spans(jax.random.fold_in(key_list[6], 71), 0)
    slab_offset = jax.random.randint(key_list[5], (1,), 0, 64 * TOK_SEQ).astype(jnp.int32)
    return dict(query_matrix=query_matrix, key_matrix=key_matrix, value_matrix=value_matrix, output_gradient=output_gradient, query_head_spans=query_head_spans, slab_offset=slab_offset)


masked_score = -1e30


def visible_pairs(query_pos, key_pos, span_per_row, doc_offset):
    distance = query_pos[:, None] - key_pos[None, :]
    same_segment = (doc_offset + key_pos[None, :]) // SEGMENT == (doc_offset + query_pos[:, None]) // SEGMENT
    inside = (distance >= 0) & (key_pos[None, :] >= 0) & same_segment
    return inside[None, None] & (distance[None, None] < span_per_row)


def round_half(values):
    return lax.optimization_barrier(values.astype(jnp.bfloat16)).astype(jnp.float32)


def reference(query_matrix, key_matrix, value_matrix, output_gradient, query_head_spans, slab_offset):
    heads_per_group = QUERY_HEADS // KEY_VALUE_HEADS
    score_scale = HEAD_WIDTH ** -0.5
    block_length = TOK_SEQ
    padding_width = REACH * block_length
    key_length = (REACH + 1) * block_length
    doc_offset = slab_offset[0]
    span_per_row = query_head_spans.reshape(KEY_VALUE_HEADS, heads_per_group, 1, 1)
    empty_row_block = jnp.zeros((KEY_VALUE_HEADS, padding_width, HEAD_WIDTH), key_matrix.dtype)
    key_pad = jnp.concatenate([empty_row_block, key_matrix], axis=1)
    value_pad = jnp.concatenate([empty_row_block, value_matrix], axis=1)

    def one_block(carried, block_idx):
        key_acc, value_acc = carried
        start_row = (block_idx * block_length).astype(jnp.int32)
        query_block = lax.dynamic_slice_in_dim(query_matrix, start_row, block_length, 1).reshape(KEY_VALUE_HEADS, heads_per_group, block_length, HEAD_WIDTH).astype(jnp.float32)
        gradient_block = lax.dynamic_slice_in_dim(output_gradient, start_row, block_length, 1).reshape(KEY_VALUE_HEADS, heads_per_group, block_length, HEAD_WIDTH).astype(jnp.float32)
        key_blk = lax.dynamic_slice_in_dim(key_pad, start_row, key_length, 1).astype(jnp.float32)
        value_blk = lax.dynamic_slice_in_dim(value_pad, start_row, key_length, 1).astype(jnp.float32)
        query_pos = start_row + jnp.arange(block_length, dtype=jnp.int32)
        key_pos = start_row - padding_width + jnp.arange(key_length, dtype=jnp.int32)
        visible = visible_pairs(query_pos, key_pos, span_per_row, doc_offset)
        scores = jnp.einsum("gaqd,gkd->gaqk", query_block, key_blk) * score_scale
        row_max = jnp.max(jnp.where(visible, scores, masked_score), axis=-1, keepdims=True)
        weights = jnp.where(visible, jnp.exp(scores - row_max), 0.0)
        row_sum = jnp.sum(weights, axis=-1, keepdims=True)
        weighted = jnp.einsum("gaqk,gkd->gaqd", round_half(weights), value_blk)
        out_blk = (weighted / row_sum).astype(jnp.bfloat16)
        log_total = row_max + jnp.log(row_sum)
        prob_rows = jnp.where(visible, jnp.exp(scores - log_total), 0.0)
        value_part = jnp.einsum("gaqk,gaqd->gkd", round_half(prob_rows), gradient_block)
        prob_grad = jnp.einsum("gaqd,gkd->gaqk", gradient_block, value_blk)
        row_delta = jnp.sum(gradient_block * out_blk.astype(jnp.float32), axis=-1, keepdims=True)
        score_grad = round_half(prob_rows * (prob_grad - row_delta) * score_scale)
        query_part = jnp.einsum("gaqk,gkd->gaqd", score_grad, key_blk).astype(jnp.bfloat16)
        key_part = jnp.einsum("gaqk,gaqd->gkd", score_grad, query_block)
        key_acc = lax.dynamic_update_slice_in_dim(key_acc, lax.dynamic_slice_in_dim(key_acc, start_row, key_length, 1) + key_part, start_row, 1)
        value_acc = lax.dynamic_update_slice_in_dim(value_acc, lax.dynamic_slice_in_dim(value_acc, start_row, key_length, 1) + value_part, start_row, 1)
        return (key_acc, value_acc), (out_blk.reshape(QUERY_HEADS, block_length, HEAD_WIDTH), query_part.reshape(QUERY_HEADS, block_length, HEAD_WIDTH))

    empty_accumulator = jnp.zeros((KEY_VALUE_HEADS, padding_width + SLAB_TOKENS, HEAD_WIDTH), jnp.float32)
    sums, blocks = lax.scan(one_block, (empty_accumulator, empty_accumulator), jnp.arange(N_SEQ, dtype=jnp.int32))
    out_blocks, query_blocks = blocks
    attn_out = jnp.transpose(out_blocks, (1, 0, 2, 3)).reshape(QUERY_HEADS, SLAB_TOKENS, HEAD_WIDTH)
    query_grad = jnp.transpose(query_blocks, (1, 0, 2, 3)).reshape(QUERY_HEADS, SLAB_TOKENS, HEAD_WIDTH)
    key_grad = sums[0][:, padding_width:].astype(jnp.bfloat16)
    value_grad = sums[1][:, padding_width:].astype(jnp.bfloat16)
    return attn_out, query_grad, key_grad, value_grad
```

```python
import math

import jax
import jax.numpy as jnp
from jax import lax
from jax.experimental import pallas as pl
from jax.experimental.pallas import tpu as pltpu
from jax.sharding import PartitionSpec as P

REACH = 2
SEGMENT = 512

masked_score = -1e30


def shifted(block, axis, distance):
    devices = range(lax.axis_size(axis))
    route = [(i - distance, i) for i in devices if i - distance in devices]
    return lax.ppermute(block, axis, route)


def swapped(block, axis):
    count = lax.axis_size(axis)
    return lax.ppermute(block, axis, [(i, count - 1 - i) for i in range(count)])


def matmul(left, right, contract):
    return lax.dot_general(
        left, right, ((contract[:1], contract[1:]), ((), ())), preferred_element_type=jnp.float32
    )


def attention_kernel(
    spans, offset, queries, keys, values, grads, back_two, back_four, back_odd,
    out, query_grad, odd_parts, own_part, two_part, four_part,
):
    groups, length, width = keys.shape
    per_group = queries.shape[0] // groups
    lanes = per_group * length
    scale = width ** (-0.5)
    start = (lax.axis_index("seq") * lax.axis_size("head") + lax.axis_index("head")) * length
    blocks = 2 * REACH + 1
    lane = lax.broadcasted_iota(jnp.int32, (1, lanes), 1)
    lane_head = lane // length
    lane_token = lane - lane_head * length
    row = lax.broadcasted_iota(jnp.int32, (length, lanes), 0)
    query_pos = start + lane_token
    doc_pos = offset[0] + query_pos
    segment_start = query_pos - lax.bitwise_and(doc_pos, SEGMENT - 1)
    floor = jnp.maximum(segment_start, 0)
    window_start = start - (blocks - 1) * length

    for g in range(groups):
        span = jnp.full((1, lanes), spans[g * per_group], jnp.int32)
        for a in range(1, per_group):
            span = jnp.where(lane_head == a, spans[g * per_group + a], span)
        first = jnp.maximum(floor, query_pos - span + 1) - window_start
        window_keys = jnp.concatenate(
            [back_four[0, g], back_odd[1, 0, g], back_two[0, g], back_odd[0, 0, g], keys[g]], axis=0
        )
        window_values = jnp.concatenate(
            [back_four[1, g], back_odd[1, 1, g], back_two[1, g], back_odd[0, 1, g], values[g]], axis=0
        )
        rows = pl.ds(g * per_group, per_group)
        query = queries[rows].reshape(lanes, width)
        grad = grads[rows].reshape(lanes, width)
        scores = matmul(window_keys, query, (1, 1)) * (scale * math.log2(math.e))
        parts = []
        for b in range(blocks):
            visible = row >= first - b * length
            if b == blocks - 1:
                visible = visible & (row <= lane_token)
            parts.append(
                jnp.where(visible, scores[b * length : (b + 1) * length], masked_score)
            )
        scores = jnp.concatenate(parts, axis=0)
        row_max = jnp.max(scores, axis=0, keepdims=True)
        weights = jnp.exp2(scores - row_max)
        inverse = 1.0 / jnp.sum(weights, axis=0, keepdims=True)
        weighted = matmul(window_values, weights.astype(jnp.bfloat16), (0, 0))
        attended = (weighted * inverse).astype(jnp.bfloat16)
        out[rows] = attended.T.reshape(per_group, length, width)
        delta = jnp.sum(
            grad.T.astype(jnp.float32) * attended.astype(jnp.float32), axis=0, keepdims=True
        )
        prob = weights * inverse
        value_part = matmul(prob.astype(jnp.bfloat16), grad, (1, 0))
        prob_grad = matmul(window_values, grad, (1, 1))
        score_grad = (prob * (prob_grad - delta) * scale).astype(jnp.bfloat16)
        key_part = matmul(score_grad, query, (1, 0))
        query_part = matmul(window_keys, score_grad, (0, 0)).astype(jnp.bfloat16)
        query_grad[rows] = query_part.T.reshape(per_group, length, width)
        for index, part in enumerate((key_part, value_part)):
            four, three, two, one, own = (
                part[b * length : (b + 1) * length] for b in range(blocks)
            )
            odd_parts[0, index, g] = one.astype(jnp.bfloat16)
            odd_parts[1, index, g] = three.astype(jnp.bfloat16)
            own_part[index, g] = own
            two_part[index, g] = two
            four_part[index, g] = four


def merge_kernel(odd_parts, own_part, two_part, four_part, own_sum, two_sum, four_sum):
    first_core = lax.axis_index("head") == 0

    @pl.when(first_core)
    def _():
        own_sum[...] = own_part[...] + odd_parts[0].astype(jnp.float32)
        two_sum[...] = (two_part[...] + odd_parts[1].astype(jnp.float32)).astype(jnp.bfloat16)
        four_sum[...] = four_part[...].astype(jnp.bfloat16)

    @pl.when(jnp.logical_not(first_core))
    def _():
        own_sum[...] = own_part[...]
        two_sum[...] = (two_part[...] + odd_parts[0].astype(jnp.float32)).astype(jnp.bfloat16)
        four_sum[...] = (four_part[...] + odd_parts[1].astype(jnp.float32)).astype(jnp.bfloat16)


def final_kernel(own_sum, two_sum, four_sum, key_grad, value_grad):
    for index, result in enumerate((key_grad, value_grad)):
        total = own_sum[index] + two_sum[index].astype(jnp.float32)
        result[...] = (total + four_sum[index].astype(jnp.float32)).astype(jnp.bfloat16)


def shards(query_matrix, key_matrix, value_matrix, output_gradient, query_head_spans, slab_offset):
    groups, length, width = key_matrix.shape
    pair_shape = (2, groups, length, width)
    smem = pl.BlockSpec(memory_space=pltpu.SMEM)
    vmem = pl.BlockSpec(memory_space=pltpu.VMEM)
    params = pltpu.CompilerParams(vmem_limit_bytes=48 * 1024 * 1024)
    own = jnp.stack([key_matrix, value_matrix])
    back_four = shifted(own, "seq", 2)
    back_two = shifted(own, "seq", 1)
    first_core = lax.axis_index("head") == 0
    back_odd = swapped(
        jnp.stack(
            [
                jnp.where(first_core, own, back_two),
                jnp.where(first_core, back_two, back_four),
            ]
        ),
        "head",
    )
    half = jax.ShapeDtypeStruct(pair_shape, jnp.bfloat16)
    full = jax.ShapeDtypeStruct(pair_shape, jnp.float32)
    attn_out, query_grad, odd_parts, own_part, two_part, four_part = pl.pallas_call(
        attention_kernel,
        out_shape=(
            jax.ShapeDtypeStruct(query_matrix.shape, jnp.bfloat16),
            jax.ShapeDtypeStruct(query_matrix.shape, jnp.bfloat16),
            jax.ShapeDtypeStruct((2,) + pair_shape, jnp.bfloat16),
            full,
            full,
            full,
        ),
        in_specs=[smem, smem] + [vmem] * 7,
        out_specs=(vmem,) * 6,
        compiler_params=params,
        name="attention",
    )(
        query_head_spans, slab_offset, query_matrix, key_matrix, value_matrix, output_gradient,
        back_two, back_four, back_odd,
    )
    own_sum, two_sum, four_sum = pl.pallas_call(
        merge_kernel,
        out_shape=(full, half, half),
        in_specs=[vmem] * 4,
        out_specs=(vmem,) * 3,
        compiler_params=params,
        name="merge",
    )(swapped(odd_parts, "head"), own_part, two_part, four_part)
    four_sum = shifted(four_sum, "seq", -2)
    two_sum = shifted(two_sum, "seq", -1)
    key_grad, value_grad = pl.pallas_call(
        final_kernel,
        out_shape=(jax.ShapeDtypeStruct(key_matrix.shape, jnp.bfloat16),) * 2,
        in_specs=[vmem] * 3,
        out_specs=(vmem,) * 2,
        compiler_params=params,
        name="total",
    )(own_sum, two_sum, four_sum)
    return (attn_out, query_grad, key_grad, value_grad)


def solution(mesh):
    tokens = P(None, ("seq", "head"), None)
    return jax.shard_map(
        shards,
        mesh=mesh,
        in_specs=(tokens, tokens, tokens, tokens, P(), P()),
        out_specs=(tokens, tokens, tokens, tokens),
        check_vma=False,
    )
```

```python
import math

import jax
import jax.numpy as jnp
from jax import lax
from jax.experimental import pallas as pl
from jax.experimental.pallas import tpu as pltpu
from jax.sharding import PartitionSpec as P

REACH = 2
SEGMENT = 512

masked_score = -1e30


def shifted(block, axis, distance):
    devices = range(lax.axis_size(axis))
    route = [(i - distance, i) for i in devices if i - distance in devices]
    return lax.ppermute(block, axis, route)


def swapped(block, axis):
    count = lax.axis_size(axis)
    return lax.ppermute(block, axis, [(i, count - 1 - i) for i in range(count)])


def matmul(left, right, contract):
    return lax.dot_general(
        left, right, ((contract[:1], contract[1:]), ((), ())), preferred_element_type=jnp.float32
    )


def window(own, two, four, odd, index, g):
    return jnp.concatenate(
        [four[index, g], odd[1, index, g], two[index, g], odd[0, index, g], own[g]], axis=0
    )


def grouped(ref, g, per_group):
    _, length, width = ref.shape
    return ref[pl.ds(g * per_group, per_group)].reshape(per_group * length, width)


def first_visible(spans, offset, groups, per_group, length):
    lanes = per_group * length
    start = (lax.axis_index("seq") * lax.axis_size("head") + lax.axis_index("head")) * length
    lane = lax.broadcasted_iota(jnp.int32, (1, lanes), 1)
    lane_head = lane // length
    query_pos = start + lane - lane_head * length
    segment_start = query_pos - lax.bitwise_and(offset[0] + query_pos, SEGMENT - 1)
    floor = jnp.maximum(segment_start, 0)
    result = []
    for g in range(groups):
        span = jnp.full((1, lanes), spans[g * per_group], jnp.int32)
        for a in range(1, per_group):
            span = jnp.where(lane_head == a, spans[g * per_group + a], span)
        result.append(jnp.maximum(floor, query_pos - span + 1) - start)
    return result


def prepare_kernel(spans, offset, queries, keys, values, grads, own_scores, own_prob_grad, grad_rows):
    groups, length, width = keys.shape
    per_group = queries.shape[0] // groups
    lanes = per_group * length
    factor = width ** (-0.5) * math.log2(math.e)
    row = lax.broadcasted_iota(jnp.int32, (length, lanes), 0)
    lane_token = lax.broadcasted_iota(jnp.int32, (length, lanes), 1) % length
    first = first_visible(spans, offset, groups, per_group, length)
    for g in range(groups):
        query = grouped(queries, g, per_group)
        grad = grouped(grads, g, per_group)
        visible = (row >= first[g]) & (row <= lane_token)
        scores = matmul(keys[g], query, (1, 1)) * factor
        own_scores[g] = jnp.where(visible, scores, masked_score)
        own_prob_grad[g] = matmul(values[g], grad, (1, 1))
        grad_rows[g] = grad.T


def attention_kernel(
    spans, offset, queries, keys, values, grads, back_two, back_four, back_odd,
    own_scores, own_prob_grad, grad_rows,
    odd_parts, attended_rows, prob_half, score_grad_half,
):
    groups, length, width = keys.shape
    per_group = queries.shape[0] // groups
    lanes = per_group * length
    scale = width ** (-0.5)
    earlier = 2 * REACH
    row = lax.broadcasted_iota(jnp.int32, (length, lanes), 0)
    first = first_visible(spans, offset, groups, per_group, length)

    for g in range(groups):
        window_keys = window(keys, back_two, back_four, back_odd, 0, g)
        window_values = window(values, back_two, back_four, back_odd, 1, g)
        query = grouped(queries, g, per_group)
        grad = grouped(grads, g, per_group)
        scores = matmul(window_keys[: earlier * length], query, (1, 1)) * (scale * math.log2(math.e))
        scores = jnp.concatenate(
            [
                jnp.where(
                    row >= first[g] + (earlier - b) * length,
                    scores[b * length : (b + 1) * length],
                    masked_score,
                )
                for b in range(earlier)
            ]
            + [own_scores[g]],
            axis=0,
        )
        row_max = jnp.max(scores, axis=0, keepdims=True)
        weights = jnp.exp2(scores - row_max)
        inverse = 1.0 / jnp.sum(weights, axis=0, keepdims=True)
        weighted = matmul(window_values, weights.astype(jnp.bfloat16), (0, 0))
        attended = (weighted * inverse).astype(jnp.bfloat16)
        attended_rows[g] = attended
        delta = jnp.sum(
            grad_rows[g].astype(jnp.float32) * attended.astype(jnp.float32), axis=0, keepdims=True
        )
        prob = weights * inverse
        prob_grad = jnp.concatenate(
            [matmul(window_values[: earlier * length], grad, (1, 1)), own_prob_grad[g]], axis=0
        )
        half = prob.astype(jnp.bfloat16)
        score_grad = (prob * (prob_grad - delta) * scale).astype(jnp.bfloat16)
        prob_half[g] = half
        score_grad_half[g] = score_grad
        for slot, back in ((0, 1), (1, 3)):
            rows = slice((earlier - back) * length, (earlier - back + 1) * length)
            odd_parts[slot, 0, g] = matmul(score_grad[rows], query, (1, 0)).astype(jnp.bfloat16)
            odd_parts[slot, 1, g] = matmul(half[rows], grad, (1, 0)).astype(jnp.bfloat16)


def even_kernel(queries, grads, prob_half, score_grad_half, two_part, four_part):
    groups = prob_half.shape[0]
    per_group = queries.shape[0] // groups
    length = queries.shape[1]
    for g in range(groups):
        query = grouped(queries, g, per_group)
        grad = grouped(grads, g, per_group)
        for part, back in ((two_part, 2), (four_part, 4)):
            rows = pl.ds((2 * REACH - back) * length, length)
            part[0, g] = matmul(score_grad_half[g, rows], query, (1, 0))
            part[1, g] = matmul(prob_half[g, rows], grad, (1, 0))


def merge_kernel(odd_parts, two_part, four_part, two_sum, four_sum):
    first_core = lax.axis_index("head") == 0

    @pl.when(first_core)
    def _():
        two_sum[...] = (two_part[...] + odd_parts[1].astype(jnp.float32)).astype(jnp.bfloat16)
        four_sum[...] = four_part[...].astype(jnp.bfloat16)

    @pl.when(jnp.logical_not(first_core))
    def _():
        two_sum[...] = (two_part[...] + odd_parts[0].astype(jnp.float32)).astype(jnp.bfloat16)
        four_sum[...] = (four_part[...] + odd_parts[1].astype(jnp.float32)).astype(jnp.bfloat16)


def query_kernel(
    queries, keys, grads, back_two, back_four, back_odd, attended_rows, prob_half, score_grad_half,
    odd_parts, out, query_grad, own_sum,
):
    groups, length, width = keys.shape
    per_group = queries.shape[0] // groups
    first_core = lax.axis_index("head") == 0
    own_rows = pl.ds(2 * REACH * length, length)
    for g in range(groups):
        rows = pl.ds(g * per_group, per_group)
        out[rows] = attended_rows[g].T.reshape(per_group, length, width)
        window_keys = window(keys, back_two, back_four, back_odd, 0, g)
        query_part = matmul(window_keys, score_grad_half[g], (0, 0)).astype(jnp.bfloat16)
        query_grad[rows] = query_part.T.reshape(per_group, length, width)
        own_sum[0, g] = matmul(score_grad_half[g, own_rows], grouped(queries, g, per_group), (1, 0))
        own_sum[1, g] = matmul(prob_half[g, own_rows], grouped(grads, g, per_group), (1, 0))

    @pl.when(first_core)
    def _():
        own_sum[...] += odd_parts[0].astype(jnp.float32)


def final_kernel(own_sum, two_sum, four_sum, key_grad, value_grad):
    for index, result in enumerate((key_grad, value_grad)):
        total = own_sum[index] + two_sum[index].astype(jnp.float32)
        result[...] = (total + four_sum[index].astype(jnp.float32)).astype(jnp.bfloat16)


def shards(query_matrix, key_matrix, value_matrix, output_gradient, query_head_spans, slab_offset):
    groups, length, width = key_matrix.shape
    heads = query_matrix.shape[0]
    lanes = heads // groups * length
    keys_seen = (2 * REACH + 1) * length
    half, full = jnp.bfloat16, jnp.float32
    pair_shape = (2, groups, length, width)

    def call(kernel, name, outs, scalars, arrays, flops):
        smem = pl.BlockSpec(memory_space=pltpu.SMEM)
        vmem = pl.BlockSpec(memory_space=pltpu.VMEM)
        return pl.pallas_call(
            kernel,
            out_shape=tuple(jax.ShapeDtypeStruct(shape, kind) for shape, kind in outs),
            in_specs=[smem] * len(scalars) + [vmem] * len(arrays),
            out_specs=(vmem,) * len(outs),
            compiler_params=pltpu.CompilerParams(vmem_limit_bytes=40 * 1024 * 1024),
            cost_estimate=pl.CostEstimate(flops=flops, bytes_accessed=2**22, transcendentals=0),
            name=name,
        )(*scalars, *arrays)

    score_flops = 2 * heads * length * keys_seen * width
    scalars = (query_head_spans, slab_offset)
    own = jnp.stack([key_matrix, value_matrix])
    back_two = shifted(own, "seq", 1)
    back_four = shifted(own, "seq", 2)
    prepared = call(
        prepare_kernel,
        "prepare",
        [((groups, length, lanes), full)] * 2 + [((groups, width, lanes), half)],
        scalars,
        (query_matrix, key_matrix, value_matrix, output_gradient),
        score_flops,
    )
    back_two, back_four, *prepared = lax.optimization_barrier((back_two, back_four, *prepared))
    first_core = lax.axis_index("head") == 0
    back_odd = swapped(
        jnp.stack(
            [
                jnp.where(first_core, own, back_two),
                jnp.where(first_core, back_two, back_four),
            ]
        ),
        "head",
    )
    odd_parts, attended_rows, prob_half, score_grad_half = call(
        attention_kernel,
        "attention",
        [
            ((2,) + pair_shape, half),
            ((groups, width, lanes), half),
            ((groups, keys_seen, lanes), half),
            ((groups, keys_seen, lanes), half),
        ],
        scalars,
        (query_matrix, key_matrix, value_matrix, output_gradient, back_two, back_four, back_odd)
        + tuple(prepared),
        4 * score_flops,
    )
    odd_arrived = swapped(odd_parts, "head")
    two_part, four_part = call(
        even_kernel,
        "even_parts",
        [(pair_shape, full)] * 2,
        (),
        (query_matrix, output_gradient, prob_half, score_grad_half),
        score_flops,
    )
    two_sum, four_sum = call(
        merge_kernel, "merge", [(pair_shape, half)] * 2, (), (odd_arrived, two_part, four_part), 1000
    )
    four_total = shifted(four_sum, "seq", -2)
    two_total = shifted(two_sum, "seq", -1)
    attn_out, query_grad, own_sum = call(
        query_kernel,
        "query_grad",
        [(query_matrix.shape, half)] * 2 + [(pair_shape, full)],
        (),
        (
            query_matrix, key_matrix, output_gradient, back_two, back_four, back_odd,
            attended_rows, prob_half, score_grad_half, odd_arrived,
        ),
        2 * score_flops,
    )
    key_grad, value_grad = call(
        final_kernel,
        "total",
        [(key_matrix.shape, half)] * 2,
        (),
        (own_sum, two_total, four_total),
        1000,
    )
    return (attn_out, query_grad, key_grad, value_grad)


def solution(mesh):
    tokens = P(None, ("seq", "head"), None)
    return jax.shard_map(
        shards,
        mesh=mesh,
        in_specs=(tokens, tokens, tokens, tokens, P(), P()),
        out_specs=(tokens, tokens, tokens, tokens),
        check_vma=False,
    )
```

```python
import math

import jax
import jax.numpy as jnp
from jax import lax
from jax.experimental import pallas as pl
from jax.experimental.pallas import tpu as pltpu
from jax.sharding import PartitionSpec as P

REACH = 2
SEGMENT = 512

masked_score = -1e30


def shifted(block, axis, distance):
    devices = range(lax.axis_size(axis))
    route = [(i - distance, i) for i in devices if i - distance in devices]
    return lax.ppermute(block, axis, route)


def swapped(block, axis):
    count = lax.axis_size(axis)
    return lax.ppermute(block, axis, [(i, count - 1 - i) for i in range(count)])


def matmul(left, right, contract):
    return lax.dot_general(
        left, right, ((contract[:1], contract[1:]), ((), ())), preferred_element_type=jnp.float32
    )


def grouped(ref, g, per_group):
    _, length, width = ref.shape
    return ref[pl.ds(g * per_group, per_group)].reshape(per_group * length, width)


def first_visible(spans, offset, groups, per_group, length):
    lanes = per_group * length
    start = (lax.axis_index("seq") * lax.axis_size("head") + lax.axis_index("head")) * length
    lane = lax.broadcasted_iota(jnp.int32, (1, lanes), 1)
    lane_head = lane // length
    query_pos = start + lane - lane_head * length
    segment_start = query_pos - lax.bitwise_and(offset[0] + query_pos, SEGMENT - 1)
    floor = jnp.maximum(segment_start, 0)
    result = []
    for g in range(groups):
        span = jnp.full((1, lanes), spans[g * per_group], jnp.int32)
        for a in range(1, per_group):
            span = jnp.where(lane_head == a, spans[g * per_group + a], span)
        result.append(jnp.maximum(floor, query_pos - span + 1) - start)
    return result


def join(*blocks):
    return jnp.concatenate(blocks, axis=0)


def masked(scores, first, backs, length):
    row = lax.broadcasted_iota(jnp.int32, (length, scores.shape[1]), 0)
    pieces = []
    for i, back in enumerate(backs):
        visible = row >= first + back * length
        if back == 0:
            lane = lax.broadcasted_iota(jnp.int32, row.shape, 1)
            visible &= row <= lane - lane // length * length
        pieces.append(jnp.where(visible, scores[i * length : (i + 1) * length], masked_score))
    return jnp.concatenate(pieces, axis=0)


def prepare_kernel(spans, offset, own, grads, own_copy, first, own_prob_grad, grad_rows):
    _, groups, length, width = own.shape
    per_group = grads.shape[0] // groups
    own_copy[...] = own[...]
    for g, rows in enumerate(first_visible(spans, offset, groups, per_group, length)):
        grad = grouped(grads, g, per_group)
        first[g] = rows
        own_prob_grad[g] = matmul(own[1, g], grad, (1, 1))
        grad_rows[g] = grad.T


def near_forward_kernel(
    first, queries, own, grads, one_keys, one_values, back_two, own_prob_grad,
    near_max, near_sum, near_out, near_weights, near_prob_grad,
):
    _, groups, length, width = own.shape
    per_group = queries.shape[0] // groups
    factor = width ** (-0.5) * math.log2(math.e)
    for g in range(groups):
        query = grouped(queries, g, per_group)
        grad = grouped(grads, g, per_group)
        scores = matmul(join(back_two[0, g], one_keys[g], own[0, g]), query, (1, 1)) * factor
        scores = masked(scores, first[g], (2, 1, 0), length)
        row_max = jnp.max(scores, axis=0, keepdims=True)
        weights = jnp.exp2(scores - row_max)
        near_max[g] = row_max
        near_sum[g] = jnp.sum(weights, axis=0, keepdims=True)
        near_weights[g] = weights
        near_out[g] = matmul(
            join(back_two[1, g], one_values[g], own[1, g]), weights.astype(jnp.bfloat16), (0, 0)
        )
        prob_grad = matmul(join(back_two[1, g], one_values[g]), grad, (1, 1))
        near_prob_grad[g] = jnp.concatenate([prob_grad, own_prob_grad[g]], axis=0)


def far_kernel(
    first, queries, grads, back_three, back_four, grad_rows, near_max, near_sum, near_out,
    attended_rows, row_delta, near_factor, prob_half, score_grad_half, three_part,
):
    _, groups, length, width = back_three.shape
    per_group = queries.shape[0] // groups
    scale = width ** (-0.5)
    for g in range(groups):
        query = grouped(queries, g, per_group)
        grad = grouped(grads, g, per_group)
        values = join(back_four[1, g], back_three[1, g])
        scores = matmul(join(back_four[0, g], back_three[0, g]), query, (1, 1))
        scores = masked(scores * (scale * math.log2(math.e)), first[g], (4, 3), length)
        row_max = jnp.maximum(near_max[g], jnp.max(scores, axis=0, keepdims=True))
        weights = jnp.exp2(scores - row_max)
        factor = jnp.exp2(near_max[g] - row_max)
        inverse = 1.0 / (near_sum[g] * factor + jnp.sum(weights, axis=0, keepdims=True))
        weighted = near_out[g] * factor + matmul(values, weights.astype(jnp.bfloat16), (0, 0))
        attended = (weighted * inverse).astype(jnp.bfloat16)
        delta = jnp.sum(
            grad_rows[g].astype(jnp.float32) * attended.astype(jnp.float32), axis=0, keepdims=True
        )
        prob = weights * inverse
        half = prob.astype(jnp.bfloat16)
        score_grad = (prob * (matmul(values, grad, (1, 1)) - delta) * scale).astype(jnp.bfloat16)
        attended_rows[g] = attended
        row_delta[g] = delta
        near_factor[g] = factor * inverse
        prob_half[g] = half
        score_grad_half[g] = score_grad
        three_part[0, g] = matmul(score_grad[length:], query, (1, 0)).astype(jnp.bfloat16)
        three_part[1, g] = matmul(half[length:], grad, (1, 0)).astype(jnp.bfloat16)


def four_kernel(queries, grads, prob_half, score_grad_half, four_part):
    groups = prob_half.shape[0]
    length = queries.shape[1]
    per_group = queries.shape[0] // groups
    for g in range(groups):
        four_part[0, g] = matmul(score_grad_half[g, :length], grouped(queries, g, per_group), (1, 0))
        four_part[1, g] = matmul(prob_half[g, :length], grouped(grads, g, per_group), (1, 0))


def four_sum_kernel(three_arrived, four_part, four_sum):
    first_core = lax.axis_index("head") == 0

    @pl.when(first_core)
    def _():
        four_sum[...] = four_part[...].astype(jnp.bfloat16)

    @pl.when(jnp.logical_not(first_core))
    def _():
        four_sum[...] = (four_part[...] + three_arrived[...].astype(jnp.float32)).astype(jnp.bfloat16)


def near_backward_kernel(
    queries, grads, near_weights, near_prob_grad, near_factor, row_delta,
    score_grad_half, one_keys, one_values, two_part, own_part,
):
    groups = near_weights.shape[0]
    length, width = queries.shape[1:]
    per_group = queries.shape[0] // groups
    for g in range(groups):
        query = grouped(queries, g, per_group)
        grad = grouped(grads, g, per_group)
        prob = near_weights[g] * near_factor[g]
        half = prob.astype(jnp.bfloat16)
        score_grad = prob * (near_prob_grad[g] - row_delta[g]) * width ** (-0.5)
        score_grad = score_grad.astype(jnp.bfloat16)
        score_grad_half[g] = score_grad
        key_part = matmul(score_grad, query, (1, 0))
        value_part = matmul(half, grad, (1, 0))
        for index, (part, one) in enumerate(((key_part, one_keys), (value_part, one_values))):
            two_part[index, g] = part[:length]
            one[g] = part[length : 2 * length].astype(jnp.bfloat16)
            own_part[index, g] = part[2 * length :]


def two_sum_kernel(one_keys, one_values, three_arrived, two_part, own_part, two_sum, own_sum):
    first_core = lax.axis_index("head") == 0
    ones = (one_keys, one_values)

    @pl.when(first_core)
    def _():
        two_sum[...] = (two_part[...] + three_arrived[...].astype(jnp.float32)).astype(jnp.bfloat16)
        for index, one in enumerate(ones):
            own_sum[index] = own_part[index] + one[...].astype(jnp.float32)

    @pl.when(jnp.logical_not(first_core))
    def _():
        for index, one in enumerate(ones):
            two_sum[index] = (two_part[index] + one[...].astype(jnp.float32)).astype(jnp.bfloat16)
        own_sum[...] = own_part[...]


def query_kernel(
    own, one_keys, back_two, back_three, back_four, attended_rows, far_grad, near_grad,
    own_sum, four_sum, out, query_grad, partial_sum,
):
    groups, length, width = own.shape[1:]
    per_group = out.shape[0] // groups
    partial_sum[...] = own_sum[...] + four_sum[...].astype(jnp.float32)
    for g in range(groups):
        rows = pl.ds(g * per_group, per_group)
        out[rows] = attended_rows[g].T.reshape(per_group, length, width)
        part = matmul(join(back_four[0, g], back_three[0, g]), far_grad[g], (0, 0))
        part += matmul(join(back_two[0, g], one_keys[g], own[0, g]), near_grad[g], (0, 0))
        query_grad[rows] = part.astype(jnp.bfloat16).T.reshape(per_group, length, width)


def final_kernel(partial_sum, two_sum, key_grad, value_grad):
    for index, result in enumerate((key_grad, value_grad)):
        total = partial_sum[index] + two_sum[index].astype(jnp.float32)
        result[...] = total.astype(jnp.bfloat16)


def shards(query_matrix, key_matrix, value_matrix, output_gradient, query_head_spans, slab_offset):
    groups, length, width = key_matrix.shape
    heads = query_matrix.shape[0]
    lanes = heads // groups * length
    half, full = jnp.bfloat16, jnp.float32
    vmem = pl.BlockSpec(memory_space=pltpu.VMEM)
    smem = pl.BlockSpec(memory_space=pltpu.SMEM)
    block_flops = 2 * heads * length * length * width

    def call(kernel, name, flops, outs, arrays, specs=None):
        return pl.pallas_call(
            kernel,
            out_shape=tuple(jax.ShapeDtypeStruct(shape, kind) for shape, kind in outs),
            in_specs=specs or [vmem] * len(arrays),
            out_specs=(vmem,) * len(outs),
            compiler_params=pltpu.CompilerParams(vmem_limit_bytes=40 * 1024 * 1024),
            cost_estimate=pl.CostEstimate(flops=flops, bytes_accessed=0, transcendentals=0),
            name=name,
        )(*arrays)

    def rows_of(count, kind):
        return ((groups, count, lanes), kind)

    single = (key_matrix.shape, half)
    pair = ((2, groups, length, width), half)
    wide_pair = ((2, groups, length, width), full)
    stat = rows_of(1, full)
    first_core = lax.axis_index("head") == 0

    own = jnp.stack([key_matrix, value_matrix])
    back_two = shifted(own, "seq", 1)
    queries, grads = query_matrix, output_gradient
    own_copy, first, own_prob_grad, grad_rows = call(
        prepare_kernel,
        "prepare",
        1,
        [
            pair, rows_of(1, jnp.int32), rows_of(length, full), rows_of(width, half),
        ],
        (query_head_spans, slab_offset, own, grads),
        specs=[smem, smem, vmem, vmem],
    )
    back_four = shifted(own_copy, "seq", 2)
    back_two, own_prob_grad = lax.optimization_barrier((back_two, own_prob_grad))
    back_one = [
        swapped(jnp.where(first_core, own[index], back_two[index]), "head") for index in range(2)
    ]
    near_max, near_sum, near_out, near_weights, near_prob_grad = call(
        near_forward_kernel,
        "near_forward",
        1,
        [stat, stat, rows_of(width, full), rows_of(3 * length, full), rows_of(3 * length, full)],
        (first, queries, own, grads, *back_one, back_two, own_prob_grad),
    )
    back_four, near_max = lax.optimization_barrier((back_four, near_max))
    back_three = swapped(jnp.where(first_core, back_two, back_four), "head")
    attended_rows, row_delta, near_factor, prob_half, far_grad, three_part = call(
        far_kernel,
        "far_forward_backward",
        1,
        [rows_of(width, half), stat, stat, rows_of(2 * length, half), rows_of(2 * length, half), pair],
        (first, queries, grads, back_three, back_four, grad_rows, near_max, near_sum, near_out),
    )
    three_arrived = swapped(three_part, "head")
    (four_part,) = call(
        four_kernel, "four_part", 1, [wide_pair], (queries, grads, prob_half, far_grad)
    )
    (four_sum,) = call(four_sum_kernel, "four_sum", 1000, [pair], (three_arrived, four_part))
    four_total = shifted(four_sum, "seq", -2)
    near_weights, four_sum = lax.optimization_barrier((near_weights, four_sum))
    near_grad, *one_parts, two_part, own_part = call(
        near_backward_kernel,
        "near_backward",
        6 * block_flops,
        [rows_of(3 * length, half), single, single, wide_pair, wide_pair],
        (queries, grads, near_weights, near_prob_grad, near_factor, row_delta),
    )
    one_arrived = [swapped(part, "head") for part in one_parts]
    two_sum, own_sum = call(
        two_sum_kernel,
        "two_sum",
        1000,
        [pair, wide_pair],
        (*one_arrived, three_arrived, two_part, own_part),
    )
    two_total = shifted(two_sum, "seq", -1)
    attn_out, query_grad, partial_sum = call(
        query_kernel,
        "query_grad",
        200 * block_flops,
        [(query_matrix.shape, half)] * 2 + [wide_pair],
        (own, back_one[0], back_two, back_three, back_four, attended_rows, far_grad, near_grad,
         own_sum, four_total),
    )
    key_grad, value_grad = call(
        final_kernel,
        "total",
        1000,
        [(key_matrix.shape, half)] * 2,
        (partial_sum, two_total),
    )
    return (attn_out, query_grad, key_grad, value_grad)


def solution(mesh):
    tokens = P(None, ("seq", "head"), None)
    return jax.shard_map(
        shards,
        mesh=mesh,
        in_specs=(tokens, tokens, tokens, tokens, P(), P()),
        out_specs=(tokens, tokens, tokens, tokens),
        check_vma=False,
    )
```

```python
import math

import jax
import jax.numpy as jnp
from jax import lax
from jax.experimental import pallas as pl
from jax.experimental.pallas import tpu as pltpu
from jax.sharding import PartitionSpec as P

REACH = 2
SEGMENT = 512

masked_score = -1e30


def shifted(block, axis, distance):
    devices = range(lax.axis_size(axis))
    route = [(i - distance, i) for i in devices if i - distance in devices]
    return lax.ppermute(block, axis, route)


def swapped(block, axis):
    count = lax.axis_size(axis)
    return lax.ppermute(block, axis, [(i, count - 1 - i) for i in range(count)])


def matmul(left, right, contract):
    return lax.dot_general(
        left, right, ((contract[:1], contract[1:]), ((), ())), preferred_element_type=jnp.float32
    )


def grouped(ref, g, per_group):
    _, length, width = ref.shape
    return ref[pl.ds(g * per_group, per_group)].reshape(per_group * length, width)


def first_visible(spans, offset, groups, per_group, length):
    lanes = per_group * length
    start = (lax.axis_index("seq") * lax.axis_size("head") + lax.axis_index("head")) * length
    lane = lax.broadcasted_iota(jnp.int32, (1, lanes), 1)
    lane_head = lane // length
    query_pos = start + lane - lane_head * length
    segment_start = query_pos - lax.bitwise_and(offset[0] + query_pos, SEGMENT - 1)
    floor = jnp.maximum(segment_start, 0)
    result = []
    for g in range(groups):
        span = jnp.full((1, lanes), spans[g * per_group], jnp.int32)
        for a in range(1, per_group):
            span = jnp.where(lane_head == a, spans[g * per_group + a], span)
        result.append(jnp.maximum(floor, query_pos - span + 1) - start)
    return result


def join(*blocks):
    return jnp.concatenate(blocks, axis=0)


def masked(scores, first, backs, length):
    row = lax.broadcasted_iota(jnp.int32, (length, scores.shape[1]), 0)
    pieces = []
    for i, back in enumerate(backs):
        visible = row >= first + back * length
        if back == 0:
            lane = lax.broadcasted_iota(jnp.int32, row.shape, 1)
            visible &= row <= lane - lane // length * length
        pieces.append(jnp.where(visible, scores[i * length : (i + 1) * length], masked_score))
    return jnp.concatenate(pieces, axis=0)


def prepare_kernel(own, grads, own_copy, own_prob_grad, grad_rows):
    _, groups, length, width = own.shape
    per_group = grads.shape[0] // groups
    own_copy[...] = own[...]
    for g in range(groups):
        grad = grouped(grads, g, per_group)
        own_prob_grad[g] = matmul(own[1, g], grad, (1, 1))
        grad_rows[g] = grad.T


def own_kernel(spans, offset, queries, own, first, own_scores):
    _, groups, length, width = own.shape
    per_group = queries.shape[0] // groups
    factor = width ** (-0.5) * math.log2(math.e)
    for g, rows in enumerate(first_visible(spans, offset, groups, per_group, length)):
        first[g] = rows
        scores = matmul(own[0, g], grouped(queries, g, per_group), (1, 1)) * factor
        own_scores[g] = masked(scores, rows, (0,), length)


def near_forward_kernel(
    first, queries, own, grads, one_keys, one_values, back_two, own_scores, own_prob_grad,
    near_max, near_sum, near_out, near_weights, near_prob_grad,
):
    _, groups, length, width = own.shape
    per_group = queries.shape[0] // groups
    factor = width ** (-0.5) * math.log2(math.e)
    for g in range(groups):
        query = grouped(queries, g, per_group)
        grad = grouped(grads, g, per_group)
        scores = matmul(join(back_two[0, g], one_keys[g]), query, (1, 1)) * factor
        scores = join(masked(scores, first[g], (2, 1), length), own_scores[g])
        row_max = jnp.max(scores, axis=0, keepdims=True)
        weights = jnp.exp2(scores - row_max)
        near_max[g] = row_max
        near_sum[g] = jnp.sum(weights, axis=0, keepdims=True)
        near_weights[g] = weights
        near_out[g] = matmul(
            join(back_two[1, g], one_values[g], own[1, g]), weights.astype(jnp.bfloat16), (0, 0)
        )
        prob_grad = matmul(join(back_two[1, g], one_values[g]), grad, (1, 1))
        near_prob_grad[g] = join(prob_grad, own_prob_grad[g])


def four_forward_kernel(
    first, queries, grads, back_four, near_max, near_sum, near_out,
    most_max, most_sum, most_out, near_factor, four_weights, four_prob_grad,
):
    _, groups, length, width = back_four.shape
    per_group = queries.shape[0] // groups
    factor = width ** (-0.5) * math.log2(math.e)
    for g in range(groups):
        query = grouped(queries, g, per_group)
        grad = grouped(grads, g, per_group)
        scores = matmul(back_four[0, g], query, (1, 1)) * factor
        scores = masked(scores, first[g], (4,), length)
        row_max = jnp.maximum(near_max[g], jnp.max(scores, axis=0, keepdims=True))
        weights = jnp.exp2(scores - row_max)
        rescale = jnp.exp2(near_max[g] - row_max)
        most_max[g] = row_max
        most_sum[g] = near_sum[g] * rescale + jnp.sum(weights, axis=0, keepdims=True)
        most_out[g] = near_out[g] * rescale + matmul(
            back_four[1, g], weights.astype(jnp.bfloat16), (0, 0)
        )
        near_factor[g] = rescale
        four_weights[g] = weights
        four_prob_grad[g] = matmul(back_four[1, g], grad, (1, 1))


def three_kernel(
    first, queries, grads, back_three, grad_rows, most_max, most_sum, most_out,
    attended_rows, row_delta, most_factor, three_grad, three_part,
):
    _, groups, length, width = back_three.shape
    per_group = queries.shape[0] // groups
    scale = width ** (-0.5)
    for g in range(groups):
        query = grouped(queries, g, per_group)
        grad = grouped(grads, g, per_group)
        scores = matmul(back_three[0, g], query, (1, 1)) * (scale * math.log2(math.e))
        scores = masked(scores, first[g], (3,), length)
        row_max = jnp.maximum(most_max[g], jnp.max(scores, axis=0, keepdims=True))
        weights = jnp.exp2(scores - row_max)
        rescale = jnp.exp2(most_max[g] - row_max)
        inverse = 1.0 / (most_sum[g] * rescale + jnp.sum(weights, axis=0, keepdims=True))
        weighted = matmul(back_three[1, g], weights.astype(jnp.bfloat16), (0, 0))
        attended = ((most_out[g] * rescale + weighted) * inverse).astype(jnp.bfloat16)
        delta = jnp.sum(
            grad_rows[g].astype(jnp.float32) * attended.astype(jnp.float32), axis=0, keepdims=True
        )
        prob = weights * inverse
        prob_grad = matmul(back_three[1, g], grad, (1, 1))
        score_grad = (prob * (prob_grad - delta) * scale).astype(jnp.bfloat16)
        attended_rows[g] = attended
        row_delta[g] = delta
        most_factor[g] = rescale * inverse
        three_grad[g] = score_grad
        three_part[0, g] = matmul(score_grad, query, (1, 0)).astype(jnp.bfloat16)
        three_part[1, g] = matmul(prob.astype(jnp.bfloat16), grad, (1, 0)).astype(jnp.bfloat16)


def four_backward_kernel(
    queries, grads, four_weights, four_prob_grad, most_factor, row_delta, four_grad, four_part
):
    groups = four_weights.shape[0]
    length, width = queries.shape[1:]
    per_group = queries.shape[0] // groups
    for g in range(groups):
        prob = four_weights[g] * most_factor[g]
        score_grad = prob * (four_prob_grad[g] - row_delta[g]) * width ** (-0.5)
        score_grad = score_grad.astype(jnp.bfloat16)
        four_grad[g] = score_grad
        four_part[0, g] = matmul(score_grad, grouped(queries, g, per_group), (1, 0))
        four_part[1, g] = matmul(prob.astype(jnp.bfloat16), grouped(grads, g, per_group), (1, 0))


def four_sum_kernel(three_arrived, four_part, four_sum):
    first_core = lax.axis_index("head") == 0

    @pl.when(first_core)
    def _():
        four_sum[...] = four_part[...].astype(jnp.bfloat16)

    @pl.when(jnp.logical_not(first_core))
    def _():
        four_sum[...] = (four_part[...] + three_arrived[...].astype(jnp.float32)).astype(jnp.bfloat16)


def near_backward_kernel(
    queries, grads, near_weights, near_prob_grad, near_factor, most_factor, row_delta,
    score_grad_half, one_part, two_part, own_part,
):
    groups = near_weights.shape[0]
    length, width = queries.shape[1:]
    per_group = queries.shape[0] // groups
    for g in range(groups):
        query = grouped(queries, g, per_group)
        grad = grouped(grads, g, per_group)
        prob = near_weights[g] * (near_factor[g] * most_factor[g])
        half = prob.astype(jnp.bfloat16)
        score_grad = prob * (near_prob_grad[g] - row_delta[g]) * width ** (-0.5)
        score_grad = score_grad.astype(jnp.bfloat16)
        score_grad_half[g] = score_grad
        key_part = matmul(score_grad, query, (1, 0))
        value_part = matmul(half, grad, (1, 0))
        for index, part in enumerate((key_part, value_part)):
            two_part[index, g] = part[:length]
            one_part[index, g] = part[length : 2 * length].astype(jnp.bfloat16)
            own_part[index, g] = part[2 * length :]


def two_sum_kernel(one_arrived, three_arrived, two_part, own_part, two_sum, own_sum):
    first_core = lax.axis_index("head") == 0

    @pl.when(first_core)
    def _():
        two_sum[...] = (two_part[...] + three_arrived[...].astype(jnp.float32)).astype(jnp.bfloat16)
        own_sum[...] = own_part[...] + one_arrived[...].astype(jnp.float32)

    @pl.when(jnp.logical_not(first_core))
    def _():
        two_sum[...] = (two_part[...] + one_arrived[...].astype(jnp.float32)).astype(jnp.bfloat16)
        own_sum[...] = own_part[...]


def query_kernel(
    own, one_keys, back_two, back_three, back_four, attended_rows, four_grad, three_grad, near_grad,
    own_sum, four_sum, out, query_grad, partial_sum,
):
    groups, length, width = own.shape[1:]
    per_group = out.shape[0] // groups
    partial_sum[...] = own_sum[...] + four_sum[...].astype(jnp.float32)
    for g in range(groups):
        rows = pl.ds(g * per_group, per_group)
        out[rows] = attended_rows[g].T.reshape(per_group, length, width)
        part = matmul(
            join(back_four[0, g], back_three[0, g], back_two[0, g], one_keys[g], own[0, g]),
            join(four_grad[g], three_grad[g], near_grad[g]),
            (0, 0),
        )
        query_grad[rows] = part.astype(jnp.bfloat16).T.reshape(per_group, length, width)


def final_kernel(partial_sum, two_sum, key_grad, value_grad):
    for index, result in enumerate((key_grad, value_grad)):
        total = partial_sum[index] + two_sum[index].astype(jnp.float32)
        result[...] = total.astype(jnp.bfloat16)


def shards(query_matrix, key_matrix, value_matrix, output_gradient, query_head_spans, slab_offset):
    groups, length, width = key_matrix.shape
    heads = query_matrix.shape[0]
    lanes = heads // groups * length
    half, full = jnp.bfloat16, jnp.float32
    vmem = pl.BlockSpec(memory_space=pltpu.VMEM)
    smem = pl.BlockSpec(memory_space=pltpu.SMEM)
    block_flops = 2 * heads * length * length * width

    def call(kernel, name, flops, outs, arrays, specs=None):
        return pl.pallas_call(
            kernel,
            out_shape=tuple(jax.ShapeDtypeStruct(shape, kind) for shape, kind in outs),
            in_specs=specs or [vmem] * len(arrays),
            out_specs=(vmem,) * len(outs),
            compiler_params=pltpu.CompilerParams(vmem_limit_bytes=40 * 1024 * 1024),
            cost_estimate=pl.CostEstimate(flops=flops, bytes_accessed=0, transcendentals=0),
            name=name,
        )(*arrays)

    def rows_of(count, kind):
        return ((groups, count, lanes), kind)

    pair = ((2, groups, length, width), half)
    wide_pair = ((2, groups, length, width), full)
    stat = rows_of(1, full)
    first_core = lax.axis_index("head") == 0

    own = jnp.stack([key_matrix, value_matrix])
    back_two = shifted(own, "seq", 1)
    queries, grads = query_matrix, output_gradient
    own_copy, own_prob_grad, grad_rows = call(
        prepare_kernel,
        "prepare",
        1,
        [pair, rows_of(length, full), rows_of(width, half)],
        (own, grads),
    )
    back_four = shifted(own_copy, "seq", 2)
    query_head_spans, own_prob_grad = lax.optimization_barrier((query_head_spans, own_prob_grad))
    first, own_scores = call(
        own_kernel,
        "own_block",
        1,
        [rows_of(1, jnp.int32), rows_of(length, full)],
        (query_head_spans, slab_offset, queries, own_copy),
        specs=[smem, smem, vmem, vmem],
    )
    back_two, own_scores = lax.optimization_barrier((back_two, own_scores))
    back_one = [
        swapped(jnp.where(first_core, own_copy[index], back_two[index]), "head")
        for index in range(2)
    ]
    near_max, near_sum, near_out, near_weights, near_prob_grad = call(
        near_forward_kernel,
        "near_forward",
        1,
        [stat, stat, rows_of(width, full), rows_of(3 * length, full), rows_of(3 * length, full)],
        (first, queries, own_copy, grads, *back_one, back_two, own_scores, own_prob_grad),
    )
    back_four, near_max = lax.optimization_barrier((back_four, near_max))
    back_three = swapped(jnp.where(first_core, back_two, back_four), "head")
    most_max, most_sum, most_out, near_factor, four_weights, four_prob_grad = call(
        four_forward_kernel,
        "four_forward",
        1,
        [stat, stat, rows_of(width, full), stat, rows_of(length, full), rows_of(length, full)],
        (first, queries, grads, back_four, near_max, near_sum, near_out),
    )
    attended_rows, row_delta, most_factor, three_grad, three_part = call(
        three_kernel,
        "three_forward_backward",
        1,
        [rows_of(width, half), stat, stat, rows_of(length, half), pair],
        (first, queries, grads, back_three, grad_rows, most_max, most_sum, most_out),
    )
    three_arrived = swapped(three_part, "head")
    four_grad, four_part = call(
        four_backward_kernel,
        "four_backward",
        1,
        [rows_of(length, half), wide_pair],
        (queries, grads, four_weights, four_prob_grad, most_factor, row_delta),
    )
    near_grad, one_part, two_part, own_part = call(
        near_backward_kernel,
        "near_backward",
        1,
        [rows_of(3 * length, half), pair, wide_pair, wide_pair],
        (queries, grads, near_weights, near_prob_grad, near_factor, most_factor, row_delta),
    )
    one_arrived = swapped(one_part, "head")
    three_arrived, near_grad = lax.optimization_barrier((three_arrived, near_grad))
    (four_sum,) = call(four_sum_kernel, "four_sum", 1, [pair], (three_arrived, four_part))
    four_total = shifted(four_sum, "seq", -2)
    two_sum, own_sum = call(
        two_sum_kernel,
        "two_sum",
        1,
        [pair, wide_pair],
        (one_arrived, three_arrived, two_part, own_part),
    )
    two_total = shifted(two_sum, "seq", -1)
    attn_out, query_grad, partial_sum = call(
        query_kernel,
        "query_grad",
        200 * block_flops,
        [(query_matrix.shape, half)] * 2 + [wide_pair],
        (own_copy, back_one[0], back_two, back_three, back_four, attended_rows, four_grad,
         three_grad, near_grad, own_sum, four_total),
    )
    key_grad, value_grad = call(
        final_kernel,
        "total",
        1000,
        [(key_matrix.shape, half)] * 2,
        (partial_sum, two_total),
    )
    return (attn_out, query_grad, key_grad, value_grad)


def solution(mesh):
    tokens = P(None, ("seq", "head"), None)
    return jax.shard_map(
        shards,
        mesh=mesh,
        in_specs=(tokens, tokens, tokens, tokens, P(), P()),
        out_specs=(tokens, tokens, tokens, tokens),
        check_vma=False,
    )
```

```python
import math

import jax
import jax.numpy as jnp
from jax import lax
from jax.experimental import pallas as pl
from jax.experimental.pallas import tpu as pltpu
from jax.sharding import PartitionSpec as P

REACH = 2
SEGMENT = 512

masked_score = -1e30


def shifted(block, axis, distance):
    devices = range(lax.axis_size(axis))
    route = [(i - distance, i) for i in devices if i - distance in devices]
    return lax.ppermute(block, axis, route)


def swapped(block, axis):
    count = lax.axis_size(axis)
    return lax.ppermute(block, axis, [(i, count - 1 - i) for i in range(count)])


def matmul(left, right, contract):
    return lax.dot_general(
        left, right, ((contract[:1], contract[1:]), ((), ())), preferred_element_type=jnp.float32
    )


def grouped(ref, g, per_group):
    _, length, width = ref.shape
    return ref[pl.ds(g * per_group, per_group)].reshape(per_group * length, width)


def first_visible(spans, offset, groups, per_group, length):
    lanes = per_group * length
    start = (lax.axis_index("seq") * lax.axis_size("head") + lax.axis_index("head")) * length
    lane = lax.broadcasted_iota(jnp.int32, (1, lanes), 1)
    lane_head = lane // length
    query_pos = start + lane - lane_head * length
    segment_start = query_pos - lax.bitwise_and(offset[0] + query_pos, SEGMENT - 1)
    floor = jnp.maximum(segment_start, 0)
    result = []
    for g in range(groups):
        span = jnp.full((1, lanes), spans[g * per_group], jnp.int32)
        for a in range(1, per_group):
            span = jnp.where(lane_head == a, spans[g * per_group + a], span)
        result.append(jnp.maximum(floor, query_pos - span + 1) - start)
    return result


def join(*blocks):
    return jnp.concatenate(blocks, axis=0)


def masked(scores, first, backs, length):
    row = lax.broadcasted_iota(jnp.int32, (length, scores.shape[1]), 0)
    pieces = []
    for i, back in enumerate(backs):
        visible = row >= first + back * length
        if back == 0:
            lane = lax.broadcasted_iota(jnp.int32, row.shape, 1)
            visible &= row <= lane - lane // length * length
        pieces.append(jnp.where(visible, scores[i * length : (i + 1) * length], masked_score))
    return jnp.concatenate(pieces, axis=0)


def prepare_kernel(own, grads, own_copy, own_prob_grad, grad_rows):
    _, groups, length, width = own.shape
    per_group = grads.shape[0] // groups
    own_copy[...] = own[...]
    for g in range(groups):
        grad = grouped(grads, g, per_group)
        own_prob_grad[g] = matmul(own[1, g], grad, (1, 1))
        grad_rows[g] = grad.T


def own_kernel(spans, offset, queries, own, first, own_max, own_total, own_out, own_weights):
    _, groups, length, width = own.shape
    per_group = queries.shape[0] // groups
    factor = width ** (-0.5) * math.log2(math.e)
    for g, rows in enumerate(first_visible(spans, offset, groups, per_group, length)):
        first[g] = rows
        scores = matmul(own[0, g], grouped(queries, g, per_group), (1, 1)) * factor
        scores = masked(scores, rows, (0,), length)
        row_max = jnp.max(scores, axis=0, keepdims=True)
        weights = jnp.exp2(scores - row_max)
        own_max[g] = row_max
        own_total[g] = jnp.sum(weights, axis=0, keepdims=True)
        own_weights[g] = weights
        own_out[g] = matmul(own[1, g], weights.astype(jnp.bfloat16), (0, 0))


def near_forward_kernel(
    first, queries, grads, one_keys, one_values, back_two, own_max, own_total, own_out,
    near_max, near_total, near_out, near_weights, near_prob_grad, own_factor,
):
    _, groups, length, width = back_two.shape
    per_group = queries.shape[0] // groups
    factor = width ** (-0.5) * math.log2(math.e)
    for g in range(groups):
        query = grouped(queries, g, per_group)
        grad = grouped(grads, g, per_group)
        values = join(back_two[1, g], one_values[g])
        scores = matmul(join(back_two[0, g], one_keys[g]), query, (1, 1)) * factor
        scores = masked(scores, first[g], (2, 1), length)
        row_max = jnp.maximum(own_max[g], jnp.max(scores, axis=0, keepdims=True))
        weights = jnp.exp2(scores - row_max)
        rescale = jnp.exp2(own_max[g] - row_max)
        own_factor[g] = rescale
        near_max[g] = row_max
        near_total[g] = own_total[g] * rescale + jnp.sum(weights, axis=0, keepdims=True)
        near_weights[g] = weights
        near_out[g] = own_out[g] * rescale + matmul(values, weights.astype(jnp.bfloat16), (0, 0))
        near_prob_grad[g] = matmul(values, grad, (1, 1))


def four_kernel(first, queries, grads, back_four, four_scores, four_prob_grad):
    _, groups, length, width = back_four.shape
    per_group = queries.shape[0] // groups
    factor = width ** (-0.5) * math.log2(math.e)
    for g in range(groups):
        scores = matmul(back_four[0, g], grouped(queries, g, per_group), (1, 1)) * factor
        four_scores[g] = masked(scores, first[g], (4,), length)
        four_prob_grad[g] = matmul(back_four[1, g], grouped(grads, g, per_group), (1, 1))


def far_kernel(
    first, queries, grads, back_three, back_four, four_scores, four_prob_grad, grad_rows,
    near_max, near_total, near_out,
    attended_rows, row_delta, near_factor, prob_half, far_grad, three_part,
):
    _, groups, length, width = back_three.shape
    per_group = queries.shape[0] // groups
    scale = width ** (-0.5)
    for g in range(groups):
        query = grouped(queries, g, per_group)
        grad = grouped(grads, g, per_group)
        scores = matmul(back_three[0, g], query, (1, 1)) * (scale * math.log2(math.e))
        scores = join(four_scores[g], masked(scores, first[g], (3,), length))
        row_max = jnp.maximum(near_max[g], jnp.max(scores, axis=0, keepdims=True))
        weights = jnp.exp2(scores - row_max)
        rescale = jnp.exp2(near_max[g] - row_max)
        inverse = 1.0 / (near_total[g] * rescale + jnp.sum(weights, axis=0, keepdims=True))
        weighted = matmul(
            join(back_four[1, g], back_three[1, g]), weights.astype(jnp.bfloat16), (0, 0)
        )
        attended = ((near_out[g] * rescale + weighted) * inverse).astype(jnp.bfloat16)
        delta = jnp.sum(
            grad_rows[g].astype(jnp.float32) * attended.astype(jnp.float32), axis=0, keepdims=True
        )
        prob = weights * inverse
        half = prob.astype(jnp.bfloat16)
        prob_grad = join(four_prob_grad[g], matmul(back_three[1, g], grad, (1, 1)))
        score_grad = (prob * (prob_grad - delta) * scale).astype(jnp.bfloat16)
        attended_rows[g] = attended
        row_delta[g] = delta
        near_factor[g] = rescale * inverse
        prob_half[g] = half
        far_grad[g] = score_grad
        three_part[0, g] = matmul(score_grad[length:], query, (1, 0)).astype(jnp.bfloat16)
        three_part[1, g] = matmul(half[length:], grad, (1, 0)).astype(jnp.bfloat16)


def four_backward_kernel(queries, grads, prob_half, far_grad, four_part):
    groups = prob_half.shape[0]
    length = queries.shape[1]
    per_group = queries.shape[0] // groups
    for g in range(groups):
        four_part[0, g] = matmul(far_grad[g, :length], grouped(queries, g, per_group), (1, 0))
        four_part[1, g] = matmul(prob_half[g, :length], grouped(grads, g, per_group), (1, 0))


def four_sum_kernel(three_arrived, four_part, four_sum):
    first_core = lax.axis_index("head") == 0

    @pl.when(first_core)
    def _():
        four_sum[...] = four_part[...].astype(jnp.bfloat16)

    @pl.when(jnp.logical_not(first_core))
    def _():
        four_sum[...] = (four_part[...] + three_arrived[...].astype(jnp.float32)).astype(jnp.bfloat16)


def near_backward_kernel(
    queries, grads, near_weights, own_weights, near_prob_grad, own_prob_grad, near_factor,
    own_factor, row_delta, near_grad, one_part, two_part, own_part,
):
    groups = near_weights.shape[0]
    length, width = queries.shape[1:]
    per_group = queries.shape[0] // groups
    for g in range(groups):
        query = grouped(queries, g, per_group)
        grad = grouped(grads, g, per_group)
        prob = join(
            near_weights[g] * near_factor[g], own_weights[g] * (own_factor[g] * near_factor[g])
        )
        prob_grad = join(near_prob_grad[g], own_prob_grad[g])
        score_grad = (prob * (prob_grad - row_delta[g]) * width ** (-0.5)).astype(jnp.bfloat16)
        near_grad[g] = score_grad
        key_part = matmul(score_grad, query, (1, 0))
        value_part = matmul(prob.astype(jnp.bfloat16), grad, (1, 0))
        for index, part in enumerate((key_part, value_part)):
            two_part[index, g] = part[:length]
            one_part[index, g] = part[length : 2 * length].astype(jnp.bfloat16)
            own_part[index, g] = part[2 * length :]


def two_sum_kernel(one_arrived, three_arrived, two_part, own_part, two_sum, own_sum):
    first_core = lax.axis_index("head") == 0

    @pl.when(first_core)
    def _():
        two_sum[...] = (two_part[...] + three_arrived[...].astype(jnp.float32)).astype(jnp.bfloat16)
        own_sum[...] = own_part[...] + one_arrived[...].astype(jnp.float32)

    @pl.when(jnp.logical_not(first_core))
    def _():
        two_sum[...] = (two_part[...] + one_arrived[...].astype(jnp.float32)).astype(jnp.bfloat16)
        own_sum[...] = own_part[...]


def query_kernel(
    own, one_keys, back_two, back_three, back_four, attended_rows, far_grad, near_grad,
    out, query_grad,
):
    groups, length, width = own.shape[1:]
    per_group = out.shape[0] // groups
    for g in range(groups):
        rows = pl.ds(g * per_group, per_group)
        out[rows] = attended_rows[g].T.reshape(per_group, length, width)
        part = matmul(
            join(back_four[0, g], back_three[0, g], back_two[0, g], one_keys[g], own[0, g]),
            join(far_grad[g], near_grad[g]),
            (0, 0),
        )
        query_grad[rows] = part.astype(jnp.bfloat16).T.reshape(per_group, length, width)


def final_kernel(own_sum, two_sum, four_sum, key_grad, value_grad):
    for index, result in enumerate((key_grad, value_grad)):
        total = own_sum[index] + two_sum[index].astype(jnp.float32)
        result[...] = (total + four_sum[index].astype(jnp.float32)).astype(jnp.bfloat16)


def shards(query_matrix, key_matrix, value_matrix, output_gradient, query_head_spans, slab_offset):
    groups, length, width = key_matrix.shape
    heads = query_matrix.shape[0]
    lanes = heads // groups * length
    half, full = jnp.bfloat16, jnp.float32
    vmem = pl.BlockSpec(memory_space=pltpu.VMEM)
    smem = pl.BlockSpec(memory_space=pltpu.SMEM)
    block_flops = 2 * heads * length * length * width

    def call(kernel, name, flops, outs, arrays, specs=None):
        return pl.pallas_call(
            kernel,
            out_shape=tuple(jax.ShapeDtypeStruct(shape, kind) for shape, kind in outs),
            in_specs=specs or [vmem] * len(arrays),
            out_specs=(vmem,) * len(outs),
            compiler_params=pltpu.CompilerParams(vmem_limit_bytes=40 * 1024 * 1024),
            cost_estimate=pl.CostEstimate(flops=flops, bytes_accessed=0, transcendentals=0),
            name=name,
        )(*arrays)

    def rows_of(count, kind):
        return ((groups, count, lanes), kind)

    pair = ((2, groups, length, width), half)
    wide_pair = ((2, groups, length, width), full)
    stat = rows_of(1, full)
    first_core = lax.axis_index("head") == 0

    own = jnp.stack([key_matrix, value_matrix])
    back_two = shifted(own, "seq", 1)
    queries, grads = query_matrix, output_gradient
    own_copy, own_prob_grad, grad_rows = call(
        prepare_kernel,
        "prepare",
        1,
        [pair, rows_of(length, full), rows_of(width, half)],
        (own, grads),
    )
    back_four = shifted(own_copy, "seq", 2)
    first, own_max, own_total, own_out, own_weights = call(
        own_kernel,
        "own_block",
        1,
        [rows_of(1, jnp.int32), stat, stat, rows_of(width, full), rows_of(length, full)],
        (query_head_spans, slab_offset, queries, own_copy),
        specs=[smem, smem, vmem, vmem],
    )
    back_two, first = lax.optimization_barrier((back_two, first))
    back_one = [
        swapped(jnp.where(first_core, own_copy[index], back_two[index]), "head")
        for index in range(2)
    ]
    near_max, near_total, near_out, near_weights, near_prob_grad, own_factor = call(
        near_forward_kernel,
        "near_forward",
        1,
        [stat, stat, rows_of(width, full), rows_of(2 * length, full), rows_of(2 * length, full),
         stat],
        (first, queries, grads, *back_one, back_two, own_max, own_total, own_out),
    )
    back_four, near_max = lax.optimization_barrier((back_four, near_max))
    back_three = swapped(jnp.where(first_core, back_two, back_four), "head")
    four_scores, four_prob_grad = call(
        four_kernel,
        "four_block",
        1,
        [rows_of(length, full), rows_of(length, full)],
        (first, queries, grads, back_four),
    )
    attended_rows, row_delta, near_factor, prob_half, far_grad, three_part = call(
        far_kernel,
        "far_forward_backward",
        1,
        [rows_of(width, half), stat, stat, rows_of(2 * length, half), rows_of(2 * length, half),
         pair],
        (first, queries, grads, back_three, back_four, four_scores, four_prob_grad, grad_rows,
         near_max, near_total, near_out),
    )
    three_arrived = swapped(three_part, "head")
    (four_part,) = call(
        four_backward_kernel,
        "four_backward",
        1,
        [wide_pair],
        (queries, grads, prob_half, far_grad),
    )
    near_grad, one_part, two_part, own_part = call(
        near_backward_kernel,
        "near_backward",
        1,
        [rows_of(3 * length, half), pair, wide_pair, wide_pair],
        (queries, grads, near_weights, own_weights, near_prob_grad, own_prob_grad, near_factor,
         own_factor, row_delta),
    )
    one_arrived = swapped(one_part, "head")
    three_arrived, near_grad = lax.optimization_barrier((three_arrived, near_grad))
    (four_sum,) = call(four_sum_kernel, "four_sum", 1, [pair], (three_arrived, four_part))
    four_total = shifted(four_sum, "seq", -2)
    two_sum, own_sum = call(
        two_sum_kernel,
        "two_sum",
        1,
        [pair, wide_pair],
        (one_arrived, three_arrived, two_part, own_part),
    )
    two_total = shifted(two_sum, "seq", -1)
    attn_out, query_grad = call(
        query_kernel,
        "query_grad",
        200 * block_flops,
        [(query_matrix.shape, half)] * 2,
        (own_copy, back_one[0], back_two, back_three, back_four, attended_rows, far_grad,
         near_grad),
    )
    key_grad, value_grad = call(
        final_kernel,
        "total",
        1,
        [(key_matrix.shape, half)] * 2,
        (own_sum, two_total, four_total),
    )
    return (attn_out, query_grad, key_grad, value_grad)


def solution(mesh):
    tokens = P(None, ("seq", "head"), None)
    return jax.shard_map(
        shards,
        mesh=mesh,
        in_specs=(tokens, tokens, tokens, tokens, P(), P()),
        out_specs=(tokens, tokens, tokens, tokens),
        check_vma=False,
    )
```

```python
import math

import jax
import jax.numpy as jnp
from jax import lax
from jax.experimental import pallas as pl
from jax.experimental.pallas import tpu as pltpu
from jax.sharding import PartitionSpec as P

REACH = 2
SEGMENT = 512

masked_score = -1e30


def shifted(block, axis, distance):
    devices = range(lax.axis_size(axis))
    route = [(i - distance, i) for i in devices if i - distance in devices]
    return lax.ppermute(block, axis, route)


def swapped(block, axis):
    count = lax.axis_size(axis)
    return lax.ppermute(block, axis, [(i, count - 1 - i) for i in range(count)])


def matmul(left, right, contract):
    return lax.dot_general(
        left, right, ((contract[:1], contract[1:]), ((), ())), preferred_element_type=jnp.float32
    )


def grouped(ref, n, count):
    _, length, width = ref.shape
    return ref[pl.ds(n * count, count)].reshape(count * length, width)


def join(*blocks):
    return jnp.concatenate(blocks, axis=0)


def core_offsets(length):
    core = lax.axis_index("head")
    return core * length, (1 - core) * length


def my_heads(count):
    return pl.ds(lax.axis_index("head") * count, count)


def other_heads(count):
    return pl.ds((1 - lax.axis_index("head")) * count, count)


def lane_tokens(count, length):
    lane = lax.broadcasted_iota(jnp.int32, (1, count * 2 * length), 1)
    token = lane - lane // (2 * length) * (2 * length)
    mine, other = core_offsets(length)
    return jnp.where(token < length, token + mine, token - length + other)


def first_visible(spans, offset, chunks, count, length):
    token = lane_tokens(count, length)
    lane_head = lax.broadcasted_iota(jnp.int32, token.shape, 1) // (2 * length)
    start = lax.axis_index("seq") * 2 * length
    segment_start = token - lax.bitwise_and(offset[0] + start + token, SEGMENT - 1)
    floor = jnp.maximum(segment_start, -start)
    base = lax.axis_index("head") * chunks * count
    result = []
    for n in range(chunks):
        span = jnp.full(token.shape, spans[base + n * count], jnp.int32)
        for a in range(1, count):
            span = jnp.where(lane_head == a, spans[base + n * count + a], span)
        result.append(jnp.maximum(floor, token - span + 1))
    return result


def masked(scores, first, chips_back, token=None):
    length = scores.shape[0] // 2
    row = lax.broadcasted_iota(jnp.int32, (length, scores.shape[1]), 0)
    pieces = []
    for part, offset in enumerate(core_offsets(length)):
        visible = row >= first + (chips_back * 2 * length - offset)
        if token is not None:
            visible &= row <= token - offset
        pieces.append(
            jnp.where(visible, scores[part * length : (part + 1) * length], masked_score)
        )
    return join(*pieces)


def split_kernel(block, *sends):
    for index, send in enumerate(sends):
        send[...] = block[index, other_heads(send.shape[0])]


def thirds(rows):
    return [2 * rows * (i + 1) // 3 - 2 * rows * i // 3 for i in range(3)]


def placed(pieces, rows):
    taken = 0
    for piece in pieces:
        count = piece.shape[0]
        for index in range(2):
            low = max(taken, index * rows)
            high = min(taken + count, (index + 1) * rows)
            if low < high:
                yield index, low - index * rows, piece.at[pl.ds(low - taken, high - low)], high - low
        taken += count


def split_rows_kernel(queries, grads, after, *sends):
    heads = queries.shape[0] // 2
    start = (1 - lax.axis_index("head")) * heads
    for index, row, piece, count in placed(sends, heads):
        piece[...] = (queries, grads)[index][pl.ds(start + row, count)]


def join_own_kernel(own, other_keys, other_values, own_head):
    groups, length = other_keys.shape[:2]
    own_head[:, :, pl.ds(0, length)] = own[:, my_heads(groups)]
    own_head[0, :, pl.ds(length, length)] = other_keys[...]
    own_head[1, :, pl.ds(length, length)] = other_values[...]


def own_kernel(
    spans, offset, queries, grads, first_third, second_third, last_third, own,
    query_head, grad_head, grad_rows, first, own_max, own_total, own_out, own_weights,
    own_prob_grad,
):
    heads, _, width = query_head.shape
    length = queries.shape[1]
    groups = own.shape[1]
    chunks = first.shape[0]
    count = heads // chunks
    query_head[:, pl.ds(0, length)] = queries[my_heads(heads)]
    grad_head[:, pl.ds(0, length)] = grads[my_heads(heads)]
    for index, row, piece, rows in placed((first_third, second_third, last_third), heads):
        (query_head, grad_head)[index][pl.ds(row, rows), pl.ds(length, length)] = piece[...]
    factor = width ** (-0.5) * math.log2(math.e)
    token = lane_tokens(count, length)
    for n, rows in enumerate(first_visible(spans, offset, chunks, count, length)):
        g = n * groups // chunks
        first[n] = rows
        grad = grouped(grad_head, n, count)
        scores = matmul(own[0, g], grouped(query_head, n, count), (1, 1)) * factor
        scores = masked(scores, rows, 0, token)
        row_max = jnp.max(scores, axis=0, keepdims=True)
        weights = jnp.exp2(scores - row_max)
        own_max[n] = row_max
        own_total[n] = jnp.sum(weights, axis=0, keepdims=True)
        own_weights[n] = weights
        own_out[n] = matmul(own[1, g], weights.astype(jnp.bfloat16), (0, 0))
        own_prob_grad[n] = matmul(own[1, g], grad, (1, 1))
        grad_rows[n] = grad.T


def one_back(back_one, one_other, index, g):
    base = lax.axis_index("head") * one_other[index].shape[0]
    return join(back_one[index, base + g], one_other[index][g])


def near_forward_kernel(
    first, query_head, grad_head, back_one, one_keys, one_values, own_max, own_total, own_out,
    near_max, near_total, near_out, near_weights, near_prob_grad, own_factor,
):
    groups = one_keys.shape[0]
    one_other = (one_keys, one_values)
    chunks = first.shape[0]
    heads, _, width = query_head.shape
    count = heads // chunks
    factor = width ** (-0.5) * math.log2(math.e)
    for n in range(chunks):
        g = n * groups // chunks
        values = one_back(back_one, one_other, 1, g)
        scores = matmul(
            one_back(back_one, one_other, 0, g), grouped(query_head, n, count), (1, 1)
        )
        scores = masked(scores * factor, first[n], 1)
        row_max = jnp.maximum(own_max[n], jnp.max(scores, axis=0, keepdims=True))
        weights = jnp.exp2(scores - row_max)
        rescale = jnp.exp2(own_max[n] - row_max)
        own_factor[n] = rescale
        near_max[n] = row_max
        near_total[n] = own_total[n] * rescale + jnp.sum(weights, axis=0, keepdims=True)
        near_weights[n] = weights
        near_out[n] = own_out[n] * rescale + matmul(values, weights.astype(jnp.bfloat16), (0, 0))
        near_prob_grad[n] = matmul(values, grouped(grad_head, n, count), (1, 1))


def far_kernel(
    first, query_head, grad_head, back_two, grad_rows, near_max, near_total, near_out,
    attended_rows, row_delta, near_factor, far_grad, far_part,
):
    groups = back_two.shape[1]
    chunks = first.shape[0]
    heads, _, width = query_head.shape
    count = heads // chunks
    scale = width ** (-0.5)
    parts = {}
    for n in range(chunks):
        g = n * groups // chunks
        query = grouped(query_head, n, count)
        grad = grouped(grad_head, n, count)
        scores = matmul(back_two[0, g], query, (1, 1)) * (scale * math.log2(math.e))
        scores = masked(scores, first[n], 2)
        row_max = jnp.maximum(near_max[n], jnp.max(scores, axis=0, keepdims=True))
        weights = jnp.exp2(scores - row_max)
        rescale = jnp.exp2(near_max[n] - row_max)
        inverse = 1.0 / (near_total[n] * rescale + jnp.sum(weights, axis=0, keepdims=True))
        weighted = matmul(back_two[1, g], weights.astype(jnp.bfloat16), (0, 0))
        attended = ((near_out[n] * rescale + weighted) * inverse).astype(jnp.bfloat16)
        delta = jnp.sum(
            grad_rows[n].astype(jnp.float32) * attended.astype(jnp.float32), axis=0, keepdims=True
        )
        prob = weights * inverse
        prob_grad = matmul(back_two[1, g], grad, (1, 1))
        score_grad = (prob * (prob_grad - delta) * scale).astype(jnp.bfloat16)
        attended_rows[n] = attended
        row_delta[n] = delta
        near_factor[n] = rescale * inverse
        far_grad[n] = score_grad
        pair = (
            matmul(score_grad, query, (1, 0)), matmul(prob.astype(jnp.bfloat16), grad, (1, 0)),
        )
        parts[g] = pair if g not in parts else (parts[g][0] + pair[0], parts[g][1] + pair[1])
        if (n + 1) * groups // chunks != g:
            for index in range(2):
                far_part[index, g] = parts[g][index].astype(jnp.bfloat16)


def near_backward_kernel(
    query_head, grad_head, near_weights, own_weights, near_prob_grad, own_prob_grad, near_factor,
    own_factor, row_delta, near_grad, one_mine, send_keys, send_values, own_part,
):
    chunks = near_weights.shape[0]
    groups, length, width = one_mine.shape[1:]
    count = query_head.shape[0] // chunks
    parts = {}
    for n in range(chunks):
        g = n * groups // chunks
        query = grouped(query_head, n, count)
        grad = grouped(grad_head, n, count)
        prob = join(
            near_weights[n] * near_factor[n], own_weights[n] * (own_factor[n] * near_factor[n])
        )
        prob_grad = join(near_prob_grad[n], own_prob_grad[n])
        score_grad = (prob * (prob_grad - row_delta[n]) * width ** (-0.5)).astype(jnp.bfloat16)
        near_grad[n] = score_grad
        pair = (
            matmul(score_grad, query, (1, 0)), matmul(prob.astype(jnp.bfloat16), grad, (1, 0)),
        )
        parts[g] = pair if g not in parts else (parts[g][0] + pair[0], parts[g][1] + pair[1])
        if (n + 1) * groups // chunks != g:
            for index in range(2):
                one_mine[index, g] = parts[g][index][:length].astype(jnp.bfloat16)
                send = (send_keys, send_values)[index]
                send[g] = parts[g][index][length : 2 * length].astype(jnp.bfloat16)
                own_part[index, g] = parts[g][index][2 * length :]


def join_one_kernel(one_mine, other_keys, other_values, one_part):
    groups = one_mine.shape[1]
    one_part[:, my_heads(groups)] = one_mine[...]
    one_part[0, other_heads(groups)] = other_keys[...]
    one_part[1, other_heads(groups)] = other_values[...]


def query_kernel(
    own, back_one, one_keys, back_two, attended_rows, far_grad, near_grad, after,
    out_mine, query_mine, first_third, second_third, last_third, query_send,
):
    sends = (first_third, second_third, last_third)
    groups = own.shape[1]
    chunks = far_grad.shape[0]
    heads, length, width = out_mine.shape
    count = heads // chunks
    for n in range(chunks):
        g = n * groups // chunks
        rows = pl.ds(n * count, count)
        keys = join(back_two[0, g], one_back(back_one, (one_keys,), 0, g), own[0, g])
        part = matmul(keys, join(far_grad[n], near_grad[n]), (0, 0)).astype(jnp.bfloat16)
        for index, (columns, mine) in enumerate(((attended_rows[n], out_mine), (part, query_mine))):
            block = columns.T.reshape(count, 2 * length, width)
            mine[rows] = block[:, :length]
            query_send[index, rows] = block[:, length:]
    for index, row, piece, taken in placed(sends, heads):
        piece[...] = query_send[index, pl.ds(row, taken)]


def assemble_kernel(
    out_mine, query_mine, first_third, second_third, last_third, out, query_grad, token
):
    heads = out_mine.shape[0]
    start = (1 - lax.axis_index("head")) * heads
    out[my_heads(heads)] = out_mine[...]
    query_grad[my_heads(heads)] = query_mine[...]
    for index, row, piece, count in placed((first_third, second_third, last_third), heads):
        (out, query_grad)[index][pl.ds(start + row, count)] = piece[...]
    token[...] = jnp.zeros(token.shape, token.dtype)


def own_sum_kernel(own_part, far_total, sum_mine, sum_send):
    length = sum_mine.shape[2]
    total = own_part[...] + far_total[...].astype(jnp.float32)
    sum_mine[...] = total[:, :, :length]
    sum_send[...] = total[:, :, length:].astype(jnp.bfloat16)


def final_kernel(sum_mine, sum_other, one_total, after, key_grad, value_grad):
    groups = sum_mine.shape[1]
    mine, other = my_heads(groups), other_heads(groups)
    for index, result in enumerate((key_grad, value_grad)):
        total = sum_mine[index] + one_total[index, mine].astype(jnp.float32)
        result[mine] = total.astype(jnp.bfloat16)
        total = sum_other[index].astype(jnp.float32) + one_total[index, other].astype(jnp.float32)
        result[other] = total.astype(jnp.bfloat16)


def shards(query_matrix, key_matrix, value_matrix, output_gradient, query_head_spans, slab_offset):
    groups, length, width = key_matrix.shape
    heads = query_matrix.shape[0]
    cores = lax.axis_size("head")
    tokens = cores * length
    groups_here, heads_here = groups // cores, heads // cores
    count = max(1, min(heads // groups, 256 // tokens))
    chunks = heads_here // count
    lanes = count * tokens
    half, full = jnp.bfloat16, jnp.float32
    vmem = pl.BlockSpec(memory_space=pltpu.VMEM)
    smem = pl.BlockSpec(memory_space=pltpu.SMEM)

    def call(kernel, name, outs, arrays, scalars=0, scratch=()):
        return pl.pallas_call(
            kernel,
            out_shape=tuple(jax.ShapeDtypeStruct(shape, kind) for shape, kind in outs),
            in_specs=[smem] * scalars + [vmem] * (len(arrays) - scalars),
            out_specs=(vmem,) * len(outs),
            scratch_shapes=scratch,
            compiler_params=pltpu.CompilerParams(vmem_limit_bytes=40 * 1024 * 1024),
            cost_estimate=pl.CostEstimate(flops=1, bytes_accessed=0, transcendentals=0),
            name=name,
        )(*arrays)

    def rows_of(rows, kind):
        return ((chunks, rows, lanes), kind)

    stat = rows_of(1, full)
    whole_pair = ((2, groups, length, width), half)
    half_block = ((groups_here, length, width), half)
    half_pair = ((2, groups_here, length, width), half)
    chip_pair = ((2, groups_here, tokens, width), half)
    half_rows = ((heads_here, length, width), half)
    third_rows = [((rows, length, width), half) for rows in thirds(heads_here)]
    chip_rows = ((heads_here, tokens, width), half)

    own = jnp.stack([key_matrix, value_matrix])
    back_one = shifted(own, "seq", 1)
    own_sends = call(split_kernel, "split_own", [half_block] * 2, (own,))
    (own_head,) = call(
        join_own_kernel, "join_own", [chip_pair], (own, *[swapped(send, "head") for send in own_sends])
    )
    back_two = shifted(own_head, "seq", 2)
    sends = call(
        split_rows_kernel,
        "split_rows",
        third_rows,
        (query_matrix, output_gradient, own),
    )
    (
        query_head, grad_head, grad_rows, first, own_max, own_total, own_out, own_weights,
        own_prob_grad,
    ) = call(
        own_kernel,
        "own_block",
        [
            chip_rows, chip_rows, rows_of(width, half), rows_of(1, jnp.int32), stat, stat,
            rows_of(width, full), rows_of(tokens, full), rows_of(tokens, full),
        ],
        (
            query_head_spans, slab_offset, query_matrix, output_gradient,
            *[swapped(send, "head") for send in sends], own_head,
        ),
        scalars=2,
    )
    back_one, first = lax.optimization_barrier((back_one, first))
    one_sends = call(split_kernel, "split_one", [half_block] * 2, (back_one,))
    one_other = [swapped(send, "head") for send in one_sends]
    near_max, near_total, near_out, near_weights, near_prob_grad, own_factor = call(
        near_forward_kernel,
        "near_forward",
        [stat, stat, rows_of(width, full), rows_of(tokens, full), rows_of(tokens, full), stat],
        (first, query_head, grad_head, back_one, *one_other, own_max, own_total, own_out),
    )
    back_two, near_max = lax.optimization_barrier((back_two, near_max))
    attended_rows, row_delta, near_factor, far_grad, far_part = call(
        far_kernel,
        "far_forward_backward",
        [rows_of(width, half), stat, stat, rows_of(tokens, half), chip_pair],
        (first, query_head, grad_head, back_two, grad_rows, near_max, near_total, near_out),
    )
    far_total = shifted(far_part, "seq", -2)
    near_grad, part_mine, *part_sends, own_part = call(
        near_backward_kernel,
        "near_backward",
        [rows_of(2 * tokens, half), half_pair, half_block, half_block, (chip_pair[0], full)],
        (
            query_head, grad_head, near_weights, own_weights, near_prob_grad, own_prob_grad,
            near_factor, own_factor, row_delta,
        ),
    )
    (one_part,) = call(
        join_one_kernel,
        "join_one",
        [whole_pair],
        (part_mine, *[swapped(send, "head") for send in part_sends]),
    )
    one_total = shifted(one_part, "seq", -1)
    out_mine, query_mine, *sends = call(
        query_kernel,
        "query_grad",
        [half_rows] * 2 + third_rows,
        (own_head, back_one, one_other[0], back_two, attended_rows, far_grad, near_grad, one_part),
        scratch=[pltpu.VMEM((2,) + half_rows[0], half)],
    )
    attn_out, query_grad, token = call(
        assemble_kernel,
        "assemble",
        [(query_matrix.shape, half)] * 2 + [((8, 128), full)],
        (out_mine, query_mine, *[swapped(send, "head") for send in sends]),
    )
    sum_mine, sum_send = call(
        own_sum_kernel, "own_sum", [(half_pair[0], full), half_pair], (own_part, far_total)
    )
    key_grad, value_grad = call(
        final_kernel,
        "total",
        [(key_matrix.shape, half)] * 2,
        (sum_mine, swapped(sum_send, "head"), one_total, token),
    )
    return (attn_out, query_grad, key_grad, value_grad)


def solution(mesh):
    tokens = P(None, ("seq", "head"), None)
    return jax.shard_map(
        shards,
        mesh=mesh,
        in_specs=(tokens, tokens, tokens, tokens, P(), P()),
        out_specs=(tokens, tokens, tokens, tokens),
        check_vma=False,
    )
```

```python
import math

import jax
import jax.numpy as jnp
from jax import lax
from jax.experimental import pallas as pl
from jax.experimental.pallas import tpu as pltpu
from jax.sharding import PartitionSpec as P

REACH = 2
SEGMENT = 512

masked_score = -1e30


def shifted(block, axis, distance):
    devices = range(lax.axis_size(axis))
    route = [(i - distance, i) for i in devices if i - distance in devices]
    return lax.ppermute(block, axis, route)


def swapped(block, axis):
    count = lax.axis_size(axis)
    return lax.ppermute(block, axis, [(i, count - 1 - i) for i in range(count)])


def matmul(left, right, contract):
    return lax.dot_general(
        left, right, ((contract[:1], contract[1:]), ((), ())), preferred_element_type=jnp.float32
    )


def grouped(ref, n, count):
    _, length, width = ref.shape
    return ref[pl.ds(n * count, count)].reshape(count * length, width)


def join(*blocks):
    return jnp.concatenate(blocks, axis=0)


def core_offsets(length):
    core = lax.axis_index("head")
    return core * length, (1 - core) * length


def my_heads(count):
    return pl.ds(lax.axis_index("head") * count, count)


def other_heads(count):
    return pl.ds((1 - lax.axis_index("head")) * count, count)


def lane_tokens(count, length):
    lane = lax.broadcasted_iota(jnp.int32, (1, count * 2 * length), 1)
    token = lane - lane // (2 * length) * (2 * length)
    mine, other = core_offsets(length)
    return jnp.where(token < length, token + mine, token - length + other)


def first_visible(spans, offset, chunks, count, length):
    token = lane_tokens(count, length)
    lane_head = lax.broadcasted_iota(jnp.int32, token.shape, 1) // (2 * length)
    start = lax.axis_index("seq") * 2 * length
    segment_start = token - lax.bitwise_and(offset[0] + start + token, SEGMENT - 1)
    floor = jnp.maximum(segment_start, -start)
    base = lax.axis_index("head") * chunks * count
    result = []
    for n in range(chunks):
        span = jnp.full(token.shape, spans[base + n * count], jnp.int32)
        for a in range(1, count):
            span = jnp.where(lane_head == a, spans[base + n * count + a], span)
        result.append(jnp.maximum(floor, token - span + 1))
    return result


def masked(scores, first, chips_back, token=None):
    length = scores.shape[0] // 2
    row = lax.broadcasted_iota(jnp.int32, (length, scores.shape[1]), 0)
    pieces = []
    for part, offset in enumerate(core_offsets(length)):
        visible = row >= first + (chips_back * 2 * length - offset)
        if token is not None:
            visible &= row <= token - offset
        pieces.append(
            jnp.where(visible, scores[part * length : (part + 1) * length], masked_score)
        )
    return join(*pieces)


def split_kernel(block, *sends):
    for index, send in enumerate(sends):
        send[...] = block[index, other_heads(send.shape[0])]


def thirds(rows):
    return [2 * rows * (i + 1) // 3 - 2 * rows * i // 3 for i in range(3)]


def placed(pieces, rows):
    taken = 0
    for piece in pieces:
        count = piece.shape[0]
        for index in range(2):
            low = max(taken, index * rows)
            high = min(taken + count, (index + 1) * rows)
            if low < high:
                yield index, low - index * rows, piece.at[pl.ds(low - taken, high - low)], high - low
        taken += count


def split_rows_kernel(queries, grads, after, *sends):
    heads = queries.shape[0] // 2
    start = (1 - lax.axis_index("head")) * heads
    for index, row, piece, count in placed(sends, heads):
        piece[...] = (queries, grads)[index][pl.ds(start + row, count)]


def join_own_kernel(own, other_keys, other_values, own_head):
    groups, length = other_keys.shape[:2]
    own_head[:, :, pl.ds(0, length)] = own[:, my_heads(groups)]
    own_head[0, :, pl.ds(length, length)] = other_keys[...]
    own_head[1, :, pl.ds(length, length)] = other_values[...]


def own_kernel(
    spans, offset, queries, grads, first_third, second_third, last_third, own,
    query_head, grad_head, grad_rows, first, own_max, own_total, own_out, own_weights,
    own_prob_grad,
):
    heads, _, width = query_head.shape
    length = queries.shape[1]
    groups = own.shape[1]
    chunks = first.shape[0]
    count = heads // chunks
    query_head[:, pl.ds(0, length)] = queries[my_heads(heads)]
    grad_head[:, pl.ds(0, length)] = grads[my_heads(heads)]
    for index, row, piece, rows in placed((first_third, second_third, last_third), heads):
        (query_head, grad_head)[index][pl.ds(row, rows), pl.ds(length, length)] = piece[...]
    factor = width ** (-0.5) * math.log2(math.e)
    token = lane_tokens(count, length)
    for n, rows in enumerate(first_visible(spans, offset, chunks, count, length)):
        first[n] = rows

    def products(n):
        g = n * groups // chunks
        own_prob_grad[n] = matmul(own[1, g], grouped(grad_head, n, count), (1, 1))
        return (matmul(own[0, g], grouped(query_head, n, count), (1, 1)),)

    def softmax(n, scores):
        scores = masked(scores * factor, first[n], 0, token)
        row_max = jnp.max(scores, axis=0, keepdims=True)
        weights = jnp.exp2(scores - row_max)
        own_max[n] = row_max
        own_total[n] = jnp.sum(weights, axis=0, keepdims=True)
        own_weights[n] = weights
        return (weights.astype(jnp.bfloat16),)

    def weigh(n, halves):
        own_out[n] = matmul(own[1, n * groups // chunks], halves, (0, 0))
        grad_rows[n] = grouped(grad_head, n, count).T

    pipelined(chunks, products, softmax, weigh)


def one_back(back_one, one_other, index, g):
    base = lax.axis_index("head") * one_other[index].shape[0]
    return join(back_one[index, base + g], one_other[index][g])


def near_forward_kernel(
    first, query_head, grad_head, back_one, one_keys, one_values, own_max, own_total, own_out,
    near_max, near_total, near_out, near_weights, near_prob_grad, own_factor,
):
    groups = one_keys.shape[0]
    one_other = (one_keys, one_values)
    chunks = first.shape[0]
    heads, _, width = query_head.shape
    count = heads // chunks
    factor = width ** (-0.5) * math.log2(math.e)

    def products(n):
        g = n * groups // chunks
        keys = one_back(back_one, one_other, 0, g)
        values = one_back(back_one, one_other, 1, g)
        near_prob_grad[n] = matmul(values, grouped(grad_head, n, count), (1, 1))
        return (matmul(keys, grouped(query_head, n, count), (1, 1)),)

    def softmax(n, scores):
        scores = masked(scores * factor, first[n], 1)
        row_max = jnp.maximum(own_max[n], jnp.max(scores, axis=0, keepdims=True))
        weights = jnp.exp2(scores - row_max)
        rescale = jnp.exp2(own_max[n] - row_max)
        own_factor[n] = rescale
        near_max[n] = row_max
        near_total[n] = own_total[n] * rescale + jnp.sum(weights, axis=0, keepdims=True)
        near_weights[n] = weights
        return rescale, weights.astype(jnp.bfloat16)

    def weigh(n, rescale, halves):
        values = one_back(back_one, one_other, 1, n * groups // chunks)
        near_out[n] = own_out[n] * rescale + matmul(values, halves, (0, 0))

    pipelined(chunks, products, softmax, weigh)


def far_kernel(
    first, query_head, grad_head, back_two, grad_rows, near_max, near_total, near_out,
    attended_rows, row_delta, near_factor, far_grad, far_part,
):
    groups = back_two.shape[1]
    chunks = first.shape[0]
    heads, _, width = query_head.shape
    count = heads // chunks
    scale = width ** (-0.5)

    def products(n):
        g = n * groups // chunks
        scores = matmul(back_two[0, g], grouped(query_head, n, count), (1, 1))
        prob_grad = matmul(back_two[1, g], grouped(grad_head, n, count), (1, 1))
        return scores, prob_grad

    def softmax(n, scores, prob_grad):
        g = n * groups // chunks
        scores = masked(scores * (scale * math.log2(math.e)), first[n], 2)
        row_max = jnp.maximum(near_max[n], jnp.max(scores, axis=0, keepdims=True))
        weights = jnp.exp2(scores - row_max)
        rescale = jnp.exp2(near_max[n] - row_max)
        inverse = 1.0 / (near_total[n] * rescale + jnp.sum(weights, axis=0, keepdims=True))
        weighted = matmul(back_two[1, g], weights.astype(jnp.bfloat16), (0, 0))
        attended = ((near_out[n] * rescale + weighted) * inverse).astype(jnp.bfloat16)
        delta = jnp.sum(
            grad_rows[n].astype(jnp.float32) * attended.astype(jnp.float32), axis=0, keepdims=True
        )
        prob = weights * inverse
        score_grad = (prob * (prob_grad - delta)).astype(jnp.bfloat16)
        attended_rows[n] = attended
        row_delta[n] = delta
        near_factor[n] = rescale * inverse
        far_grad[n] = score_grad
        return score_grad, prob.astype(jnp.bfloat16)

    accumulate = accumulator(query_head, grad_head, chunks, groups)

    def store(g, key_part, value_part):
        far_part[0, g] = (key_part * scale).astype(jnp.bfloat16)
        far_part[1, g] = value_part.astype(jnp.bfloat16)

    pipelined(chunks, products, softmax, lambda n, *halves: accumulate(n, *halves, store))


def pipelined(chunks, before, middle, after):
    ready = before(0)
    done = None
    for n in range(chunks):
        upcoming = before(n + 1) if n + 1 < chunks else None
        result = middle(n, *ready)
        if done is not None:
            after(n - 1, *done)
        ready, done = upcoming, result
    after(chunks - 1, *done)


def accumulator(query_head, grad_head, chunks, groups):
    count = query_head.shape[0] // chunks
    parts = {}

    def accumulate(n, score_grad, half, store):
        g = n * groups // chunks
        key_part = matmul(score_grad, grouped(query_head, n, count), (1, 0))
        value_part = matmul(half, grouped(grad_head, n, count), (1, 0))
        if g in parts:
            key_part, value_part = parts[g][0] + key_part, parts[g][1] + value_part
        parts[g] = (key_part, value_part)
        if (n + 1) * groups // chunks != g:
            store(g, key_part, value_part)

    return accumulate


def one_backward_kernel(
    query_head, grad_head, near_weights, near_prob_grad, near_factor, row_delta,
    one_grad, one_mine, send_keys, send_values,
):
    chunks = near_weights.shape[0]
    groups, length, width = one_mine.shape[1:]
    accumulate = accumulator(query_head, grad_head, chunks, groups)

    def store(g, key_part, value_part):
        for index, (part, send) in enumerate(
            ((key_part * width ** (-0.5), send_keys), (value_part, send_values))
        ):
            one_mine[index, g] = part[:length].astype(jnp.bfloat16)
            send[g] = part[length:].astype(jnp.bfloat16)

    for n in range(chunks):
        prob = near_weights[n] * near_factor[n]
        score_grad = (prob * (near_prob_grad[n] - row_delta[n])).astype(jnp.bfloat16)
        one_grad[n] = score_grad
        accumulate(n, score_grad, prob.astype(jnp.bfloat16), store)


def own_backward_kernel(
    query_head, grad_head, own_weights, own_prob_grad, near_factor, own_factor, row_delta,
    after, own_grad, own_part,
):
    chunks = own_weights.shape[0]
    groups, _, width = own_part.shape[1:]
    accumulate = accumulator(query_head, grad_head, chunks, groups)

    def store(g, key_part, value_part):
        own_part[0, g] = key_part * width ** (-0.5)
        own_part[1, g] = value_part

    for n in range(chunks):
        prob = own_weights[n] * (own_factor[n] * near_factor[n])
        score_grad = (prob * (own_prob_grad[n] - row_delta[n])).astype(jnp.bfloat16)
        own_grad[n] = score_grad
        accumulate(n, score_grad, prob.astype(jnp.bfloat16), store)


def join_one_kernel(one_mine, other_keys, other_values, one_part):
    groups = one_mine.shape[1]
    one_part[:, my_heads(groups)] = one_mine[...]
    one_part[0, other_heads(groups)] = other_keys[...]
    one_part[1, other_heads(groups)] = other_values[...]


def query_kernel(
    own, back_one, one_keys, back_two, attended_rows, far_grad, one_grad, own_grad,
    out_mine, query_mine, first_third, second_third, last_third, query_send,
):
    sends = (first_third, second_third, last_third)
    groups = own.shape[1]
    chunks = far_grad.shape[0]
    heads, length, width = out_mine.shape
    count = heads // chunks
    for n in range(chunks):
        g = n * groups // chunks
        rows = pl.ds(n * count, count)
        keys = join(back_two[0, g], one_back(back_one, (one_keys,), 0, g), own[0, g])
        part = matmul(keys, join(far_grad[n], one_grad[n], own_grad[n]), (0, 0))
        part = (part * width ** (-0.5)).astype(jnp.bfloat16)
        for index, (columns, mine) in enumerate(((attended_rows[n], out_mine), (part, query_mine))):
            block = columns.T.reshape(count, 2 * length, width)
            mine[rows] = block[:, :length]
            query_send[index, rows] = block[:, length:]
    for index, row, piece, taken in placed(sends, heads):
        piece[...] = query_send[index, pl.ds(row, taken)]


def assemble_kernel(
    out_mine, query_mine, first_third, second_third, last_third, out, query_grad, token
):
    heads = out_mine.shape[0]
    start = (1 - lax.axis_index("head")) * heads
    out[my_heads(heads)] = out_mine[...]
    query_grad[my_heads(heads)] = query_mine[...]
    for index, row, piece, count in placed((first_third, second_third, last_third), heads):
        (out, query_grad)[index][pl.ds(start + row, count)] = piece[...]
    token[...] = jnp.zeros(token.shape, token.dtype)


def own_sum_kernel(own_part, far_total, sum_mine, sum_send):
    length = sum_mine.shape[2]
    total = own_part[...] + far_total[...].astype(jnp.float32)
    sum_mine[...] = total[:, :, :length]
    sum_send[...] = total[:, :, length:].astype(jnp.bfloat16)


def final_kernel(sum_mine, sum_other, one_total, after, key_grad, value_grad):
    groups = sum_mine.shape[1]
    mine, other = my_heads(groups), other_heads(groups)
    for index, result in enumerate((key_grad, value_grad)):
        total = sum_mine[index] + one_total[index, mine].astype(jnp.float32)
        result[mine] = total.astype(jnp.bfloat16)
        total = sum_other[index].astype(jnp.float32) + one_total[index, other].astype(jnp.float32)
        result[other] = total.astype(jnp.bfloat16)


def shards(query_matrix, key_matrix, value_matrix, output_gradient, query_head_spans, slab_offset):
    groups, length, width = key_matrix.shape
    heads = query_matrix.shape[0]
    cores = lax.axis_size("head")
    tokens = cores * length
    groups_here, heads_here = groups // cores, heads // cores
    count = max(1, min(heads // groups, 256 // tokens))
    chunks = heads_here // count
    lanes = count * tokens
    half, full = jnp.bfloat16, jnp.float32
    vmem = pl.BlockSpec(memory_space=pltpu.VMEM)
    smem = pl.BlockSpec(memory_space=pltpu.SMEM)

    def call(kernel, name, outs, arrays, scalars=0, scratch=()):
        return pl.pallas_call(
            kernel,
            out_shape=tuple(jax.ShapeDtypeStruct(shape, kind) for shape, kind in outs),
            in_specs=[smem] * scalars + [vmem] * (len(arrays) - scalars),
            out_specs=(vmem,) * len(outs),
            scratch_shapes=scratch,
            compiler_params=pltpu.CompilerParams(vmem_limit_bytes=40 * 1024 * 1024),
            cost_estimate=pl.CostEstimate(flops=1, bytes_accessed=0, transcendentals=0),
            name=name,
        )(*arrays)

    def rows_of(rows, kind):
        return ((chunks, rows, lanes), kind)

    stat = rows_of(1, full)
    whole_pair = ((2, groups, length, width), half)
    half_block = ((groups_here, length, width), half)
    half_pair = ((2, groups_here, length, width), half)
    chip_pair = ((2, groups_here, tokens, width), half)
    half_rows = ((heads_here, length, width), half)
    third_rows = [((rows, length, width), half) for rows in thirds(heads_here)]
    chip_rows = ((heads_here, tokens, width), half)

    own = jnp.stack([key_matrix, value_matrix])
    back_one = shifted(own, "seq", 1)
    own_sends = call(split_kernel, "split_own", [half_block] * 2, (own,))
    (own_head,) = call(
        join_own_kernel, "join_own", [chip_pair], (own, *[swapped(send, "head") for send in own_sends])
    )
    back_two = shifted(own_head, "seq", 2)
    sends = call(
        split_rows_kernel,
        "split_rows",
        third_rows,
        (query_matrix, output_gradient, own),
    )
    (
        query_head, grad_head, grad_rows, first, own_max, own_total, own_out, own_weights,
        own_prob_grad,
    ) = call(
        own_kernel,
        "own_block",
        [
            chip_rows, chip_rows, rows_of(width, half), rows_of(1, jnp.int32), stat, stat,
            rows_of(width, full), rows_of(tokens, full), rows_of(tokens, full),
        ],
        (
            query_head_spans, slab_offset, query_matrix, output_gradient,
            *[swapped(send, "head") for send in sends], own_head,
        ),
        scalars=2,
    )
    back_one, first = lax.optimization_barrier((back_one, first))
    one_sends = call(split_kernel, "split_one", [half_block] * 2, (back_one,))
    one_other = [swapped(send, "head") for send in one_sends]
    near_max, near_total, near_out, near_weights, near_prob_grad, own_factor = call(
        near_forward_kernel,
        "near_forward",
        [stat, stat, rows_of(width, full), rows_of(tokens, full), rows_of(tokens, full), stat],
        (first, query_head, grad_head, back_one, *one_other, own_max, own_total, own_out),
    )
    back_two, near_max = lax.optimization_barrier((back_two, near_max))
    attended_rows, row_delta, near_factor, far_grad, far_part = call(
        far_kernel,
        "far_forward_backward",
        [rows_of(width, half), stat, stat, rows_of(tokens, half), chip_pair],
        (first, query_head, grad_head, back_two, grad_rows, near_max, near_total, near_out),
    )
    far_total = shifted(far_part, "seq", -2)
    one_grad, part_mine, *part_sends = call(
        one_backward_kernel,
        "one_backward",
        [rows_of(tokens, half), half_pair, half_block, half_block],
        (query_head, grad_head, near_weights, near_prob_grad, near_factor, row_delta),
    )
    (one_part,) = call(
        join_one_kernel,
        "join_one",
        [whole_pair],
        (part_mine, *[swapped(send, "head") for send in part_sends]),
    )
    one_total = shifted(one_part, "seq", -1)
    own_grad, own_part = call(
        own_backward_kernel,
        "own_backward",
        [rows_of(tokens, half), (chip_pair[0], full)],
        (
            query_head, grad_head, own_weights, own_prob_grad, near_factor, own_factor, row_delta,
            one_part,
        ),
    )
    out_mine, query_mine, *sends = call(
        query_kernel,
        "query_grad",
        [half_rows] * 2 + third_rows,
        (own_head, back_one, one_other[0], back_two, attended_rows, far_grad, one_grad, own_grad),
        scratch=[pltpu.VMEM((2,) + half_rows[0], half)],
    )
    attn_out, query_grad, token = call(
        assemble_kernel,
        "assemble",
        [(query_matrix.shape, half)] * 2 + [((8, 128), full)],
        (out_mine, query_mine, *[swapped(send, "head") for send in sends]),
    )
    sum_mine, sum_send = call(
        own_sum_kernel, "own_sum", [(half_pair[0], full), half_pair], (own_part, far_total)
    )
    key_grad, value_grad = call(
        final_kernel,
        "total",
        [(key_matrix.shape, half)] * 2,
        (sum_mine, swapped(sum_send, "head"), one_total, token),
    )
    return (attn_out, query_grad, key_grad, value_grad)


def solution(mesh):
    tokens = P(None, ("seq", "head"), None)
    return jax.shard_map(
        shards,
        mesh=mesh,
        in_specs=(tokens, tokens, tokens, tokens, P(), P()),
        out_specs=(tokens, tokens, tokens, tokens),
        check_vma=False,
    )
```

```python
import math

import jax
import jax.numpy as jnp
from jax import lax
from jax.experimental import pallas as pl
from jax.experimental.pallas import tpu as pltpu
from jax.sharding import PartitionSpec as P

REACH = 2
SEGMENT = 512

masked_score = -1e30


def shifted(block, axis, distance):
    devices = range(lax.axis_size(axis))
    route = [(i - distance, i) for i in devices if i - distance in devices]
    return lax.ppermute(block, axis, route)


def swapped(block, axis):
    count = lax.axis_size(axis)
    return lax.ppermute(block, axis, [(i, count - 1 - i) for i in range(count)])


def matmul(left, right, contract):
    return lax.dot_general(
        left, right, ((contract[:1], contract[1:]), ((), ())), preferred_element_type=jnp.float32
    )


def grouped(ref, n, count):
    _, length, width = ref.shape
    return ref[pl.ds(n * count, count)].reshape(count * length, width)


def join(*blocks):
    return jnp.concatenate(blocks, axis=0)


def core_offsets(length):
    core = lax.axis_index("head")
    return core * length, (1 - core) * length


def my_heads(count):
    return pl.ds(lax.axis_index("head") * count, count)


def other_heads(count):
    return pl.ds((1 - lax.axis_index("head")) * count, count)


def lane_tokens(count, length):
    lane = lax.broadcasted_iota(jnp.int32, (1, count * 2 * length), 1)
    token = lane - lane // (2 * length) * (2 * length)
    mine, other = core_offsets(length)
    return jnp.where(token < length, token + mine, token - length + other)


def first_visible(spans, offset, chunks, count, length):
    token = lane_tokens(count, length)
    lane_head = lax.broadcasted_iota(jnp.int32, token.shape, 1) // (2 * length)
    start = lax.axis_index("seq") * 2 * length
    segment_start = token - lax.bitwise_and(offset[0] + start + token, SEGMENT - 1)
    floor = jnp.maximum(segment_start, -start)
    base = lax.axis_index("head") * chunks * count
    result = []
    for n in range(chunks):
        span = jnp.full(token.shape, spans[base + n * count], jnp.int32)
        for a in range(1, count):
            span = jnp.where(lane_head == a, spans[base + n * count + a], span)
        result.append(jnp.maximum(floor, token - span + 1))
    return result


def masked(scores, first, chips_back, token=None):
    length = scores.shape[0] // 2
    row = lax.broadcasted_iota(jnp.int32, (length, scores.shape[1]), 0)
    pieces = []
    for part, offset in enumerate(core_offsets(length)):
        visible = row >= first + (chips_back * 2 * length - offset)
        if token is not None:
            visible &= row <= token - offset
        pieces.append(
            jnp.where(visible, scores[part * length : (part + 1) * length], masked_score)
        )
    return join(*pieces)


def split_kernel(block, *sends):
    for index, send in enumerate(sends):
        send[...] = block[index, other_heads(send.shape[0])]


def thirds(rows):
    return [2 * rows * (i + 1) // 3 - 2 * rows * i // 3 for i in range(3)]


def placed(pieces, rows):
    taken = 0
    for piece in pieces:
        count = piece.shape[0]
        for index in range(2):
            low = max(taken, index * rows)
            high = min(taken + count, (index + 1) * rows)
            if low < high:
                yield index, low - index * rows, piece.at[pl.ds(low - taken, high - low)], high - low
        taken += count


def split_rows_kernel(queries, grads, after, *sends):
    heads = queries.shape[0] // 2
    start = (1 - lax.axis_index("head")) * heads
    for index, row, piece, count in placed(sends, heads):
        piece[...] = (queries, grads)[index][pl.ds(start + row, count)]


def join_own_kernel(own, other_keys, other_values, own_head):
    groups, length = other_keys.shape[:2]
    own_head[:, :, pl.ds(0, length)] = own[:, my_heads(groups)]
    own_head[0, :, pl.ds(length, length)] = other_keys[...]
    own_head[1, :, pl.ds(length, length)] = other_values[...]


def own_kernel(
    spans, offset, queries, grads, first_third, second_third, last_third, own,
    query_head, grad_head, grad_rows, first, own_max, own_total, own_out, own_weights,
    own_prob_grad,
):
    heads, _, width = query_head.shape
    length = queries.shape[1]
    groups = own.shape[1]
    chunks = first.shape[0]
    count = heads // chunks
    query_head[:, pl.ds(0, length)] = queries[my_heads(heads)]
    grad_head[:, pl.ds(0, length)] = grads[my_heads(heads)]
    for index, row, piece, rows in placed((first_third, second_third, last_third), heads):
        (query_head, grad_head)[index][pl.ds(row, rows), pl.ds(length, length)] = piece[...]
    factor = width ** (-0.5) * math.log2(math.e)
    token = lane_tokens(count, length)
    for n, rows in enumerate(first_visible(spans, offset, chunks, count, length)):
        first[n] = rows

    def products(n):
        g = n * groups // chunks
        own_prob_grad[n] = matmul(own[1, g], grouped(grad_head, n, count), (1, 1))
        return (matmul(own[0, g], grouped(query_head, n, count), (1, 1)),)

    def softmax(n, scores):
        scores = masked(scores * factor, first[n], 0, token)
        row_max = jnp.max(scores, axis=0, keepdims=True)
        weights = jnp.exp2(scores - row_max)
        own_max[n] = row_max
        own_total[n] = jnp.sum(weights, axis=0, keepdims=True)
        own_weights[n] = weights
        return (weights.astype(jnp.bfloat16),)

    def weigh(n, halves):
        own_out[n] = matmul(own[1, n * groups // chunks], halves, (0, 0))
        grad_rows[n] = grouped(grad_head, n, count).T

    pipelined(chunks, products, softmax, weigh)


def two_back(back_two, two_other, index, g):
    base = lax.axis_index("head") * two_other[index].shape[0]
    return join(back_two[index, base + g], two_other[index][g])


def near_forward_kernel(
    first, query_head, grad_head, back_two, two_keys, two_values, own_max, own_total, own_out,
    near_max, near_total, near_out, near_weights, near_prob_grad, own_factor,
):
    groups = two_keys.shape[0]
    two_other = (two_keys, two_values)
    chunks = first.shape[0]
    heads, _, width = query_head.shape
    count = heads // chunks
    factor = width ** (-0.5) * math.log2(math.e)

    def products(n):
        g = n * groups // chunks
        keys = two_back(back_two, two_other, 0, g)
        values = two_back(back_two, two_other, 1, g)
        near_prob_grad[n] = matmul(values, grouped(grad_head, n, count), (1, 1))
        return (matmul(keys, grouped(query_head, n, count), (1, 1)),)

    def softmax(n, scores):
        scores = masked(scores * factor, first[n], 2)
        row_max = jnp.maximum(own_max[n], jnp.max(scores, axis=0, keepdims=True))
        weights = jnp.exp2(scores - row_max)
        rescale = jnp.exp2(own_max[n] - row_max)
        own_factor[n] = rescale
        near_max[n] = row_max
        near_total[n] = own_total[n] * rescale + jnp.sum(weights, axis=0, keepdims=True)
        near_weights[n] = weights
        return rescale, weights.astype(jnp.bfloat16)

    def weigh(n, rescale, halves):
        values = two_back(back_two, two_other, 1, n * groups // chunks)
        near_out[n] = own_out[n] * rescale + matmul(values, halves, (0, 0))

    pipelined(chunks, products, softmax, weigh)


def last_kernel(
    first, query_head, grad_head, back_one, grad_rows, near_max, near_total, near_out,
    attended_rows, row_delta, near_factor, one_grad, one_part,
):
    groups = back_one.shape[1]
    chunks = first.shape[0]
    heads, _, width = query_head.shape
    count = heads // chunks
    scale = width ** (-0.5)

    def products(n):
        g = n * groups // chunks
        scores = matmul(back_one[0, g], grouped(query_head, n, count), (1, 1))
        prob_grad = matmul(back_one[1, g], grouped(grad_head, n, count), (1, 1))
        return scores, prob_grad

    def softmax(n, scores, prob_grad):
        g = n * groups // chunks
        scores = masked(scores * (scale * math.log2(math.e)), first[n], 1)
        row_max = jnp.maximum(near_max[n], jnp.max(scores, axis=0, keepdims=True))
        weights = jnp.exp2(scores - row_max)
        rescale = jnp.exp2(near_max[n] - row_max)
        inverse = 1.0 / (near_total[n] * rescale + jnp.sum(weights, axis=0, keepdims=True))
        weighted = matmul(back_one[1, g], weights.astype(jnp.bfloat16), (0, 0))
        attended = ((near_out[n] * rescale + weighted) * inverse).astype(jnp.bfloat16)
        delta = jnp.sum(
            grad_rows[n].astype(jnp.float32) * attended.astype(jnp.float32), axis=0, keepdims=True
        )
        prob = weights * inverse
        score_grad = (prob * (prob_grad - delta)).astype(jnp.bfloat16)
        attended_rows[n] = attended
        row_delta[n] = delta
        near_factor[n] = rescale * inverse
        one_grad[n] = score_grad
        return score_grad, prob.astype(jnp.bfloat16)

    accumulate = accumulator(query_head, grad_head, chunks, groups)

    def store(g, key_part, value_part):
        one_part[0, g] = (key_part * scale).astype(jnp.bfloat16)
        one_part[1, g] = value_part.astype(jnp.bfloat16)

    pipelined(chunks, products, softmax, lambda n, *halves: accumulate(n, *halves, store))


def pipelined(chunks, before, middle, after):
    ready = before(0)
    done = None
    for n in range(chunks):
        upcoming = before(n + 1) if n + 1 < chunks else None
        result = middle(n, *ready)
        if done is not None:
            after(n - 1, *done)
        ready, done = upcoming, result
    after(chunks - 1, *done)


def accumulator(query_head, grad_head, chunks, groups):
    count = query_head.shape[0] // chunks
    parts = {}

    def accumulate(n, score_grad, half, store):
        g = n * groups // chunks
        key_part = matmul(score_grad, grouped(query_head, n, count), (1, 0))
        value_part = matmul(half, grouped(grad_head, n, count), (1, 0))
        if g in parts:
            key_part, value_part = parts[g][0] + key_part, parts[g][1] + value_part
        parts[g] = (key_part, value_part)
        if (n + 1) * groups // chunks != g:
            store(g, key_part, value_part)

    return accumulate


def two_backward_kernel(
    query_head, grad_head, near_weights, near_prob_grad, near_factor, row_delta,
    two_grad, two_part,
):
    chunks = near_weights.shape[0]
    groups, _, width = two_part.shape[1:]
    accumulate = accumulator(query_head, grad_head, chunks, groups)

    def store(g, key_part, value_part):
        two_part[0, g] = (key_part * width ** (-0.5)).astype(jnp.bfloat16)
        two_part[1, g] = value_part.astype(jnp.bfloat16)

    for n in range(chunks):
        prob = near_weights[n] * near_factor[n]
        score_grad = (prob * (near_prob_grad[n] - row_delta[n])).astype(jnp.bfloat16)
        two_grad[n] = score_grad
        accumulate(n, score_grad, prob.astype(jnp.bfloat16), store)


def own_backward_kernel(
    query_head, grad_head, own_weights, own_prob_grad, near_factor, own_factor, row_delta,
    after, own_grad, own_part,
):
    chunks = own_weights.shape[0]
    groups, _, width = own_part.shape[1:]
    accumulate = accumulator(query_head, grad_head, chunks, groups)

    def store(g, key_part, value_part):
        own_part[0, g] = key_part * width ** (-0.5)
        own_part[1, g] = value_part

    for n in range(chunks):
        prob = own_weights[n] * (own_factor[n] * near_factor[n])
        score_grad = (prob * (own_prob_grad[n] - row_delta[n])).astype(jnp.bfloat16)
        own_grad[n] = score_grad
        accumulate(n, score_grad, prob.astype(jnp.bfloat16), store)


def join_one_kernel(one_part, one_other, one_joined):
    groups, tokens = one_part.shape[1:3]
    length = tokens // 2
    one_joined[:, my_heads(groups)] = one_part[:, :, pl.ds(0, length)]
    one_joined[:, other_heads(groups)] = one_other[:, :, pl.ds(length, length)]


def query_kernel(
    own, back_one, back_two, two_keys, attended_rows, two_grad, one_grad, own_grad,
    out_mine, query_mine, first_third, second_third, last_third, query_send,
):
    sends = (first_third, second_third, last_third)
    groups = own.shape[1]
    chunks = own_grad.shape[0]
    heads, length, width = out_mine.shape
    count = heads // chunks
    for n in range(chunks):
        g = n * groups // chunks
        rows = pl.ds(n * count, count)
        keys = join(two_back(back_two, (two_keys,), 0, g), back_one[0, g], own[0, g])
        part = matmul(keys, join(two_grad[n], one_grad[n], own_grad[n]), (0, 0))
        part = (part * width ** (-0.5)).astype(jnp.bfloat16)
        for index, (columns, mine) in enumerate(((attended_rows[n], out_mine), (part, query_mine))):
            block = columns.T.reshape(count, 2 * length, width)
            mine[rows] = block[:, :length]
            query_send[index, rows] = block[:, length:]
    for index, row, piece, taken in placed(sends, heads):
        piece[...] = query_send[index, pl.ds(row, taken)]


def assemble_kernel(
    out_mine, query_mine, first_third, second_third, last_third, out, query_grad, token
):
    heads = out_mine.shape[0]
    start = (1 - lax.axis_index("head")) * heads
    out[my_heads(heads)] = out_mine[...]
    query_grad[my_heads(heads)] = query_mine[...]
    for index, row, piece, count in placed((first_third, second_third, last_third), heads):
        (out, query_grad)[index][pl.ds(start + row, count)] = piece[...]
    token[...] = jnp.zeros(token.shape, token.dtype)


def own_sum_kernel(own_part, two_total, sum_mine, sum_send):
    length = sum_mine.shape[2]
    total = own_part[...] + two_total[...].astype(jnp.float32)
    sum_mine[...] = total[:, :, :length]
    sum_send[...] = total[:, :, length:].astype(jnp.bfloat16)


def final_kernel(sum_mine, sum_other, one_total, after, key_grad, value_grad):
    groups = sum_mine.shape[1]
    mine, other = my_heads(groups), other_heads(groups)
    for index, result in enumerate((key_grad, value_grad)):
        total = sum_mine[index] + one_total[index, mine].astype(jnp.float32)
        result[mine] = total.astype(jnp.bfloat16)
        total = sum_other[index].astype(jnp.float32) + one_total[index, other].astype(jnp.float32)
        result[other] = total.astype(jnp.bfloat16)


def shards(query_matrix, key_matrix, value_matrix, output_gradient, query_head_spans, slab_offset):
    groups, length, width = key_matrix.shape
    heads = query_matrix.shape[0]
    cores = lax.axis_size("head")
    tokens = cores * length
    groups_here, heads_here = groups // cores, heads // cores
    count = max(1, min(heads // groups, 256 // tokens))
    chunks = heads_here // count
    lanes = count * tokens
    half, full = jnp.bfloat16, jnp.float32
    vmem = pl.BlockSpec(memory_space=pltpu.VMEM)
    smem = pl.BlockSpec(memory_space=pltpu.SMEM)

    def call(kernel, name, outs, arrays, scalars=0, scratch=()):
        return pl.pallas_call(
            kernel,
            out_shape=tuple(jax.ShapeDtypeStruct(shape, kind) for shape, kind in outs),
            in_specs=[smem] * scalars + [vmem] * (len(arrays) - scalars),
            out_specs=(vmem,) * len(outs),
            scratch_shapes=scratch,
            compiler_params=pltpu.CompilerParams(vmem_limit_bytes=40 * 1024 * 1024),
            cost_estimate=pl.CostEstimate(flops=1, bytes_accessed=0, transcendentals=0),
            name=name,
        )(*arrays)

    def rows_of(rows, kind):
        return ((chunks, rows, lanes), kind)

    stat = rows_of(1, full)
    whole_pair = ((2, groups, length, width), half)
    half_block = ((groups_here, length, width), half)
    half_pair = ((2, groups_here, length, width), half)
    chip_pair = ((2, groups_here, tokens, width), half)
    half_rows = ((heads_here, length, width), half)
    third_rows = [((rows, length, width), half) for rows in thirds(heads_here)]
    chip_rows = ((heads_here, tokens, width), half)

    own = jnp.stack([key_matrix, value_matrix])
    back_two = shifted(own, "seq", 2)
    own_sends = call(split_kernel, "split_own", [half_block] * 2, (own,))
    (own_head,) = call(
        join_own_kernel, "join_own", [chip_pair], (own, *[swapped(send, "head") for send in own_sends])
    )
    back_one = shifted(own_head, "seq", 1)
    sends = call(
        split_rows_kernel,
        "split_rows",
        third_rows,
        (query_matrix, output_gradient, own),
    )
    (
        query_head, grad_head, grad_rows, first, own_max, own_total, own_out, own_weights,
        own_prob_grad,
    ) = call(
        own_kernel,
        "own_block",
        [
            chip_rows, chip_rows, rows_of(width, half), rows_of(1, jnp.int32), stat, stat,
            rows_of(width, full), rows_of(tokens, full), rows_of(tokens, full),
        ],
        (
            query_head_spans, slab_offset, query_matrix, output_gradient,
            *[swapped(send, "head") for send in sends], own_head,
        ),
        scalars=2,
    )
    back_two, first = lax.optimization_barrier((back_two, first))
    two_sends = call(split_kernel, "split_two", [half_block] * 2, (back_two,))
    two_other = [swapped(send, "head") for send in two_sends]
    near_max, near_total, near_out, near_weights, near_prob_grad, own_factor = call(
        near_forward_kernel,
        "near_forward",
        [stat, stat, rows_of(width, full), rows_of(tokens, full), rows_of(tokens, full), stat],
        (first, query_head, grad_head, back_two, *two_other, own_max, own_total, own_out),
    )
    back_one, near_max = lax.optimization_barrier((back_one, near_max))
    attended_rows, row_delta, near_factor, one_grad, chip_part = call(
        last_kernel,
        "last_forward_backward",
        [rows_of(width, half), stat, stat, rows_of(tokens, half), chip_pair],
        (first, query_head, grad_head, back_one, grad_rows, near_max, near_total, near_out),
    )
    chip_other = swapped(chip_part, "head")
    two_grad, two_part = call(
        two_backward_kernel,
        "two_backward",
        [rows_of(tokens, half), chip_pair],
        (query_head, grad_head, near_weights, near_prob_grad, near_factor, row_delta),
    )
    two_total = shifted(two_part, "seq", -2)
    (one_part,) = call(join_one_kernel, "join_one", [whole_pair], (chip_part, chip_other))
    one_total = shifted(one_part, "seq", -1)
    own_grad, own_part = call(
        own_backward_kernel,
        "own_backward",
        [rows_of(tokens, half), (chip_pair[0], full)],
        (
            query_head, grad_head, own_weights, own_prob_grad, near_factor, own_factor, row_delta,
            one_part,
        ),
    )
    out_mine, query_mine, *sends = call(
        query_kernel,
        "query_grad",
        [half_rows] * 2 + third_rows,
        (own_head, back_one, back_two, two_other[0], attended_rows, two_grad, one_grad, own_grad),
        scratch=[pltpu.VMEM((2,) + half_rows[0], half)],
    )
    attn_out, query_grad, token = call(
        assemble_kernel,
        "assemble",
        [(query_matrix.shape, half)] * 2 + [((8, 128), full)],
        (out_mine, query_mine, *[swapped(send, "head") for send in sends]),
    )
    sum_mine, sum_send = call(
        own_sum_kernel, "own_sum", [(half_pair[0], full), half_pair], (own_part, two_total)
    )
    key_grad, value_grad = call(
        final_kernel,
        "total",
        [(key_matrix.shape, half)] * 2,
        (sum_mine, swapped(sum_send, "head"), one_total, token),
    )
    return (attn_out, query_grad, key_grad, value_grad)


def solution(mesh):
    tokens = P(None, ("seq", "head"), None)
    return jax.shard_map(
        shards,
        mesh=mesh,
        in_specs=(tokens, tokens, tokens, tokens, P(), P()),
        out_specs=(tokens, tokens, tokens, tokens),
        check_vma=False,
    )
```

```python
import math

import jax
import jax.numpy as jnp
from jax import lax
from jax.experimental import pallas as pl
from jax.experimental.pallas import tpu as pltpu
from jax.sharding import PartitionSpec as P

REACH = 2
SEGMENT = 512

masked_score = -1e30


def shifted(block, axis, distance):
    devices = range(lax.axis_size(axis))
    route = [(i - distance, i) for i in devices if i - distance in devices]
    return lax.ppermute(block, axis, route)


def swapped(block, axis):
    count = lax.axis_size(axis)
    return lax.ppermute(block, axis, [(i, count - 1 - i) for i in range(count)])


def matmul(left, right, contract):
    return lax.dot_general(
        left, right, ((contract[:1], contract[1:]), ((), ())), preferred_element_type=jnp.float32
    )


def grouped(ref, n, count):
    _, length, width = ref.shape
    return ref[pl.ds(n * count, count)].reshape(count * length, width)


def join(*blocks):
    return jnp.concatenate(blocks, axis=0)


def core_offsets(length):
    core = lax.axis_index("head")
    return core * length, (1 - core) * length


def my_heads(count):
    return pl.ds(lax.axis_index("head") * count, count)


def other_heads(count):
    return pl.ds((1 - lax.axis_index("head")) * count, count)


def lane_tokens(count, length):
    lane = lax.broadcasted_iota(jnp.int32, (1, count * 2 * length), 1)
    token = lane - lane // (2 * length) * (2 * length)
    mine, other = core_offsets(length)
    return jnp.where(token < length, token + mine, token - length + other)


def first_visible(spans, offset, chunks, count, length):
    token = lane_tokens(count, length)
    lane_head = lax.broadcasted_iota(jnp.int32, token.shape, 1) // (2 * length)
    start = lax.axis_index("seq") * 2 * length
    segment_start = token - lax.bitwise_and(offset[0] + start + token, SEGMENT - 1)
    floor = jnp.maximum(segment_start, -start)
    base = lax.axis_index("head") * chunks * count
    result = []
    for n in range(chunks):
        span = jnp.full(token.shape, spans[base + n * count], jnp.int32)
        for a in range(1, count):
            span = jnp.where(lane_head == a, spans[base + n * count + a], span)
        result.append(jnp.maximum(floor, token - span + 1))
    return result


def masked(scores, first, chips_back, token=None):
    length = scores.shape[0] // 2
    row = lax.broadcasted_iota(jnp.int32, (length, scores.shape[1]), 0)
    pieces = []
    for part, offset in enumerate(core_offsets(length)):
        visible = row >= first + (chips_back * 2 * length - offset)
        if token is not None:
            visible &= row <= token - offset
        pieces.append(
            jnp.where(visible, scores[part * length : (part + 1) * length], masked_score)
        )
    return join(*pieces)


def split_kernel(block, *sends):
    for index, send in enumerate(sends):
        send[...] = block[index, other_heads(send.shape[0])]


def join_own_kernel(own, other_keys, other_values, own_head):
    groups, length = other_keys.shape[:2]
    own_head[:, :, pl.ds(0, length)] = own[:, my_heads(groups)]
    own_head[0, :, pl.ds(length, length)] = other_keys[...]
    own_head[1, :, pl.ds(length, length)] = other_values[...]


def own_kernel(
    spans, offset, queries, grads, queries_other, grads_other, own,
    query_head, grad_head, grad_rows, first, own_max, own_total, own_out, own_weights,
    own_prob_grad,
):
    heads, _, width = query_head.shape
    length = queries.shape[1]
    groups = own.shape[1]
    chunks = first.shape[0]
    count = heads // chunks
    mine = my_heads(heads)
    query_head[:, pl.ds(0, length)] = queries[mine]
    query_head[:, pl.ds(length, length)] = queries_other[mine]
    grad_head[:, pl.ds(0, length)] = grads[mine]
    grad_head[:, pl.ds(length, length)] = grads_other[mine]
    factor = width ** (-0.5) * math.log2(math.e)
    token = lane_tokens(count, length)
    for n, rows in enumerate(first_visible(spans, offset, chunks, count, length)):
        first[n] = rows

    def products(n):
        g = n * groups // chunks
        own_prob_grad[n] = matmul(own[1, g], grouped(grad_head, n, count), (1, 1))
        return (matmul(own[0, g], grouped(query_head, n, count), (1, 1)),)

    def softmax(n, scores):
        scores = masked(scores * factor, first[n], 0, token)
        row_max = jnp.max(scores, axis=0, keepdims=True)
        weights = jnp.exp2(scores - row_max)
        own_max[n] = row_max
        own_total[n] = jnp.sum(weights, axis=0, keepdims=True)
        own_weights[n] = weights
        return (weights.astype(jnp.bfloat16),)

    def weigh(n, halves):
        own_out[n] = matmul(own[1, n * groups // chunks], halves, (0, 0))
        grad_rows[n] = grouped(grad_head, n, count).T

    pipelined(chunks, products, softmax, weigh)


def one_back(back_one, one_other, index, g):
    base = lax.axis_index("head") * one_other[index].shape[0]
    return join(back_one[index, base + g], one_other[index][g])


def near_forward_kernel(
    first, query_head, grad_head, back_one, one_keys, one_values, own_max, own_total, own_out,
    near_max, near_total, near_out, near_weights, near_prob_grad, own_factor,
):
    groups = one_keys.shape[0]
    one_other = (one_keys, one_values)
    chunks = first.shape[0]
    heads, _, width = query_head.shape
    count = heads // chunks
    factor = width ** (-0.5) * math.log2(math.e)

    def products(n):
        g = n * groups // chunks
        keys = one_back(back_one, one_other, 0, g)
        values = one_back(back_one, one_other, 1, g)
        near_prob_grad[n] = matmul(values, grouped(grad_head, n, count), (1, 1))
        return (matmul(keys, grouped(query_head, n, count), (1, 1)),)

    def softmax(n, scores):
        scores = masked(scores * factor, first[n], 1)
        row_max = jnp.maximum(own_max[n], jnp.max(scores, axis=0, keepdims=True))
        weights = jnp.exp2(scores - row_max)
        rescale = jnp.exp2(own_max[n] - row_max)
        own_factor[n] = rescale
        near_max[n] = row_max
        near_total[n] = own_total[n] * rescale + jnp.sum(weights, axis=0, keepdims=True)
        near_weights[n] = weights
        return rescale, weights.astype(jnp.bfloat16)

    def weigh(n, rescale, halves):
        values = one_back(back_one, one_other, 1, n * groups // chunks)
        near_out[n] = own_out[n] * rescale + matmul(values, halves, (0, 0))

    pipelined(chunks, products, softmax, weigh)


def far_kernel(
    first, query_head, grad_head, back_two, grad_rows, near_max, near_total, near_out,
    attended_rows, row_delta, near_factor, far_grad, far_part,
):
    groups = back_two.shape[1]
    chunks = first.shape[0]
    heads, _, width = query_head.shape
    count = heads // chunks
    scale = width ** (-0.5)

    def products(n):
        g = n * groups // chunks
        scores = matmul(back_two[0, g], grouped(query_head, n, count), (1, 1))
        prob_grad = matmul(back_two[1, g], grouped(grad_head, n, count), (1, 1))
        return scores, prob_grad

    def softmax(n, scores, prob_grad):
        g = n * groups // chunks
        scores = masked(scores * (scale * math.log2(math.e)), first[n], 2)
        row_max = jnp.maximum(near_max[n], jnp.max(scores, axis=0, keepdims=True))
        weights = jnp.exp2(scores - row_max)
        rescale = jnp.exp2(near_max[n] - row_max)
        inverse = 1.0 / (near_total[n] * rescale + jnp.sum(weights, axis=0, keepdims=True))
        weighted = matmul(back_two[1, g], weights.astype(jnp.bfloat16), (0, 0))
        attended = ((near_out[n] * rescale + weighted) * inverse).astype(jnp.bfloat16)
        delta = jnp.sum(
            grad_rows[n].astype(jnp.float32) * attended.astype(jnp.float32), axis=0, keepdims=True
        )
        prob = weights * inverse
        score_grad = (prob * (prob_grad - delta)).astype(jnp.bfloat16)
        attended_rows[n] = attended
        row_delta[n] = delta
        near_factor[n] = rescale * inverse
        far_grad[n] = score_grad
        return score_grad, prob.astype(jnp.bfloat16)

    accumulate = accumulator(query_head, grad_head, chunks, groups)

    def store(g, key_part, value_part):
        far_part[0, g] = (key_part * scale).astype(jnp.bfloat16)
        far_part[1, g] = value_part.astype(jnp.bfloat16)

    pipelined(chunks, products, softmax, lambda n, *halves: accumulate(n, *halves, store))


def pipelined(chunks, before, middle, after):
    ready = before(0)
    done = None
    for n in range(chunks):
        upcoming = before(n + 1) if n + 1 < chunks else None
        result = middle(n, *ready)
        if done is not None:
            after(n - 1, *done)
        ready, done = upcoming, result
    after(chunks - 1, *done)


def accumulator(query_head, grad_head, chunks, groups):
    count = query_head.shape[0] // chunks
    parts = {}

    def accumulate(n, score_grad, half, store):
        g = n * groups // chunks
        key_part = matmul(score_grad, grouped(query_head, n, count), (1, 0))
        value_part = matmul(half, grouped(grad_head, n, count), (1, 0))
        if g in parts:
            key_part, value_part = parts[g][0] + key_part, parts[g][1] + value_part
        parts[g] = (key_part, value_part)
        if (n + 1) * groups // chunks != g:
            store(g, key_part, value_part)

    return accumulate


def one_backward_kernel(
    query_head, grad_head, near_weights, near_prob_grad, near_factor, row_delta,
    one_grad, one_mine, send_keys, send_values,
):
    chunks = near_weights.shape[0]
    groups, length, width = one_mine.shape[1:]
    accumulate = accumulator(query_head, grad_head, chunks, groups)

    def store(g, key_part, value_part):
        for index, (part, send) in enumerate(
            ((key_part * width ** (-0.5), send_keys), (value_part, send_values))
        ):
            one_mine[index, g] = part[:length].astype(jnp.bfloat16)
            send[g] = part[length:].astype(jnp.bfloat16)

    for n in range(chunks):
        prob = near_weights[n] * near_factor[n]
        score_grad = (prob * (near_prob_grad[n] - row_delta[n])).astype(jnp.bfloat16)
        one_grad[n] = score_grad
        accumulate(n, score_grad, prob.astype(jnp.bfloat16), store)


def own_backward_kernel(
    query_head, grad_head, own_weights, own_prob_grad, near_factor, own_factor, row_delta,
    own_grad, own_part,
):
    chunks = own_weights.shape[0]
    groups, _, width = own_part.shape[1:]
    accumulate = accumulator(query_head, grad_head, chunks, groups)

    def store(g, key_part, value_part):
        own_part[0, g] = key_part * width ** (-0.5)
        own_part[1, g] = value_part

    for n in range(chunks):
        prob = own_weights[n] * (own_factor[n] * near_factor[n])
        score_grad = (prob * (own_prob_grad[n] - row_delta[n])).astype(jnp.bfloat16)
        own_grad[n] = score_grad
        accumulate(n, score_grad, prob.astype(jnp.bfloat16), store)


def join_one_kernel(one_mine, other_keys, other_values, after, one_part):
    groups = one_mine.shape[1]
    one_part[:, my_heads(groups)] = one_mine[...]
    one_part[0, other_heads(groups)] = other_keys[...]
    one_part[1, other_heads(groups)] = other_values[...]


def query_kernel(
    own, back_one, one_keys, back_two, attended_rows, far_grad, one_grad, own_grad,
    out_mine, query_mine, out_send, query_send,
):
    groups = own.shape[1]
    chunks = far_grad.shape[0]
    heads, length, width = out_mine.shape
    count = heads // chunks
    for n in range(chunks):
        g = n * groups // chunks
        rows = pl.ds(n * count, count)
        keys = join(back_two[0, g], one_back(back_one, (one_keys,), 0, g), own[0, g])
        part = matmul(keys, join(far_grad[n], one_grad[n], own_grad[n]), (0, 0))
        part = (part * width ** (-0.5)).astype(jnp.bfloat16)
        for columns, mine, send in (
            (attended_rows[n], out_mine, out_send), (part, query_mine, query_send),
        ):
            block = columns.T.reshape(count, 2 * length, width)
            mine[rows] = block[:, :length]
            send[rows] = block[:, length:]


def assemble_kernel(
    out_mine, query_mine, out_other, query_other, out, query_grad, token
):
    mine, other = my_heads(out_mine.shape[0]), other_heads(out_mine.shape[0])
    out[mine] = out_mine[...]
    out[other] = out_other[...]
    query_grad[mine] = query_mine[...]
    query_grad[other] = query_other[...]
    token[...] = jnp.zeros(token.shape, token.dtype)


def own_sum_kernel(own_part, far_total, sum_mine, sum_send):
    length = sum_mine.shape[2]
    total = own_part[...] + far_total[...].astype(jnp.float32)
    sum_mine[...] = total[:, :, :length]
    sum_send[...] = total[:, :, length:].astype(jnp.bfloat16)


def final_kernel(sum_mine, sum_other, one_total, after, key_grad, value_grad):
    groups = sum_mine.shape[1]
    mine, other = my_heads(groups), other_heads(groups)
    for index, result in enumerate((key_grad, value_grad)):
        total = sum_mine[index] + one_total[index, mine].astype(jnp.float32)
        result[mine] = total.astype(jnp.bfloat16)
        total = sum_other[index].astype(jnp.float32) + one_total[index, other].astype(jnp.float32)
        result[other] = total.astype(jnp.bfloat16)


def shards(query_matrix, key_matrix, value_matrix, output_gradient, query_head_spans, slab_offset):
    groups, length, width = key_matrix.shape
    heads = query_matrix.shape[0]
    cores = lax.axis_size("head")
    tokens = cores * length
    groups_here, heads_here = groups // cores, heads // cores
    count = max(1, min(heads // groups, 256 // tokens))
    chunks = heads_here // count
    lanes = count * tokens
    half, full = jnp.bfloat16, jnp.float32
    vmem = pl.BlockSpec(memory_space=pltpu.VMEM)
    smem = pl.BlockSpec(memory_space=pltpu.SMEM)

    def call(kernel, name, outs, arrays, scalars=0, scratch=()):
        return pl.pallas_call(
            kernel,
            out_shape=tuple(jax.ShapeDtypeStruct(shape, kind) for shape, kind in outs),
            in_specs=[smem] * scalars + [vmem] * (len(arrays) - scalars),
            out_specs=(vmem,) * len(outs),
            scratch_shapes=scratch,
            compiler_params=pltpu.CompilerParams(vmem_limit_bytes=40 * 1024 * 1024),
            cost_estimate=pl.CostEstimate(flops=1, bytes_accessed=0, transcendentals=0),
            name=name,
        )(*arrays)

    def rows_of(rows, kind):
        return ((chunks, rows, lanes), kind)

    stat = rows_of(1, full)
    whole_pair = ((2, groups, length, width), half)
    half_block = ((groups_here, length, width), half)
    half_pair = ((2, groups_here, length, width), half)
    chip_pair = ((2, groups_here, tokens, width), half)
    half_rows = ((heads_here, length, width), half)
    chip_rows = ((heads_here, tokens, width), half)

    own = jnp.stack([key_matrix, value_matrix])
    back_one = shifted(own, "seq", 1)
    own_sends = call(split_kernel, "split_own", [half_block] * 2, (own,))
    (own_head,) = call(
        join_own_kernel, "join_own", [chip_pair], (own, *[swapped(send, "head") for send in own_sends])
    )
    back_two = shifted(own_head, "seq", 2)
    (
        query_head, grad_head, grad_rows, first, own_max, own_total, own_out, own_weights,
        own_prob_grad,
    ) = call(
        own_kernel,
        "own_block",
        [
            chip_rows, chip_rows, rows_of(width, half), rows_of(1, jnp.int32), stat, stat,
            rows_of(width, full), rows_of(tokens, full), rows_of(tokens, full),
        ],
        (
            query_head_spans, slab_offset, query_matrix, output_gradient,
            swapped(query_matrix, "head"), swapped(output_gradient, "head"), own_head,
        ),
        scalars=2,
    )
    back_one, first = lax.optimization_barrier((back_one, first))
    one_sends = call(split_kernel, "split_one", [half_block] * 2, (back_one,))
    one_other = [swapped(send, "head") for send in one_sends]
    near_max, near_total, near_out, near_weights, near_prob_grad, own_factor = call(
        near_forward_kernel,
        "near_forward",
        [stat, stat, rows_of(width, full), rows_of(tokens, full), rows_of(tokens, full), stat],
        (first, query_head, grad_head, back_one, *one_other, own_max, own_total, own_out),
    )
    back_two, near_max = lax.optimization_barrier((back_two, near_max))
    attended_rows, row_delta, near_factor, far_grad, far_part = call(
        far_kernel,
        "far_forward_backward",
        [rows_of(width, half), stat, stat, rows_of(tokens, half), chip_pair],
        (first, query_head, grad_head, back_two, grad_rows, near_max, near_total, near_out),
    )
    far_total = shifted(far_part, "seq", -2)
    one_grad, part_mine, *part_sends = call(
        one_backward_kernel,
        "one_backward",
        [rows_of(tokens, half), half_pair, half_block, half_block],
        (query_head, grad_head, near_weights, near_prob_grad, near_factor, row_delta),
    )
    one_arrived = [swapped(send, "head") for send in part_sends]
    own_grad, own_part = call(
        own_backward_kernel,
        "own_backward",
        [rows_of(tokens, half), (chip_pair[0], full)],
        (
            query_head, grad_head, own_weights, own_prob_grad, near_factor, own_factor, row_delta,
        ),
    )
    out_mine, query_mine, out_send, query_send = call(
        query_kernel,
        "query_grad",
        [half_rows] * 4,
        (own_head, back_one, one_other[0], back_two, attended_rows, far_grad, one_grad, own_grad),
    )
    (one_part,) = call(
        join_one_kernel,
        "join_one",
        [whole_pair],
        (part_mine, *one_arrived, query_send),
    )
    one_total = shifted(one_part, "seq", -1)
    attn_out, query_grad, token = call(
        assemble_kernel,
        "assemble",
        [(query_matrix.shape, half)] * 2 + [((8, 128), full)],
        (out_mine, query_mine, swapped(out_send, "head"), swapped(query_send, "head")),
    )
    sum_mine, sum_send = call(
        own_sum_kernel, "own_sum", [(half_pair[0], full), half_pair], (own_part, far_total)
    )
    key_grad, value_grad = call(
        final_kernel,
        "total",
        [(key_matrix.shape, half)] * 2,
        (sum_mine, swapped(sum_send, "head"), one_total, token),
    )
    return (attn_out, query_grad, key_grad, value_grad)


def solution(mesh):
    tokens = P(None, ("seq", "head"), None)
    return jax.shard_map(
        shards,
        mesh=mesh,
        in_specs=(tokens, tokens, tokens, tokens, P(), P()),
        out_specs=(tokens, tokens, tokens, tokens),
        check_vma=False,
    )
```

```python
import math

import jax
import jax.numpy as jnp
from jax import lax
from jax.experimental import pallas as pl
from jax.experimental.pallas import tpu as pltpu
from jax.sharding import PartitionSpec as P

REACH = 2
SEGMENT = 512

masked_score = -1e30


def shifted(block, axis, distance):
    devices = range(lax.axis_size(axis))
    route = [(i - distance, i) for i in devices if i - distance in devices]
    return lax.ppermute(block, axis, route)


def swapped(block, axis):
    count = lax.axis_size(axis)
    return lax.ppermute(block, axis, [(i, count - 1 - i) for i in range(count)])


def matmul(left, right, contract):
    return lax.dot_general(
        left, right, ((contract[:1], contract[1:]), ((), ())), preferred_element_type=jnp.float32
    )


def grouped(ref, n, count):
    _, length, width = ref.shape
    return ref[pl.ds(n * count, count)].reshape(count * length, width)


def join(*blocks):
    return jnp.concatenate(blocks, axis=0)


def core_offsets(length):
    core = lax.axis_index("head")
    return core * length, (1 - core) * length


def my_heads(count):
    return pl.ds(lax.axis_index("head") * count, count)


def other_heads(count):
    return pl.ds((1 - lax.axis_index("head")) * count, count)


def lane_tokens(count, length):
    lane = lax.broadcasted_iota(jnp.int32, (1, count * 2 * length), 1)
    token = lane - lane // (2 * length) * (2 * length)
    mine, other = core_offsets(length)
    return jnp.where(token < length, token + mine, token - length + other)


def first_visible(spans, offset, chunks, count, length):
    token = lane_tokens(count, length)
    lane_head = lax.broadcasted_iota(jnp.int32, token.shape, 1) // (2 * length)
    start = lax.axis_index("seq") * 2 * length
    segment_start = token - lax.bitwise_and(offset[0] + start + token, SEGMENT - 1)
    floor = jnp.maximum(segment_start, -start)
    base = lax.axis_index("head") * chunks * count
    result = []
    for n in range(chunks):
        span = jnp.full(token.shape, spans[base + n * count], jnp.int32)
        for a in range(1, count):
            span = jnp.where(lane_head == a, spans[base + n * count + a], span)
        result.append(jnp.maximum(floor, token - span + 1))
    return result


def masked(scores, first, chips_back, token=None):
    length = scores.shape[0] // 2
    row = lax.broadcasted_iota(jnp.int32, (length, scores.shape[1]), 0)
    pieces = []
    for part, offset in enumerate(core_offsets(length)):
        visible = row >= first + (chips_back * 2 * length - offset)
        if token is not None:
            visible &= row <= token - offset
        pieces.append(
            jnp.where(visible, scores[part * length : (part + 1) * length], masked_score)
        )
    return join(*pieces)


def split_kernel(block, *sends):
    for index, send in enumerate(sends):
        send[...] = block[index, other_heads(send.shape[0])]


def thirds(rows):
    return [2 * rows * (i + 1) // 3 - 2 * rows * i // 3 for i in range(3)]


def placed(pieces, rows):
    taken = 0
    for piece in pieces:
        count = piece.shape[0]
        for index in range(2):
            low = max(taken, index * rows)
            high = min(taken + count, (index + 1) * rows)
            if low < high:
                yield index, low - index * rows, piece.at[pl.ds(low - taken, high - low)], high - low
        taken += count


def split_rows_kernel(queries, grads, after, *sends):
    heads = queries.shape[0] // 2
    start = (1 - lax.axis_index("head")) * heads
    for index, row, piece, count in placed(sends, heads):
        piece[...] = (queries, grads)[index][pl.ds(start + row, count)]


def split_own_kernel(own, own_send):
    own_send[...] = own[:, other_heads(own_send.shape[1])]


def join_own_kernel(own, own_other, own_head):
    groups, length = own_other.shape[1:3]
    own_head[:, :, pl.ds(0, length)] = own[:, my_heads(groups)]
    own_head[:, :, pl.ds(length, length)] = own_other[...]


def own_kernel(
    spans, offset, queries, grads, first_third, second_third, last_third, own,
    query_head, grad_head, grad_rows, first, own_max, own_total, own_out, own_weights,
    own_prob_grad,
):
    heads, _, width = query_head.shape
    length = queries.shape[1]
    groups = own.shape[1]
    chunks = first.shape[0]
    count = heads // chunks
    query_head[:, pl.ds(0, length)] = queries[my_heads(heads)]
    grad_head[:, pl.ds(0, length)] = grads[my_heads(heads)]
    for index, row, piece, rows in placed((first_third, second_third, last_third), heads):
        (query_head, grad_head)[index][pl.ds(row, rows), pl.ds(length, length)] = piece[...]
    factor = width ** (-0.5) * math.log2(math.e)
    token = lane_tokens(count, length)
    for n, rows in enumerate(first_visible(spans, offset, chunks, count, length)):
        first[n] = rows

    def products(n):
        g = n * groups // chunks
        own_prob_grad[n] = matmul(own[1, g], grouped(grad_head, n, count), (1, 1))
        return (matmul(own[0, g], grouped(query_head, n, count), (1, 1)),)

    def softmax(n, scores):
        scores = masked(scores * factor, first[n], 0, token)
        row_max = jnp.max(scores, axis=0, keepdims=True)
        weights = jnp.exp2(scores - row_max)
        own_max[n] = row_max
        own_total[n] = jnp.sum(weights, axis=0, keepdims=True)
        own_weights[n] = weights
        return (weights.astype(jnp.bfloat16),)

    def weigh(n, halves):
        own_out[n] = matmul(own[1, n * groups // chunks], halves, (0, 0))
        grad_rows[n] = grouped(grad_head, n, count).T

    pipelined(chunks, products, softmax, weigh)


def two_back(back_two, two_other, index, g):
    base = lax.axis_index("head") * two_other[index].shape[0]
    return join(back_two[index, base + g], two_other[index][g])


def near_forward_kernel(
    first, query_head, grad_head, back_two, two_keys, two_values, own_max, own_total, own_out,
    near_max, near_total, near_out, near_weights, near_prob_grad, own_factor,
):
    groups = two_keys.shape[0]
    two_other = (two_keys, two_values)
    chunks = first.shape[0]
    heads, _, width = query_head.shape
    count = heads // chunks
    factor = width ** (-0.5) * math.log2(math.e)

    def products(n):
        g = n * groups // chunks
        keys = two_back(back_two, two_other, 0, g)
        values = two_back(back_two, two_other, 1, g)
        near_prob_grad[n] = matmul(values, grouped(grad_head, n, count), (1, 1))
        return (matmul(keys, grouped(query_head, n, count), (1, 1)),)

    def softmax(n, scores):
        scores = masked(scores * factor, first[n], 2)
        row_max = jnp.maximum(own_max[n], jnp.max(scores, axis=0, keepdims=True))
        weights = jnp.exp2(scores - row_max)
        rescale = jnp.exp2(own_max[n] - row_max)
        own_factor[n] = rescale
        near_max[n] = row_max
        near_total[n] = own_total[n] * rescale + jnp.sum(weights, axis=0, keepdims=True)
        near_weights[n] = weights
        return rescale, weights.astype(jnp.bfloat16)

    def weigh(n, rescale, halves):
        values = two_back(back_two, two_other, 1, n * groups // chunks)
        near_out[n] = own_out[n] * rescale + matmul(values, halves, (0, 0))

    pipelined(chunks, products, softmax, weigh)


def last_kernel(
    first, query_head, grad_head, back_one, grad_rows, near_max, near_total, near_out,
    attended_rows, row_delta, near_factor, one_grad, one_part,
):
    groups = back_one.shape[1]
    chunks = first.shape[0]
    heads, _, width = query_head.shape
    count = heads // chunks
    scale = width ** (-0.5)

    def products(n):
        g = n * groups // chunks
        scores = matmul(back_one[0, g], grouped(query_head, n, count), (1, 1))
        prob_grad = matmul(back_one[1, g], grouped(grad_head, n, count), (1, 1))
        return scores, prob_grad

    def softmax(n, scores, prob_grad):
        g = n * groups // chunks
        scores = masked(scores * (scale * math.log2(math.e)), first[n], 1)
        row_max = jnp.maximum(near_max[n], jnp.max(scores, axis=0, keepdims=True))
        weights = jnp.exp2(scores - row_max)
        rescale = jnp.exp2(near_max[n] - row_max)
        inverse = 1.0 / (near_total[n] * rescale + jnp.sum(weights, axis=0, keepdims=True))
        weighted = matmul(back_one[1, g], weights.astype(jnp.bfloat16), (0, 0))
        attended = ((near_out[n] * rescale + weighted) * inverse).astype(jnp.bfloat16)
        delta = jnp.sum(
            grad_rows[n].astype(jnp.float32) * attended.astype(jnp.float32), axis=0, keepdims=True
        )
        prob = weights * inverse
        score_grad = (prob * (prob_grad - delta)).astype(jnp.bfloat16)
        attended_rows[n] = attended
        row_delta[n] = delta
        near_factor[n] = rescale * inverse
        one_grad[n] = score_grad
        return score_grad, prob.astype(jnp.bfloat16)

    accumulate = accumulator(query_head, grad_head, chunks, groups)

    def store(g, key_part, value_part):
        one_part[0, g] = (key_part * scale).astype(jnp.bfloat16)
        one_part[1, g] = value_part.astype(jnp.bfloat16)

    pipelined(chunks, products, softmax, lambda n, *halves: accumulate(n, *halves, store))


def pipelined(chunks, before, middle, after):
    ready = before(0)
    done = None
    for n in range(chunks):
        upcoming = before(n + 1) if n + 1 < chunks else None
        result = middle(n, *ready)
        if done is not None:
            after(n - 1, *done)
        ready, done = upcoming, result
    after(chunks - 1, *done)


def accumulator(query_head, grad_head, chunks, groups):
    count = query_head.shape[0] // chunks
    parts = {}

    def accumulate(n, score_grad, half, store):
        g = n * groups // chunks
        key_part = matmul(score_grad, grouped(query_head, n, count), (1, 0))
        value_part = matmul(half, grouped(grad_head, n, count), (1, 0))
        if g in parts:
            key_part, value_part = parts[g][0] + key_part, parts[g][1] + value_part
        parts[g] = (key_part, value_part)
        if (n + 1) * groups // chunks != g:
            store(g, key_part, value_part)

    return accumulate


def two_backward_kernel(
    query_head, grad_head, near_weights, near_prob_grad, near_factor, row_delta,
    two_grad, two_part,
):
    chunks = near_weights.shape[0]
    groups, _, width = two_part.shape[1:]
    accumulate = accumulator(query_head, grad_head, chunks, groups)

    def store(g, key_part, value_part):
        two_part[0, g] = (key_part * width ** (-0.5)).astype(jnp.bfloat16)
        two_part[1, g] = value_part.astype(jnp.bfloat16)

    for n in range(chunks):
        prob = near_weights[n] * near_factor[n]
        score_grad = (prob * (near_prob_grad[n] - row_delta[n])).astype(jnp.bfloat16)
        two_grad[n] = score_grad
        accumulate(n, score_grad, prob.astype(jnp.bfloat16), store)


def own_backward_kernel(
    query_head, grad_head, own_weights, own_prob_grad, near_factor, own_factor, row_delta,
    after, own_grad, own_part,
):
    chunks = own_weights.shape[0]
    groups, _, width = own_part.shape[1:]
    accumulate = accumulator(query_head, grad_head, chunks, groups)

    def store(g, key_part, value_part):
        own_part[0, g] = key_part * width ** (-0.5)
        own_part[1, g] = value_part

    for n in range(chunks):
        prob = own_weights[n] * (own_factor[n] * near_factor[n])
        score_grad = (prob * (own_prob_grad[n] - row_delta[n])).astype(jnp.bfloat16)
        own_grad[n] = score_grad
        accumulate(n, score_grad, prob.astype(jnp.bfloat16), store)


def join_one_kernel(one_part, one_other, one_joined):
    groups, tokens = one_part.shape[1:3]
    length = tokens // 2
    one_joined[:, my_heads(groups)] = one_part[:, :, pl.ds(0, length)]
    one_joined[:, other_heads(groups)] = one_other[:, :, pl.ds(length, length)]


def query_kernel(
    own, back_one, back_two, two_keys, attended_rows, two_grad, one_grad, own_grad,
    out_mine, query_mine, first_third, second_third, last_third, query_send,
):
    sends = (first_third, second_third, last_third)
    groups = own.shape[1]
    chunks = own_grad.shape[0]
    heads, length, width = out_mine.shape
    count = heads // chunks
    for n in range(chunks):
        g = n * groups // chunks
        rows = pl.ds(n * count, count)
        keys = join(two_back(back_two, (two_keys,), 0, g), back_one[0, g], own[0, g])
        part = matmul(keys, join(two_grad[n], one_grad[n], own_grad[n]), (0, 0))
        part = (part * width ** (-0.5)).astype(jnp.bfloat16)
        for index, (columns, mine) in enumerate(((attended_rows[n], out_mine), (part, query_mine))):
            block = columns.T.reshape(count, 2 * length, width)
            mine[rows] = block[:, :length]
            query_send[index, rows] = block[:, length:]
    for index, row, piece, taken in placed(sends, heads):
        piece[...] = query_send[index, pl.ds(row, taken)]


def assemble_kernel(
    out_mine, query_mine, first_third, second_third, last_third, out, query_grad, token
):
    heads = out_mine.shape[0]
    start = (1 - lax.axis_index("head")) * heads
    out[my_heads(heads)] = out_mine[...]
    query_grad[my_heads(heads)] = query_mine[...]
    for index, row, piece, count in placed((first_third, second_third, last_third), heads):
        (out, query_grad)[index][pl.ds(start + row, count)] = piece[...]
    token[...] = jnp.zeros(token.shape, token.dtype)


def own_sum_kernel(own_part, two_total, sum_mine, sum_send):
    length = sum_mine.shape[2]
    total = own_part[...] + two_total[...].astype(jnp.float32)
    sum_mine[...] = total[:, :, :length]
    sum_send[...] = total[:, :, length:].astype(jnp.bfloat16)


def final_kernel(sum_mine, sum_other, one_total, after, key_grad, value_grad):
    groups = sum_mine.shape[1]
    mine, other = my_heads(groups), other_heads(groups)
    for index, result in enumerate((key_grad, value_grad)):
        total = sum_mine[index] + one_total[index, mine].astype(jnp.float32)
        result[mine] = total.astype(jnp.bfloat16)
        total = sum_other[index].astype(jnp.float32) + one_total[index, other].astype(jnp.float32)
        result[other] = total.astype(jnp.bfloat16)


def shards(query_matrix, key_matrix, value_matrix, output_gradient, query_head_spans, slab_offset):
    groups, length, width = key_matrix.shape
    heads = query_matrix.shape[0]
    cores = lax.axis_size("head")
    tokens = cores * length
    groups_here, heads_here = groups // cores, heads // cores
    count = max(1, min(heads // groups, 256 // tokens))
    chunks = heads_here // count
    lanes = count * tokens
    half, full = jnp.bfloat16, jnp.float32
    vmem = pl.BlockSpec(memory_space=pltpu.VMEM)
    smem = pl.BlockSpec(memory_space=pltpu.SMEM)

    def call(kernel, name, outs, arrays, scalars=0, scratch=()):
        return pl.pallas_call(
            kernel,
            out_shape=tuple(jax.ShapeDtypeStruct(shape, kind) for shape, kind in outs),
            in_specs=[smem] * scalars + [vmem] * (len(arrays) - scalars),
            out_specs=(vmem,) * len(outs),
            scratch_shapes=scratch,
            compiler_params=pltpu.CompilerParams(vmem_limit_bytes=40 * 1024 * 1024),
            cost_estimate=pl.CostEstimate(flops=1, bytes_accessed=0, transcendentals=0),
            name=name,
        )(*arrays)

    def rows_of(rows, kind):
        return ((chunks, rows, lanes), kind)

    stat = rows_of(1, full)
    whole_pair = ((2, groups, length, width), half)
    half_block = ((groups_here, length, width), half)
    half_pair = ((2, groups_here, length, width), half)
    chip_pair = ((2, groups_here, tokens, width), half)
    half_rows = ((heads_here, length, width), half)
    third_rows = [((rows, length, width), half) for rows in thirds(heads_here)]
    chip_rows = ((heads_here, tokens, width), half)

    own = jnp.stack([key_matrix, value_matrix])
    back_two = shifted(own, "seq", 2)
    (own_send,) = call(split_own_kernel, "split_own", [half_pair], (own,))
    (own_head,) = call(
        join_own_kernel, "join_own", [chip_pair], (own, swapped(own_send, "head"))
    )
    back_one = shifted(own_head, "seq", 1)
    sends = call(
        split_rows_kernel,
        "split_rows",
        third_rows,
        (query_matrix, output_gradient, own),
    )
    (
        query_head, grad_head, grad_rows, first, own_max, own_total, own_out, own_weights,
        own_prob_grad,
    ) = call(
        own_kernel,
        "own_block",
        [
            chip_rows, chip_rows, rows_of(width, half), rows_of(1, jnp.int32), stat, stat,
            rows_of(width, full), rows_of(tokens, full), rows_of(tokens, full),
        ],
        (
            query_head_spans, slab_offset, query_matrix, output_gradient,
            *[swapped(send, "head") for send in sends], own_head,
        ),
        scalars=2,
    )
    back_two, first = lax.optimization_barrier((back_two, first))
    two_sends = call(split_kernel, "split_two", [half_block] * 2, (back_two,))
    two_other = [swapped(send, "head") for send in two_sends]
    near_max, near_total, near_out, near_weights, near_prob_grad, own_factor = call(
        near_forward_kernel,
        "near_forward",
        [stat, stat, rows_of(width, full), rows_of(tokens, full), rows_of(tokens, full), stat],
        (first, query_head, grad_head, back_two, *two_other, own_max, own_total, own_out),
    )
    back_one, near_max = lax.optimization_barrier((back_one, near_max))
    attended_rows, row_delta, near_factor, one_grad, chip_part = call(
        last_kernel,
        "last_forward_backward",
        [rows_of(width, half), stat, stat, rows_of(tokens, half), chip_pair],
        (first, query_head, grad_head, back_one, grad_rows, near_max, near_total, near_out),
    )
    chip_other = swapped(chip_part, "head")
    two_grad, two_part = call(
        two_backward_kernel,
        "two_backward",
        [rows_of(tokens, half), chip_pair],
        (query_head, grad_head, near_weights, near_prob_grad, near_factor, row_delta),
    )
    two_total = shifted(two_part, "seq", -2)
    (one_part,) = call(join_one_kernel, "join_one", [whole_pair], (chip_part, chip_other))
    one_total = shifted(one_part, "seq", -1)
    own_grad, own_part = call(
        own_backward_kernel,
        "own_backward",
        [rows_of(tokens, half), (chip_pair[0], full)],
        (
            query_head, grad_head, own_weights, own_prob_grad, near_factor, own_factor, row_delta,
            one_part,
        ),
    )
    out_mine, query_mine, *sends = call(
        query_kernel,
        "query_grad",
        [half_rows] * 2 + third_rows,
        (own_head, back_one, back_two, two_other[0], attended_rows, two_grad, one_grad, own_grad),
        scratch=[pltpu.VMEM((2,) + half_rows[0], half)],
    )
    attn_out, query_grad, token = call(
        assemble_kernel,
        "assemble",
        [(query_matrix.shape, half)] * 2 + [((8, 128), full)],
        (out_mine, query_mine, *[swapped(send, "head") for send in sends]),
    )
    sum_mine, sum_send = call(
        own_sum_kernel, "own_sum", [(half_pair[0], full), half_pair], (own_part, two_total)
    )
    key_grad, value_grad = call(
        final_kernel,
        "total",
        [(key_matrix.shape, half)] * 2,
        (sum_mine, swapped(sum_send, "head"), one_total, token),
    )
    return (attn_out, query_grad, key_grad, value_grad)


def solution(mesh):
    tokens = P(None, ("seq", "head"), None)
    return jax.shard_map(
        shards,
        mesh=mesh,
        in_specs=(tokens, tokens, tokens, tokens, P(), P()),
        out_specs=(tokens, tokens, tokens, tokens),
        check_vma=False,
    )
```

```python
import math

import jax
import jax.numpy as jnp
from jax import lax
from jax.experimental import pallas as pl
from jax.experimental.pallas import tpu as pltpu
from jax.sharding import PartitionSpec as P

REACH = 2
SEGMENT = 512

masked_score = -1e30


def shifted(block, axis, distance):
    devices = range(lax.axis_size(axis))
    route = [(i - distance, i) for i in devices if i - distance in devices]
    return lax.ppermute(block, axis, route)


def swapped(block, axis):
    count = lax.axis_size(axis)
    return lax.ppermute(block, axis, [(i, count - 1 - i) for i in range(count)])


def matmul(left, right, contract):
    return lax.dot_general(
        left, right, ((contract[:1], contract[1:]), ((), ())), preferred_element_type=jnp.float32
    )


def grouped(ref, n, count):
    _, length, width = ref.shape
    return ref[pl.ds(n * count, count)].reshape(count * length, width)


def join(*blocks):
    return jnp.concatenate(blocks, axis=0)


def core_offsets(length):
    core = lax.axis_index("head")
    return core * length, (1 - core) * length


def my_heads(count):
    return pl.ds(lax.axis_index("head") * count, count)


def other_heads(count):
    return pl.ds((1 - lax.axis_index("head")) * count, count)


def lane_tokens(count, length):
    lane = lax.broadcasted_iota(jnp.int32, (1, count * 2 * length), 1)
    token = lane - lane // (2 * length) * (2 * length)
    mine, other = core_offsets(length)
    return jnp.where(token < length, token + mine, token - length + other)


def first_visible(spans, offset, chunks, count, length):
    token = lane_tokens(count, length)
    lane_head = lax.broadcasted_iota(jnp.int32, token.shape, 1) // (2 * length)
    start = lax.axis_index("seq") * 2 * length
    segment_start = token - lax.bitwise_and(offset[0] + start + token, SEGMENT - 1)
    floor = jnp.maximum(segment_start, -start)
    base = lax.axis_index("head") * chunks * count
    result = []
    for n in range(chunks):
        span = jnp.full(token.shape, spans[base + n * count], jnp.int32)
        for a in range(1, count):
            span = jnp.where(lane_head == a, spans[base + n * count + a], span)
        result.append(jnp.maximum(floor, token - span + 1))
    return result


def masked(scores, first, chips_back, token=None):
    length = scores.shape[0] // 2
    row = lax.broadcasted_iota(jnp.int32, (length, scores.shape[1]), 0)
    pieces = []
    for part, offset in enumerate(core_offsets(length)):
        visible = row >= first + (chips_back * 2 * length - offset)
        if token is not None:
            visible &= row <= token - offset
        pieces.append(
            jnp.where(visible, scores[part * length : (part + 1) * length], masked_score)
        )
    return join(*pieces)


def split_kernel(block, *sends):
    for index, send in enumerate(sends):
        send[...] = block[index, other_heads(send.shape[0])]


def thirds(rows):
    return [2 * rows * (i + 1) // 3 - 2 * rows * i // 3 for i in range(3)]


def placed(pieces, rows):
    taken = 0
    for piece in pieces:
        count = piece.shape[0]
        for index in range(2):
            low = max(taken, index * rows)
            high = min(taken + count, (index + 1) * rows)
            if low < high:
                yield index, low - index * rows, piece.at[pl.ds(low - taken, high - low)], high - low
        taken += count


def split_rows_kernel(queries, grads, after, *sends):
    heads = queries.shape[0] // 2
    start = (1 - lax.axis_index("head")) * heads
    for index, row, piece, count in placed(sends, heads):
        piece[...] = (queries, grads)[index][pl.ds(start + row, count)]


def join_own_kernel(own, other_keys, other_values, own_head):
    groups, length = other_keys.shape[:2]
    own_head[:, :, pl.ds(0, length)] = own[:, my_heads(groups)]
    own_head[0, :, pl.ds(length, length)] = other_keys[...]
    own_head[1, :, pl.ds(length, length)] = other_values[...]


def own_kernel(
    spans, offset, queries, grads, first_third, second_third, last_third, own,
    query_head, grad_head, grad_rows, first, own_max, own_total, own_out, own_weights,
    own_prob_grad,
):
    heads, _, width = query_head.shape
    length = queries.shape[1]
    groups = own.shape[1]
    chunks = first.shape[0]
    count = heads // chunks
    query_head[:, pl.ds(0, length)] = queries[my_heads(heads)]
    grad_head[:, pl.ds(0, length)] = grads[my_heads(heads)]
    for index, row, piece, rows in placed((first_third, second_third, last_third), heads):
        (query_head, grad_head)[index][pl.ds(row, rows), pl.ds(length, length)] = piece[...]
    factor = width ** (-0.5) * math.log2(math.e)
    token = lane_tokens(count, length)
    for n, rows in enumerate(first_visible(spans, offset, chunks, count, length)):
        first[n] = rows

    def products(n):
        g = n * groups // chunks
        own_prob_grad[n] = matmul(own[1, g], grouped(grad_head, n, count), (1, 1))
        return (matmul(own[0, g], grouped(query_head, n, count), (1, 1)),)

    def softmax(n, scores):
        scores = masked(scores * factor, first[n], 0, token)
        row_max = jnp.max(scores, axis=0, keepdims=True)
        weights = jnp.exp2(scores - row_max)
        own_max[n] = row_max
        own_total[n] = jnp.sum(weights, axis=0, keepdims=True)
        own_weights[n] = weights
        return (weights.astype(jnp.bfloat16),)

    def weigh(n, halves):
        own_out[n] = matmul(own[1, n * groups // chunks], halves, (0, 0))
        grad_rows[n] = grouped(grad_head, n, count).T

    pipelined(chunks, products, softmax, weigh)


def one_back(back_one, one_other, index, g):
    base = lax.axis_index("head") * one_other[index].shape[0]
    return join(back_one[index, base + g], one_other[index][g])


def near_forward_kernel(
    first, query_head, grad_head, back_one, one_keys, one_values, own_max, own_total, own_out,
    near_max, near_total, near_out, near_weights, near_prob_grad, own_factor,
):
    groups = one_keys.shape[0]
    one_other = (one_keys, one_values)
    chunks = first.shape[0]
    heads, _, width = query_head.shape
    count = heads // chunks
    factor = width ** (-0.5) * math.log2(math.e)

    def products(n):
        g = n * groups // chunks
        keys = one_back(back_one, one_other, 0, g)
        values = one_back(back_one, one_other, 1, g)
        near_prob_grad[n] = matmul(values, grouped(grad_head, n, count), (1, 1))
        return (matmul(keys, grouped(query_head, n, count), (1, 1)),)

    def softmax(n, scores):
        scores = masked(scores * factor, first[n], 1)
        row_max = jnp.maximum(own_max[n], jnp.max(scores, axis=0, keepdims=True))
        weights = jnp.exp2(scores - row_max)
        rescale = jnp.exp2(own_max[n] - row_max)
        own_factor[n] = rescale
        near_max[n] = row_max
        near_total[n] = own_total[n] * rescale + jnp.sum(weights, axis=0, keepdims=True)
        near_weights[n] = weights
        return rescale, weights.astype(jnp.bfloat16)

    def weigh(n, rescale, halves):
        values = one_back(back_one, one_other, 1, n * groups // chunks)
        near_out[n] = own_out[n] * rescale + matmul(values, halves, (0, 0))

    pipelined(chunks, products, softmax, weigh)


def far_kernel(
    first, query_head, grad_head, back_two, grad_rows, near_max, near_total, near_out,
    attended_rows, row_delta, near_factor, far_grad, far_part,
):
    groups = back_two.shape[1]
    chunks = first.shape[0]
    heads, _, width = query_head.shape
    count = heads // chunks
    scale = width ** (-0.5)

    def products(n):
        g = n * groups // chunks
        scores = matmul(back_two[0, g], grouped(query_head, n, count), (1, 1))
        prob_grad = matmul(back_two[1, g], grouped(grad_head, n, count), (1, 1))
        return scores, prob_grad

    def softmax(n, scores, prob_grad):
        g = n * groups // chunks
        scores = masked(scores * (scale * math.log2(math.e)), first[n], 2)
        row_max = jnp.maximum(near_max[n], jnp.max(scores, axis=0, keepdims=True))
        weights = jnp.exp2(scores - row_max)
        rescale = jnp.exp2(near_max[n] - row_max)
        inverse = 1.0 / (near_total[n] * rescale + jnp.sum(weights, axis=0, keepdims=True))
        weighted = matmul(back_two[1, g], weights.astype(jnp.bfloat16), (0, 0))
        attended = ((near_out[n] * rescale + weighted) * inverse).astype(jnp.bfloat16)
        delta = jnp.sum(
            grad_rows[n].astype(jnp.float32) * attended.astype(jnp.float32), axis=0, keepdims=True
        )
        prob = weights * inverse
        score_grad = (prob * (prob_grad - delta)).astype(jnp.bfloat16)
        attended_rows[n] = attended
        row_delta[n] = delta
        near_factor[n] = rescale * inverse
        far_grad[n] = score_grad
        return score_grad, prob.astype(jnp.bfloat16)

    accumulate = accumulator(query_head, grad_head, chunks, groups)

    def store(g, key_part, value_part):
        far_part[0, g] = (key_part * scale).astype(jnp.bfloat16)
        far_part[1, g] = value_part.astype(jnp.bfloat16)

    pipelined(chunks, products, softmax, lambda n, *halves: accumulate(n, *halves, store))


def pipelined(chunks, before, middle, after):
    ready = before(0)
    done = None
    for n in range(chunks):
        upcoming = before(n + 1) if n + 1 < chunks else None
        result = middle(n, *ready)
        if done is not None:
            after(n - 1, *done)
        ready, done = upcoming, result
    after(chunks - 1, *done)


def accumulator(query_head, grad_head, chunks, groups):
    count = query_head.shape[0] // chunks
    parts = {}

    def accumulate(n, score_grad, half, store):
        g = n * groups // chunks
        key_part = matmul(score_grad, grouped(query_head, n, count), (1, 0))
        value_part = matmul(half, grouped(grad_head, n, count), (1, 0))
        if g in parts:
            key_part, value_part = parts[g][0] + key_part, parts[g][1] + value_part
        parts[g] = (key_part, value_part)
        if (n + 1) * groups // chunks != g:
            store(g, key_part, value_part)

    return accumulate


def one_backward_kernel(
    query_head, grad_head, near_weights, near_prob_grad, near_factor, row_delta,
    one_grad, one_mine, send_keys, send_values,
):
    chunks = near_weights.shape[0]
    groups, length, width = one_mine.shape[1:]
    accumulate = accumulator(query_head, grad_head, chunks, groups)

    def store(g, key_part, value_part):
        for index, (part, send) in enumerate(
            ((key_part * width ** (-0.5), send_keys), (value_part, send_values))
        ):
            one_mine[index, g] = part[:length].astype(jnp.bfloat16)
            send[g] = part[length:].astype(jnp.bfloat16)

    for n in range(chunks):
        prob = near_weights[n] * near_factor[n]
        score_grad = (prob * (near_prob_grad[n] - row_delta[n])).astype(jnp.bfloat16)
        one_grad[n] = score_grad
        accumulate(n, score_grad, prob.astype(jnp.bfloat16), store)


def own_backward_kernel(
    query_head, grad_head, own_weights, own_prob_grad, near_factor, own_factor, row_delta,
    after, own_grad, own_part,
):
    chunks = own_weights.shape[0]
    groups, _, width = own_part.shape[1:]
    accumulate = accumulator(query_head, grad_head, chunks, groups)

    def store(g, key_part, value_part):
        own_part[0, g] = key_part * width ** (-0.5)
        own_part[1, g] = value_part

    for n in range(chunks):
        prob = own_weights[n] * (own_factor[n] * near_factor[n])
        score_grad = (prob * (own_prob_grad[n] - row_delta[n])).astype(jnp.bfloat16)
        own_grad[n] = score_grad
        accumulate(n, score_grad, prob.astype(jnp.bfloat16), store)


def join_one_kernel(one_mine, other_keys, other_values, one_part):
    groups = one_mine.shape[1]
    one_part[:, my_heads(groups)] = one_mine[...]
    one_part[0, other_heads(groups)] = other_keys[...]
    one_part[1, other_heads(groups)] = other_values[...]


def query_kernel(
    own, back_one, one_keys, back_two, attended_rows, far_grad, one_grad, own_grad,
    out_mine, query_mine, first_third, second_third, last_third, query_send,
):
    sends = (first_third, second_third, last_third)
    groups = own.shape[1]
    chunks = far_grad.shape[0]
    heads, length, width = out_mine.shape
    count = heads // chunks
    for n in range(chunks):
        g = n * groups // chunks
        rows = pl.ds(n * count, count)
        keys = join(back_two[0, g], one_back(back_one, (one_keys,), 0, g), own[0, g])
        part = matmul(keys, join(far_grad[n], one_grad[n], own_grad[n]), (0, 0))
        part = (part * width ** (-0.5)).astype(jnp.bfloat16)
        for index, (columns, mine) in enumerate(((attended_rows[n], out_mine), (part, query_mine))):
            block = columns.T.reshape(count, 2 * length, width)
            mine[rows] = block[:, :length]
            query_send[index, rows] = block[:, length:]
    for index, row, piece, taken in placed(sends, heads):
        piece[...] = query_send[index, pl.ds(row, taken)]


def assemble_kernel(
    out_mine, query_mine, first_third, second_third, last_third, out, query_grad, token
):
    heads = out_mine.shape[0]
    start = (1 - lax.axis_index("head")) * heads
    out[my_heads(heads)] = out_mine[...]
    query_grad[my_heads(heads)] = query_mine[...]
    for index, row, piece, count in placed((first_third, second_third, last_third), heads):
        (out, query_grad)[index][pl.ds(start + row, count)] = piece[...]
    token[...] = jnp.zeros(token.shape, token.dtype)


def own_sum_kernel(own_part, far_total, sum_mine, sum_send):
    length = sum_mine.shape[2]
    total = own_part[...] + far_total[...].astype(jnp.float32)
    sum_mine[...] = total[:, :, :length]
    sum_send[...] = total[:, :, length:].astype(jnp.bfloat16)


def final_kernel(sum_mine, sum_other, one_total, after, key_grad, value_grad):
    groups = sum_mine.shape[1]
    mine, other = my_heads(groups), other_heads(groups)
    for index, result in enumerate((key_grad, value_grad)):
        total = sum_mine[index] + one_total[index, mine].astype(jnp.float32)
        result[mine] = total.astype(jnp.bfloat16)
        total = sum_other[index].astype(jnp.float32) + one_total[index, other].astype(jnp.float32)
        result[other] = total.astype(jnp.bfloat16)


def shards(query_matrix, key_matrix, value_matrix, output_gradient, query_head_spans, slab_offset):
    groups, length, width = key_matrix.shape
    heads = query_matrix.shape[0]
    cores = lax.axis_size("head")
    tokens = cores * length
    groups_here, heads_here = groups // cores, heads // cores
    count = max(1, min(heads // groups, 256 // tokens))
    chunks = heads_here // count
    lanes = count * tokens
    half, full = jnp.bfloat16, jnp.float32
    vmem = pl.BlockSpec(memory_space=pltpu.VMEM)
    smem = pl.BlockSpec(memory_space=pltpu.SMEM)

    def call(kernel, name, outs, arrays, scalars=0, scratch=()):
        return pl.pallas_call(
            kernel,
            out_shape=tuple(jax.ShapeDtypeStruct(shape, kind) for shape, kind in outs),
            in_specs=[smem] * scalars + [vmem] * (len(arrays) - scalars),
            out_specs=(vmem,) * len(outs),
            scratch_shapes=scratch,
            compiler_params=pltpu.CompilerParams(vmem_limit_bytes=40 * 1024 * 1024),
            cost_estimate=pl.CostEstimate(flops=1, bytes_accessed=0, transcendentals=0),
            name=name,
        )(*arrays)

    def rows_of(rows, kind):
        return ((chunks, rows, lanes), kind)

    stat = rows_of(1, full)
    whole_pair = ((2, groups, length, width), half)
    half_block = ((groups_here, length, width), half)
    half_pair = ((2, groups_here, length, width), half)
    chip_pair = ((2, groups_here, tokens, width), half)
    half_rows = ((heads_here, length, width), half)
    third_rows = [((rows, length, width), half) for rows in thirds(heads_here)]
    chip_rows = ((heads_here, tokens, width), half)

    own = jnp.stack([key_matrix, value_matrix])
    count_seq = lax.axis_size("seq")
    pairs = [[i, i + 1] for i in range(0, count_seq, 2)]
    gathered = lax.all_gather(own, "seq", axis_index_groups=pairs)
    crossing = lax.ppermute(own, "seq", [(i - 1, i) for i in range(2, count_seq, 2)])
    back_one = jnp.where(lax.bitwise_and(lax.axis_index("seq"), 1) == 1, gathered[0], crossing)
    own_sends = call(split_kernel, "split_own", [half_block] * 2, (own,))
    (own_head,) = call(
        join_own_kernel, "join_own", [chip_pair], (own, *[swapped(send, "head") for send in own_sends])
    )
    back_two = shifted(own_head, "seq", 2)
    sends = call(
        split_rows_kernel,
        "split_rows",
        third_rows,
        (query_matrix, output_gradient, own),
    )
    (
        query_head, grad_head, grad_rows, first, own_max, own_total, own_out, own_weights,
        own_prob_grad,
    ) = call(
        own_kernel,
        "own_block",
        [
            chip_rows, chip_rows, rows_of(width, half), rows_of(1, jnp.int32), stat, stat,
            rows_of(width, full), rows_of(tokens, full), rows_of(tokens, full),
        ],
        (
            query_head_spans, slab_offset, query_matrix, output_gradient,
            *[swapped(send, "head") for send in sends], own_head,
        ),
        scalars=2,
    )
    back_one, first = lax.optimization_barrier((back_one, first))
    one_sends = call(split_kernel, "split_one", [half_block] * 2, (back_one,))
    one_other = [swapped(send, "head") for send in one_sends]
    near_max, near_total, near_out, near_weights, near_prob_grad, own_factor = call(
        near_forward_kernel,
        "near_forward",
        [stat, stat, rows_of(width, full), rows_of(tokens, full), rows_of(tokens, full), stat],
        (first, query_head, grad_head, back_one, *one_other, own_max, own_total, own_out),
    )
    back_two, near_max = lax.optimization_barrier((back_two, near_max))
    attended_rows, row_delta, near_factor, far_grad, far_part = call(
        far_kernel,
        "far_forward_backward",
        [rows_of(width, half), stat, stat, rows_of(tokens, half), chip_pair],
        (first, query_head, grad_head, back_two, grad_rows, near_max, near_total, near_out),
    )
    far_total = shifted(far_part, "seq", -2)
    one_grad, part_mine, *part_sends = call(
        one_backward_kernel,
        "one_backward",
        [rows_of(tokens, half), half_pair, half_block, half_block],
        (query_head, grad_head, near_weights, near_prob_grad, near_factor, row_delta),
    )
    (one_part,) = call(
        join_one_kernel,
        "join_one",
        [whole_pair],
        (part_mine, *[swapped(send, "head") for send in part_sends]),
    )
    one_total = shifted(one_part, "seq", -1)
    own_grad, own_part = call(
        own_backward_kernel,
        "own_backward",
        [rows_of(tokens, half), (chip_pair[0], full)],
        (
            query_head, grad_head, own_weights, own_prob_grad, near_factor, own_factor, row_delta,
            one_part,
        ),
    )
    out_mine, query_mine, *sends = call(
        query_kernel,
        "query_grad",
        [half_rows] * 2 + third_rows,
        (own_head, back_one, one_other[0], back_two, attended_rows, far_grad, one_grad, own_grad),
        scratch=[pltpu.VMEM((2,) + half_rows[0], half)],
    )
    attn_out, query_grad, token = call(
        assemble_kernel,
        "assemble",
        [(query_matrix.shape, half)] * 2 + [((8, 128), full)],
        (out_mine, query_mine, *[swapped(send, "head") for send in sends]),
    )
    sum_mine, sum_send = call(
        own_sum_kernel, "own_sum", [(half_pair[0], full), half_pair], (own_part, far_total)
    )
    key_grad, value_grad = call(
        final_kernel,
        "total",
        [(key_matrix.shape, half)] * 2,
        (sum_mine, swapped(sum_send, "head"), one_total, token),
    )
    return (attn_out, query_grad, key_grad, value_grad)


def solution(mesh):
    tokens = P(None, ("seq", "head"), None)
    return jax.shard_map(
        shards,
        mesh=mesh,
        in_specs=(tokens, tokens, tokens, tokens, P(), P()),
        out_specs=(tokens, tokens, tokens, tokens),
        check_vma=False,
    )
```

```python
import math

import jax
import jax.numpy as jnp
from jax import lax
from jax.experimental import pallas as pl
from jax.experimental.pallas import tpu as pltpu
from jax.sharding import PartitionSpec as P

REACH = 2
SEGMENT = 512

masked_score = -1e30


def shifted(block, axis, distance):
    devices = range(lax.axis_size(axis))
    route = [(i - distance, i) for i in devices if i - distance in devices]
    return lax.ppermute(block, axis, route)


def swapped(block, axis):
    count = lax.axis_size(axis)
    return lax.ppermute(block, axis, [(i, count - 1 - i) for i in range(count)])


def matmul(left, right, contract):
    return lax.dot_general(
        left, right, ((contract[:1], contract[1:]), ((), ())), preferred_element_type=jnp.float32
    )


def grouped(ref, n, count):
    _, length, width = ref.shape
    return ref[pl.ds(n * count, count)].reshape(count * length, width)


def join(*blocks):
    return jnp.concatenate(blocks, axis=0)


def core_offsets(length):
    core = lax.axis_index("head")
    return core * length, (1 - core) * length


def my_heads(count):
    return pl.ds(lax.axis_index("head") * count, count)


def other_heads(count):
    return pl.ds((1 - lax.axis_index("head")) * count, count)


def lane_tokens(count, length):
    lane = lax.broadcasted_iota(jnp.int32, (1, count * 2 * length), 1)
    token = lane - lane // (2 * length) * (2 * length)
    mine, other = core_offsets(length)
    return jnp.where(token < length, token + mine, token - length + other)


def first_visible(spans, offset, chunks, count, length):
    token = lane_tokens(count, length)
    lane_head = lax.broadcasted_iota(jnp.int32, token.shape, 1) // (2 * length)
    start = lax.axis_index("seq") * 2 * length
    segment_start = token - lax.bitwise_and(offset[0] + start + token, SEGMENT - 1)
    floor = jnp.maximum(segment_start, -start)
    base = lax.axis_index("head") * chunks * count
    result = []
    for n in range(chunks):
        span = jnp.full(token.shape, spans[base + n * count], jnp.int32)
        for a in range(1, count):
            span = jnp.where(lane_head == a, spans[base + n * count + a], span)
        result.append(jnp.maximum(floor, token - span + 1))
    return result


def masked(scores, first, chips_back, token=None):
    length = scores.shape[0] // 2
    row = lax.broadcasted_iota(jnp.int32, (length, scores.shape[1]), 0)
    pieces = []
    for part, offset in enumerate(core_offsets(length)):
        visible = row >= first + (chips_back * 2 * length - offset)
        if token is not None:
            visible &= row <= token - offset
        pieces.append(
            jnp.where(visible, scores[part * length : (part + 1) * length], masked_score)
        )
    return join(*pieces)


def split_kernel(block, *sends):
    for index, send in enumerate(sends):
        send[...] = block[index, other_heads(send.shape[0])]


def thirds(rows):
    return [2 * rows * (i + 1) // 3 - 2 * rows * i // 3 for i in range(3)]


def placed(pieces, rows):
    taken = 0
    for piece in pieces:
        count = piece.shape[0]
        for index in range(2):
            low = max(taken, index * rows)
            high = min(taken + count, (index + 1) * rows)
            if low < high:
                yield index, low - index * rows, piece.at[pl.ds(low - taken, high - low)], high - low
        taken += count


def split_rows_kernel(queries, grads, after, *sends):
    heads = queries.shape[0] // 2
    start = (1 - lax.axis_index("head")) * heads
    for index, row, piece, count in placed(sends, heads):
        piece[...] = (queries, grads)[index][pl.ds(start + row, count)]


def join_own_kernel(own, other_keys, other_values, own_head):
    groups, length = other_keys.shape[:2]
    own_head[:, :, pl.ds(0, length)] = own[:, my_heads(groups)]
    own_head[0, :, pl.ds(length, length)] = other_keys[...]
    own_head[1, :, pl.ds(length, length)] = other_values[...]


def own_kernel(
    spans, offset, queries, grads, first_third, second_third, last_third, own,
    query_head, grad_head, grad_rows, first, own_max, own_total, own_out, own_weights,
    own_prob_grad,
):
    heads, _, width = query_head.shape
    length = queries.shape[1]
    groups = own.shape[1]
    chunks = first.shape[0]
    count = heads // chunks
    query_head[:, pl.ds(0, length)] = queries[my_heads(heads)]
    grad_head[:, pl.ds(0, length)] = grads[my_heads(heads)]
    for index, row, piece, rows in placed((first_third, second_third, last_third), heads):
        (query_head, grad_head)[index][pl.ds(row, rows), pl.ds(length, length)] = piece[...]
    factor = width ** (-0.5) * math.log2(math.e)
    token = lane_tokens(count, length)
    for n, rows in enumerate(first_visible(spans, offset, chunks, count, length)):
        first[n] = rows

    def products(n):
        g = n * groups // chunks
        own_prob_grad[n] = matmul(own[1, g], grouped(grad_head, n, count), (1, 1))
        return (matmul(own[0, g], grouped(query_head, n, count), (1, 1)),)

    def softmax(n, scores):
        scores = masked(scores * factor, first[n], 0, token)
        row_max = jnp.max(scores, axis=0, keepdims=True)
        weights = jnp.exp2(scores - row_max)
        own_max[n] = row_max
        own_total[n] = jnp.sum(weights, axis=0, keepdims=True)
        own_weights[n] = weights
        return (weights.astype(jnp.bfloat16),)

    def weigh(n, halves):
        own_out[n] = matmul(own[1, n * groups // chunks], halves, (0, 0))
        grad_rows[n] = grouped(grad_head, n, count).T

    pipelined(chunks, products, softmax, weigh)


def two_back(back_two, two_other, index, g):
    base = lax.axis_index("head") * two_other[index].shape[0]
    return join(back_two[index, base + g], two_other[index][g])


def near_forward_kernel(
    first, query_head, grad_head, back_two, two_keys, two_values, own_max, own_total, own_out,
    near_max, near_total, near_out, near_weights, near_prob_grad, own_factor,
):
    groups = two_keys.shape[0]
    two_other = (two_keys, two_values)
    chunks = first.shape[0]
    heads, _, width = query_head.shape
    count = heads // chunks
    factor = width ** (-0.5) * math.log2(math.e)

    def products(n):
        g = n * groups // chunks
        keys = two_back(back_two, two_other, 0, g)
        values = two_back(back_two, two_other, 1, g)
        near_prob_grad[n] = matmul(values, grouped(grad_head, n, count), (1, 1))
        return (matmul(keys, grouped(query_head, n, count), (1, 1)),)

    def softmax(n, scores):
        scores = masked(scores * factor, first[n], 2)
        row_max = jnp.maximum(own_max[n], jnp.max(scores, axis=0, keepdims=True))
        weights = jnp.exp2(scores - row_max)
        rescale = jnp.exp2(own_max[n] - row_max)
        own_factor[n] = rescale
        near_max[n] = row_max
        near_total[n] = own_total[n] * rescale + jnp.sum(weights, axis=0, keepdims=True)
        near_weights[n] = weights
        return rescale, weights.astype(jnp.bfloat16)

    def weigh(n, rescale, halves):
        values = two_back(back_two, two_other, 1, n * groups // chunks)
        near_out[n] = own_out[n] * rescale + matmul(values, halves, (0, 0))

    pipelined(chunks, products, softmax, weigh)


def last_kernel(
    first, query_head, grad_head, back_one, grad_rows, near_max, near_total, near_out,
    attended_rows, row_delta, near_factor, one_grad, one_part,
):
    groups = back_one.shape[1]
    chunks = first.shape[0]
    heads, _, width = query_head.shape
    count = heads // chunks
    scale = width ** (-0.5)

    def products(n):
        g = n * groups // chunks
        scores = matmul(back_one[0, g], grouped(query_head, n, count), (1, 1))
        prob_grad = matmul(back_one[1, g], grouped(grad_head, n, count), (1, 1))
        return scores, prob_grad

    def softmax(n, scores, prob_grad):
        scores = masked(scores * (scale * math.log2(math.e)), first[n], 1)
        row_max = jnp.maximum(near_max[n], jnp.max(scores, axis=0, keepdims=True))
        weights = jnp.exp2(scores - row_max)
        rescale = jnp.exp2(near_max[n] - row_max)
        inverse = 1.0 / (near_total[n] * rescale + jnp.sum(weights, axis=0, keepdims=True))
        weighted = matmul(
            back_one[1, n * groups // chunks], weights.astype(jnp.bfloat16), (0, 0)
        )
        near_factor[n] = rescale * inverse
        return prob_grad, weights, weighted, rescale, inverse

    def differentiate(n, prob_grad, weights, weighted, rescale, inverse):
        attended = ((near_out[n] * rescale + weighted) * inverse).astype(jnp.bfloat16)
        delta = jnp.sum(
            grad_rows[n].astype(jnp.float32) * attended.astype(jnp.float32), axis=0, keepdims=True
        )
        prob = weights * inverse
        score_grad = (prob * (prob_grad - delta)).astype(jnp.bfloat16)
        attended_rows[n] = attended
        row_delta[n] = delta
        one_grad[n] = score_grad
        return score_grad, prob.astype(jnp.bfloat16)

    def store(g, key_part, value_part):
        one_part[0, g] = (key_part * scale).astype(jnp.bfloat16)
        one_part[1, g] = value_part.astype(jnp.bfloat16)

    accumulate = accumulator(query_head, grad_head, chunks, groups, store)
    pipelined(chunks, products, softmax, differentiate, accumulate)


def pipelined(chunks, *stages):
    ready = [{} for _ in range(len(stages) + 1)]
    for step in range(chunks + len(stages) - 1):
        for depth, stage in enumerate(stages):
            n = step - depth
            if 0 <= n < chunks:
                ready[depth + 1][n] = stage(n, *ready[depth].pop(n, ())) or ()


def accumulator(query_head, grad_head, chunks, groups, store):
    count = query_head.shape[0] // chunks
    parts = {}

    def accumulate(n, score_grad, half):
        g = n * groups // chunks
        key_part = matmul(score_grad, grouped(query_head, n, count), (1, 0))
        value_part = matmul(half, grouped(grad_head, n, count), (1, 0))
        if g in parts:
            key_part, value_part = parts[g][0] + key_part, parts[g][1] + value_part
        parts[g] = (key_part, value_part)
        if (n + 1) * groups // chunks != g:
            store(g, key_part, value_part)

    return accumulate


def two_backward_kernel(
    query_head, grad_head, near_weights, near_prob_grad, near_factor, row_delta,
    two_grad, two_mine, send_keys, send_values,
):
    chunks = near_weights.shape[0]
    groups, length, width = two_mine.shape[1:]

    def differentiate(n):
        prob = near_weights[n] * near_factor[n]
        score_grad = (prob * (near_prob_grad[n] - row_delta[n])).astype(jnp.bfloat16)
        two_grad[n] = score_grad
        return score_grad, prob.astype(jnp.bfloat16)

    def store(g, key_part, value_part):
        for index, (part, send) in enumerate(
            ((key_part * width ** (-0.5), send_keys), (value_part, send_values))
        ):
            two_mine[index, g] = part[:length].astype(jnp.bfloat16)
            send[g] = part[length:].astype(jnp.bfloat16)

    accumulate = accumulator(query_head, grad_head, chunks, groups, store)
    pipelined(chunks, differentiate, accumulate)


def own_backward_kernel(
    query_head, grad_head, own_weights, own_prob_grad, near_factor, own_factor, row_delta,
    after, own_grad, own_part,
):
    chunks = own_weights.shape[0]
    groups, _, width = own_part.shape[1:]

    def differentiate(n):
        prob = own_weights[n] * (own_factor[n] * near_factor[n])
        score_grad = (prob * (own_prob_grad[n] - row_delta[n])).astype(jnp.bfloat16)
        own_grad[n] = score_grad
        return score_grad, prob.astype(jnp.bfloat16)

    def store(g, key_part, value_part):
        own_part[0, g] = key_part * width ** (-0.5)
        own_part[1, g] = value_part

    accumulate = accumulator(query_head, grad_head, chunks, groups, store)
    pipelined(chunks, differentiate, accumulate)


def join_two_kernel(two_mine, other_keys, other_values, two_part):
    groups = two_mine.shape[1]
    two_part[:, my_heads(groups)] = two_mine[...]
    two_part[0, other_heads(groups)] = other_keys[...]
    two_part[1, other_heads(groups)] = other_values[...]


def query_kernel(
    own, back_one, back_two, two_keys, attended_rows, two_grad, one_grad, own_grad,
    out_mine, query_mine, first_third, second_third, last_third, query_send,
):
    sends = (first_third, second_third, last_third)
    groups = own.shape[1]
    chunks = own_grad.shape[0]
    heads, length, width = out_mine.shape
    count = heads // chunks
    for n in range(chunks):
        g = n * groups // chunks
        rows = pl.ds(n * count, count)
        keys = join(two_back(back_two, (two_keys,), 0, g), back_one[0, g], own[0, g])
        part = matmul(keys, join(two_grad[n], one_grad[n], own_grad[n]), (0, 0))
        part = (part * width ** (-0.5)).astype(jnp.bfloat16)
        for index, (columns, mine) in enumerate(((attended_rows[n], out_mine), (part, query_mine))):
            block = columns.T.reshape(count, 2 * length, width)
            mine[rows] = block[:, :length]
            query_send[index, rows] = block[:, length:]
    for index, row, piece, taken in placed(sends, heads):
        piece[...] = query_send[index, pl.ds(row, taken)]


def assemble_kernel(
    out_mine, query_mine, first_third, second_third, last_third, out, query_grad, token
):
    heads = out_mine.shape[0]
    start = (1 - lax.axis_index("head")) * heads
    out[my_heads(heads)] = out_mine[...]
    query_grad[my_heads(heads)] = query_mine[...]
    for index, row, piece, count in placed((first_third, second_third, last_third), heads):
        (out, query_grad)[index][pl.ds(start + row, count)] = piece[...]
    token[...] = jnp.zeros(token.shape, token.dtype)


def own_sum_kernel(own_part, one_total, sum_mine, sum_send):
    length = sum_mine.shape[2]
    total = own_part[...] + one_total[...].astype(jnp.float32)
    sum_mine[...] = total[:, :, :length]
    sum_send[...] = total[:, :, length:].astype(jnp.bfloat16)


def final_kernel(sum_mine, sum_other, two_total, after, key_grad, value_grad):
    groups = sum_mine.shape[1]
    mine, other = my_heads(groups), other_heads(groups)
    for index, result in enumerate((key_grad, value_grad)):
        total = sum_mine[index] + two_total[index, mine].astype(jnp.float32)
        result[mine] = total.astype(jnp.bfloat16)
        total = sum_other[index].astype(jnp.float32) + two_total[index, other].astype(jnp.float32)
        result[other] = total.astype(jnp.bfloat16)


def shards(query_matrix, key_matrix, value_matrix, output_gradient, query_head_spans, slab_offset):
    groups, length, width = key_matrix.shape
    heads = query_matrix.shape[0]
    cores = lax.axis_size("head")
    tokens = cores * length
    groups_here, heads_here = groups // cores, heads // cores
    count = max(1, min(heads // groups, 256 // tokens))
    chunks = heads_here // count
    lanes = count * tokens
    half, full = jnp.bfloat16, jnp.float32
    vmem = pl.BlockSpec(memory_space=pltpu.VMEM)
    smem = pl.BlockSpec(memory_space=pltpu.SMEM)

    def call(kernel, name, outs, arrays, scalars=0, scratch=()):
        return pl.pallas_call(
            kernel,
            out_shape=tuple(jax.ShapeDtypeStruct(shape, kind) for shape, kind in outs),
            in_specs=[smem] * scalars + [vmem] * (len(arrays) - scalars),
            out_specs=(vmem,) * len(outs),
            scratch_shapes=scratch,
            compiler_params=pltpu.CompilerParams(vmem_limit_bytes=40 * 1024 * 1024),
            cost_estimate=pl.CostEstimate(flops=1, bytes_accessed=0, transcendentals=0),
            name=name,
        )(*arrays)

    def rows_of(rows, kind):
        return ((chunks, rows, lanes), kind)

    stat = rows_of(1, full)
    whole_pair = ((2, groups, length, width), half)
    half_block = ((groups_here, length, width), half)
    half_pair = ((2, groups_here, length, width), half)
    chip_pair = ((2, groups_here, tokens, width), half)
    half_rows = ((heads_here, length, width), half)
    third_rows = [((rows, length, width), half) for rows in thirds(heads_here)]
    chip_rows = ((heads_here, tokens, width), half)

    own = jnp.stack([key_matrix, value_matrix])
    back_two = shifted(own, "seq", 2)
    own_sends = call(split_kernel, "split_own", [half_block] * 2, (own,))
    (own_head,) = call(
        join_own_kernel, "join_own", [chip_pair], (own, *[swapped(send, "head") for send in own_sends])
    )
    back_one = shifted(own_head, "seq", 1)
    sends = call(
        split_rows_kernel,
        "split_rows",
        third_rows,
        (query_matrix, output_gradient, own),
    )
    (
        query_head, grad_head, grad_rows, first, own_max, own_total, own_out, own_weights,
        own_prob_grad,
    ) = call(
        own_kernel,
        "own_block",
        [
            chip_rows, chip_rows, rows_of(width, half), rows_of(1, jnp.int32), stat, stat,
            rows_of(width, full), rows_of(tokens, full), rows_of(tokens, full),
        ],
        (
            query_head_spans, slab_offset, query_matrix, output_gradient,
            *[swapped(send, "head") for send in sends], own_head,
        ),
        scalars=2,
    )
    back_two, first = lax.optimization_barrier((back_two, first))
    two_sends = call(split_kernel, "split_two", [half_block] * 2, (back_two,))
    two_other = [swapped(send, "head") for send in two_sends]
    near_max, near_total, near_out, near_weights, near_prob_grad, own_factor = call(
        near_forward_kernel,
        "near_forward",
        [stat, stat, rows_of(width, full), rows_of(tokens, full), rows_of(tokens, full), stat],
        (first, query_head, grad_head, back_two, *two_other, own_max, own_total, own_out),
    )
    back_one, near_max = lax.optimization_barrier((back_one, near_max))
    attended_rows, row_delta, near_factor, one_grad, one_part = call(
        last_kernel,
        "last_forward_backward",
        [rows_of(width, half), stat, stat, rows_of(tokens, half), chip_pair],
        (first, query_head, grad_head, back_one, grad_rows, near_max, near_total, near_out),
    )
    one_total = shifted(one_part, "seq", -1)
    two_grad, part_mine, *part_sends = call(
        two_backward_kernel,
        "two_backward",
        [rows_of(tokens, half), half_pair, half_block, half_block],
        (query_head, grad_head, near_weights, near_prob_grad, near_factor, row_delta),
    )
    (two_part,) = call(
        join_two_kernel,
        "join_two",
        [whole_pair],
        (part_mine, *[swapped(send, "head") for send in part_sends]),
    )
    two_total = shifted(two_part, "seq", -2)
    own_grad, own_part = call(
        own_backward_kernel,
        "own_backward",
        [rows_of(tokens, half), (chip_pair[0], full)],
        (
            query_head, grad_head, own_weights, own_prob_grad, near_factor, own_factor, row_delta,
            two_part,
        ),
    )
    out_mine, query_mine, *sends = call(
        query_kernel,
        "query_grad",
        [half_rows] * 2 + third_rows,
        (own_head, back_one, back_two, two_other[0], attended_rows, two_grad, one_grad, own_grad),
        scratch=[pltpu.VMEM((2,) + half_rows[0], half)],
    )
    attn_out, query_grad, token = call(
        assemble_kernel,
        "assemble",
        [(query_matrix.shape, half)] * 2 + [((8, 128), full)],
        (out_mine, query_mine, *[swapped(send, "head") for send in sends]),
    )
    sum_mine, sum_send = call(
        own_sum_kernel, "own_sum", [(half_pair[0], full), half_pair], (own_part, one_total)
    )
    key_grad, value_grad = call(
        final_kernel,
        "total",
        [(key_matrix.shape, half)] * 2,
        (sum_mine, swapped(sum_send, "head"), two_total, token),
    )
    return (attn_out, query_grad, key_grad, value_grad)


def solution(mesh):
    tokens = P(None, ("seq", "head"), None)
    return jax.shard_map(
        shards,
        mesh=mesh,
        in_specs=(tokens, tokens, tokens, tokens, P(), P()),
        out_specs=(tokens, tokens, tokens, tokens),
        check_vma=False,
    )
```

```python
import math

import jax
import jax.numpy as jnp
from jax import lax
from jax.experimental import pallas as pl
from jax.experimental.pallas import tpu as pltpu
from jax.sharding import PartitionSpec as P

REACH = 2
SEGMENT = 512

masked_score = -1e30


def shifted(block, axis, distance):
    devices = range(lax.axis_size(axis))
    route = [(i - distance, i) for i in devices if i - distance in devices]
    return lax.ppermute(block, axis, route)


def swapped(block, axis):
    count = lax.axis_size(axis)
    return lax.ppermute(block, axis, [(i, count - 1 - i) for i in range(count)])


def matmul(left, right, contract):
    return lax.dot_general(
        left, right, ((contract[:1], contract[1:]), ((), ())), preferred_element_type=jnp.float32
    )


def grouped(ref, n, count):
    _, length, width = ref.shape
    return ref[pl.ds(n * count, count)].reshape(count * length, width)


def join(*blocks):
    return jnp.concatenate(blocks, axis=0)


def core_offsets(length):
    core = lax.axis_index("head")
    return core * length, (1 - core) * length


def my_heads(count):
    return pl.ds(lax.axis_index("head") * count, count)


def other_heads(count):
    return pl.ds((1 - lax.axis_index("head")) * count, count)


def lane_tokens(count, length):
    lane = lax.broadcasted_iota(jnp.int32, (1, count * 2 * length), 1)
    token = lane - lane // (2 * length) * (2 * length)
    mine, other = core_offsets(length)
    return jnp.where(token < length, token + mine, token - length + other)


def first_visible(spans, offset, chunks, count, length):
    token = lane_tokens(count, length)
    lane_head = lax.broadcasted_iota(jnp.int32, token.shape, 1) // (2 * length)
    start = lax.axis_index("seq") * 2 * length
    segment_start = token - lax.bitwise_and(offset[0] + start + token, SEGMENT - 1)
    floor = jnp.maximum(segment_start, -start)
    base = lax.axis_index("head") * chunks * count
    result = []
    for n in range(chunks):
        span = jnp.full(token.shape, spans[base + n * count], jnp.int32)
        for a in range(1, count):
            span = jnp.where(lane_head == a, spans[base + n * count + a], span)
        result.append(jnp.maximum(floor, token - span + 1))
    return result


def masked(scores, first, chips_back, token=None):
    length = scores.shape[0] // 2
    row = lax.broadcasted_iota(jnp.int32, (length, scores.shape[1]), 0)
    pieces = []
    for part, offset in enumerate(core_offsets(length)):
        visible = row >= first + (chips_back * 2 * length - offset)
        if token is not None:
            visible &= row <= token - offset
        pieces.append(
            jnp.where(visible, scores[part * length : (part + 1) * length], masked_score)
        )
    return join(*pieces)


def split_kernel(block, *sends):
    for index, send in enumerate(sends):
        send[...] = block[index, other_heads(send.shape[0])]


def thirds(rows):
    return [2 * rows * (i + 1) // 3 - 2 * rows * i // 3 for i in range(3)]


def placed(pieces, rows):
    taken = 0
    for piece in pieces:
        count = piece.shape[0]
        for index in range(2):
            low = max(taken, index * rows)
            high = min(taken + count, (index + 1) * rows)
            if low < high:
                yield index, low - index * rows, piece.at[pl.ds(low - taken, high - low)], high - low
        taken += count


def split_rows_kernel(queries, grads, after, *sends):
    heads = queries.shape[0] // 2
    start = (1 - lax.axis_index("head")) * heads
    for index, row, piece, count in placed(sends, heads):
        piece[...] = (queries, grads)[index][pl.ds(start + row, count)]


def join_own_kernel(own, other_keys, other_values, own_head):
    groups, length = other_keys.shape[:2]
    own_head[:, :, pl.ds(0, length)] = own[:, my_heads(groups)]
    own_head[0, :, pl.ds(length, length)] = other_keys[...]
    own_head[1, :, pl.ds(length, length)] = other_values[...]


def own_kernel(
    spans, offset, queries, grads, first_third, second_third, last_third, own,
    query_head, grad_head, grad_rows, first, own_max, own_total, own_out, own_weights,
    own_prob_grad,
):
    heads, _, width = query_head.shape
    length = queries.shape[1]
    groups = own.shape[1]
    chunks = first.shape[0]
    count = heads // chunks
    query_head[:, pl.ds(0, length)] = queries[my_heads(heads)]
    grad_head[:, pl.ds(0, length)] = grads[my_heads(heads)]
    for index, row, piece, rows in placed((first_third, second_third, last_third), heads):
        (query_head, grad_head)[index][pl.ds(row, rows), pl.ds(length, length)] = piece[...]
    factor = width ** (-0.5) * math.log2(math.e)
    token = lane_tokens(count, length)
    for n, rows in enumerate(first_visible(spans, offset, chunks, count, length)):
        first[n] = rows

    def products(n):
        g = n * groups // chunks
        own_prob_grad[n] = matmul(own[1, g], grouped(grad_head, n, count), (1, 1))
        return (matmul(own[0, g], grouped(query_head, n, count), (1, 1)),)

    def softmax(n, scores):
        scores = masked(scores * factor, first[n], 0, token)
        row_max = jnp.max(scores, axis=0, keepdims=True)
        weights = jnp.exp2(scores - row_max)
        own_max[n] = row_max
        own_total[n] = jnp.sum(weights, axis=0, keepdims=True)
        own_weights[n] = weights
        return (weights.astype(jnp.bfloat16),)

    def weigh(n, halves):
        own_out[n] = matmul(own[1, n * groups // chunks], halves, (0, 0))
        grad_rows[n] = grouped(grad_head, n, count).T

    pipelined(chunks, products, softmax, weigh)


def two_back(back_two, two_other, index, g):
    base = lax.axis_index("head") * two_other[index].shape[0]
    return join(back_two[index, base + g], two_other[index][g])


def near_forward_kernel(
    first, query_head, grad_head, back_two, two_keys, two_values, own_max, own_total, own_out,
    near_max, near_total, near_out, near_weights, near_prob_grad, own_factor,
):
    groups = two_keys.shape[0]
    two_other = (two_keys, two_values)
    chunks = first.shape[0]
    heads, _, width = query_head.shape
    count = heads // chunks
    factor = width ** (-0.5) * math.log2(math.e)

    def products(n):
        g = n * groups // chunks
        keys = two_back(back_two, two_other, 0, g)
        values = two_back(back_two, two_other, 1, g)
        near_prob_grad[n] = matmul(values, grouped(grad_head, n, count), (1, 1))
        return (matmul(keys, grouped(query_head, n, count), (1, 1)),)

    def softmax(n, scores):
        scores = masked(scores * factor, first[n], 2)
        row_max = jnp.maximum(own_max[n], jnp.max(scores, axis=0, keepdims=True))
        weights = jnp.exp2(scores - row_max)
        rescale = jnp.exp2(own_max[n] - row_max)
        own_factor[n] = rescale
        near_max[n] = row_max
        near_total[n] = own_total[n] * rescale + jnp.sum(weights, axis=0, keepdims=True)
        near_weights[n] = weights
        return rescale, weights.astype(jnp.bfloat16)

    def weigh(n, rescale, halves):
        values = two_back(back_two, two_other, 1, n * groups // chunks)
        near_out[n] = own_out[n] * rescale + matmul(values, halves, (0, 0))

    pipelined(chunks, products, softmax, weigh)


def last_kernel(
    first, query_head, grad_head, back_one, grad_rows, near_max, near_total, near_out,
    attended_rows, row_delta, near_factor, one_grad, one_part,
):
    groups = back_one.shape[1]
    chunks = first.shape[0]
    heads, _, width = query_head.shape
    count = heads // chunks
    scale = width ** (-0.5)

    def products(n):
        g = n * groups // chunks
        scores = matmul(back_one[0, g], grouped(query_head, n, count), (1, 1))
        prob_grad = matmul(back_one[1, g], grouped(grad_head, n, count), (1, 1))
        return scores, prob_grad

    def softmax(n, scores, prob_grad):
        scores = masked(scores * (scale * math.log2(math.e)), first[n], 1)
        row_max = jnp.maximum(near_max[n], jnp.max(scores, axis=0, keepdims=True))
        weights = jnp.exp2(scores - row_max)
        rescale = jnp.exp2(near_max[n] - row_max)
        inverse = 1.0 / (near_total[n] * rescale + jnp.sum(weights, axis=0, keepdims=True))
        weighted = matmul(
            back_one[1, n * groups // chunks], weights.astype(jnp.bfloat16), (0, 0)
        )
        near_factor[n] = rescale * inverse
        return prob_grad, weights, weighted, rescale, inverse

    def differentiate(n, prob_grad, weights, weighted, rescale, inverse):
        attended = ((near_out[n] * rescale + weighted) * inverse).astype(jnp.bfloat16)
        delta = jnp.sum(
            grad_rows[n].astype(jnp.float32) * attended.astype(jnp.float32), axis=0, keepdims=True
        )
        prob = weights * inverse
        score_grad = (prob * (prob_grad - delta)).astype(jnp.bfloat16)
        attended_rows[n] = attended
        row_delta[n] = delta
        one_grad[n] = score_grad
        return score_grad, prob.astype(jnp.bfloat16)

    def store(g, key_part, value_part):
        one_part[0, g] = (key_part * scale).astype(jnp.bfloat16)
        one_part[1, g] = value_part.astype(jnp.bfloat16)

    accumulate = accumulator(query_head, grad_head, chunks, groups, store)
    pipelined(chunks, products, softmax, differentiate, accumulate)


def pipelined(chunks, *stages):
    ready = [{} for _ in range(len(stages) + 1)]
    for step in range(chunks + len(stages) - 1):
        for depth, stage in enumerate(stages):
            n = step - depth
            if 0 <= n < chunks:
                ready[depth + 1][n] = stage(n, *ready[depth].pop(n, ())) or ()


def accumulator(query_head, grad_head, chunks, groups, store):
    count = query_head.shape[0] // chunks
    parts = {}

    def accumulate(n, score_grad, half):
        g = n * groups // chunks
        key_part = matmul(score_grad, grouped(query_head, n, count), (1, 0))
        value_part = matmul(half, grouped(grad_head, n, count), (1, 0))
        if g in parts:
            key_part, value_part = parts[g][0] + key_part, parts[g][1] + value_part
        parts[g] = (key_part, value_part)
        if (n + 1) * groups // chunks != g:
            store(g, key_part, value_part)

    return accumulate


def two_backward_kernel(
    query_head, grad_head, near_weights, near_prob_grad, near_factor, row_delta,
    two_grad, two_mine, send_keys, send_values,
):
    chunks = near_weights.shape[0]
    groups, length, width = two_mine.shape[1:]

    def differentiate(n):
        prob = near_weights[n] * near_factor[n]
        score_grad = (prob * (near_prob_grad[n] - row_delta[n])).astype(jnp.bfloat16)
        two_grad[n] = score_grad
        return score_grad, prob.astype(jnp.bfloat16)

    def store(g, key_part, value_part):
        for index, (part, send) in enumerate(
            ((key_part * width ** (-0.5), send_keys), (value_part, send_values))
        ):
            two_mine[index, g] = part[:length].astype(jnp.bfloat16)
            send[g] = part[length:].astype(jnp.bfloat16)

    accumulate = accumulator(query_head, grad_head, chunks, groups, store)
    pipelined(chunks, differentiate, accumulate)


def own_backward_kernel(
    query_head, grad_head, own_weights, own_prob_grad, near_factor, own_factor, row_delta,
    after, own_grad, own_part,
):
    chunks = own_weights.shape[0]
    groups, _, width = own_part.shape[1:]

    def differentiate(n):
        prob = own_weights[n] * (own_factor[n] * near_factor[n])
        score_grad = (prob * (own_prob_grad[n] - row_delta[n])).astype(jnp.bfloat16)
        own_grad[n] = score_grad
        return score_grad, prob.astype(jnp.bfloat16)

    def store(g, key_part, value_part):
        own_part[0, g] = key_part * width ** (-0.5)
        own_part[1, g] = value_part

    accumulate = accumulator(query_head, grad_head, chunks, groups, store)
    pipelined(chunks, differentiate, accumulate)


def join_two_kernel(two_mine, other_keys, other_values, two_part):
    groups = two_mine.shape[1]
    two_part[:, my_heads(groups)] = two_mine[...]
    two_part[0, other_heads(groups)] = other_keys[...]
    two_part[1, other_heads(groups)] = other_values[...]


def query_kernel(
    own, back_one, back_two, two_keys, attended_rows, two_grad, one_grad, own_grad,
    out_mine, query_mine, first_third, second_third, last_third, query_send,
):
    sends = (first_third, second_third, last_third)
    groups = own.shape[1]
    chunks = own_grad.shape[0]
    heads, length, width = out_mine.shape
    count = heads // chunks
    for n in range(chunks):
        g = n * groups // chunks
        rows = pl.ds(n * count, count)
        keys = join(two_back(back_two, (two_keys,), 0, g), back_one[0, g], own[0, g])
        part = matmul(keys, join(two_grad[n], one_grad[n], own_grad[n]), (0, 0))
        part = (part * width ** (-0.5)).astype(jnp.bfloat16)
        for index, (columns, mine) in enumerate(((attended_rows[n], out_mine), (part, query_mine))):
            block = columns.T.reshape(count, 2 * length, width)
            mine[rows] = block[:, :length]
            query_send[index, rows] = block[:, length:]
    for index, row, piece, taken in placed(sends, heads):
        piece[...] = query_send[index, pl.ds(row, taken)]


def assemble_kernel(
    out_mine, query_mine, first_third, second_third, last_third, out, query_grad, token
):
    heads = out_mine.shape[0]
    start = (1 - lax.axis_index("head")) * heads
    out[my_heads(heads)] = out_mine[...]
    query_grad[my_heads(heads)] = query_mine[...]
    for index, row, piece, count in placed((first_third, second_third, last_third), heads):
        (out, query_grad)[index][pl.ds(start + row, count)] = piece[...]
    token[...] = jnp.zeros(token.shape, token.dtype)


def own_sum_kernel(own_part, one_total, sum_mine, sum_send):
    length = sum_mine.shape[2]
    total = own_part[...] + one_total[...].astype(jnp.float32)
    sum_mine[...] = total[:, :, :length]
    sum_send[...] = total[:, :, length:].astype(jnp.bfloat16)


def final_kernel(sum_mine, sum_other, two_total, after, key_grad, value_grad):
    groups = sum_mine.shape[1]
    mine, other = my_heads(groups), other_heads(groups)
    for index, result in enumerate((key_grad, value_grad)):
        total = sum_mine[index] + two_total[index, mine].astype(jnp.float32)
        result[mine] = total.astype(jnp.bfloat16)
        total = sum_other[index].astype(jnp.float32) + two_total[index, other].astype(jnp.float32)
        result[other] = total.astype(jnp.bfloat16)


def shards(query_matrix, key_matrix, value_matrix, output_gradient, query_head_spans, slab_offset):
    groups, length, width = key_matrix.shape
    heads = query_matrix.shape[0]
    cores = lax.axis_size("head")
    tokens = cores * length
    groups_here, heads_here = groups // cores, heads // cores
    count = max(1, min(heads // groups, 256 // tokens))
    chunks = heads_here // count
    lanes = count * tokens
    half, full = jnp.bfloat16, jnp.float32
    vmem = pl.BlockSpec(memory_space=pltpu.VMEM)
    smem = pl.BlockSpec(memory_space=pltpu.SMEM)

    def call(kernel, name, outs, arrays, scalars=0, scratch=()):
        return pl.pallas_call(
            kernel,
            out_shape=tuple(jax.ShapeDtypeStruct(shape, kind) for shape, kind in outs),
            in_specs=[smem] * scalars + [vmem] * (len(arrays) - scalars),
            out_specs=(vmem,) * len(outs),
            scratch_shapes=scratch,
            compiler_params=pltpu.CompilerParams(vmem_limit_bytes=40 * 1024 * 1024),
            cost_estimate=pl.CostEstimate(flops=1, bytes_accessed=0, transcendentals=0),
            name=name,
        )(*arrays)

    def rows_of(rows, kind):
        return ((chunks, rows, lanes), kind)

    stat = rows_of(1, full)
    whole_pair = ((2, groups, length, width), half)
    half_block = ((groups_here, length, width), half)
    half_pair = ((2, groups_here, length, width), half)
    chip_pair = ((2, groups_here, tokens, width), half)
    half_rows = ((heads_here, length, width), half)
    third_rows = [((rows, length, width), half) for rows in thirds(heads_here)]
    chip_rows = ((heads_here, tokens, width), half)

    own = jnp.stack([key_matrix, value_matrix])
    chips = lax.axis_size("seq")
    back_two = lax.ppermute(own, "seq", [(i, (i + 2) % chips) for i in range(chips)])
    own_sends = call(split_kernel, "split_own", [half_block] * 2, (own,))
    (own_head,) = call(
        join_own_kernel, "join_own", [chip_pair], (own, *[swapped(send, "head") for send in own_sends])
    )
    back_one = shifted(own_head, "seq", 1)
    sends = call(
        split_rows_kernel,
        "split_rows",
        third_rows,
        (query_matrix, output_gradient, own),
    )
    (
        query_head, grad_head, grad_rows, first, own_max, own_total, own_out, own_weights,
        own_prob_grad,
    ) = call(
        own_kernel,
        "own_block",
        [
            chip_rows, chip_rows, rows_of(width, half), rows_of(1, jnp.int32), stat, stat,
            rows_of(width, full), rows_of(tokens, full), rows_of(tokens, full),
        ],
        (
            query_head_spans, slab_offset, query_matrix, output_gradient,
            *[swapped(send, "head") for send in sends], own_head,
        ),
        scalars=2,
    )
    back_two, first = lax.optimization_barrier((back_two, first))
    two_sends = call(split_kernel, "split_two", [half_block] * 2, (back_two,))
    two_other = [swapped(send, "head") for send in two_sends]
    near_max, near_total, near_out, near_weights, near_prob_grad, own_factor = call(
        near_forward_kernel,
        "near_forward",
        [stat, stat, rows_of(width, full), rows_of(tokens, full), rows_of(tokens, full), stat],
        (first, query_head, grad_head, back_two, *two_other, own_max, own_total, own_out),
    )
    back_one, near_max = lax.optimization_barrier((back_one, near_max))
    attended_rows, row_delta, near_factor, one_grad, one_part = call(
        last_kernel,
        "last_forward_backward",
        [rows_of(width, half), stat, stat, rows_of(tokens, half), chip_pair],
        (first, query_head, grad_head, back_one, grad_rows, near_max, near_total, near_out),
    )
    one_total = shifted(one_part, "seq", -1)
    two_grad, part_mine, *part_sends = call(
        two_backward_kernel,
        "two_backward",
        [rows_of(tokens, half), half_pair, half_block, half_block],
        (query_head, grad_head, near_weights, near_prob_grad, near_factor, row_delta),
    )
    (two_part,) = call(
        join_two_kernel,
        "join_two",
        [whole_pair],
        (part_mine, *[swapped(send, "head") for send in part_sends]),
    )
    two_total = shifted(two_part, "seq", -2)
    own_grad, own_part = call(
        own_backward_kernel,
        "own_backward",
        [rows_of(tokens, half), (chip_pair[0], full)],
        (
            query_head, grad_head, own_weights, own_prob_grad, near_factor, own_factor, row_delta,
            two_part,
        ),
    )
    out_mine, query_mine, *sends = call(
        query_kernel,
        "query_grad",
        [half_rows] * 2 + third_rows,
        (own_head, back_one, back_two, two_other[0], attended_rows, two_grad, one_grad, own_grad),
        scratch=[pltpu.VMEM((2,) + half_rows[0], half)],
    )
    attn_out, query_grad, token = call(
        assemble_kernel,
        "assemble",
        [(query_matrix.shape, half)] * 2 + [((8, 128), full)],
        (out_mine, query_mine, *[swapped(send, "head") for send in sends]),
    )
    sum_mine, sum_send = call(
        own_sum_kernel, "own_sum", [(half_pair[0], full), half_pair], (own_part, one_total)
    )
    key_grad, value_grad = call(
        final_kernel,
        "total",
        [(key_matrix.shape, half)] * 2,
        (sum_mine, swapped(sum_send, "head"), two_total, token),
    )
    return (attn_out, query_grad, key_grad, value_grad)


def solution(mesh):
    tokens = P(None, ("seq", "head"), None)
    return jax.shard_map(
        shards,
        mesh=mesh,
        in_specs=(tokens, tokens, tokens, tokens, P(), P()),
        out_specs=(tokens, tokens, tokens, tokens),
        check_vma=False,
    )
```

```python
import math

import jax
import jax.numpy as jnp
from jax import lax
from jax.experimental import pallas as pl
from jax.experimental.pallas import tpu as pltpu
from jax.sharding import PartitionSpec as P

REACH = 2
SEGMENT = 512

masked_score = -1e30


def shifted(block, axis, distance):
    count = lax.axis_size(axis)
    return lax.ppermute(block, axis, [(i, (i + distance) % count) for i in range(count)])


def swapped(block, axis):
    count = lax.axis_size(axis)
    return lax.ppermute(block, axis, [(i, count - 1 - i) for i in range(count)])


def matmul(left, right, contract):
    return lax.dot_general(
        left, right, ((contract[:1], contract[1:]), ((), ())), preferred_element_type=jnp.float32
    )


def grouped(ref, n, count):
    _, length, width = ref.shape
    return ref[pl.ds(n * count, count)].reshape(count * length, width)


def join(*blocks):
    return jnp.concatenate(blocks, axis=0)


def core_offsets(length):
    core = lax.axis_index("head")
    return core * length, (1 - core) * length


def my_heads(count):
    return pl.ds(lax.axis_index("head") * count, count)


def other_heads(count):
    return pl.ds((1 - lax.axis_index("head")) * count, count)


def lane_tokens(count, length):
    lane = lax.broadcasted_iota(jnp.int32, (1, count * 2 * length), 1)
    token = lane - lane // (2 * length) * (2 * length)
    mine, other = core_offsets(length)
    return jnp.where(token < length, token + mine, token - length + other)


def first_visible(spans, offset, chunks, count, length):
    token = lane_tokens(count, length)
    lane_head = lax.broadcasted_iota(jnp.int32, token.shape, 1) // (2 * length)
    start = lax.axis_index("seq") * 2 * length
    segment_start = token - lax.bitwise_and(offset[0] + start + token, SEGMENT - 1)
    floor = jnp.maximum(segment_start, -start)
    base = lax.axis_index("head") * chunks * count
    result = []
    for n in range(chunks):
        span = jnp.full(token.shape, spans[base + n * count], jnp.int32)
        for a in range(1, count):
            span = jnp.where(lane_head == a, spans[base + n * count + a], span)
        result.append(jnp.maximum(floor, token - span + 1))
    return result


def masked(scores, first, chips_back, token=None):
    length = scores.shape[0] // 2
    row = lax.broadcasted_iota(jnp.int32, (length, scores.shape[1]), 0)
    pieces = []
    for part, offset in enumerate(core_offsets(length)):
        visible = row >= first + (chips_back * 2 * length - offset)
        if token is not None:
            visible &= row <= token - offset
        pieces.append(
            jnp.where(visible, scores[part * length : (part + 1) * length], masked_score)
        )
    return join(*pieces)


def split_kernel(block, *sends):
    for index, send in enumerate(sends):
        send[...] = block[index, other_heads(send.shape[0])]


def thirds(rows):
    return [2 * rows * (i + 1) // 3 - 2 * rows * i // 3 for i in range(3)]


def placed(pieces, rows):
    taken = 0
    for piece in pieces:
        count = piece.shape[0]
        for index in range(2):
            low = max(taken, index * rows)
            high = min(taken + count, (index + 1) * rows)
            if low < high:
                yield index, low - index * rows, piece.at[pl.ds(low - taken, high - low)], high - low
        taken += count


def split_rows_kernel(queries, grads, after, *sends):
    heads = queries.shape[0] // 2
    start = (1 - lax.axis_index("head")) * heads
    for index, row, piece, count in placed(sends, heads):
        piece[...] = (queries, grads)[index][pl.ds(start + row, count)]


def join_own_kernel(own, other_keys, other_values, own_head):
    groups, length = other_keys.shape[:2]
    own_head[:, :, pl.ds(0, length)] = own[:, my_heads(groups)]
    own_head[0, :, pl.ds(length, length)] = other_keys[...]
    own_head[1, :, pl.ds(length, length)] = other_values[...]


def own_kernel(
    spans, offset, queries, grads, first_third, second_third, last_third, own,
    query_head, grad_head, grad_rows, first, own_max, own_total, own_out, own_weights,
    own_prob_grad,
):
    heads, _, width = query_head.shape
    length = queries.shape[1]
    groups = own.shape[1]
    chunks = first.shape[0]
    count = heads // chunks
    query_head[:, pl.ds(0, length)] = queries[my_heads(heads)]
    grad_head[:, pl.ds(0, length)] = grads[my_heads(heads)]
    for index, row, piece, rows in placed((first_third, second_third, last_third), heads):
        (query_head, grad_head)[index][pl.ds(row, rows), pl.ds(length, length)] = piece[...]
    factor = width ** (-0.5) * math.log2(math.e)
    token = lane_tokens(count, length)
    for n, rows in enumerate(first_visible(spans, offset, chunks, count, length)):
        first[n] = rows

    def products(n):
        g = n * groups // chunks
        own_prob_grad[n] = matmul(own[1, g], grouped(grad_head, n, count), (1, 1))
        return (matmul(own[0, g], grouped(query_head, n, count), (1, 1)),)

    def softmax(n, scores):
        scores = masked(scores * factor, first[n], 0, token)
        row_max = jnp.max(scores, axis=0, keepdims=True)
        weights = jnp.exp2(scores - row_max)
        own_max[n] = row_max
        own_total[n] = jnp.sum(weights, axis=0, keepdims=True)
        own_weights[n] = weights
        return (weights.astype(jnp.bfloat16),)

    def weigh(n, halves):
        own_out[n] = matmul(own[1, n * groups // chunks], halves, (0, 0))
        grad_rows[n] = grouped(grad_head, n, count).T

    pipelined(chunks, products, softmax, weigh)


def two_back(back_two, two_other, index, g):
    base = lax.axis_index("head") * two_other[index].shape[0]
    return join(back_two[index, base + g], two_other[index][g])


def near_forward_kernel(
    first, query_head, grad_head, back_two, two_keys, two_values, own_max, own_total, own_out,
    near_max, near_total, near_out, near_weights, near_prob_grad, own_factor,
):
    groups = two_keys.shape[0]
    two_other = (two_keys, two_values)
    chunks = first.shape[0]
    heads, _, width = query_head.shape
    count = heads // chunks
    factor = width ** (-0.5) * math.log2(math.e)

    def products(n):
        g = n * groups // chunks
        keys = two_back(back_two, two_other, 0, g)
        values = two_back(back_two, two_other, 1, g)
        near_prob_grad[n] = matmul(values, grouped(grad_head, n, count), (1, 1))
        return (matmul(keys, grouped(query_head, n, count), (1, 1)),)

    def softmax(n, scores):
        scores = masked(scores * factor, first[n], 2)
        row_max = jnp.maximum(own_max[n], jnp.max(scores, axis=0, keepdims=True))
        weights = jnp.exp2(scores - row_max)
        rescale = jnp.exp2(own_max[n] - row_max)
        own_factor[n] = rescale
        near_max[n] = row_max
        near_total[n] = own_total[n] * rescale + jnp.sum(weights, axis=0, keepdims=True)
        near_weights[n] = weights
        return rescale, weights.astype(jnp.bfloat16)

    def weigh(n, rescale, halves):
        values = two_back(back_two, two_other, 1, n * groups // chunks)
        near_out[n] = own_out[n] * rescale + matmul(values, halves, (0, 0))

    pipelined(chunks, products, softmax, weigh)


def last_kernel(
    first, query_head, grad_head, back_one, grad_rows, near_max, near_total, near_out,
    attended_rows, row_delta, near_factor, one_grad, one_part,
):
    groups = back_one.shape[1]
    chunks = first.shape[0]
    heads, _, width = query_head.shape
    count = heads // chunks
    scale = width ** (-0.5)

    def products(n):
        g = n * groups // chunks
        scores = matmul(back_one[0, g], grouped(query_head, n, count), (1, 1))
        prob_grad = matmul(back_one[1, g], grouped(grad_head, n, count), (1, 1))
        return scores, prob_grad

    def softmax(n, scores, prob_grad):
        scores = masked(scores * (scale * math.log2(math.e)), first[n], 1)
        row_max = jnp.maximum(near_max[n], jnp.max(scores, axis=0, keepdims=True))
        weights = jnp.exp2(scores - row_max)
        rescale = jnp.exp2(near_max[n] - row_max)
        inverse = 1.0 / (near_total[n] * rescale + jnp.sum(weights, axis=0, keepdims=True))
        weighted = matmul(
            back_one[1, n * groups // chunks], weights.astype(jnp.bfloat16), (0, 0)
        )
        near_factor[n] = rescale * inverse
        return prob_grad, weights, weighted, rescale, inverse

    def differentiate(n, prob_grad, weights, weighted, rescale, inverse):
        attended = ((near_out[n] * rescale + weighted) * inverse).astype(jnp.bfloat16)
        delta = jnp.sum(
            grad_rows[n].astype(jnp.float32) * attended.astype(jnp.float32), axis=0, keepdims=True
        )
        prob = weights * inverse
        score_grad = (prob * (prob_grad - delta)).astype(jnp.bfloat16)
        attended_rows[n] = attended
        row_delta[n] = delta
        one_grad[n] = score_grad
        return score_grad, prob.astype(jnp.bfloat16)

    def store(g, key_part, value_part):
        one_part[0, g] = (key_part * scale).astype(jnp.bfloat16)
        one_part[1, g] = value_part.astype(jnp.bfloat16)

    accumulate = accumulator(query_head, grad_head, chunks, groups, store)
    pipelined(chunks, products, softmax, differentiate, accumulate)


def pipelined(chunks, *stages):
    ready = [{} for _ in range(len(stages) + 1)]
    for step in range(chunks + len(stages) - 1):
        for depth, stage in enumerate(stages):
            n = step - depth
            if 0 <= n < chunks:
                ready[depth + 1][n] = stage(n, *ready[depth].pop(n, ())) or ()


def accumulator(query_head, grad_head, chunks, groups, store):
    count = query_head.shape[0] // chunks
    parts = {}

    def accumulate(n, score_grad, half):
        g = n * groups // chunks
        key_part = matmul(score_grad, grouped(query_head, n, count), (1, 0))
        value_part = matmul(half, grouped(grad_head, n, count), (1, 0))
        if g in parts:
            key_part, value_part = parts[g][0] + key_part, parts[g][1] + value_part
        parts[g] = (key_part, value_part)
        if (n + 1) * groups // chunks != g:
            store(g, key_part, value_part)

    return accumulate


def two_backward_kernel(
    query_head, grad_head, near_weights, near_prob_grad, near_factor, row_delta,
    two_grad, two_mine, send_keys, send_values,
):
    chunks = near_weights.shape[0]
    groups, length, width = two_mine.shape[1:]

    def differentiate(n):
        prob = near_weights[n] * near_factor[n]
        score_grad = (prob * (near_prob_grad[n] - row_delta[n])).astype(jnp.bfloat16)
        two_grad[n] = score_grad
        return score_grad, prob.astype(jnp.bfloat16)

    def store(g, key_part, value_part):
        for index, (part, send) in enumerate(
            ((key_part * width ** (-0.5), send_keys), (value_part, send_values))
        ):
            two_mine[index, g] = part[:length].astype(jnp.bfloat16)
            send[g] = part[length:].astype(jnp.bfloat16)

    accumulate = accumulator(query_head, grad_head, chunks, groups, store)
    pipelined(chunks, differentiate, accumulate)


def own_backward_kernel(
    query_head, grad_head, own_weights, own_prob_grad, near_factor, own_factor, row_delta,
    after, own_grad, own_part,
):
    chunks = own_weights.shape[0]
    groups, _, width = own_part.shape[1:]

    def differentiate(n):
        prob = own_weights[n] * (own_factor[n] * near_factor[n])
        score_grad = (prob * (own_prob_grad[n] - row_delta[n])).astype(jnp.bfloat16)
        own_grad[n] = score_grad
        return score_grad, prob.astype(jnp.bfloat16)

    def store(g, key_part, value_part):
        own_part[0, g] = key_part * width ** (-0.5)
        own_part[1, g] = value_part

    accumulate = accumulator(query_head, grad_head, chunks, groups, store)
    pipelined(chunks, differentiate, accumulate)


def join_two_kernel(two_mine, other_keys, other_values, two_part):
    groups = two_mine.shape[1]
    two_part[:, my_heads(groups)] = two_mine[...]
    two_part[0, other_heads(groups)] = other_keys[...]
    two_part[1, other_heads(groups)] = other_values[...]


def query_kernel(
    own, back_one, back_two, two_keys, attended_rows, two_grad, one_grad, own_grad,
    out_mine, query_mine, first_third, second_third, last_third, query_send,
):
    sends = (first_third, second_third, last_third)
    groups = own.shape[1]
    chunks = own_grad.shape[0]
    heads, length, width = out_mine.shape
    count = heads // chunks
    for n in range(chunks):
        g = n * groups // chunks
        rows = pl.ds(n * count, count)
        keys = join(two_back(back_two, (two_keys,), 0, g), back_one[0, g], own[0, g])
        part = matmul(keys, join(two_grad[n], one_grad[n], own_grad[n]), (0, 0))
        part = (part * width ** (-0.5)).astype(jnp.bfloat16)
        for index, (columns, mine) in enumerate(((attended_rows[n], out_mine), (part, query_mine))):
            block = columns.T.reshape(count, 2 * length, width)
            mine[rows] = block[:, :length]
            query_send[index, rows] = block[:, length:]
    for index, row, piece, taken in placed(sends, heads):
        piece[...] = query_send[index, pl.ds(row, taken)]


def assemble_kernel(
    out_mine, query_mine, first_third, second_third, last_third, out, query_grad, token
):
    heads = out_mine.shape[0]
    start = (1 - lax.axis_index("head")) * heads
    out[my_heads(heads)] = out_mine[...]
    query_grad[my_heads(heads)] = query_mine[...]
    for index, row, piece, count in placed((first_third, second_third, last_third), heads):
        (out, query_grad)[index][pl.ds(start + row, count)] = piece[...]
    token[...] = jnp.zeros(token.shape, token.dtype)


def own_sum_kernel(own_part, one_total, sum_mine, sum_send):
    length = sum_mine.shape[2]
    total = own_part[...] + one_total[...].astype(jnp.float32)
    sum_mine[...] = total[:, :, :length]
    sum_send[...] = total[:, :, length:].astype(jnp.bfloat16)


def final_kernel(sum_mine, sum_other, two_total, after, key_grad, value_grad):
    groups = sum_mine.shape[1]
    mine, other = my_heads(groups), other_heads(groups)
    for index, result in enumerate((key_grad, value_grad)):
        total = sum_mine[index] + two_total[index, mine].astype(jnp.float32)
        result[mine] = total.astype(jnp.bfloat16)
        total = sum_other[index].astype(jnp.float32) + two_total[index, other].astype(jnp.float32)
        result[other] = total.astype(jnp.bfloat16)


def shards(query_matrix, key_matrix, value_matrix, output_gradient, query_head_spans, slab_offset):
    groups, length, width = key_matrix.shape
    heads = query_matrix.shape[0]
    cores = lax.axis_size("head")
    tokens = cores * length
    groups_here, heads_here = groups // cores, heads // cores
    count = max(1, min(heads // groups, 256 // tokens))
    chunks = heads_here // count
    lanes = count * tokens
    half, full = jnp.bfloat16, jnp.float32
    vmem = pl.BlockSpec(memory_space=pltpu.VMEM)
    smem = pl.BlockSpec(memory_space=pltpu.SMEM)

    def call(kernel, name, outs, arrays, scalars=0, scratch=()):
        return pl.pallas_call(
            kernel,
            out_shape=tuple(jax.ShapeDtypeStruct(shape, kind) for shape, kind in outs),
            in_specs=[smem] * scalars + [vmem] * (len(arrays) - scalars),
            out_specs=(vmem,) * len(outs),
            scratch_shapes=scratch,
            compiler_params=pltpu.CompilerParams(vmem_limit_bytes=40 * 1024 * 1024),
            cost_estimate=pl.CostEstimate(flops=1, bytes_accessed=0, transcendentals=0),
            name=name,
        )(*arrays)

    def rows_of(rows, kind):
        return ((chunks, rows, lanes), kind)

    stat = rows_of(1, full)
    whole_pair = ((2, groups, length, width), half)
    half_block = ((groups_here, length, width), half)
    half_pair = ((2, groups_here, length, width), half)
    chip_pair = ((2, groups_here, tokens, width), half)
    half_rows = ((heads_here, length, width), half)
    third_rows = [((rows, length, width), half) for rows in thirds(heads_here)]
    chip_rows = ((heads_here, tokens, width), half)

    own = jnp.stack([key_matrix, value_matrix])
    back_two = shifted(own, "seq", 2)
    own_sends = call(split_kernel, "split_own", [half_block] * 2, (own,))
    (own_head,) = call(
        join_own_kernel, "join_own", [chip_pair], (own, *[swapped(send, "head") for send in own_sends])
    )
    back_one = shifted(own_head, "seq", 1)
    sends = call(
        split_rows_kernel,
        "split_rows",
        third_rows,
        (query_matrix, output_gradient, own),
    )
    (
        query_head, grad_head, grad_rows, first, own_max, own_total, own_out, own_weights,
        own_prob_grad,
    ) = call(
        own_kernel,
        "own_block",
        [
            chip_rows, chip_rows, rows_of(width, half), rows_of(1, jnp.int32), stat, stat,
            rows_of(width, full), rows_of(tokens, full), rows_of(tokens, full),
        ],
        (
            query_head_spans, slab_offset, query_matrix, output_gradient,
            *[swapped(send, "head") for send in sends], own_head,
        ),
        scalars=2,
    )
    back_two, first = lax.optimization_barrier((back_two, first))
    two_sends = call(split_kernel, "split_two", [half_block] * 2, (back_two,))
    two_other = [swapped(send, "head") for send in two_sends]
    near_max, near_total, near_out, near_weights, near_prob_grad, own_factor = call(
        near_forward_kernel,
        "near_forward",
        [stat, stat, rows_of(width, full), rows_of(tokens, full), rows_of(tokens, full), stat],
        (first, query_head, grad_head, back_two, *two_other, own_max, own_total, own_out),
    )
    back_one, near_max = lax.optimization_barrier((back_one, near_max))
    attended_rows, row_delta, near_factor, one_grad, one_part = call(
        last_kernel,
        "last_forward_backward",
        [rows_of(width, half), stat, stat, rows_of(tokens, half), chip_pair],
        (first, query_head, grad_head, back_one, grad_rows, near_max, near_total, near_out),
    )
    one_total = shifted(one_part, "seq", -1)
    two_grad, part_mine, *part_sends = call(
        two_backward_kernel,
        "two_backward",
        [rows_of(tokens, half), half_pair, half_block, half_block],
        (query_head, grad_head, near_weights, near_prob_grad, near_factor, row_delta),
    )
    (two_part,) = call(
        join_two_kernel,
        "join_two",
        [whole_pair],
        (part_mine, *[swapped(send, "head") for send in part_sends]),
    )
    two_total = shifted(two_part, "seq", -2)
    own_grad, own_part = call(
        own_backward_kernel,
        "own_backward",
        [rows_of(tokens, half), (chip_pair[0], full)],
        (
            query_head, grad_head, own_weights, own_prob_grad, near_factor, own_factor, row_delta,
            two_part,
        ),
    )
    out_mine, query_mine, *sends = call(
        query_kernel,
        "query_grad",
        [half_rows] * 2 + third_rows,
        (own_head, back_one, back_two, two_other[0], attended_rows, two_grad, one_grad, own_grad),
        scratch=[pltpu.VMEM((2,) + half_rows[0], half)],
    )
    attn_out, query_grad, token = call(
        assemble_kernel,
        "assemble",
        [(query_matrix.shape, half)] * 2 + [((8, 128), full)],
        (out_mine, query_mine, *[swapped(send, "head") for send in sends]),
    )
    sum_mine, sum_send = call(
        own_sum_kernel, "own_sum", [(half_pair[0], full), half_pair], (own_part, one_total)
    )
    key_grad, value_grad = call(
        final_kernel,
        "total",
        [(key_matrix.shape, half)] * 2,
        (sum_mine, swapped(sum_send, "head"), two_total, token),
    )
    return (attn_out, query_grad, key_grad, value_grad)


def solution(mesh):
    tokens = P(None, ("seq", "head"), None)
    return jax.shard_map(
        shards,
        mesh=mesh,
        in_specs=(tokens, tokens, tokens, tokens, P(), P()),
        out_specs=(tokens, tokens, tokens, tokens),
        check_vma=False,
    )
```

```python
import functools
import math

import jax
import jax.numpy as jnp
from jax import lax
from jax.experimental import pallas as pl
from jax.experimental.pallas import tpu as pltpu
from jax.sharding import PartitionSpec as P

REACH = 2
SEGMENT = 512

masked_score = -1e30


def shifted(block, axis, distance):
    count = lax.axis_size(axis)
    return lax.ppermute(block, axis, [(i, (i + distance) % count) for i in range(count)])


def swapped(block, axis):
    count = lax.axis_size(axis)
    return lax.ppermute(block, axis, [(i, count - 1 - i) for i in range(count)])


def matmul(left, right, contract):
    return lax.dot_general(
        left, right, ((contract[:1], contract[1:]), ((), ())), preferred_element_type=jnp.float32
    )


def grouped(ref, n, count):
    _, length, width = ref.shape
    return ref[pl.ds(n * count, count)].reshape(count * length, width)


def join(*blocks):
    return jnp.concatenate(blocks, axis=0)


def core_offsets(length):
    core = lax.axis_index("head")
    return core * length, (1 - core) * length


def my_heads(count):
    return pl.ds(lax.axis_index("head") * count, count)


def other_heads(count):
    return pl.ds((1 - lax.axis_index("head")) * count, count)


def lane_tokens(count, length):
    lane = lax.broadcasted_iota(jnp.int32, (1, count * 2 * length), 1)
    token = lane - lane // (2 * length) * (2 * length)
    mine, other = core_offsets(length)
    return jnp.where(token < length, token + mine, token - length + other)


def first_visible(spans, offset, chunks, count, length):
    token = lane_tokens(count, length)
    lane_head = lax.broadcasted_iota(jnp.int32, token.shape, 1) // (2 * length)
    start = lax.axis_index("seq") * 2 * length
    segment_start = token - lax.bitwise_and(offset[0] + start + token, SEGMENT - 1)
    floor = jnp.maximum(segment_start, -start)
    base = lax.axis_index("head") * chunks * count
    result = []
    for n in range(chunks):
        span = jnp.full(token.shape, spans[base + n * count], jnp.int32)
        for a in range(1, count):
            span = jnp.where(lane_head == a, spans[base + n * count + a], span)
        result.append(jnp.maximum(floor, token - span + 1))
    return result


def masked(scores, first, chips_back, token=None):
    length = scores.shape[0] // 2
    row = lax.broadcasted_iota(jnp.int32, (length, scores.shape[1]), 0)
    pieces = []
    for part, offset in enumerate(core_offsets(length)):
        visible = row >= first + (chips_back * 2 * length - offset)
        if token is not None:
            visible &= row <= token - offset
        pieces.append(
            jnp.where(visible, scores[part * length : (part + 1) * length], masked_score)
        )
    return join(*pieces)


def split_kernel(own, first_send, own_send):
    groups, part = own_send.shape[1], first_send.shape[2]
    for core in range(2):
        first_send[:, core] = own[:, core * groups : core * groups + part]
    own_send[...] = own[:, other_heads(groups)]


def join_own_kernel(own, own_other, *halves):
    groups, length = own_other.shape[1:3]
    part = halves[0].shape[1]
    start = lax.axis_index("head") * groups
    for index, target in enumerate(halves):
        target[:, :, pl.ds(0, length)] = own[:, pl.ds(start + index * part, part)]
        target[:, :, pl.ds(length, length)] = own_other[:, pl.ds(index * part, part)]


def split_two_kernel(back_two, *sends):
    for index, send in enumerate(sends):
        send[...] = back_two[index, 1 - lax.axis_index("head")]


def join_two_kernel(back_two, other_keys, other_values, target):
    length = other_keys.shape[1]
    target[:, :, pl.ds(0, length)] = back_two[:, lax.axis_index("head")]
    for index, other in enumerate((other_keys, other_values)):
        target[index, :, pl.ds(length, length)] = other[...]


def own_kernel(
    spans, offset, queries, grads, queries_other, grads_other, *refs
):
    (
        *halves, query_head, grad_head, grad_rows, first, own_max, own_total, own_out,
        own_weights, own_prob_grad,
    ) = refs
    heads, _, width = query_head.shape
    length = queries.shape[1]
    part = halves[0].shape[1]
    groups = part * len(halves)
    chunks = first.shape[0]
    count = heads // chunks
    mine = my_heads(heads)
    query_head[:, pl.ds(0, length)] = queries[mine]
    query_head[:, pl.ds(length, length)] = queries_other[mine]
    grad_head[:, pl.ds(0, length)] = grads[mine]
    grad_head[:, pl.ds(length, length)] = grads_other[mine]
    factor = width ** (-0.5) * math.log2(math.e)
    token = lane_tokens(count, length)
    for n, rows in enumerate(first_visible(spans, offset, chunks, count, length)):
        first[n] = rows

    def block(index, n):
        g = n * groups // chunks
        return halves[g // part][index, g % part]

    def products(n):
        own_prob_grad[n] = matmul(block(1, n), grouped(grad_head, n, count), (1, 1))
        return (matmul(block(0, n), grouped(query_head, n, count), (1, 1)),)

    def softmax(n, scores):
        scores = masked(scores * factor, first[n], 0, token)
        row_max = jnp.max(scores, axis=0, keepdims=True)
        weights = jnp.exp2(scores - row_max)
        own_max[n] = row_max
        own_total[n] = jnp.sum(weights, axis=0, keepdims=True)
        own_weights[n] = weights
        return (weights.astype(jnp.bfloat16),)

    def weigh(n, halved):
        own_out[n] = matmul(block(1, n), halved, (0, 0))
        grad_rows[n] = grouped(grad_head, n, count).T

    pipelined(chunks, products, softmax, weigh)


def near_kernel(
    base, first, query_head, grad_head, back_two, own_max, own_total, own_out, after,
    near_max, near_total, near_out, near_weights, near_prob_grad, own_factor,
):
    groups = back_two.shape[1]
    chunks = near_max.shape[0]
    heads, _, width = query_head.shape
    count = heads // first.shape[0]
    factor = width ** (-0.5) * math.log2(math.e)

    def products(n):
        g = n * groups // chunks
        near_prob_grad[n] = matmul(back_two[1, g], grouped(grad_head, base + n, count), (1, 1))
        return (matmul(back_two[0, g], grouped(query_head, base + n, count), (1, 1)),)

    def softmax(n, scores):
        scores = masked(scores * factor, first[base + n], 2)
        before = own_max[base + n]
        row_max = jnp.maximum(before, jnp.max(scores, axis=0, keepdims=True))
        weights = jnp.exp2(scores - row_max)
        rescale = jnp.exp2(before - row_max)
        own_factor[n] = rescale
        near_max[n] = row_max
        near_total[n] = own_total[base + n] * rescale + jnp.sum(weights, axis=0, keepdims=True)
        near_weights[n] = weights
        return rescale, weights.astype(jnp.bfloat16)

    def weigh(n, rescale, halved):
        weighted = matmul(back_two[1, n * groups // chunks], halved, (0, 0))
        near_out[n] = own_out[base + n] * rescale + weighted

    pipelined(chunks, products, softmax, weigh)


def last_kernel(
    base, first, query_head, grad_head, back_one, grad_rows, near_max, near_total, near_out,
    attended_rows, row_delta, near_factor, one_grad, *targets,
):
    groups = back_one.shape[1]
    chunks = near_max.shape[0]
    heads, _, width = query_head.shape
    count = heads // first.shape[0]
    scale = width ** (-0.5)

    def products(n):
        g = n * groups // chunks
        scores = matmul(back_one[0, g], grouped(query_head, base + n, count), (1, 1))
        prob_grad = matmul(back_one[1, g], grouped(grad_head, base + n, count), (1, 1))
        return scores, prob_grad

    def softmax(n, scores, prob_grad):
        scores = masked(scores * (scale * math.log2(math.e)), first[base + n], 1)
        row_max = jnp.maximum(near_max[n], jnp.max(scores, axis=0, keepdims=True))
        weights = jnp.exp2(scores - row_max)
        rescale = jnp.exp2(near_max[n] - row_max)
        inverse = 1.0 / (near_total[n] * rescale + jnp.sum(weights, axis=0, keepdims=True))
        weighted = matmul(
            back_one[1, n * groups // chunks], weights.astype(jnp.bfloat16), (0, 0)
        )
        near_factor[n] = rescale * inverse
        return prob_grad, weights, weighted, rescale, inverse

    def differentiate(n, prob_grad, weights, weighted, rescale, inverse):
        attended = ((near_out[n] * rescale + weighted) * inverse).astype(jnp.bfloat16)
        delta = jnp.sum(
            grad_rows[base + n].astype(jnp.float32) * attended.astype(jnp.float32),
            axis=0,
            keepdims=True,
        )
        prob = weights * inverse
        score_grad = (prob * (prob_grad - delta)).astype(jnp.bfloat16)
        attended_rows[n] = attended
        row_delta[n] = delta
        one_grad[n] = score_grad
        return score_grad, prob.astype(jnp.bfloat16)

    store = functools.partial(store_rows, targets, scale)
    accumulate = accumulator(query_head, grad_head, base, count, chunks, groups, store)
    pipelined(chunks, products, softmax, differentiate, accumulate)


def store_rows(targets, scale, g, key_part, value_part):
    length = targets[0].shape[2]
    for index, part in enumerate((key_part * scale, value_part)):
        for place, target in enumerate(targets):
            rows = part[place * length : (place + 1) * length]
            target[index, g] = rows.astype(target.dtype)


def pipelined(chunks, *stages):
    ready = [{} for _ in range(len(stages) + 1)]
    for step in range(chunks + len(stages) - 1):
        for depth, stage in enumerate(stages):
            n = step - depth
            if 0 <= n < chunks:
                ready[depth + 1][n] = stage(n, *ready[depth].pop(n, ())) or ()


def accumulator(query_head, grad_head, base, count, chunks, groups, store):
    parts = {}

    def accumulate(n, score_grad, half):
        g = n * groups // chunks
        key_part = matmul(score_grad, grouped(query_head, base + n, count), (1, 0))
        value_part = matmul(half, grouped(grad_head, base + n, count), (1, 0))
        if g in parts:
            key_part, value_part = parts[g][0] + key_part, parts[g][1] + value_part
        parts[g] = (key_part, value_part)
        if (n + 1) * groups // chunks != g:
            store(g, key_part, value_part)

    return accumulate


def two_backward_kernel(
    base, count, query_head, grad_head, near_weights, near_prob_grad, near_factor, row_delta,
    two_grad, *targets,
):
    chunks = near_weights.shape[0]
    groups, _, width = targets[0].shape[1:]

    def differentiate(n):
        prob = near_weights[n] * near_factor[n]
        score_grad = (prob * (near_prob_grad[n] - row_delta[n])).astype(jnp.bfloat16)
        two_grad[n] = score_grad
        return score_grad, prob.astype(jnp.bfloat16)

    store = functools.partial(store_rows, targets, width ** (-0.5))
    accumulate = accumulator(query_head, grad_head, base, count, chunks, groups, store)
    pipelined(chunks, differentiate, accumulate)


def own_backward_kernel(
    base, query_head, grad_head, own_weights, own_prob_grad, near_factor, own_factor, row_delta,
    own_grad, *targets,
):
    chunks = own_grad.shape[0]
    groups, _, width = targets[0].shape[1:]
    count = query_head.shape[0] // own_weights.shape[0]

    def differentiate(n):
        prob = own_weights[base + n] * (own_factor[n] * near_factor[n])
        score_grad = (prob * (own_prob_grad[base + n] - row_delta[n])).astype(jnp.bfloat16)
        own_grad[n] = score_grad
        return score_grad, prob.astype(jnp.bfloat16)

    store = functools.partial(store_rows, targets, width ** (-0.5))
    accumulate = accumulator(query_head, grad_head, base, count, chunks, groups, store)
    pipelined(chunks, differentiate, accumulate)


def pack_kernel(first, second, both):
    both[0] = first[...]
    both[1] = second[...]


def join_back_kernel(first, second, other, *targets):
    core = lax.axis_index("head")
    for index, (mine, target) in enumerate(zip((first, second), targets)):
        target[:, core] = mine[...]
        target[:, 1 - core] = other[index]


def query_kernel(
    own, back_one, back_two, attended_rows, own_grad, one_grad, two_grad, mine, send
):
    chunks, part = own_grad.shape[0], own.shape[1]
    heads, length, width = mine.shape[1:]
    count = heads // chunks
    for n in range(chunks):
        g = n * part // chunks
        rows = pl.ds(n * count, count)
        keys = join(back_two[0, g], back_one[0, g], own[0, g])
        total = matmul(keys, join(two_grad[n], one_grad[n], own_grad[n]), (0, 0))
        total = (total * width ** (-0.5)).astype(jnp.bfloat16)
        for index, columns in enumerate((attended_rows[n], total)):
            block = columns.T.reshape(count, 2 * length, width)
            mine[index, rows] = block[:, :length]
            send[index, rows] = block[:, length:]


def assemble_kernel(
    first_mine, first_other, second_mine, second_other, out, query_grad, token
):
    count = first_mine.shape[1]
    start = lax.axis_index("head") * 2 * count
    other_start = (1 - lax.axis_index("head")) * 2 * count
    for index, target in enumerate((out, query_grad)):
        target[pl.ds(start, count)] = first_mine[index]
        target[pl.ds(other_start, count)] = first_other[index]
        target[pl.ds(start + count, count)] = second_mine[index]
        target[pl.ds(other_start + count, count)] = second_other[index]
    token[...] = jnp.zeros(token.shape, token.dtype)


def sum_kernel(
    own_first, one_first, two_first, own_mine, own_send, sum_mine, sum_send
):
    length, part = sum_mine.shape[2], own_first.shape[1]
    arrived = one_first[...].astype(jnp.float32) + two_first[...].astype(jnp.float32)
    total = own_first[...] + arrived
    sum_mine[:, pl.ds(0, part)] = total[:, :, :length]
    sum_send[:, pl.ds(0, part)] = total[:, :, length:].astype(jnp.bfloat16)
    sum_mine[:, pl.ds(part, part)] = own_mine[...]
    sum_send[:, pl.ds(part, part)] = own_send[...]


def final_kernel(sum_mine, sum_other, one_total, two_total, after, key_grad, value_grad):
    groups, part = sum_mine.shape[1], two_total.shape[2]
    core = lax.axis_index("head")
    for index, result in enumerate((key_grad, value_grad)):
        for place, sums in ((core, sum_mine), (1 - core, sum_other)):
            start = place * groups
            first = sums[index, pl.ds(0, part)].astype(jnp.float32)
            second = sums[index, pl.ds(part, part)].astype(jnp.float32)
            second += one_total[index, place].astype(jnp.float32)
            second += two_total[index, place].astype(jnp.float32)
            result[pl.ds(start, part)] = first.astype(jnp.bfloat16)
            result[pl.ds(start + part, part)] = second.astype(jnp.bfloat16)


def shards(query_matrix, key_matrix, value_matrix, output_gradient, query_head_spans, slab_offset):
    groups, length, width = key_matrix.shape
    heads = query_matrix.shape[0]
    cores = lax.axis_size("head")
    tokens = cores * length
    groups_here, heads_here = groups // cores, heads // cores
    part = groups_here // 2
    count = max(1, min(heads // groups, 256 // tokens))
    chunks = heads_here // count
    each = chunks // 2
    lanes = count * tokens
    half, full = jnp.bfloat16, jnp.float32
    vmem = pl.BlockSpec(memory_space=pltpu.VMEM)
    smem = pl.BlockSpec(memory_space=pltpu.SMEM)

    def call(kernel, name, outs, arrays, scalars=0, flops=1):
        return pl.pallas_call(
            kernel,
            out_shape=tuple(jax.ShapeDtypeStruct(shape, kind) for shape, kind in outs),
            in_specs=[smem] * scalars + [vmem] * (len(arrays) - scalars),
            out_specs=(vmem,) * len(outs),
            compiler_params=pltpu.CompilerParams(vmem_limit_bytes=40 * 1024 * 1024),
            cost_estimate=pl.CostEstimate(flops=flops, bytes_accessed=0, transcendentals=0),
            name=name,
        )(*arrays)

    def rows_of(rows, kind, number=each):
        return ((number, rows, lanes), kind)

    stat = rows_of(1, full)
    pair = (2, groups_here, length, width)
    token_half = ((2, cores, part, length, width), half)
    small_half = ((2, part, length, width), half)
    chip_half = ((2, part, tokens, width), half)
    half_rows = ((heads_here, length, width), half)
    chip_rows = ((heads_here, tokens, width), half)

    queries_other = swapped(query_matrix, "head")
    grads_other = swapped(output_gradient, "head")
    own = jnp.stack([key_matrix, value_matrix])
    first_send, own_send = call(split_kernel, "split_own", [token_half, (pair, half)], (own,))
    back_two_first = shifted(first_send, "seq", 2)
    own_halves = call(
        join_own_kernel, "join_own", [chip_half] * 2, (own, swapped(own_send, "head"))
    )
    back_one = [shifted(own_halves[0], "seq", 1)]
    back_two = [None, shifted(own_halves[1], "seq", 2)]
    back_one.append(shifted(own_halves[1], "seq", 1))
    (
        query_head, grad_head, grad_rows, first, own_max, own_total, own_out, own_weights,
        own_prob_grad,
    ) = call(
        own_kernel,
        "own_block",
        [
            chip_rows, chip_rows, rows_of(width, half, chunks), rows_of(1, jnp.int32, chunks),
            rows_of(1, full, chunks), rows_of(1, full, chunks), rows_of(width, full, chunks),
            rows_of(tokens, full, chunks), rows_of(tokens, full, chunks),
        ],
        (
            query_head_spans, slab_offset, query_matrix, output_gradient, queries_other,
            grads_other, *own_halves,
        ),
        scalars=2,
    )
    back_two_first, first = lax.optimization_barrier((back_two_first, first))
    two_sends = call(
        split_two_kernel, "split_two", [((part, length, width), half)] * 2, (back_two_first,)
    )
    (back_two[0],) = call(
        join_two_kernel,
        "join_two",
        [chip_half],
        (back_two_first, *[swapped(send, "head") for send in two_sends]),
    )

    split_half = [small_half] * 2
    kept = []
    after = first
    for index in range(2):
        base = index * each
        label = "ab"[index]
        parts = [chip_half] if index == 0 else split_half
        near_max, near_total, near_out, near_weights, near_prob_grad, own_factor = call(
            functools.partial(near_kernel, base),
            "near_" + label,
            [stat, stat, rows_of(width, full), rows_of(tokens, full), rows_of(tokens, full), stat],
            (first, query_head, grad_head, back_two[index], own_max, own_total, own_out, after),
        )
        back_one[index], near_max = lax.optimization_barrier((back_one[index], near_max))
        attended_rows, row_delta, near_factor, one_grad, *one_parts = call(
            functools.partial(last_kernel, base),
            "last_" + label,
            [rows_of(width, half), stat, stat, rows_of(tokens, half)] + parts,
            (
                first, query_head, grad_head, back_one[index], grad_rows, near_max, near_total,
                near_out,
            ),
        )
        two_grad, *two_parts = call(
            functools.partial(two_backward_kernel, base, count),
            "two_back_" + label,
            [rows_of(tokens, half)] + parts,
            (query_head, grad_head, near_weights, near_prob_grad, near_factor, row_delta),
        )
        if index == 0:
            one_part, two_part = one_parts[0], two_parts[0]
            after = two_part
        else:
            (both,) = call(
                pack_kernel, "pack", [((2,) + small_half[0], half)], (one_parts[1], two_parts[1])
            )
            one_part, two_part = call(
                join_back_kernel,
                "join_back",
                [token_half] * 2,
                (one_parts[0], two_parts[0], swapped(both, "head")),
            )
        one_total = shifted(one_part, "seq", -1)
        two_total = shifted(two_part, "seq", -2)
        own_grad, *own_parts = call(
            functools.partial(own_backward_kernel, base),
            "own_back_" + label,
            [rows_of(tokens, half)]
            + ([(chip_half[0], full)] if index == 0 else [(small_half[0], full), small_half]),
            (
                query_head, grad_head, own_weights, own_prob_grad, near_factor, own_factor,
                row_delta,
            ),
        )
        rows_half = (heads_here // 2, length, width)
        mine, *sends = call(
            query_kernel,
            "query_" + label,
            [((2,) + rows_half, half)]
            + [((2,) + rows_half, half)],
            (
                own_halves[index], back_one[index], back_two[index], attended_rows, own_grad,
                one_grad, two_grad,
            ),
        )
        others = [swapped(send, "head") for send in sends]
        kept.append((one_total, two_total, own_parts, mine, others))
    token_shape = ((8, 128), full)
    attn_out, query_grad, token = call(
        assemble_kernel,
        "assemble",
        [(query_matrix.shape, half)] * 2 + [token_shape],
        (kept[0][3], kept[0][4][0], kept[1][3], kept[1][4][0]),
    )
    sum_mine, sum_send = call(
        sum_kernel,
        "sum",
        [(pair, full), (pair, half)],
        (*kept[0][2], kept[0][0], kept[0][1], *kept[1][2]),
        flops=10**8,
    )
    key_grad, value_grad = call(
        final_kernel,
        "total",
        [(key_matrix.shape, half)] * 2,
        (sum_mine, swapped(sum_send, "head"), kept[1][0], kept[1][1], token),
    )
    return (attn_out, query_grad, key_grad, value_grad)


def solution(mesh):
    tokens = P(None, ("seq", "head"), None)
    return jax.shard_map(
        shards,
        mesh=mesh,
        in_specs=(tokens, tokens, tokens, tokens, P(), P()),
        out_specs=(tokens, tokens, tokens, tokens),
        check_vma=False,
    )
```

```python
import math

import jax
import jax.numpy as jnp
from jax import lax
from jax.experimental import pallas as pl
from jax.experimental.pallas import tpu as pltpu
from jax.sharding import PartitionSpec as P

REACH = 2
SEGMENT = 512

masked_score = -1e30


def shifted(block, axis, distance, ring=True):
    count = lax.axis_size(axis)
    route = [(i, (i + distance) % count) for i in range(count) if ring or i + distance < count]
    return lax.ppermute(block, axis, route)


def swapped(block, axis):
    count = lax.axis_size(axis)
    return lax.ppermute(block, axis, [(i, count - 1 - i) for i in range(count)])


def matmul(left, right, contract):
    return lax.dot_general(
        left, right, ((contract[:1], contract[1:]), ((), ())), preferred_element_type=jnp.float32
    )


def grouped(ref, n, count):
    _, length, width = ref.shape
    return ref[pl.ds(n * count, count)].reshape(count * length, width)


def join(*blocks):
    return jnp.concatenate(blocks, axis=0)


def core_offsets(length):
    core = lax.axis_index("head")
    return core * length, (1 - core) * length


def my_heads(count):
    return pl.ds(lax.axis_index("head") * count, count)


def other_heads(count):
    return pl.ds((1 - lax.axis_index("head")) * count, count)


def lane_tokens(count, length):
    lane = lax.broadcasted_iota(jnp.int32, (1, count * 2 * length), 1)
    token = lane - lane // (2 * length) * (2 * length)
    mine, other = core_offsets(length)
    return jnp.where(token < length, token + mine, token - length + other)


def first_visible(spans, offset, chunks, count, length):
    token = lane_tokens(count, length)
    lane_head = lax.broadcasted_iota(jnp.int32, token.shape, 1) // (2 * length)
    start = lax.axis_index("seq") * 2 * length
    segment_start = token - lax.bitwise_and(offset[0] + start + token, SEGMENT - 1)
    floor = jnp.maximum(segment_start, -start)
    base = lax.axis_index("head") * chunks * count
    result = []
    for n in range(chunks):
        span = jnp.full(token.shape, spans[base + n * count], jnp.int32)
        for a in range(1, count):
            span = jnp.where(lane_head == a, spans[base + n * count + a], span)
        result.append(jnp.maximum(floor, token - span + 1))
    return result


def masked(scores, first, chips_back, token=None):
    length = scores.shape[0] // 2
    row = lax.broadcasted_iota(jnp.int32, (length, scores.shape[1]), 0)
    pieces = []
    for part, offset in enumerate(core_offsets(length)):
        visible = row >= first + (chips_back * 2 * length - offset)
        if token is not None:
            visible &= row <= token - offset
        pieces.append(
            jnp.where(visible, scores[part * length : (part + 1) * length], masked_score)
        )
    return join(*pieces)


def split_kernel(block, *sends):
    for index, send in enumerate(sends):
        send[...] = block[index, other_heads(send.shape[0])]


def thirds(rows):
    return [2 * rows * (i + 1) // 3 - 2 * rows * i // 3 for i in range(3)]


def placed(pieces, rows):
    taken = 0
    for piece in pieces:
        count = piece.shape[0]
        for index in range(2):
            low = max(taken, index * rows)
            high = min(taken + count, (index + 1) * rows)
            if low < high:
                yield index, low - index * rows, piece.at[pl.ds(low - taken, high - low)], high - low
        taken += count


def split_rows_kernel(queries, grads, after, *sends):
    heads = queries.shape[0] // 2
    start = (1 - lax.axis_index("head")) * heads
    for index, row, piece, count in placed(sends, heads):
        piece[...] = (queries, grads)[index][pl.ds(start + row, count)]


def join_own_kernel(own, other_keys, other_values, own_head):
    groups, length = other_keys.shape[:2]
    own_head[:, :, pl.ds(0, length)] = own[:, my_heads(groups)]
    own_head[0, :, pl.ds(length, length)] = other_keys[...]
    own_head[1, :, pl.ds(length, length)] = other_values[...]


def own_kernel(
    spans, offset, queries, grads, first_third, second_third, last_third, own,
    query_head, grad_head, grad_rows, first, own_max, own_total, own_out, own_weights,
    own_prob_grad,
):
    heads, _, width = query_head.shape
    length = queries.shape[1]
    groups = own.shape[1]
    chunks = first.shape[0]
    count = heads // chunks
    query_head[:, pl.ds(0, length)] = queries[my_heads(heads)]
    grad_head[:, pl.ds(0, length)] = grads[my_heads(heads)]
    for index, row, piece, rows in placed((first_third, second_third, last_third), heads):
        (query_head, grad_head)[index][pl.ds(row, rows), pl.ds(length, length)] = piece[...]
    factor = width ** (-0.5) * math.log2(math.e)
    token = lane_tokens(count, length)
    for n, rows in enumerate(first_visible(spans, offset, chunks, count, length)):
        first[n] = rows

    def products(n):
        g = n * groups // chunks
        own_prob_grad[n] = matmul(own[1, g], grouped(grad_head, n, count), (1, 1))
        return (matmul(own[0, g], grouped(query_head, n, count), (1, 1)),)

    def softmax(n, scores):
        scores = masked(scores * factor, first[n], 0, token)
        row_max = jnp.max(scores, axis=0, keepdims=True)
        weights = jnp.exp2(scores - row_max)
        own_max[n] = row_max
        own_total[n] = jnp.sum(weights, axis=0, keepdims=True)
        own_weights[n] = weights
        return (weights.astype(jnp.bfloat16),)

    def weigh(n, halves):
        own_out[n] = matmul(own[1, n * groups // chunks], halves, (0, 0))
        grad_rows[n] = grouped(grad_head, n, count).T

    pipelined(chunks, products, softmax, weigh)


def two_back(back_two, two_other, index, g):
    base = lax.axis_index("head") * two_other[index].shape[0]
    return join(back_two[index, base + g], two_other[index][g])


def near_forward_kernel(
    first, query_head, grad_head, back_two, two_keys, two_values, own_max, own_total, own_out,
    near_max, near_total, near_out, near_weights, near_prob_grad, own_factor,
):
    groups = two_keys.shape[0]
    two_other = (two_keys, two_values)
    chunks = first.shape[0]
    heads, _, width = query_head.shape
    count = heads // chunks
    factor = width ** (-0.5) * math.log2(math.e)

    def products(n):
        g = n * groups // chunks
        keys = two_back(back_two, two_other, 0, g)
        values = two_back(back_two, two_other, 1, g)
        near_prob_grad[n] = matmul(values, grouped(grad_head, n, count), (1, 1))
        return (matmul(keys, grouped(query_head, n, count), (1, 1)),)

    def softmax(n, scores):
        scores = masked(scores * factor, first[n], 2)
        row_max = jnp.maximum(own_max[n], jnp.max(scores, axis=0, keepdims=True))
        weights = jnp.exp2(scores - row_max)
        rescale = jnp.exp2(own_max[n] - row_max)
        own_factor[n] = rescale
        near_max[n] = row_max
        near_total[n] = own_total[n] * rescale + jnp.sum(weights, axis=0, keepdims=True)
        near_weights[n] = weights
        return rescale, weights.astype(jnp.bfloat16)

    def weigh(n, rescale, halves):
        values = two_back(back_two, two_other, 1, n * groups // chunks)
        near_out[n] = own_out[n] * rescale + matmul(values, halves, (0, 0))

    pipelined(chunks, products, softmax, weigh)


def last_kernel(
    first, query_head, grad_head, back_one, grad_rows, near_max, near_total, near_out,
    attended_rows, row_delta, near_factor, one_grad, one_part,
):
    groups = back_one.shape[1]
    chunks = first.shape[0]
    heads, _, width = query_head.shape
    count = heads // chunks
    scale = width ** (-0.5)

    def products(n):
        g = n * groups // chunks
        scores = matmul(back_one[0, g], grouped(query_head, n, count), (1, 1))
        prob_grad = matmul(back_one[1, g], grouped(grad_head, n, count), (1, 1))
        return scores, prob_grad

    def softmax(n, scores, prob_grad):
        scores = masked(scores * (scale * math.log2(math.e)), first[n], 1)
        row_max = jnp.maximum(near_max[n], jnp.max(scores, axis=0, keepdims=True))
        weights = jnp.exp2(scores - row_max)
        rescale = jnp.exp2(near_max[n] - row_max)
        inverse = 1.0 / (near_total[n] * rescale + jnp.sum(weights, axis=0, keepdims=True))
        weighted = matmul(
            back_one[1, n * groups // chunks], weights.astype(jnp.bfloat16), (0, 0)
        )
        near_factor[n] = rescale * inverse
        return prob_grad, weights, weighted, rescale, inverse

    def differentiate(n, prob_grad, weights, weighted, rescale, inverse):
        attended = ((near_out[n] * rescale + weighted) * inverse).astype(jnp.bfloat16)
        delta = jnp.sum(
            grad_rows[n].astype(jnp.float32) * attended.astype(jnp.float32), axis=0, keepdims=True
        )
        prob = weights * inverse
        score_grad = (prob * (prob_grad - delta)).astype(jnp.bfloat16)
        attended_rows[n] = attended
        row_delta[n] = delta
        one_grad[n] = score_grad
        return score_grad, prob.astype(jnp.bfloat16)

    def store(g, key_part, value_part):
        one_part[0, g] = (key_part * scale).astype(jnp.bfloat16)
        one_part[1, g] = value_part.astype(jnp.bfloat16)

    accumulate = accumulator(query_head, grad_head, chunks, groups, store)
    pipelined(chunks, products, softmax, differentiate, accumulate)


def pipelined(chunks, *stages):
    ready = [{} for _ in range(len(stages) + 1)]
    for step in range(chunks + len(stages) - 1):
        for depth, stage in enumerate(stages):
            n = step - depth
            if 0 <= n < chunks:
                ready[depth + 1][n] = stage(n, *ready[depth].pop(n, ())) or ()


def accumulator(query_head, grad_head, chunks, groups, store):
    count = query_head.shape[0] // chunks
    parts = {}

    def accumulate(n, score_grad, half):
        g = n * groups // chunks
        key_part = matmul(score_grad, grouped(query_head, n, count), (1, 0))
        value_part = matmul(half, grouped(grad_head, n, count), (1, 0))
        if g in parts:
            key_part, value_part = parts[g][0] + key_part, parts[g][1] + value_part
        parts[g] = (key_part, value_part)
        if (n + 1) * groups // chunks != g:
            store(g, key_part, value_part)

    return accumulate


def two_backward_kernel(
    query_head, grad_head, near_weights, near_prob_grad, near_factor, row_delta,
    two_grad, two_mine, send_keys, send_values,
):
    chunks = near_weights.shape[0]
    groups, length, width = two_mine.shape[1:]

    def differentiate(n):
        prob = near_weights[n] * near_factor[n]
        score_grad = (prob * (near_prob_grad[n] - row_delta[n])).astype(jnp.bfloat16)
        two_grad[n] = score_grad
        return score_grad, prob.astype(jnp.bfloat16)

    def store(g, key_part, value_part):
        for index, (part, send) in enumerate(
            ((key_part * width ** (-0.5), send_keys), (value_part, send_values))
        ):
            two_mine[index, g] = part[:length].astype(jnp.bfloat16)
            send[g] = part[length:].astype(jnp.bfloat16)

    accumulate = accumulator(query_head, grad_head, chunks, groups, store)
    pipelined(chunks, differentiate, accumulate)


def own_backward_kernel(
    query_head, grad_head, own_weights, own_prob_grad, near_factor, own_factor, row_delta,
    after, own_grad, own_part,
):
    chunks = own_weights.shape[0]
    groups, _, width = own_part.shape[1:]

    def differentiate(n):
        prob = own_weights[n] * (own_factor[n] * near_factor[n])
        score_grad = (prob * (own_prob_grad[n] - row_delta[n])).astype(jnp.bfloat16)
        own_grad[n] = score_grad
        return score_grad, prob.astype(jnp.bfloat16)

    def store(g, key_part, value_part):
        own_part[0, g] = key_part * width ** (-0.5)
        own_part[1, g] = value_part

    accumulate = accumulator(query_head, grad_head, chunks, groups, store)
    pipelined(chunks, differentiate, accumulate)


def join_two_kernel(two_mine, other_keys, other_values, two_part):
    groups = two_mine.shape[1]
    two_part[:, my_heads(groups)] = two_mine[...]
    two_part[0, other_heads(groups)] = other_keys[...]
    two_part[1, other_heads(groups)] = other_values[...]


def query_kernel(
    own, back_one, back_two, two_keys, attended_rows, two_grad, one_grad, own_grad,
    out_mine, query_mine, first_third, second_third, last_third, query_send,
):
    sends = (first_third, second_third, last_third)
    groups = own.shape[1]
    chunks = own_grad.shape[0]
    heads, length, width = out_mine.shape
    count = heads // chunks
    for n in range(chunks):
        g = n * groups // chunks
        rows = pl.ds(n * count, count)
        keys = join(two_back(back_two, (two_keys,), 0, g), back_one[0, g], own[0, g])
        part = matmul(keys, join(two_grad[n], one_grad[n], own_grad[n]), (0, 0))
        part = (part * width ** (-0.5)).astype(jnp.bfloat16)
        for index, (columns, mine) in enumerate(((attended_rows[n], out_mine), (part, query_mine))):
            block = columns.T.reshape(count, 2 * length, width)
            mine[rows] = block[:, :length]
            query_send[index, rows] = block[:, length:]
    for index, row, piece, taken in placed(sends, heads):
        piece[...] = query_send[index, pl.ds(row, taken)]


def assemble_kernel(
    out_mine, query_mine, first_third, second_third, last_third, out, query_grad, token
):
    heads = out_mine.shape[0]
    start = (1 - lax.axis_index("head")) * heads
    out[my_heads(heads)] = out_mine[...]
    query_grad[my_heads(heads)] = query_mine[...]
    for index, row, piece, count in placed((first_third, second_third, last_third), heads):
        (out, query_grad)[index][pl.ds(start + row, count)] = piece[...]
    token[...] = jnp.zeros(token.shape, token.dtype)


def own_sum_kernel(own_part, one_total, sum_mine, sum_send):
    length = sum_mine.shape[2]
    total = own_part[...] + one_total[...].astype(jnp.float32)
    sum_mine[...] = total[:, :, :length]
    sum_send[...] = total[:, :, length:].astype(jnp.bfloat16)


def final_kernel(sum_mine, sum_other, two_total, after, key_grad, value_grad):
    groups = sum_mine.shape[1]
    mine, other = my_heads(groups), other_heads(groups)
    for index, result in enumerate((key_grad, value_grad)):
        total = sum_mine[index] + two_total[index, mine].astype(jnp.float32)
        result[mine] = total.astype(jnp.bfloat16)
        total = sum_other[index].astype(jnp.float32) + two_total[index, other].astype(jnp.float32)
        result[other] = total.astype(jnp.bfloat16)


def shards(query_matrix, key_matrix, value_matrix, output_gradient, query_head_spans, slab_offset):
    groups, length, width = key_matrix.shape
    heads = query_matrix.shape[0]
    cores = lax.axis_size("head")
    tokens = cores * length
    groups_here, heads_here = groups // cores, heads // cores
    count = max(1, min(heads // groups, 256 // tokens))
    chunks = heads_here // count
    lanes = count * tokens
    half, full = jnp.bfloat16, jnp.float32
    vmem = pl.BlockSpec(memory_space=pltpu.VMEM)
    smem = pl.BlockSpec(memory_space=pltpu.SMEM)

    def call(kernel, name, outs, arrays, scalars=0, scratch=()):
        return pl.pallas_call(
            kernel,
            out_shape=tuple(jax.ShapeDtypeStruct(shape, kind) for shape, kind in outs),
            in_specs=[smem] * scalars + [vmem] * (len(arrays) - scalars),
            out_specs=(vmem,) * len(outs),
            scratch_shapes=scratch,
            compiler_params=pltpu.CompilerParams(vmem_limit_bytes=40 * 1024 * 1024),
            cost_estimate=pl.CostEstimate(flops=1, bytes_accessed=0, transcendentals=0),
            name=name,
        )(*arrays)

    def rows_of(rows, kind):
        return ((chunks, rows, lanes), kind)

    stat = rows_of(1, full)
    whole_pair = ((2, groups, length, width), half)
    half_block = ((groups_here, length, width), half)
    half_pair = ((2, groups_here, length, width), half)
    chip_pair = ((2, groups_here, tokens, width), half)
    half_rows = ((heads_here, length, width), half)
    third_rows = [((rows, length, width), half) for rows in thirds(heads_here)]
    chip_rows = ((heads_here, tokens, width), half)

    own = jnp.stack([key_matrix, value_matrix])
    back_two = shifted(own, "seq", 2)
    own_sends = call(split_kernel, "split_own", [half_block] * 2, (own,))
    (own_head,) = call(
        join_own_kernel, "join_own", [chip_pair], (own, *[swapped(send, "head") for send in own_sends])
    )
    back_one = shifted(own_head, "seq", 1, ring=False)
    sends = call(
        split_rows_kernel,
        "split_rows",
        third_rows,
        (query_matrix, output_gradient, own),
    )
    (
        query_head, grad_head, grad_rows, first, own_max, own_total, own_out, own_weights,
        own_prob_grad,
    ) = call(
        own_kernel,
        "own_block",
        [
            chip_rows, chip_rows, rows_of(width, half), rows_of(1, jnp.int32), stat, stat,
            rows_of(width, full), rows_of(tokens, full), rows_of(tokens, full),
        ],
        (
            query_head_spans, slab_offset, query_matrix, output_gradient,
            *[swapped(send, "head") for send in sends], own_head,
        ),
        scalars=2,
    )
    back_two, first = lax.optimization_barrier((back_two, first))
    two_sends = call(split_kernel, "split_two", [half_block] * 2, (back_two,))
    two_other = [swapped(send, "head") for send in two_sends]
    near_max, near_total, near_out, near_weights, near_prob_grad, own_factor = call(
        near_forward_kernel,
        "near_forward",
        [stat, stat, rows_of(width, full), rows_of(tokens, full), rows_of(tokens, full), stat],
        (first, query_head, grad_head, back_two, *two_other, own_max, own_total, own_out),
    )
    back_one, near_max = lax.optimization_barrier((back_one, near_max))
    attended_rows, row_delta, near_factor, one_grad, one_part = call(
        last_kernel,
        "last_forward_backward",
        [rows_of(width, half), stat, stat, rows_of(tokens, half), chip_pair],
        (first, query_head, grad_head, back_one, grad_rows, near_max, near_total, near_out),
    )
    one_total = shifted(one_part, "seq", -1)
    two_grad, part_mine, *part_sends = call(
        two_backward_kernel,
        "two_backward",
        [rows_of(tokens, half), half_pair, half_block, half_block],
        (query_head, grad_head, near_weights, near_prob_grad, near_factor, row_delta),
    )
    (two_part,) = call(
        join_two_kernel,
        "join_two",
        [whole_pair],
        (part_mine, *[swapped(send, "head") for send in part_sends]),
    )
    two_total = shifted(two_part, "seq", -2)
    own_grad, own_part = call(
        own_backward_kernel,
        "own_backward",
        [rows_of(tokens, half), (chip_pair[0], full)],
        (
            query_head, grad_head, own_weights, own_prob_grad, near_factor, own_factor, row_delta,
            two_part,
        ),
    )
    out_mine, query_mine, *sends = call(
        query_kernel,
        "query_grad",
        [half_rows] * 2 + third_rows,
        (own_head, back_one, back_two, two_other[0], attended_rows, two_grad, one_grad, own_grad),
        scratch=[pltpu.VMEM((2,) + half_rows[0], half)],
    )
    attn_out, query_grad, token = call(
        assemble_kernel,
        "assemble",
        [(query_matrix.shape, half)] * 2 + [((8, 128), full)],
        (out_mine, query_mine, *[swapped(send, "head") for send in sends]),
    )
    sum_mine, sum_send = call(
        own_sum_kernel, "own_sum", [(half_pair[0], full), half_pair], (own_part, one_total)
    )
    key_grad, value_grad = call(
        final_kernel,
        "total",
        [(key_matrix.shape, half)] * 2,
        (sum_mine, swapped(sum_send, "head"), two_total, token),
    )
    return (attn_out, query_grad, key_grad, value_grad)


def solution(mesh):
    tokens = P(None, ("seq", "head"), None)
    return jax.shard_map(
        shards,
        mesh=mesh,
        in_specs=(tokens, tokens, tokens, tokens, P(), P()),
        out_specs=(tokens, tokens, tokens, tokens),
        check_vma=False,
    )
```

```python
import functools
import math

import jax
import jax.numpy as jnp
from jax import lax
from jax.experimental import pallas as pl
from jax.experimental.pallas import tpu as pltpu
from jax.sharding import PartitionSpec as P

REACH = 2
SEGMENT = 512

masked_score = -1e30


def shifted(block, axis, distance, ring=True):
    count = lax.axis_size(axis)
    route = [(i, (i + distance) % count) for i in range(count) if ring or i + distance < count]
    return lax.ppermute(block, axis, route)


def swapped(block, axis):
    count = lax.axis_size(axis)
    return lax.ppermute(block, axis, [(i, count - 1 - i) for i in range(count)])


def matmul(left, right, contract):
    return lax.dot_general(
        left, right, ((contract[:1], contract[1:]), ((), ())), preferred_element_type=jnp.float32
    )


def grouped(ref, n, count):
    _, length, width = ref.shape
    return ref[pl.ds(n * count, count)].reshape(count * length, width)


def join(*blocks):
    return jnp.concatenate(blocks, axis=0)


def core_offsets(length):
    core = lax.axis_index("head")
    return core * length, (1 - core) * length


def my_heads(count):
    return pl.ds(lax.axis_index("head") * count, count)


def other_heads(count):
    return pl.ds((1 - lax.axis_index("head")) * count, count)


def lane_tokens(count, length):
    lane = lax.broadcasted_iota(jnp.int32, (1, count * 2 * length), 1)
    token = lane - lane // (2 * length) * (2 * length)
    mine, other = core_offsets(length)
    return jnp.where(token < length, token + mine, token - length + other)


def first_visible(spans, offset, chunks, count, length):
    token = lane_tokens(count, length)
    lane_head = lax.broadcasted_iota(jnp.int32, token.shape, 1) // (2 * length)
    start = lax.axis_index("seq") * 2 * length
    segment_start = token - lax.bitwise_and(offset[0] + start + token, SEGMENT - 1)
    floor = jnp.maximum(segment_start, -start)
    base = lax.axis_index("head") * chunks * count
    result = []
    for n in range(chunks):
        span = jnp.full(token.shape, spans[base + n * count], jnp.int32)
        for a in range(1, count):
            span = jnp.where(lane_head == a, spans[base + n * count + a], span)
        result.append(jnp.maximum(floor, token - span + 1))
    return result


def masked(scores, first, chips_back, token=None):
    length = scores.shape[0] // 2
    row = lax.broadcasted_iota(jnp.int32, (length, scores.shape[1]), 0)
    pieces = []
    for part, offset in enumerate(core_offsets(length)):
        visible = row >= first + (chips_back * 2 * length - offset)
        if token is not None:
            visible &= row <= token - offset
        pieces.append(
            jnp.where(visible, scores[part * length : (part + 1) * length], masked_score)
        )
    return join(*pieces)


def split_kernel(block, *sends):
    for index, send in enumerate(sends):
        send[...] = block[index, other_heads(send.shape[0])]


def thirds(rows):
    return [2 * rows * (i + 1) // 3 - 2 * rows * i // 3 for i in range(3)]


def placed(pieces, rows):
    taken = 0
    for piece in pieces:
        count = piece.shape[0]
        for index in range(2):
            low = max(taken, index * rows)
            high = min(taken + count, (index + 1) * rows)
            if low < high:
                yield index, low - index * rows, piece.at[pl.ds(low - taken, high - low)], high - low
        taken += count


def join_own_kernel(own, other_keys, other_values, *halves):
    groups, length = other_keys.shape[:2]
    part = halves[0].shape[1]
    start = lax.axis_index("head") * groups
    for place, target in enumerate(halves):
        target[:, :, pl.ds(0, length)] = own[:, pl.ds(start + place * part, part)]
        for index, other in enumerate((other_keys, other_values)):
            target[index, :, pl.ds(length, length)] = other[pl.ds(place * part, part)]


def own_kernel(
    spans, offset, queries, grads, queries_other, grads_other, first_half, second_half,
    query_head, grad_head, grad_rows, first, own_max, own_total, own_out, own_weights,
    own_prob_grad,
):
    heads, _, width = query_head.shape
    length = queries.shape[1]
    part = first_half.shape[1]
    groups = 2 * part
    chunks = first.shape[0]
    count = heads // chunks
    mine = my_heads(heads)
    query_head[:, pl.ds(0, length)] = queries[mine]
    query_head[:, pl.ds(length, length)] = queries_other[mine]
    grad_head[:, pl.ds(0, length)] = grads[mine]
    grad_head[:, pl.ds(length, length)] = grads_other[mine]

    def block(index, n):
        g = n * groups // chunks
        return (first_half, second_half)[g // part][index, g % part]

    factor = width ** (-0.5) * math.log2(math.e)
    token = lane_tokens(count, length)
    for n, rows in enumerate(first_visible(spans, offset, chunks, count, length)):
        first[n] = rows

    def products(n):
        own_prob_grad[n] = matmul(block(1, n), grouped(grad_head, n, count), (1, 1))
        return (matmul(block(0, n), grouped(query_head, n, count), (1, 1)),)

    def softmax(n, scores):
        scores = masked(scores * factor, first[n], 0, token)
        row_max = jnp.max(scores, axis=0, keepdims=True)
        weights = jnp.exp2(scores - row_max)
        own_max[n] = row_max
        own_total[n] = jnp.sum(weights, axis=0, keepdims=True)
        own_weights[n] = weights
        return (weights.astype(jnp.bfloat16),)

    def weigh(n, halves):
        own_out[n] = matmul(block(1, n), halves, (0, 0))
        grad_rows[n] = grouped(grad_head, n, count).T

    pipelined(chunks, products, softmax, weigh)


def two_back(back_two, two_other, index, g):
    base = lax.axis_index("head") * two_other[index].shape[0]
    return join(back_two[index, base + g], two_other[index][g])


def near_forward_kernel(
    first, query_head, grad_head, back_two, two_keys, two_values, own_max, own_total, own_out,
    near_max, near_total, near_out, near_weights, near_prob_grad, own_factor,
):
    groups = two_keys.shape[0]
    two_other = (two_keys, two_values)
    chunks = first.shape[0]
    heads, _, width = query_head.shape
    count = heads // chunks
    factor = width ** (-0.5) * math.log2(math.e)

    def products(n):
        g = n * groups // chunks
        keys = two_back(back_two, two_other, 0, g)
        values = two_back(back_two, two_other, 1, g)
        near_prob_grad[n] = matmul(values, grouped(grad_head, n, count), (1, 1))
        return (matmul(keys, grouped(query_head, n, count), (1, 1)),)

    def softmax(n, scores):
        scores = masked(scores * factor, first[n], 2)
        row_max = jnp.maximum(own_max[n], jnp.max(scores, axis=0, keepdims=True))
        weights = jnp.exp2(scores - row_max)
        rescale = jnp.exp2(own_max[n] - row_max)
        own_factor[n] = rescale
        near_max[n] = row_max
        near_total[n] = own_total[n] * rescale + jnp.sum(weights, axis=0, keepdims=True)
        near_weights[n] = weights
        return rescale, weights.astype(jnp.bfloat16)

    def weigh(n, rescale, halves):
        values = two_back(back_two, two_other, 1, n * groups // chunks)
        near_out[n] = own_out[n] * rescale + matmul(values, halves, (0, 0))

    pipelined(chunks, products, softmax, weigh)


def last_kernel(
    base, first, query_head, grad_head, back_one, grad_rows, near_max, near_total, near_out, after,
    attended_rows, row_delta, near_factor, one_grad, one_part,
):
    groups = back_one.shape[1]
    chunks = row_delta.shape[0]
    heads, _, width = query_head.shape
    count = heads // first.shape[0]
    scale = width ** (-0.5)

    def products(n):
        g = n * groups // chunks
        scores = matmul(back_one[0, g], grouped(query_head, base + n, count), (1, 1))
        prob_grad = matmul(back_one[1, g], grouped(grad_head, base + n, count), (1, 1))
        return scores, prob_grad

    def softmax(n, scores, prob_grad):
        scores = masked(scores * (scale * math.log2(math.e)), first[base + n], 1)
        row_max = jnp.maximum(near_max[base + n], jnp.max(scores, axis=0, keepdims=True))
        weights = jnp.exp2(scores - row_max)
        rescale = jnp.exp2(near_max[base + n] - row_max)
        inverse = 1.0 / (near_total[base + n] * rescale + jnp.sum(weights, axis=0, keepdims=True))
        weighted = matmul(
            back_one[1, n * groups // chunks], weights.astype(jnp.bfloat16), (0, 0)
        )
        near_factor[n] = rescale * inverse
        return prob_grad, weights, weighted, rescale, inverse

    def differentiate(n, prob_grad, weights, weighted, rescale, inverse):
        attended = ((near_out[base + n] * rescale + weighted) * inverse).astype(jnp.bfloat16)
        delta = jnp.sum(
            grad_rows[base + n].astype(jnp.float32) * attended.astype(jnp.float32), axis=0, keepdims=True
        )
        prob = weights * inverse
        score_grad = (prob * (prob_grad - delta)).astype(jnp.bfloat16)
        attended_rows[n] = attended
        row_delta[n] = delta
        one_grad[n] = score_grad
        return score_grad, prob.astype(jnp.bfloat16)

    def store(g, key_part, value_part):
        one_part[0, g] = (key_part * scale).astype(jnp.bfloat16)
        one_part[1, g] = value_part.astype(jnp.bfloat16)

    accumulate = accumulator(query_head, grad_head, base, count, chunks, groups, store)
    pipelined(chunks, products, softmax, differentiate, accumulate)


def pipelined(chunks, *stages):
    ready = [{} for _ in range(len(stages) + 1)]
    for step in range(chunks + len(stages) - 1):
        for depth, stage in enumerate(stages):
            n = step - depth
            if 0 <= n < chunks:
                ready[depth + 1][n] = stage(n, *ready[depth].pop(n, ())) or ()


def accumulator(query_head, grad_head, base, count, chunks, groups, store):
    parts = {}

    def accumulate(n, score_grad, half):
        g = n * groups // chunks
        key_part = matmul(score_grad, grouped(query_head, base + n, count), (1, 0))
        value_part = matmul(half, grouped(grad_head, base + n, count), (1, 0))
        if g in parts:
            key_part, value_part = parts[g][0] + key_part, parts[g][1] + value_part
        parts[g] = (key_part, value_part)
        if (n + 1) * groups // chunks != g:
            store(g, key_part, value_part)

    return accumulate


def of_half(n, first, second):
    each = first.shape[0]
    return first[n] if n < each else second[n - each]


def two_backward_kernel(
    query_head, grad_head, near_weights, near_prob_grad, factor_a, delta_a, factor_b, delta_b,
    two_grad, two_mine, send_keys, send_values,
):
    chunks = near_weights.shape[0]
    groups, length, width = two_mine.shape[1:]

    def differentiate(n):
        prob = near_weights[n] * of_half(n, factor_a, factor_b)
        score_grad = prob * (near_prob_grad[n] - of_half(n, delta_a, delta_b))
        score_grad = score_grad.astype(jnp.bfloat16)
        two_grad[n] = score_grad
        return score_grad, prob.astype(jnp.bfloat16)

    def store(g, key_part, value_part):
        for index, (part, send) in enumerate(
            ((key_part * width ** (-0.5), send_keys), (value_part, send_values))
        ):
            two_mine[index, g] = part[:length].astype(jnp.bfloat16)
            send[g] = part[length:].astype(jnp.bfloat16)

    accumulate = accumulator(query_head, grad_head, 0, query_head.shape[0] // chunks, chunks, groups, store)
    pipelined(chunks, differentiate, accumulate)


def own_backward_kernel(
    query_head, grad_head, own_weights, own_prob_grad, own_factor, factor_a, delta_a, factor_b,
    delta_b, after, own_grad, own_part,
):
    chunks = own_weights.shape[0]
    groups, _, width = own_part.shape[1:]

    def differentiate(n):
        prob = own_weights[n] * (own_factor[n] * of_half(n, factor_a, factor_b))
        score_grad = prob * (own_prob_grad[n] - of_half(n, delta_a, delta_b))
        score_grad = score_grad.astype(jnp.bfloat16)
        own_grad[n] = score_grad
        return score_grad, prob.astype(jnp.bfloat16)

    def store(g, key_part, value_part):
        own_part[0, g] = key_part * width ** (-0.5)
        own_part[1, g] = value_part

    accumulate = accumulator(query_head, grad_head, 0, query_head.shape[0] // chunks, chunks, groups, store)
    pipelined(chunks, differentiate, accumulate)


def join_two_kernel(two_mine, other_keys, other_values, two_part):
    groups = two_mine.shape[1]
    two_part[:, my_heads(groups)] = two_mine[...]
    two_part[0, other_heads(groups)] = other_keys[...]
    two_part[1, other_heads(groups)] = other_values[...]


def query_kernel(
    own_a, own_b, one_a, one_b, rows_a, rows_b, grad_a, grad_b, back_two, two_keys, two_grad,
    own_grad, after, out_mine, query_mine, first_third, second_third, last_third, query_send,
):
    part, chunks = own_a.shape[1], own_grad.shape[0]
    heads, length, width = out_mine.shape
    count = heads // chunks
    for n in range(chunks):
        g = n * 2 * part // chunks
        own, one = ((own_a, one_a), (own_b, one_b))[g // part]
        rows = pl.ds(n * count, count)
        keys = join(two_back(back_two, (two_keys,), 0, g), one[0, g % part], own[0, g % part])
        total = matmul(keys, join(two_grad[n], of_half(n, grad_a, grad_b), own_grad[n]), (0, 0))
        total = (total * width ** (-0.5)).astype(jnp.bfloat16)
        for index, (columns, mine) in enumerate(
            ((of_half(n, rows_a, rows_b), out_mine), (total, query_mine))
        ):
            block = columns.T.reshape(count, 2 * length, width)
            mine[rows] = block[:, :length]
            query_send[index, rows] = block[:, length:]
    for index, row, piece, taken in placed((first_third, second_third, last_third), heads):
        piece[...] = query_send[index, pl.ds(row, taken)]


def assemble_kernel(
    out_mine, query_mine, first_third, second_third, last_third, out, query_grad, token
):
    heads = out_mine.shape[0]
    start = (1 - lax.axis_index("head")) * heads
    out[my_heads(heads)] = out_mine[...]
    query_grad[my_heads(heads)] = query_mine[...]
    for index, row, piece, count in placed((first_third, second_third, last_third), heads):
        (out, query_grad)[index][pl.ds(start + row, count)] = piece[...]
    token[...] = jnp.zeros(token.shape, token.dtype)


def first_sum_kernel(own_part, one_total, total, token):
    total[...] = own_part[:, pl.ds(0, one_total.shape[1])] + one_total[...].astype(jnp.float32)
    token[...] = jnp.zeros(token.shape, token.dtype)


def own_sum_kernel(own_part, first_sum, one_total, sum_mine, sum_send):
    length, part = sum_mine.shape[2], first_sum.shape[1]
    second = own_part[:, pl.ds(part, part)] + one_total[...].astype(jnp.float32)
    for index, total in enumerate((first_sum[...], second)):
        groups = pl.ds(index * part, part)
        sum_mine[:, groups] = total[:, :, :length]
        sum_send[:, groups] = total[:, :, length:].astype(jnp.bfloat16)


def final_kernel(sum_mine, sum_other, two_total, after, key_grad, value_grad):
    groups = sum_mine.shape[1]
    mine, other = my_heads(groups), other_heads(groups)
    for index, result in enumerate((key_grad, value_grad)):
        total = sum_mine[index] + two_total[index, mine].astype(jnp.float32)
        result[mine] = total.astype(jnp.bfloat16)
        total = sum_other[index].astype(jnp.float32) + two_total[index, other].astype(jnp.float32)
        result[other] = total.astype(jnp.bfloat16)


def shards(query_matrix, key_matrix, value_matrix, output_gradient, query_head_spans, slab_offset):
    groups, length, width = key_matrix.shape
    heads = query_matrix.shape[0]
    cores = lax.axis_size("head")
    tokens = cores * length
    groups_here, heads_here = groups // cores, heads // cores
    count = max(1, min(heads // groups, 256 // tokens))
    chunks = heads_here // count
    lanes = count * tokens
    half, full = jnp.bfloat16, jnp.float32
    vmem = pl.BlockSpec(memory_space=pltpu.VMEM)
    smem = pl.BlockSpec(memory_space=pltpu.SMEM)

    def call(kernel, name, outs, arrays, scalars=0, scratch=(), flops=1):
        return pl.pallas_call(
            kernel,
            out_shape=tuple(jax.ShapeDtypeStruct(shape, kind) for shape, kind in outs),
            in_specs=[smem] * scalars + [vmem] * (len(arrays) - scalars),
            out_specs=(vmem,) * len(outs),
            scratch_shapes=scratch,
            compiler_params=pltpu.CompilerParams(vmem_limit_bytes=40 * 1024 * 1024),
            cost_estimate=pl.CostEstimate(flops=flops, bytes_accessed=0, transcendentals=0),
            name=name,
        )(*arrays)

    def rows_of(rows, kind):
        return ((chunks, rows, lanes), kind)

    stat = rows_of(1, full)
    whole_pair = ((2, groups, length, width), half)
    half_block = ((groups_here, length, width), half)
    half_pair = ((2, groups_here, length, width), half)
    chip_pair = ((2, groups_here, tokens, width), half)
    half_rows = ((heads_here, length, width), half)
    part, each = groups_here // 2, chunks // 2
    chip_half = ((2, part, tokens, width), half)
    half_stat = ((each, 1, lanes), full)
    chip_rows = ((heads_here, tokens, width), half)

    queries_other = swapped(query_matrix, "head")
    grads_other = swapped(output_gradient, "head")
    own = jnp.stack([key_matrix, value_matrix])
    back_two = shifted(own, "seq", 2)
    own_sends = call(split_kernel, "split_own", [half_block] * 2, (own,))
    own_halves = call(
        join_own_kernel,
        "join_own",
        [chip_half] * 2,
        (own, *[swapped(send, "head") for send in own_sends]),
    )
    back_one = [
        shifted(block, "seq", 1, ring=index == 0) for index, block in enumerate(own_halves)
    ]
    (
        query_head, grad_head, grad_rows, first, own_max, own_total, own_out, own_weights,
        own_prob_grad,
    ) = call(
        own_kernel,
        "own_block",
        [
            chip_rows, chip_rows, rows_of(width, half), rows_of(1, jnp.int32), stat, stat,
            rows_of(width, full), rows_of(tokens, full), rows_of(tokens, full),
        ],
        (
            query_head_spans, slab_offset, query_matrix, output_gradient,
            queries_other, grads_other, *own_halves,
        ),
        scalars=2,
    )
    back_two, first = lax.optimization_barrier((back_two, first))
    two_sends = call(split_kernel, "split_two", [half_block] * 2, (back_two,))
    two_other = [swapped(send, "head") for send in two_sends]
    near_max, near_total, near_out, near_weights, near_prob_grad, own_factor = call(
        near_forward_kernel,
        "near_forward",
        [stat, stat, rows_of(width, full), rows_of(tokens, full), rows_of(tokens, full), stat],
        (first, query_head, grad_head, back_two, *two_other, own_max, own_total, own_out),
    )
    after = near_max
    halves = []
    for index in range(2):
        back_one[index], after = lax.optimization_barrier((back_one[index], after))
        rows, delta, factor, one_grad, one_part = call(
            functools.partial(last_kernel, index * each),
            "last_" + "ab"[index],
            [
                ((each, width, lanes), half), half_stat, half_stat, ((each, tokens, lanes), half),
                chip_half,
            ],
            (
                first, query_head, grad_head, back_one[index], grad_rows, near_max, near_total,
                near_out, after,
            ),
        )
        halves.append((factor, delta, rows, one_grad, shifted(one_part, "seq", -1)))
        after = delta
    stats = (*halves[0][:2], *halves[1][:2])
    two_grad, part_mine, *part_sends = call(
        two_backward_kernel,
        "two_backward",
        [rows_of(tokens, half), half_pair, half_block, half_block],
        (query_head, grad_head, near_weights, near_prob_grad, *stats),
    )
    (two_part,) = call(
        join_two_kernel,
        "join_two",
        [whole_pair],
        (part_mine, *[swapped(send, "head") for send in part_sends]),
    )
    two_total = shifted(two_part, "seq", -2)
    own_grad, own_part = call(
        own_backward_kernel,
        "own_backward",
        [rows_of(tokens, half), (chip_pair[0], full)],
        (
            query_head, grad_head, own_weights, own_prob_grad, own_factor, *stats, two_part,
        ),
    )
    first_sum, sum_token = call(
        first_sum_kernel,
        "sum_a",
        [(chip_half[0], full), ((8, 128), full)],
        (own_part, halves[0][4]),
        flops=5 * 10**8,
    )
    out_mine, query_mine, *sends = call(
        query_kernel,
        "query_grad",
        [half_rows] * 2 + [((rows, length, width), half) for rows in thirds(heads_here)],
        (
            *own_halves, *back_one, halves[0][2], halves[1][2], halves[0][3], halves[1][3],
            back_two, two_other[0], two_grad, own_grad, sum_token,
        ),
        scratch=[pltpu.VMEM((2,) + half_rows[0], half)],
    )
    attn_out, query_grad, token = call(
        assemble_kernel,
        "assemble",
        [(query_matrix.shape, half)] * 2 + [((8, 128), full)],
        (out_mine, query_mine, *[swapped(send, "head") for send in sends]),
    )
    sum_mine, sum_send = call(
        own_sum_kernel,
        "sum_b",
        [(half_pair[0], full), half_pair],
        (own_part, first_sum, halves[1][4]),
    )
    key_grad, value_grad = call(
        final_kernel,
        "total",
        [(key_matrix.shape, half)] * 2,
        (sum_mine, swapped(sum_send, "head"), two_total, token),
    )
    return (attn_out, query_grad, key_grad, value_grad)


def solution(mesh):
    tokens = P(None, ("seq", "head"), None)
    return jax.shard_map(
        shards,
        mesh=mesh,
        in_specs=(tokens, tokens, tokens, tokens, P(), P()),
        out_specs=(tokens, tokens, tokens, tokens),
        check_vma=False,
    )
```

```python
import math

import jax
import jax.numpy as jnp
from jax import lax
from jax.experimental import pallas as pl
from jax.experimental.pallas import tpu as pltpu
from jax.sharding import PartitionSpec as P

REACH = 2
SEGMENT = 512

masked_score = -1e30


def shifted(block, axis, distance, ring=True):
    count = lax.axis_size(axis)
    route = [(i, (i + distance) % count) for i in range(count) if ring or 0 <= i + distance < count]
    return lax.ppermute(block, axis, route)


def swapped(block, axis):
    count = lax.axis_size(axis)
    return lax.ppermute(block, axis, [(i, count - 1 - i) for i in range(count)])


def matmul(left, right, contract):
    return lax.dot_general(
        left, right, ((contract[:1], contract[1:]), ((), ())), preferred_element_type=jnp.float32
    )


def grouped(ref, n, count):
    _, length, width = ref.shape
    return ref[pl.ds(n * count, count)].reshape(count * length, width)


def join(*blocks):
    return jnp.concatenate(blocks, axis=0)


def core_offsets(length):
    core = lax.axis_index("head")
    return core * length, (1 - core) * length


def my_heads(count):
    return pl.ds(lax.axis_index("head") * count, count)


def other_heads(count):
    return pl.ds((1 - lax.axis_index("head")) * count, count)


def lane_tokens(count, length):
    lane = lax.broadcasted_iota(jnp.int32, (1, count * 2 * length), 1)
    token = lane - lane // (2 * length) * (2 * length)
    mine, other = core_offsets(length)
    return jnp.where(token < length, token + mine, token - length + other)


def first_visible(spans, offset, chunks, count, length):
    token = lane_tokens(count, length)
    lane_head = lax.broadcasted_iota(jnp.int32, token.shape, 1) // (2 * length)
    start = lax.axis_index("seq") * 2 * length
    segment_start = token - lax.bitwise_and(offset[0] + start + token, SEGMENT - 1)
    floor = jnp.maximum(segment_start, -start)
    base = lax.axis_index("head") * chunks * count
    result = []
    for n in range(chunks):
        span = jnp.full(token.shape, spans[base + n * count], jnp.int32)
        for a in range(1, count):
            span = jnp.where(lane_head == a, spans[base + n * count + a], span)
        result.append(jnp.maximum(floor, token - span + 1))
    return result


def masked(scores, first, chips_back, token=None):
    length = scores.shape[0] // 2
    row = lax.broadcasted_iota(jnp.int32, (length, scores.shape[1]), 0)
    pieces = []
    for part, offset in enumerate(core_offsets(length)):
        visible = row >= first + (chips_back * 2 * length - offset)
        if token is not None:
            visible &= row <= token - offset
        pieces.append(
            jnp.where(visible, scores[part * length : (part + 1) * length], masked_score)
        )
    return join(*pieces)


def split_kernel(block, *sends):
    for index, send in enumerate(sends):
        send[...] = block[index, other_heads(send.shape[0])]


def thirds(rows):
    return [2 * rows * (i + 1) // 3 - 2 * rows * i // 3 for i in range(3)]


def placed(pieces, rows):
    taken = 0
    for piece in pieces:
        count = piece.shape[0]
        for index in range(2):
            low = max(taken, index * rows)
            high = min(taken + count, (index + 1) * rows)
            if low < high:
                yield index, low - index * rows, piece.at[pl.ds(low - taken, high - low)], high - low
        taken += count


def split_rows_kernel(queries, grads, after, *sends):
    heads = queries.shape[0] // 2
    start = (1 - lax.axis_index("head")) * heads
    for index, row, piece, count in placed(sends, heads):
        piece[...] = (queries, grads)[index][pl.ds(start + row, count)]


def join_own_kernel(own, other_keys, other_values, own_head):
    groups, length = other_keys.shape[:2]
    own_head[:, :, pl.ds(0, length)] = own[:, my_heads(groups)]
    own_head[0, :, pl.ds(length, length)] = other_keys[...]
    own_head[1, :, pl.ds(length, length)] = other_values[...]


def own_kernel(
    spans, offset, queries, grads, first_third, second_third, last_third, own,
    query_head, grad_head, grad_rows, first, own_max, own_total, own_out, own_weights,
    own_prob_grad,
):
    heads, _, width = query_head.shape
    length = queries.shape[1]
    groups = own.shape[1]
    chunks = first.shape[0]
    count = heads // chunks
    query_head[:, pl.ds(0, length)] = queries[my_heads(heads)]
    grad_head[:, pl.ds(0, length)] = grads[my_heads(heads)]
    for index, row, piece, rows in placed((first_third, second_third, last_third), heads):
        (query_head, grad_head)[index][pl.ds(row, rows), pl.ds(length, length)] = piece[...]
    factor = width ** (-0.5) * math.log2(math.e)
    token = lane_tokens(count, length)
    for n, rows in enumerate(first_visible(spans, offset, chunks, count, length)):
        first[n] = rows

    def products(n):
        g = n * groups // chunks
        own_prob_grad[n] = matmul(own[1, g], grouped(grad_head, n, count), (1, 1))
        return (matmul(own[0, g], grouped(query_head, n, count), (1, 1)),)

    def softmax(n, scores):
        scores = masked(scores * factor, first[n], 0, token)
        row_max = jnp.max(scores, axis=0, keepdims=True)
        weights = jnp.exp2(scores - row_max)
        own_max[n] = row_max
        own_total[n] = jnp.sum(weights, axis=0, keepdims=True)
        own_weights[n] = weights
        return (weights.astype(jnp.bfloat16),)

    def weigh(n, halves):
        own_out[n] = matmul(own[1, n * groups // chunks], halves, (0, 0))
        grad_rows[n] = grouped(grad_head, n, count).T

    pipelined(chunks, products, softmax, weigh)


def two_back(back_two, two_other, index, g):
    base = lax.axis_index("head") * two_other[index].shape[0]
    return join(back_two[index, base + g], two_other[index][g])


def near_forward_kernel(
    first, query_head, grad_head, back_two, two_keys, two_values, own_max, own_total, own_out,
    near_max, near_total, near_out, near_weights, near_prob_grad, own_factor,
):
    groups = two_keys.shape[0]
    two_other = (two_keys, two_values)
    chunks = first.shape[0]
    heads, _, width = query_head.shape
    count = heads // chunks
    factor = width ** (-0.5) * math.log2(math.e)

    def products(n):
        g = n * groups // chunks
        keys = two_back(back_two, two_other, 0, g)
        values = two_back(back_two, two_other, 1, g)
        near_prob_grad[n] = matmul(values, grouped(grad_head, n, count), (1, 1))
        return (matmul(keys, grouped(query_head, n, count), (1, 1)),)

    def softmax(n, scores):
        scores = masked(scores * factor, first[n], 2)
        row_max = jnp.maximum(own_max[n], jnp.max(scores, axis=0, keepdims=True))
        weights = jnp.exp2(scores - row_max)
        rescale = jnp.exp2(own_max[n] - row_max)
        own_factor[n] = rescale
        near_max[n] = row_max
        near_total[n] = own_total[n] * rescale + jnp.sum(weights, axis=0, keepdims=True)
        near_weights[n] = weights
        return rescale, weights.astype(jnp.bfloat16)

    def weigh(n, rescale, halves):
        values = two_back(back_two, two_other, 1, n * groups // chunks)
        near_out[n] = own_out[n] * rescale + matmul(values, halves, (0, 0))

    pipelined(chunks, products, softmax, weigh)


def last_kernel(
    first, query_head, grad_head, back_one, grad_rows, near_max, near_total, near_out,
    attended_rows, row_delta, near_factor, one_grad, one_part,
):
    groups = back_one.shape[1]
    chunks = first.shape[0]
    heads, _, width = query_head.shape
    count = heads // chunks
    scale = width ** (-0.5)

    def products(n):
        g = n * groups // chunks
        scores = matmul(back_one[0, g], grouped(query_head, n, count), (1, 1))
        prob_grad = matmul(back_one[1, g], grouped(grad_head, n, count), (1, 1))
        return scores, prob_grad

    def softmax(n, scores, prob_grad):
        scores = masked(scores * (scale * math.log2(math.e)), first[n], 1)
        row_max = jnp.maximum(near_max[n], jnp.max(scores, axis=0, keepdims=True))
        weights = jnp.exp2(scores - row_max)
        rescale = jnp.exp2(near_max[n] - row_max)
        inverse = 1.0 / (near_total[n] * rescale + jnp.sum(weights, axis=0, keepdims=True))
        weighted = matmul(
            back_one[1, n * groups // chunks], weights.astype(jnp.bfloat16), (0, 0)
        )
        near_factor[n] = rescale * inverse
        return prob_grad, weights, weighted, rescale, inverse

    def differentiate(n, prob_grad, weights, weighted, rescale, inverse):
        attended = ((near_out[n] * rescale + weighted) * inverse).astype(jnp.bfloat16)
        delta = jnp.sum(
            grad_rows[n].astype(jnp.float32) * attended.astype(jnp.float32), axis=0, keepdims=True
        )
        prob = weights * inverse
        score_grad = (prob * (prob_grad - delta)).astype(jnp.bfloat16)
        attended_rows[n] = attended
        row_delta[n] = delta
        one_grad[n] = score_grad
        return score_grad, prob.astype(jnp.bfloat16)

    def store(g, key_part, value_part):
        one_part[0, g] = (key_part * scale).astype(jnp.bfloat16)
        one_part[1, g] = value_part.astype(jnp.bfloat16)

    accumulate = accumulator(query_head, grad_head, chunks, groups, store)
    pipelined(chunks, products, softmax, differentiate, accumulate)


def pipelined(chunks, *stages):
    ready = [{} for _ in range(len(stages) + 1)]
    for step in range(chunks + len(stages) - 1):
        for depth, stage in enumerate(stages):
            n = step - depth
            if 0 <= n < chunks:
                ready[depth + 1][n] = stage(n, *ready[depth].pop(n, ())) or ()


def accumulator(query_head, grad_head, chunks, groups, store):
    count = query_head.shape[0] // chunks
    parts = {}

    def accumulate(n, score_grad, half):
        g = n * groups // chunks
        key_part = matmul(score_grad, grouped(query_head, n, count), (1, 0))
        value_part = matmul(half, grouped(grad_head, n, count), (1, 0))
        if g in parts:
            key_part, value_part = parts[g][0] + key_part, parts[g][1] + value_part
        parts[g] = (key_part, value_part)
        if (n + 1) * groups // chunks != g:
            store(g, key_part, value_part)

    return accumulate


def two_backward_kernel(
    query_head, grad_head, near_weights, near_prob_grad, near_factor, row_delta,
    two_grad, two_mine, send_keys, send_values,
):
    chunks = near_weights.shape[0]
    groups, length, width = two_mine.shape[1:]

    def differentiate(n):
        prob = near_weights[n] * near_factor[n]
        score_grad = (prob * (near_prob_grad[n] - row_delta[n])).astype(jnp.bfloat16)
        two_grad[n] = score_grad
        return score_grad, prob.astype(jnp.bfloat16)

    def store(g, key_part, value_part):
        for index, (part, send) in enumerate(
            ((key_part * width ** (-0.5), send_keys), (value_part, send_values))
        ):
            two_mine[index, g] = part[:length].astype(jnp.bfloat16)
            send[g] = part[length:].astype(jnp.bfloat16)

    accumulate = accumulator(query_head, grad_head, chunks, groups, store)
    pipelined(chunks, differentiate, accumulate)


def own_backward_kernel(
    query_head, grad_head, own_weights, own_prob_grad, near_factor, own_factor, row_delta,
    after, own_grad, own_part,
):
    chunks = own_weights.shape[0]
    groups, _, width = own_part.shape[1:]

    def differentiate(n):
        prob = own_weights[n] * (own_factor[n] * near_factor[n])
        score_grad = (prob * (own_prob_grad[n] - row_delta[n])).astype(jnp.bfloat16)
        own_grad[n] = score_grad
        return score_grad, prob.astype(jnp.bfloat16)

    def store(g, key_part, value_part):
        own_part[0, g] = key_part * width ** (-0.5)
        own_part[1, g] = value_part

    accumulate = accumulator(query_head, grad_head, chunks, groups, store)
    pipelined(chunks, differentiate, accumulate)


def join_two_kernel(two_mine, other_keys, other_values, two_part):
    groups = two_mine.shape[1]
    two_part[:, my_heads(groups)] = two_mine[...]
    two_part[0, other_heads(groups)] = other_keys[...]
    two_part[1, other_heads(groups)] = other_values[...]


def query_kernel(
    own, back_one, back_two, two_keys, attended_rows, two_grad, one_grad, own_grad,
    out_mine, query_mine, first_third, second_third, last_third, query_send,
):
    sends = (first_third, second_third, last_third)
    groups = own.shape[1]
    chunks = own_grad.shape[0]
    heads, length, width = out_mine.shape
    count = heads // chunks
    for n in range(chunks):
        g = n * groups // chunks
        rows = pl.ds(n * count, count)
        keys = join(two_back(back_two, (two_keys,), 0, g), back_one[0, g], own[0, g])
        part = matmul(keys, join(two_grad[n], one_grad[n], own_grad[n]), (0, 0))
        part = (part * width ** (-0.5)).astype(jnp.bfloat16)
        for index, (columns, mine) in enumerate(((attended_rows[n], out_mine), (part, query_mine))):
            block = columns.T.reshape(count, 2 * length, width)
            mine[rows] = block[:, :length]
            query_send[index, rows] = block[:, length:]
    for index, row, piece, taken in placed(sends, heads):
        piece[...] = query_send[index, pl.ds(row, taken)]


def assemble_kernel(
    out_mine, query_mine, first_third, second_third, last_third, out, query_grad, token
):
    heads = out_mine.shape[0]
    start = (1 - lax.axis_index("head")) * heads
    out[my_heads(heads)] = out_mine[...]
    query_grad[my_heads(heads)] = query_mine[...]
    for index, row, piece, count in placed((first_third, second_third, last_third), heads):
        (out, query_grad)[index][pl.ds(start + row, count)] = piece[...]
    token[...] = jnp.zeros(token.shape, token.dtype)


def own_sum_kernel(own_part, one_total, sum_mine, sum_send):
    length = sum_mine.shape[2]
    total = own_part[...] + one_total[...].astype(jnp.float32)
    sum_mine[...] = total[:, :, :length]
    sum_send[...] = total[:, :, length:].astype(jnp.bfloat16)


def final_kernel(sum_mine, sum_other, two_total, after, key_grad, value_grad):
    groups = sum_mine.shape[1]
    mine, other = my_heads(groups), other_heads(groups)
    for index, result in enumerate((key_grad, value_grad)):
        total = sum_mine[index] + two_total[index, mine].astype(jnp.float32)
        result[mine] = total.astype(jnp.bfloat16)
        total = sum_other[index].astype(jnp.float32) + two_total[index, other].astype(jnp.float32)
        result[other] = total.astype(jnp.bfloat16)


def shards(query_matrix, key_matrix, value_matrix, output_gradient, query_head_spans, slab_offset):
    groups, length, width = key_matrix.shape
    heads = query_matrix.shape[0]
    cores = lax.axis_size("head")
    tokens = cores * length
    groups_here, heads_here = groups // cores, heads // cores
    count = max(1, min(heads // groups, 256 // tokens))
    chunks = heads_here // count
    lanes = count * tokens
    half, full = jnp.bfloat16, jnp.float32
    vmem = pl.BlockSpec(memory_space=pltpu.VMEM)
    smem = pl.BlockSpec(memory_space=pltpu.SMEM)

    def call(kernel, name, outs, arrays, scalars=0, scratch=()):
        return pl.pallas_call(
            kernel,
            out_shape=tuple(jax.ShapeDtypeStruct(shape, kind) for shape, kind in outs),
            in_specs=[smem] * scalars + [vmem] * (len(arrays) - scalars),
            out_specs=(vmem,) * len(outs),
            scratch_shapes=scratch,
            compiler_params=pltpu.CompilerParams(vmem_limit_bytes=40 * 1024 * 1024),
            cost_estimate=pl.CostEstimate(flops=1, bytes_accessed=0, transcendentals=0),
            name=name,
        )(*arrays)

    def rows_of(rows, kind):
        return ((chunks, rows, lanes), kind)

    stat = rows_of(1, full)
    whole_pair = ((2, groups, length, width), half)
    half_block = ((groups_here, length, width), half)
    half_pair = ((2, groups_here, length, width), half)
    chip_pair = ((2, groups_here, tokens, width), half)
    half_rows = ((heads_here, length, width), half)
    third_rows = [((rows, length, width), half) for rows in thirds(heads_here)]
    chip_rows = ((heads_here, tokens, width), half)

    own = jnp.stack([key_matrix, value_matrix])
    back_two = shifted(own, "seq", 2)
    own_sends = call(split_kernel, "split_own", [half_block] * 2, (own,))
    (own_head,) = call(
        join_own_kernel, "join_own", [chip_pair], (own, *[swapped(send, "head") for send in own_sends])
    )
    back_one = shifted(own_head, "seq", 1, ring=False)
    sends = call(
        split_rows_kernel,
        "split_rows",
        third_rows,
        (query_matrix, output_gradient, own),
    )
    (
        query_head, grad_head, grad_rows, first, own_max, own_total, own_out, own_weights,
        own_prob_grad,
    ) = call(
        own_kernel,
        "own_block",
        [
            chip_rows, chip_rows, rows_of(width, half), rows_of(1, jnp.int32), stat, stat,
            rows_of(width, full), rows_of(tokens, full), rows_of(tokens, full),
        ],
        (
            query_head_spans, slab_offset, query_matrix, output_gradient,
            *[swapped(send, "head") for send in sends], own_head,
        ),
        scalars=2,
    )
    back_two, first = lax.optimization_barrier((back_two, first))
    two_sends = call(split_kernel, "split_two", [half_block] * 2, (back_two,))
    two_other = [swapped(send, "head") for send in two_sends]
    near_max, near_total, near_out, near_weights, near_prob_grad, own_factor = call(
        near_forward_kernel,
        "near_forward",
        [stat, stat, rows_of(width, full), rows_of(tokens, full), rows_of(tokens, full), stat],
        (first, query_head, grad_head, back_two, *two_other, own_max, own_total, own_out),
    )
    back_one, near_max = lax.optimization_barrier((back_one, near_max))
    attended_rows, row_delta, near_factor, one_grad, one_part = call(
        last_kernel,
        "last_forward_backward",
        [rows_of(width, half), stat, stat, rows_of(tokens, half), chip_pair],
        (first, query_head, grad_head, back_one, grad_rows, near_max, near_total, near_out),
    )
    one_total = shifted(one_part, "seq", -1)
    two_grad, part_mine, *part_sends = call(
        two_backward_kernel,
        "two_backward",
        [rows_of(tokens, half), half_pair, half_block, half_block],
        (query_head, grad_head, near_weights, near_prob_grad, near_factor, row_delta),
    )
    (two_part,) = call(
        join_two_kernel,
        "join_two",
        [whole_pair],
        (part_mine, *[swapped(send, "head") for send in part_sends]),
    )
    two_total = shifted(two_part, "seq", -2, ring=False)
    own_grad, own_part = call(
        own_backward_kernel,
        "own_backward",
        [rows_of(tokens, half), (chip_pair[0], full)],
        (
            query_head, grad_head, own_weights, own_prob_grad, near_factor, own_factor, row_delta,
            two_part,
        ),
    )
    out_mine, query_mine, *sends = call(
        query_kernel,
        "query_grad",
        [half_rows] * 2 + third_rows,
        (own_head, back_one, back_two, two_other[0], attended_rows, two_grad, one_grad, own_grad),
        scratch=[pltpu.VMEM((2,) + half_rows[0], half)],
    )
    attn_out, query_grad, token = call(
        assemble_kernel,
        "assemble",
        [(query_matrix.shape, half)] * 2 + [((8, 128), full)],
        (out_mine, query_mine, *[swapped(send, "head") for send in sends]),
    )
    sum_mine, sum_send = call(
        own_sum_kernel, "own_sum", [(half_pair[0], full), half_pair], (own_part, one_total)
    )
    key_grad, value_grad = call(
        final_kernel,
        "total",
        [(key_matrix.shape, half)] * 2,
        (sum_mine, swapped(sum_send, "head"), two_total, token),
    )
    return (attn_out, query_grad, key_grad, value_grad)


def solution(mesh):
    tokens = P(None, ("seq", "head"), None)
    return jax.shard_map(
        shards,
        mesh=mesh,
        in_specs=(tokens, tokens, tokens, tokens, P(), P()),
        out_specs=(tokens, tokens, tokens, tokens),
        check_vma=False,
    )
```

```python
import math

import jax
import jax.numpy as jnp
from jax import lax
from jax.experimental import pallas as pl
from jax.experimental.pallas import tpu as pltpu
from jax.sharding import PartitionSpec as P

REACH = 2
SEGMENT = 512

masked_score = -1e30


def shifted(block, axis, distance, ring=True):
    count = lax.axis_size(axis)
    route = [(i, (i + distance) % count) for i in range(count) if ring or i + distance < count]
    return lax.ppermute(block, axis, route)


def swapped(block, axis):
    count = lax.axis_size(axis)
    return lax.ppermute(block, axis, [(i, count - 1 - i) for i in range(count)])


def matmul(left, right, contract):
    return lax.dot_general(
        left, right, ((contract[:1], contract[1:]), ((), ())), preferred_element_type=jnp.float32
    )


def grouped(ref, n, count):
    _, length, width = ref.shape
    return ref[pl.ds(n * count, count)].reshape(count * length, width)


def join(*blocks):
    return jnp.concatenate(blocks, axis=0)


def core_offsets(length):
    core = lax.axis_index("head")
    return core * length, (1 - core) * length


def my_heads(count):
    return pl.ds(lax.axis_index("head") * count, count)


def other_heads(count):
    return pl.ds((1 - lax.axis_index("head")) * count, count)


def lane_tokens(count, length):
    lane = lax.broadcasted_iota(jnp.int32, (1, count * 2 * length), 1)
    token = lane - lane // (2 * length) * (2 * length)
    mine, other = core_offsets(length)
    return jnp.where(token < length, token + mine, token - length + other)


def first_visible(spans, offset, chunks, count, length):
    token = lane_tokens(count, length)
    lane_head = lax.broadcasted_iota(jnp.int32, token.shape, 1) // (2 * length)
    start = lax.axis_index("seq") * 2 * length
    segment_start = token - lax.bitwise_and(offset[0] + start + token, SEGMENT - 1)
    floor = jnp.maximum(segment_start, -start)
    base = lax.axis_index("head") * chunks * count
    result = []
    for n in range(chunks):
        span = jnp.full(token.shape, spans[base + n * count], jnp.int32)
        for a in range(1, count):
            span = jnp.where(lane_head == a, spans[base + n * count + a], span)
        result.append(jnp.maximum(floor, token - span + 1))
    return result


def masked(scores, first, chips_back, token=None):
    length = scores.shape[0] // 2
    row = lax.broadcasted_iota(jnp.int32, (length, scores.shape[1]), 0)
    pieces = []
    for part, offset in enumerate(core_offsets(length)):
        visible = row >= first + (chips_back * 2 * length - offset)
        if token is not None:
            visible &= row <= token - offset
        pieces.append(
            jnp.where(visible, scores[part * length : (part + 1) * length], masked_score)
        )
    return join(*pieces)


def split_kernel(block, *sends):
    for index, send in enumerate(sends):
        send[...] = block[index, other_heads(send.shape[0])]


def thirds(rows):
    return [2 * rows * (i + 1) // 3 - 2 * rows * i // 3 for i in range(3)]


def placed(pieces, rows):
    taken = 0
    for piece in pieces:
        count = piece.shape[0]
        for index in range(2):
            low = max(taken, index * rows)
            high = min(taken + count, (index + 1) * rows)
            if low < high:
                yield index, low - index * rows, piece.at[pl.ds(low - taken, high - low)], high - low
        taken += count


def split_rows_kernel(queries, grads, after, *sends):
    heads = queries.shape[0] // 2
    start = (1 - lax.axis_index("head")) * heads
    for index, row, piece, count in placed(sends, heads):
        piece[...] = (queries, grads)[index][pl.ds(start + row, count)]


def join_own_kernel(own, other_keys, other_values, own_head):
    groups, length = other_keys.shape[:2]
    own_head[:, :, pl.ds(0, length)] = own[:, my_heads(groups)]
    own_head[0, :, pl.ds(length, length)] = other_keys[...]
    own_head[1, :, pl.ds(length, length)] = other_values[...]


def own_kernel(
    spans, offset, queries, grads, first_third, second_third, last_third, own,
    query_head, grad_head, grad_rows, first, own_max, own_total, own_out, own_weights,
    own_prob_grad,
):
    heads, _, width = query_head.shape
    length = queries.shape[1]
    groups = own.shape[1]
    chunks = first.shape[0]
    count = heads // chunks
    query_head[:, pl.ds(0, length)] = queries[my_heads(heads)]
    grad_head[:, pl.ds(0, length)] = grads[my_heads(heads)]
    for index, row, piece, rows in placed((first_third, second_third, last_third), heads):
        (query_head, grad_head)[index][pl.ds(row, rows), pl.ds(length, length)] = piece[...]
    factor = width ** (-0.5) * math.log2(math.e)
    token = lane_tokens(count, length)
    for n, rows in enumerate(first_visible(spans, offset, chunks, count, length)):
        first[n] = rows

    def products(n):
        g = n * groups // chunks
        own_prob_grad[n] = matmul(own[1, g], grouped(grad_head, n, count), (1, 1))
        return (matmul(own[0, g], grouped(query_head, n, count), (1, 1)),)

    def softmax(n, scores):
        scores = masked(scores * factor, first[n], 0, token)
        row_max = jnp.max(scores, axis=0, keepdims=True)
        weights = jnp.exp2(scores - row_max)
        own_max[n] = row_max
        own_total[n] = jnp.sum(weights, axis=0, keepdims=True)
        own_weights[n] = weights
        return (weights.astype(jnp.bfloat16),)

    def weigh(n, halves):
        own_out[n] = matmul(own[1, n * groups // chunks], halves, (0, 0))
        grad_rows[n] = grouped(grad_head, n, count).T

    pipelined(chunks, products, softmax, weigh)


def two_back(back_two, two_other, index, g):
    base = lax.axis_index("head") * two_other[index].shape[0]
    return join(back_two[index, base + g], two_other[index][g])


def near_forward_kernel(
    first, query_head, grad_head, back_two, two_keys, two_values, own_max, own_total, own_out,
    near_max, near_total, near_out, near_weights, near_prob_grad, own_factor,
):
    groups = two_keys.shape[0]
    two_other = (two_keys, two_values)
    chunks = first.shape[0]
    heads, _, width = query_head.shape
    count = heads // chunks
    factor = width ** (-0.5) * math.log2(math.e)

    def products(n):
        g = n * groups // chunks
        keys = two_back(back_two, two_other, 0, g)
        values = two_back(back_two, two_other, 1, g)
        near_prob_grad[n] = matmul(values, grouped(grad_head, n, count), (1, 1))
        return (matmul(keys, grouped(query_head, n, count), (1, 1)),)

    def softmax(n, scores):
        scores = masked(scores * factor, first[n], 2)
        row_max = jnp.maximum(own_max[n], jnp.max(scores, axis=0, keepdims=True))
        weights = jnp.exp2(scores - row_max)
        rescale = jnp.exp2(own_max[n] - row_max)
        own_factor[n] = rescale
        near_max[n] = row_max
        near_total[n] = own_total[n] * rescale + jnp.sum(weights, axis=0, keepdims=True)
        near_weights[n] = weights
        return rescale, weights.astype(jnp.bfloat16)

    def weigh(n, rescale, halves):
        values = two_back(back_two, two_other, 1, n * groups // chunks)
        near_out[n] = own_out[n] * rescale + matmul(values, halves, (0, 0))

    pipelined(chunks, products, softmax, weigh)


def last_kernel(
    first, query_head, grad_head, back_one, grad_rows, near_max, near_total, near_out,
    attended_rows, row_delta, near_factor, one_grad, one_part,
):
    groups = back_one.shape[1]
    chunks = first.shape[0]
    heads, _, width = query_head.shape
    count = heads // chunks
    scale = width ** (-0.5)

    def products(n):
        g = n * groups // chunks
        scores = matmul(back_one[0, g], grouped(query_head, n, count), (1, 1))
        prob_grad = matmul(back_one[1, g], grouped(grad_head, n, count), (1, 1))
        return scores, prob_grad

    def softmax(n, scores, prob_grad):
        scores = masked(scores * (scale * math.log2(math.e)), first[n], 1)
        row_max = jnp.maximum(near_max[n], jnp.max(scores, axis=0, keepdims=True))
        weights = jnp.exp2(scores - row_max)
        rescale = jnp.exp2(near_max[n] - row_max)
        inverse = 1.0 / (near_total[n] * rescale + jnp.sum(weights, axis=0, keepdims=True))
        weighted = matmul(
            back_one[1, n * groups // chunks], weights.astype(jnp.bfloat16), (0, 0)
        )
        near_factor[n] = rescale * inverse
        return prob_grad, weights, weighted, rescale, inverse

    def differentiate(n, prob_grad, weights, weighted, rescale, inverse):
        attended = ((near_out[n] * rescale + weighted) * inverse).astype(jnp.bfloat16)
        delta = jnp.sum(
            grad_rows[n].astype(jnp.float32) * attended.astype(jnp.float32), axis=0, keepdims=True
        )
        prob = weights * inverse
        score_grad = (prob * (prob_grad - delta)).astype(jnp.bfloat16)
        attended_rows[n] = attended
        row_delta[n] = delta
        one_grad[n] = score_grad
        return score_grad, prob.astype(jnp.bfloat16)

    def store(g, key_part, value_part):
        one_part[0, g] = (key_part * scale).astype(jnp.bfloat16)
        one_part[1, g] = value_part.astype(jnp.bfloat16)

    accumulate = accumulator(query_head, grad_head, chunks, groups, store)
    pipelined(chunks, products, softmax, differentiate, accumulate)


def pipelined(chunks, *stages):
    ready = [{} for _ in range(len(stages) + 1)]
    for step in range(chunks + len(stages) - 1):
        for depth, stage in enumerate(stages):
            n = step - depth
            if 0 <= n < chunks:
                ready[depth + 1][n] = stage(n, *ready[depth].pop(n, ())) or ()


def accumulator(query_head, grad_head, chunks, groups, store):
    count = query_head.shape[0] // chunks
    parts = {}

    def accumulate(n, score_grad, half):
        g = n * groups // chunks
        key_part = matmul(score_grad, grouped(query_head, n, count), (1, 0))
        value_part = matmul(half, grouped(grad_head, n, count), (1, 0))
        if g in parts:
            key_part, value_part = parts[g][0] + key_part, parts[g][1] + value_part
        parts[g] = (key_part, value_part)
        if (n + 1) * groups // chunks != g:
            store(g, key_part, value_part)

    return accumulate


def two_backward_kernel(
    query_head, grad_head, near_weights, near_prob_grad, near_factor, row_delta,
    two_grad, two_part,
):
    chunks = near_weights.shape[0]
    groups, _, width = two_part.shape[1:]

    def differentiate(n):
        prob = near_weights[n] * near_factor[n]
        score_grad = (prob * (near_prob_grad[n] - row_delta[n])).astype(jnp.bfloat16)
        two_grad[n] = score_grad
        return score_grad, prob.astype(jnp.bfloat16)

    def store(g, key_part, value_part):
        two_part[0, g] = (key_part * width ** (-0.5)).astype(jnp.bfloat16)
        two_part[1, g] = value_part.astype(jnp.bfloat16)

    accumulate = accumulator(query_head, grad_head, chunks, groups, store)
    pipelined(chunks, differentiate, accumulate)


def own_backward_kernel(
    query_head, grad_head, own_weights, own_prob_grad, near_factor, own_factor, row_delta,
    after, own_grad, own_part,
):
    chunks = own_weights.shape[0]
    groups, _, width = own_part.shape[1:]

    def differentiate(n):
        prob = own_weights[n] * (own_factor[n] * near_factor[n])
        score_grad = (prob * (own_prob_grad[n] - row_delta[n])).astype(jnp.bfloat16)
        own_grad[n] = score_grad
        return score_grad, prob.astype(jnp.bfloat16)

    def store(g, key_part, value_part):
        own_part[0, g] = key_part * width ** (-0.5)
        own_part[1, g] = value_part

    accumulate = accumulator(query_head, grad_head, chunks, groups, store)
    pipelined(chunks, differentiate, accumulate)


def join_one_kernel(one_part, one_other, joined):
    groups, tokens = one_part.shape[1:3]
    length = tokens // 2
    joined[:, my_heads(groups)] = one_part[:, :, pl.ds(0, length)]
    joined[:, other_heads(groups)] = one_other[:, :, pl.ds(length, length)]


def query_kernel(
    own, back_one, back_two, two_keys, attended_rows, two_grad, one_grad, own_grad,
    out_mine, query_mine, first_third, second_third, last_third, query_send,
):
    sends = (first_third, second_third, last_third)
    groups = own.shape[1]
    chunks = own_grad.shape[0]
    heads, length, width = out_mine.shape
    count = heads // chunks
    for n in range(chunks):
        g = n * groups // chunks
        rows = pl.ds(n * count, count)
        keys = join(two_back(back_two, (two_keys,), 0, g), back_one[0, g], own[0, g])
        part = matmul(keys, join(two_grad[n], one_grad[n], own_grad[n]), (0, 0))
        part = (part * width ** (-0.5)).astype(jnp.bfloat16)
        for index, (columns, mine) in enumerate(((attended_rows[n], out_mine), (part, query_mine))):
            block = columns.T.reshape(count, 2 * length, width)
            mine[rows] = block[:, :length]
            query_send[index, rows] = block[:, length:]
    for index, row, piece, taken in placed(sends, heads):
        piece[...] = query_send[index, pl.ds(row, taken)]


def assemble_kernel(
    out_mine, query_mine, first_third, second_third, last_third, out, query_grad, token
):
    heads = out_mine.shape[0]
    start = (1 - lax.axis_index("head")) * heads
    out[my_heads(heads)] = out_mine[...]
    query_grad[my_heads(heads)] = query_mine[...]
    for index, row, piece, count in placed((first_third, second_third, last_third), heads):
        (out, query_grad)[index][pl.ds(start + row, count)] = piece[...]
    token[...] = jnp.zeros(token.shape, token.dtype)


def own_sum_kernel(own_part, two_total, sum_mine, sum_send):
    length = sum_mine.shape[2]
    total = own_part[...] + two_total[...].astype(jnp.float32)
    sum_mine[...] = total[:, :, :length]
    sum_send[...] = total[:, :, length:].astype(jnp.bfloat16)


def final_kernel(sum_mine, sum_other, one_total, after, key_grad, value_grad):
    groups = sum_mine.shape[1]
    mine, other = my_heads(groups), other_heads(groups)
    for index, result in enumerate((key_grad, value_grad)):
        total = sum_mine[index] + one_total[index, mine].astype(jnp.float32)
        result[mine] = total.astype(jnp.bfloat16)
        total = sum_other[index].astype(jnp.float32) + one_total[index, other].astype(jnp.float32)
        result[other] = total.astype(jnp.bfloat16)


def shards(query_matrix, key_matrix, value_matrix, output_gradient, query_head_spans, slab_offset):
    groups, length, width = key_matrix.shape
    heads = query_matrix.shape[0]
    cores = lax.axis_size("head")
    tokens = cores * length
    groups_here, heads_here = groups // cores, heads // cores
    count = max(1, min(heads // groups, 256 // tokens))
    chunks = heads_here // count
    lanes = count * tokens
    half, full = jnp.bfloat16, jnp.float32
    vmem = pl.BlockSpec(memory_space=pltpu.VMEM)
    smem = pl.BlockSpec(memory_space=pltpu.SMEM)

    def call(kernel, name, outs, arrays, scalars=0, scratch=()):
        return pl.pallas_call(
            kernel,
            out_shape=tuple(jax.ShapeDtypeStruct(shape, kind) for shape, kind in outs),
            in_specs=[smem] * scalars + [vmem] * (len(arrays) - scalars),
            out_specs=(vmem,) * len(outs),
            scratch_shapes=scratch,
            compiler_params=pltpu.CompilerParams(vmem_limit_bytes=40 * 1024 * 1024),
            cost_estimate=pl.CostEstimate(flops=1, bytes_accessed=0, transcendentals=0),
            name=name,
        )(*arrays)

    def rows_of(rows, kind):
        return ((chunks, rows, lanes), kind)

    stat = rows_of(1, full)
    whole_pair = ((2, groups, length, width), half)
    half_block = ((groups_here, length, width), half)
    half_pair = ((2, groups_here, length, width), half)
    chip_pair = ((2, groups_here, tokens, width), half)
    half_rows = ((heads_here, length, width), half)
    third_rows = [((rows, length, width), half) for rows in thirds(heads_here)]
    chip_rows = ((heads_here, tokens, width), half)

    own = jnp.stack([key_matrix, value_matrix])
    back_two = shifted(own, "seq", 2)
    own_sends = call(split_kernel, "split_own", [half_block] * 2, (own,))
    (own_head,) = call(
        join_own_kernel, "join_own", [chip_pair], (own, *[swapped(send, "head") for send in own_sends])
    )
    back_one = shifted(own_head, "seq", 1, ring=False)
    sends = call(
        split_rows_kernel,
        "split_rows",
        third_rows,
        (query_matrix, output_gradient, own),
    )
    (
        query_head, grad_head, grad_rows, first, own_max, own_total, own_out, own_weights,
        own_prob_grad,
    ) = call(
        own_kernel,
        "own_block",
        [
            chip_rows, chip_rows, rows_of(width, half), rows_of(1, jnp.int32), stat, stat,
            rows_of(width, full), rows_of(tokens, full), rows_of(tokens, full),
        ],
        (
            query_head_spans, slab_offset, query_matrix, output_gradient,
            *[swapped(send, "head") for send in sends], own_head,
        ),
        scalars=2,
    )
    back_two, first = lax.optimization_barrier((back_two, first))
    two_sends = call(split_kernel, "split_two", [half_block] * 2, (back_two,))
    two_other = [swapped(send, "head") for send in two_sends]
    near_max, near_total, near_out, near_weights, near_prob_grad, own_factor = call(
        near_forward_kernel,
        "near_forward",
        [stat, stat, rows_of(width, full), rows_of(tokens, full), rows_of(tokens, full), stat],
        (first, query_head, grad_head, back_two, *two_other, own_max, own_total, own_out),
    )
    back_one, near_max = lax.optimization_barrier((back_one, near_max))
    attended_rows, row_delta, near_factor, one_grad, one_part = call(
        last_kernel,
        "last_forward_backward",
        [rows_of(width, half), stat, stat, rows_of(tokens, half), chip_pair],
        (first, query_head, grad_head, back_one, grad_rows, near_max, near_total, near_out),
    )
    one_other = swapped(one_part, "head")
    two_grad, two_part = call(
        two_backward_kernel,
        "two_backward",
        [rows_of(tokens, half), chip_pair],
        (query_head, grad_head, near_weights, near_prob_grad, near_factor, row_delta),
    )
    two_total = shifted(two_part, "seq", -2)
    (joined,) = call(join_one_kernel, "join_one", [whole_pair], (one_part, one_other))
    one_total = shifted(joined, "seq", -1)
    own_grad, own_part = call(
        own_backward_kernel,
        "own_backward",
        [rows_of(tokens, half), (chip_pair[0], full)],
        (
            query_head, grad_head, own_weights, own_prob_grad, near_factor, own_factor, row_delta,
            joined,
        ),
    )
    out_mine, query_mine, *sends = call(
        query_kernel,
        "query_grad",
        [half_rows] * 2 + third_rows,
        (own_head, back_one, back_two, two_other[0], attended_rows, two_grad, one_grad, own_grad),
        scratch=[pltpu.VMEM((2,) + half_rows[0], half)],
    )
    attn_out, query_grad, token = call(
        assemble_kernel,
        "assemble",
        [(query_matrix.shape, half)] * 2 + [((8, 128), full)],
        (out_mine, query_mine, *[swapped(send, "head") for send in sends]),
    )
    sum_mine, sum_send = call(
        own_sum_kernel, "own_sum", [(half_pair[0], full), half_pair], (own_part, two_total)
    )
    key_grad, value_grad = call(
        final_kernel,
        "total",
        [(key_matrix.shape, half)] * 2,
        (sum_mine, swapped(sum_send, "head"), one_total, token),
    )
    return (attn_out, query_grad, key_grad, value_grad)


def solution(mesh):
    tokens = P(None, ("seq", "head"), None)
    return jax.shard_map(
        shards,
        mesh=mesh,
        in_specs=(tokens, tokens, tokens, tokens, P(), P()),
        out_specs=(tokens, tokens, tokens, tokens),
        check_vma=False,
    )
```

```python
import functools
import math

import jax
import jax.numpy as jnp
from jax import lax
from jax.experimental import pallas as pl
from jax.experimental.pallas import tpu as pltpu
from jax.sharding import PartitionSpec as P

REACH = 2
SEGMENT = 512

masked_score = -1e30


def shifted(block, axis, distance, ring=True):
    count = lax.axis_size(axis)
    route = [(i, (i + distance) % count) for i in range(count) if ring or i + distance < count]
    return lax.ppermute(block, axis, route)


def swapped(block, axis):
    count = lax.axis_size(axis)
    return lax.ppermute(block, axis, [(i, count - 1 - i) for i in range(count)])


def matmul(left, right, contract):
    return lax.dot_general(
        left, right, ((contract[:1], contract[1:]), ((), ())), preferred_element_type=jnp.float32
    )


def grouped(ref, n, count):
    _, length, width = ref.shape
    return ref[pl.ds(n * count, count)].reshape(count * length, width)


def join(*blocks):
    return jnp.concatenate(blocks, axis=0)


def core_offsets(length):
    core = lax.axis_index("head")
    return core * length, (1 - core) * length


def my_heads(count):
    return pl.ds(lax.axis_index("head") * count, count)


def other_heads(count):
    return pl.ds((1 - lax.axis_index("head")) * count, count)


def lane_tokens(count, length):
    lane = lax.broadcasted_iota(jnp.int32, (1, count * 2 * length), 1)
    token = lane - lane // (2 * length) * (2 * length)
    mine, other = core_offsets(length)
    return jnp.where(token < length, token + mine, token - length + other)


def first_visible(spans, offset, chunks, count, length):
    token = lane_tokens(count, length)
    lane_head = lax.broadcasted_iota(jnp.int32, token.shape, 1) // (2 * length)
    start = lax.axis_index("seq") * 2 * length
    segment_start = token - lax.bitwise_and(offset[0] + start + token, SEGMENT - 1)
    floor = jnp.maximum(segment_start, -start)
    base = lax.axis_index("head") * chunks * count
    result = []
    for n in range(chunks):
        span = jnp.full(token.shape, spans[base + n * count], jnp.int32)
        for a in range(1, count):
            span = jnp.where(lane_head == a, spans[base + n * count + a], span)
        result.append(jnp.maximum(floor, token - span + 1))
    return result


def masked(scores, first, chips_back, token=None):
    length = scores.shape[0] // 2
    row = lax.broadcasted_iota(jnp.int32, (length, scores.shape[1]), 0)
    pieces = []
    for part, offset in enumerate(core_offsets(length)):
        visible = row >= first + (chips_back * 2 * length - offset)
        if token is not None:
            visible &= row <= token - offset
        pieces.append(
            jnp.where(visible, scores[part * length : (part + 1) * length], masked_score)
        )
    return join(*pieces)


def split_kernel(block, *sends):
    for index, send in enumerate(sends):
        send[...] = block[index, other_heads(send.shape[0])]


def thirds(rows):
    return [2 * rows * (i + 1) // 3 - 2 * rows * i // 3 for i in range(3)]


def placed(pieces, rows):
    taken = 0
    for piece in pieces:
        count = piece.shape[0]
        for index in range(2):
            low = max(taken, index * rows)
            high = min(taken + count, (index + 1) * rows)
            if low < high:
                yield index, low - index * rows, piece.at[pl.ds(low - taken, high - low)], high - low
        taken += count


def split_rows_kernel(queries, grads, after, *sends):
    heads = queries.shape[0] // 2
    start = (1 - lax.axis_index("head")) * heads
    for index, row, piece, count in placed(sends, heads):
        piece[...] = (queries, grads)[index][pl.ds(start + row, count)]


def join_own_kernel(own, other_keys, other_values, own_head):
    groups, length = other_keys.shape[:2]
    own_head[:, :, pl.ds(0, length)] = own[:, my_heads(groups)]
    own_head[0, :, pl.ds(length, length)] = other_keys[...]
    own_head[1, :, pl.ds(length, length)] = other_values[...]


def own_kernel(
    spans, offset, queries, grads, first_third, second_third, last_third, own,
    query_head, grad_head, grad_rows, first, own_max, own_total, own_out, own_weights,
    own_prob_grad,
):
    heads, _, width = query_head.shape
    length = queries.shape[1]
    groups = own.shape[1]
    chunks = first.shape[0]
    count = heads // chunks
    query_head[:, pl.ds(0, length)] = queries[my_heads(heads)]
    grad_head[:, pl.ds(0, length)] = grads[my_heads(heads)]
    for index, row, piece, rows in placed((first_third, second_third, last_third), heads):
        (query_head, grad_head)[index][pl.ds(row, rows), pl.ds(length, length)] = piece[...]
    factor = width ** (-0.5) * math.log2(math.e)
    token = lane_tokens(count, length)
    for n, rows in enumerate(first_visible(spans, offset, chunks, count, length)):
        first[n] = rows

    def products(n):
        g = n * groups // chunks
        own_prob_grad[n] = matmul(own[1, g], grouped(grad_head, n, count), (1, 1))
        return (matmul(own[0, g], grouped(query_head, n, count), (1, 1)),)

    def softmax(n, scores):
        scores = masked(scores * factor, first[n], 0, token)
        row_max = jnp.max(scores, axis=0, keepdims=True)
        weights = jnp.exp2(scores - row_max)
        own_max[n] = row_max
        own_total[n] = jnp.sum(weights, axis=0, keepdims=True)
        own_weights[n] = weights
        return (weights.astype(jnp.bfloat16),)

    def weigh(n, halves):
        own_out[n] = matmul(own[1, n * groups // chunks], halves, (0, 0))
        grad_rows[n] = grouped(grad_head, n, count).T

    pipelined(chunks, products, softmax, weigh)


def two_back(back_two, two_other, index, g):
    base = lax.axis_index("head") * two_other[index].shape[0]
    return join(back_two[index, base + g], two_other[index][g])


def near_forward_kernel(
    first, query_head, grad_head, back_two, two_keys, two_values, own_max, own_total, own_out,
    near_max, near_total, near_out, near_weights, near_prob_grad, own_factor,
):
    groups = two_keys.shape[0]
    two_other = (two_keys, two_values)
    chunks = first.shape[0]
    heads, _, width = query_head.shape
    count = heads // chunks
    factor = width ** (-0.5) * math.log2(math.e)

    def products(n):
        g = n * groups // chunks
        keys = two_back(back_two, two_other, 0, g)
        values = two_back(back_two, two_other, 1, g)
        near_prob_grad[n] = matmul(values, grouped(grad_head, n, count), (1, 1))
        return (matmul(keys, grouped(query_head, n, count), (1, 1)),)

    def softmax(n, scores):
        scores = masked(scores * factor, first[n], 2)
        row_max = jnp.maximum(own_max[n], jnp.max(scores, axis=0, keepdims=True))
        weights = jnp.exp2(scores - row_max)
        rescale = jnp.exp2(own_max[n] - row_max)
        own_factor[n] = rescale
        near_max[n] = row_max
        near_total[n] = own_total[n] * rescale + jnp.sum(weights, axis=0, keepdims=True)
        near_weights[n] = weights
        return rescale, weights.astype(jnp.bfloat16)

    def weigh(n, rescale, halves):
        values = two_back(back_two, two_other, 1, n * groups // chunks)
        near_out[n] = own_out[n] * rescale + matmul(values, halves, (0, 0))

    pipelined(chunks, products, softmax, weigh)


def last_kernel(
    base, first, query_head, grad_head, back_one, grad_rows, near_max, near_total, near_out, after,
    attended_rows, row_delta, near_factor, one_grad, one_part,
):
    groups = one_part.shape[1]
    g_base = base * back_one.shape[1] // first.shape[0]
    chunks = row_delta.shape[0]
    heads, _, width = query_head.shape
    count = heads // first.shape[0]
    scale = width ** (-0.5)

    def products(n):
        g = n * groups // chunks
        scores = matmul(back_one[0, g_base + g], grouped(query_head, base + n, count), (1, 1))
        prob_grad = matmul(back_one[1, g_base + g], grouped(grad_head, base + n, count), (1, 1))
        return scores, prob_grad

    def softmax(n, scores, prob_grad):
        scores = masked(scores * (scale * math.log2(math.e)), first[base + n], 1)
        row_max = jnp.maximum(near_max[base + n], jnp.max(scores, axis=0, keepdims=True))
        weights = jnp.exp2(scores - row_max)
        rescale = jnp.exp2(near_max[base + n] - row_max)
        inverse = 1.0 / (near_total[base + n] * rescale + jnp.sum(weights, axis=0, keepdims=True))
        weighted = matmul(
            back_one[1, g_base + n * groups // chunks], weights.astype(jnp.bfloat16), (0, 0)
        )
        near_factor[n] = rescale * inverse
        return prob_grad, weights, weighted, rescale, inverse

    def differentiate(n, prob_grad, weights, weighted, rescale, inverse):
        attended = ((near_out[base + n] * rescale + weighted) * inverse).astype(jnp.bfloat16)
        delta = jnp.sum(
            grad_rows[base + n].astype(jnp.float32) * attended.astype(jnp.float32), axis=0, keepdims=True
        )
        prob = weights * inverse
        score_grad = (prob * (prob_grad - delta)).astype(jnp.bfloat16)
        attended_rows[n] = attended
        row_delta[n] = delta
        one_grad[n] = score_grad
        return score_grad, prob.astype(jnp.bfloat16)

    def store(g, key_part, value_part):
        one_part[0, g] = (key_part * scale).astype(jnp.bfloat16)
        one_part[1, g] = value_part.astype(jnp.bfloat16)

    accumulate = accumulator(query_head, grad_head, base, count, chunks, groups, store)
    pipelined(chunks, products, softmax, differentiate, accumulate)


def pipelined(chunks, *stages):
    ready = [{} for _ in range(len(stages) + 1)]
    for step in range(chunks + len(stages) - 1):
        for depth, stage in enumerate(stages):
            n = step - depth
            if 0 <= n < chunks:
                ready[depth + 1][n] = stage(n, *ready[depth].pop(n, ())) or ()


def accumulator(query_head, grad_head, base, count, chunks, groups, store):
    parts = {}

    def accumulate(n, score_grad, half):
        g = n * groups // chunks
        key_part = matmul(score_grad, grouped(query_head, base + n, count), (1, 0))
        value_part = matmul(half, grouped(grad_head, base + n, count), (1, 0))
        if g in parts:
            key_part, value_part = parts[g][0] + key_part, parts[g][1] + value_part
        parts[g] = (key_part, value_part)
        if (n + 1) * groups // chunks != g:
            store(g, key_part, value_part)

    return accumulate


def of_half(n, first, second):
    each = first.shape[0]
    return first[n] if n < each else second[n - each]


def two_backward_kernel(
    query_head, grad_head, near_weights, near_prob_grad, factor_a, delta_a, factor_b, delta_b,
    two_grad, two_mine, send_keys, send_values,
):
    chunks = near_weights.shape[0]
    groups, length, width = two_mine.shape[1:]

    def differentiate(n):
        prob = near_weights[n] * of_half(n, factor_a, factor_b)
        score_grad = prob * (near_prob_grad[n] - of_half(n, delta_a, delta_b))
        score_grad = score_grad.astype(jnp.bfloat16)
        two_grad[n] = score_grad
        return score_grad, prob.astype(jnp.bfloat16)

    def store(g, key_part, value_part):
        for index, (part, send) in enumerate(
            ((key_part * width ** (-0.5), send_keys), (value_part, send_values))
        ):
            two_mine[index, g] = part[:length].astype(jnp.bfloat16)
            send[g] = part[length:].astype(jnp.bfloat16)

    accumulate = accumulator(query_head, grad_head, 0, query_head.shape[0] // chunks, chunks, groups, store)
    pipelined(chunks, differentiate, accumulate)


def own_backward_kernel(
    query_head, grad_head, own_weights, own_prob_grad, own_factor, factor_a, delta_a, factor_b,
    delta_b, after, own_grad, own_part,
):
    chunks = own_weights.shape[0]
    groups, _, width = own_part.shape[1:]

    def differentiate(n):
        prob = own_weights[n] * (own_factor[n] * of_half(n, factor_a, factor_b))
        score_grad = prob * (own_prob_grad[n] - of_half(n, delta_a, delta_b))
        score_grad = score_grad.astype(jnp.bfloat16)
        own_grad[n] = score_grad
        return score_grad, prob.astype(jnp.bfloat16)

    def store(g, key_part, value_part):
        own_part[0, g] = key_part * width ** (-0.5)
        own_part[1, g] = value_part

    accumulate = accumulator(query_head, grad_head, 0, query_head.shape[0] // chunks, chunks, groups, store)
    pipelined(chunks, differentiate, accumulate)


def join_two_kernel(two_mine, other_keys, other_values, two_part):
    groups = two_mine.shape[1]
    two_part[:, my_heads(groups)] = two_mine[...]
    two_part[0, other_heads(groups)] = other_keys[...]
    two_part[1, other_heads(groups)] = other_values[...]


def query_kernel(
    own, back_one, back_two, two_keys, rows_a, rows_b, two_grad, grad_a, grad_b, own_grad, after,
    out_mine, query_mine, first_third, second_third, last_third, query_send,
):
    sends = (first_third, second_third, last_third)
    groups = own.shape[1]
    chunks = own_grad.shape[0]
    heads, length, width = out_mine.shape
    count = heads // chunks
    for n in range(chunks):
        g = n * groups // chunks
        rows = pl.ds(n * count, count)
        keys = join(two_back(back_two, (two_keys,), 0, g), back_one[0, g], own[0, g])
        part = matmul(keys, join(two_grad[n], of_half(n, grad_a, grad_b), own_grad[n]), (0, 0))
        part = (part * width ** (-0.5)).astype(jnp.bfloat16)
        for index, (columns, mine) in enumerate(
            ((of_half(n, rows_a, rows_b), out_mine), (part, query_mine))
        ):
            block = columns.T.reshape(count, 2 * length, width)
            mine[rows] = block[:, :length]
            query_send[index, rows] = block[:, length:]
    for index, row, piece, taken in placed(sends, heads):
        piece[...] = query_send[index, pl.ds(row, taken)]


def assemble_kernel(
    out_mine, query_mine, first_third, second_third, last_third, out, query_grad, token
):
    heads = out_mine.shape[0]
    start = (1 - lax.axis_index("head")) * heads
    out[my_heads(heads)] = out_mine[...]
    query_grad[my_heads(heads)] = query_mine[...]
    for index, row, piece, count in placed((first_third, second_third, last_third), heads):
        (out, query_grad)[index][pl.ds(start + row, count)] = piece[...]
    token[...] = jnp.zeros(token.shape, token.dtype)


def first_sum_kernel(own_part, one_total, total, token):
    total[...] = own_part[:, pl.ds(0, one_total.shape[1])] + one_total[...].astype(jnp.float32)
    token[...] = jnp.zeros(token.shape, token.dtype)


def own_sum_kernel(own_part, first_sum, one_total, sum_mine, sum_send):
    length, part = sum_mine.shape[2], first_sum.shape[1]
    second = own_part[:, pl.ds(part, part)] + one_total[...].astype(jnp.float32)
    for index, total in enumerate((first_sum[...], second)):
        groups = pl.ds(index * part, part)
        sum_mine[:, groups] = total[:, :, :length]
        sum_send[:, groups] = total[:, :, length:].astype(jnp.bfloat16)


def final_kernel(sum_mine, sum_other, two_total, after, key_grad, value_grad):
    groups = sum_mine.shape[1]
    mine, other = my_heads(groups), other_heads(groups)
    for index, result in enumerate((key_grad, value_grad)):
        total = sum_mine[index] + two_total[index, mine].astype(jnp.float32)
        result[mine] = total.astype(jnp.bfloat16)
        total = sum_other[index].astype(jnp.float32) + two_total[index, other].astype(jnp.float32)
        result[other] = total.astype(jnp.bfloat16)


def shards(query_matrix, key_matrix, value_matrix, output_gradient, query_head_spans, slab_offset):
    groups, length, width = key_matrix.shape
    heads = query_matrix.shape[0]
    cores = lax.axis_size("head")
    tokens = cores * length
    groups_here, heads_here = groups // cores, heads // cores
    count = max(1, min(heads // groups, 256 // tokens))
    chunks = heads_here // count
    lanes = count * tokens
    half, full = jnp.bfloat16, jnp.float32
    vmem = pl.BlockSpec(memory_space=pltpu.VMEM)
    smem = pl.BlockSpec(memory_space=pltpu.SMEM)

    def call(kernel, name, outs, arrays, scalars=0, scratch=(), flops=1):
        return pl.pallas_call(
            kernel,
            out_shape=tuple(jax.ShapeDtypeStruct(shape, kind) for shape, kind in outs),
            in_specs=[smem] * scalars + [vmem] * (len(arrays) - scalars),
            out_specs=(vmem,) * len(outs),
            scratch_shapes=scratch,
            compiler_params=pltpu.CompilerParams(vmem_limit_bytes=40 * 1024 * 1024),
            cost_estimate=pl.CostEstimate(flops=flops, bytes_accessed=0, transcendentals=0),
            name=name,
        )(*arrays)

    def rows_of(rows, kind):
        return ((chunks, rows, lanes), kind)

    stat = rows_of(1, full)
    whole_pair = ((2, groups, length, width), half)
    half_block = ((groups_here, length, width), half)
    half_pair = ((2, groups_here, length, width), half)
    chip_pair = ((2, groups_here, tokens, width), half)
    half_rows = ((heads_here, length, width), half)
    third_rows = [((rows, length, width), half) for rows in thirds(heads_here)]
    chip_rows = ((heads_here, tokens, width), half)
    part, each = groups_here // 2, chunks // 2
    chip_half = ((2, part, tokens, width), half)
    half_stat = ((each, 1, lanes), full)

    own = jnp.stack([key_matrix, value_matrix])
    back_two = shifted(own, "seq", 2)
    own_sends = call(split_kernel, "split_own", [half_block] * 2, (own,))
    (own_head,) = call(
        join_own_kernel, "join_own", [chip_pair], (own, *[swapped(send, "head") for send in own_sends])
    )
    back_one = shifted(own_head, "seq", 1, ring=False)
    sends = call(
        split_rows_kernel,
        "split_rows",
        third_rows,
        (query_matrix, output_gradient, own),
    )
    (
        query_head, grad_head, grad_rows, first, own_max, own_total, own_out, own_weights,
        own_prob_grad,
    ) = call(
        own_kernel,
        "own_block",
        [
            chip_rows, chip_rows, rows_of(width, half), rows_of(1, jnp.int32), stat, stat,
            rows_of(width, full), rows_of(tokens, full), rows_of(tokens, full),
        ],
        (
            query_head_spans, slab_offset, query_matrix, output_gradient,
            *[swapped(send, "head") for send in sends], own_head,
        ),
        scalars=2,
    )
    back_two, first = lax.optimization_barrier((back_two, first))
    two_sends = call(split_kernel, "split_two", [half_block] * 2, (back_two,))
    two_other = [swapped(send, "head") for send in two_sends]
    near_max, near_total, near_out, near_weights, near_prob_grad, own_factor = call(
        near_forward_kernel,
        "near_forward",
        [stat, stat, rows_of(width, full), rows_of(tokens, full), rows_of(tokens, full), stat],
        (first, query_head, grad_head, back_two, *two_other, own_max, own_total, own_out),
    )
    back_one, near_max = lax.optimization_barrier((back_one, near_max))
    after = near_max
    halves = []
    for index in range(2):
        rows, delta, factor, one_grad, one_part = call(
            functools.partial(last_kernel, index * each),
            "last_" + "ab"[index],
            [
                ((each, width, lanes), half), half_stat, half_stat, ((each, tokens, lanes), half),
                chip_half,
            ],
            (
                first, query_head, grad_head, back_one, grad_rows, near_max, near_total, near_out,
                after,
            ),
        )
        halves.append((factor, delta, rows, one_grad, shifted(one_part, "seq", -1)))
        after = delta
    stats = (*halves[0][:2], *halves[1][:2])
    two_grad, part_mine, *part_sends = call(
        two_backward_kernel,
        "two_backward",
        [rows_of(tokens, half), half_pair, half_block, half_block],
        (query_head, grad_head, near_weights, near_prob_grad, *stats),
    )
    (two_part,) = call(
        join_two_kernel,
        "join_two",
        [whole_pair],
        (part_mine, *[swapped(send, "head") for send in part_sends]),
    )
    two_total = shifted(two_part, "seq", -2)
    own_grad, own_part = call(
        own_backward_kernel,
        "own_backward",
        [rows_of(tokens, half), (chip_pair[0], full)],
        (
            query_head, grad_head, own_weights, own_prob_grad, own_factor, *stats, two_part,
        ),
    )
    first_sum, sum_token = call(
        first_sum_kernel,
        "sum_a",
        [(chip_half[0], full), ((8, 128), full)],
        (own_part, halves[0][4]),
        flops=5 * 10**8,
    )
    out_mine, query_mine, *sends = call(
        query_kernel,
        "query_grad",
        [half_rows] * 2 + third_rows,
        (
            own_head, back_one, back_two, two_other[0], halves[0][2], halves[1][2], two_grad,
            halves[0][3], halves[1][3], own_grad, sum_token,
        ),
        scratch=[pltpu.VMEM((2,) + half_rows[0], half)],
    )
    attn_out, query_grad, token = call(
        assemble_kernel,
        "assemble",
        [(query_matrix.shape, half)] * 2 + [((8, 128), full)],
        (out_mine, query_mine, *[swapped(send, "head") for send in sends]),
    )
    sum_mine, sum_send = call(
        own_sum_kernel, "own_sum", [(half_pair[0], full), half_pair], (own_part, first_sum, halves[1][4])
    )
    key_grad, value_grad = call(
        final_kernel,
        "total",
        [(key_matrix.shape, half)] * 2,
        (sum_mine, swapped(sum_send, "head"), two_total, token),
    )
    return (attn_out, query_grad, key_grad, value_grad)


def solution(mesh):
    tokens = P(None, ("seq", "head"), None)
    return jax.shard_map(
        shards,
        mesh=mesh,
        in_specs=(tokens, tokens, tokens, tokens, P(), P()),
        out_specs=(tokens, tokens, tokens, tokens),
        check_vma=False,
    )
```

```python
import math

import jax
import jax.numpy as jnp
from jax import lax
from jax.experimental import pallas as pl
from jax.experimental.pallas import tpu as pltpu
from jax.sharding import PartitionSpec as P

REACH = 2
SEGMENT = 512

masked_score = -1e30


def shifted(block, axis, distance, ring=True):
    count = lax.axis_size(axis)
    route = [(i, (i + distance) % count) for i in range(count) if ring or i + distance < count]
    return lax.ppermute(block, axis, route)


def swapped(block, axis):
    count = lax.axis_size(axis)
    return lax.ppermute(block, axis, [(i, count - 1 - i) for i in range(count)])


def matmul(left, right, contract):
    return lax.dot_general(
        left, right, ((contract[:1], contract[1:]), ((), ())), preferred_element_type=jnp.float32
    )


def grouped(ref, n, count):
    _, length, width = ref.shape
    return ref[pl.ds(n * count, count)].reshape(count * length, width)


def join(*blocks):
    return jnp.concatenate(blocks, axis=0)


def core_offsets(length):
    core = lax.axis_index("head")
    return core * length, (1 - core) * length


def my_heads(count):
    return pl.ds(lax.axis_index("head") * count, count)


def other_heads(count):
    return pl.ds((1 - lax.axis_index("head")) * count, count)


def lane_tokens(count, length):
    lane = lax.broadcasted_iota(jnp.int32, (1, count * 2 * length), 1)
    token = lane - lane // (2 * length) * (2 * length)
    mine, other = core_offsets(length)
    return jnp.where(token < length, token + mine, token - length + other)


def first_visible(spans, offset, chunks, count, length):
    token = lane_tokens(count, length)
    lane_head = lax.broadcasted_iota(jnp.int32, token.shape, 1) // (2 * length)
    start = lax.axis_index("seq") * 2 * length
    segment_start = token - lax.bitwise_and(offset[0] + start + token, SEGMENT - 1)
    floor = jnp.maximum(segment_start, -start)
    base = lax.axis_index("head") * chunks * count
    result = []
    for n in range(chunks):
        span = jnp.full(token.shape, spans[base + n * count], jnp.int32)
        for a in range(1, count):
            span = jnp.where(lane_head == a, spans[base + n * count + a], span)
        result.append(jnp.maximum(floor, token - span + 1))
    return result


def masked(scores, first, chips_back, token=None):
    length = scores.shape[0] // 2
    row = lax.broadcasted_iota(jnp.int32, (length, scores.shape[1]), 0)
    pieces = []
    for part, offset in enumerate(core_offsets(length)):
        visible = row >= first + (chips_back * 2 * length - offset)
        if token is not None:
            visible &= row <= token - offset
        pieces.append(
            jnp.where(visible, scores[part * length : (part + 1) * length], masked_score)
        )
    return join(*pieces)


def split_kernel(block, *sends):
    for index, send in enumerate(sends):
        send[...] = block[index, other_heads(send.shape[0])]


def thirds(rows):
    return [2 * rows * (i + 1) // 3 - 2 * rows * i // 3 for i in range(3)]


def placed(pieces, rows):
    taken = 0
    for piece in pieces:
        count = piece.shape[0]
        for index in range(2):
            low = max(taken, index * rows)
            high = min(taken + count, (index + 1) * rows)
            if low < high:
                yield index, low - index * rows, piece.at[pl.ds(low - taken, high - low)], high - low
        taken += count


def split_rows_kernel(queries, grads, after, *sends):
    heads = queries.shape[0] // 2
    start = (1 - lax.axis_index("head")) * heads
    for index, row, piece, count in placed(sends, heads):
        piece[...] = (queries, grads)[index][pl.ds(start + row, count)]


def join_own_kernel(own, other_keys, other_values, own_head):
    groups, length = other_keys.shape[:2]
    own_head[:, :, pl.ds(0, length)] = own[:, my_heads(groups)]
    own_head[0, :, pl.ds(length, length)] = other_keys[...]
    own_head[1, :, pl.ds(length, length)] = other_values[...]


def own_kernel(
    spans, offset, queries, grads, first_third, second_third, last_third, own,
    query_head, grad_head, grad_rows, first, own_max, own_total, own_out, own_weights,
    own_prob_grad,
):
    heads, _, width = query_head.shape
    length = queries.shape[1]
    groups = own.shape[1]
    chunks = first.shape[0]
    count = heads // chunks
    query_head[:, pl.ds(0, length)] = queries[my_heads(heads)]
    grad_head[:, pl.ds(0, length)] = grads[my_heads(heads)]
    for index, row, piece, rows in placed((first_third, second_third, last_third), heads):
        (query_head, grad_head)[index][pl.ds(row, rows), pl.ds(length, length)] = piece[...]
    factor = width ** (-0.5) * math.log2(math.e)
    token = lane_tokens(count, length)
    for n, rows in enumerate(first_visible(spans, offset, chunks, count, length)):
        first[n] = rows

    def products(n):
        g = n * groups // chunks
        own_prob_grad[n] = matmul(own[1, g], grouped(grad_head, n, count), (1, 1))
        return (matmul(own[0, g], grouped(query_head, n, count), (1, 1)),)

    def softmax(n, scores):
        scores = masked(scores * factor, first[n], 0, token)
        row_max = jnp.max(scores, axis=0, keepdims=True)
        weights = jnp.exp2(scores - row_max)
        own_max[n] = row_max
        own_total[n] = jnp.sum(weights, axis=0, keepdims=True)
        own_weights[n] = weights
        return (weights.astype(jnp.bfloat16),)

    def weigh(n, halves):
        own_out[n] = matmul(own[1, n * groups // chunks], halves, (0, 0))
        grad_rows[n] = grouped(grad_head, n, count).T

    pipelined(chunks, products, softmax, weigh)


def two_back(back_two, two_other, index, g):
    base = lax.axis_index("head") * two_other[index].shape[0]
    return join(back_two[index, base + g], two_other[index][g])


def near_forward_kernel(
    first, query_head, grad_head, back_two, two_keys, two_values, own_max, own_total, own_out,
    near_max, near_total, near_out, near_weights, near_prob_grad, own_factor,
):
    groups = two_keys.shape[0]
    two_other = (two_keys, two_values)
    chunks = first.shape[0]
    heads, _, width = query_head.shape
    count = heads // chunks
    factor = width ** (-0.5) * math.log2(math.e)

    def products(n):
        g = n * groups // chunks
        keys = two_back(back_two, two_other, 0, g)
        values = two_back(back_two, two_other, 1, g)
        near_prob_grad[n] = matmul(values, grouped(grad_head, n, count), (1, 1))
        return (matmul(keys, grouped(query_head, n, count), (1, 1)),)

    def softmax(n, scores):
        scores = masked(scores * factor, first[n], 2)
        row_max = jnp.maximum(own_max[n], jnp.max(scores, axis=0, keepdims=True))
        weights = jnp.exp2(scores - row_max)
        rescale = jnp.exp2(own_max[n] - row_max)
        own_factor[n] = rescale
        near_max[n] = row_max
        near_total[n] = own_total[n] * rescale + jnp.sum(weights, axis=0, keepdims=True)
        near_weights[n] = weights
        return rescale, weights.astype(jnp.bfloat16)

    def weigh(n, rescale, halves):
        values = two_back(back_two, two_other, 1, n * groups // chunks)
        near_out[n] = own_out[n] * rescale + matmul(values, halves, (0, 0))

    pipelined(chunks, products, softmax, weigh)


def last_kernel(
    first, query_head, grad_head, back_one, grad_rows, near_max, near_total, near_out,
    attended_rows, row_delta, near_factor, one_grad, one_part,
):
    groups = back_one.shape[1]
    chunks = first.shape[0]
    heads, _, width = query_head.shape
    count = heads // chunks
    scale = width ** (-0.5)

    def products(n):
        g = n * groups // chunks
        scores = matmul(back_one[0, g], grouped(query_head, n, count), (1, 1))
        prob_grad = matmul(back_one[1, g], grouped(grad_head, n, count), (1, 1))
        return scores, prob_grad

    def softmax(n, scores, prob_grad):
        scores = masked(scores * (scale * math.log2(math.e)), first[n], 1)
        row_max = jnp.maximum(near_max[n], jnp.max(scores, axis=0, keepdims=True))
        weights = jnp.exp2(scores - row_max)
        rescale = jnp.exp2(near_max[n] - row_max)
        inverse = 1.0 / (near_total[n] * rescale + jnp.sum(weights, axis=0, keepdims=True))
        weighted = matmul(
            back_one[1, n * groups // chunks], weights.astype(jnp.bfloat16), (0, 0)
        )
        near_factor[n] = rescale * inverse
        return prob_grad, weights, weighted, rescale, inverse

    def differentiate(n, prob_grad, weights, weighted, rescale, inverse):
        attended = ((near_out[n] * rescale + weighted) * inverse).astype(jnp.bfloat16)
        delta = jnp.sum(
            grad_rows[n].astype(jnp.float32) * attended.astype(jnp.float32), axis=0, keepdims=True
        )
        prob = weights * inverse
        score_grad = (prob * (prob_grad - delta)).astype(jnp.bfloat16)
        attended_rows[n] = attended
        row_delta[n] = delta
        one_grad[n] = score_grad
        return score_grad, prob.astype(jnp.bfloat16)

    def store(g, key_part, value_part):
        one_part[0, g] = (key_part * scale).astype(jnp.bfloat16)
        one_part[1, g] = value_part.astype(jnp.bfloat16)

    accumulate = accumulator(query_head, grad_head, chunks, groups, store)
    pipelined(chunks, products, softmax, differentiate, accumulate)


def pipelined(chunks, *stages):
    ready = [{} for _ in range(len(stages) + 1)]
    for step in range(chunks + len(stages) - 1):
        for depth, stage in enumerate(stages):
            n = step - depth
            if 0 <= n < chunks:
                ready[depth + 1][n] = stage(n, *ready[depth].pop(n, ())) or ()


def accumulator(query_head, grad_head, chunks, groups, store):
    count = query_head.shape[0] // chunks
    parts = {}

    def accumulate(n, score_grad, half):
        g = n * groups // chunks
        key_part = matmul(score_grad, grouped(query_head, n, count), (1, 0))
        value_part = matmul(half, grouped(grad_head, n, count), (1, 0))
        if g in parts:
            key_part, value_part = parts[g][0] + key_part, parts[g][1] + value_part
        parts[g] = (key_part, value_part)
        if (n + 1) * groups // chunks != g:
            store(g, key_part, value_part)

    return accumulate


def two_backward_kernel(
    query_head, grad_head, near_weights, near_prob_grad, near_factor, row_delta,
    two_grad, two_mine, send_keys, send_values,
):
    chunks = near_weights.shape[0]
    groups, length, width = two_mine.shape[1:]

    def differentiate(n):
        prob = near_weights[n] * near_factor[n]
        score_grad = (prob * (near_prob_grad[n] - row_delta[n])).astype(jnp.bfloat16)
        two_grad[n] = score_grad
        return score_grad, prob.astype(jnp.bfloat16)

    def store(g, key_part, value_part):
        for index, (part, send) in enumerate(
            ((key_part * width ** (-0.5), send_keys), (value_part, send_values))
        ):
            two_mine[index, g] = part[:length].astype(jnp.bfloat16)
            send[g] = part[length:].astype(jnp.bfloat16)

    accumulate = accumulator(query_head, grad_head, chunks, groups, store)
    pipelined(chunks, differentiate, accumulate)


def own_backward_kernel(
    query_head, grad_head, own_weights, own_prob_grad, near_factor, own_factor, row_delta,
    after, own_grad, own_part,
):
    chunks = own_weights.shape[0]
    groups, _, width = own_part.shape[1:]

    def differentiate(n):
        prob = own_weights[n] * (own_factor[n] * near_factor[n])
        score_grad = (prob * (own_prob_grad[n] - row_delta[n])).astype(jnp.bfloat16)
        own_grad[n] = score_grad
        return score_grad, prob.astype(jnp.bfloat16)

    def store(g, key_part, value_part):
        own_part[0, g] = key_part * width ** (-0.5)
        own_part[1, g] = value_part

    accumulate = accumulator(query_head, grad_head, chunks, groups, store)
    pipelined(chunks, differentiate, accumulate)


def join_two_kernel(two_mine, other_keys, other_values, two_part):
    groups = two_mine.shape[1]
    two_part[:, my_heads(groups)] = two_mine[...]
    two_part[0, other_heads(groups)] = other_keys[...]
    two_part[1, other_heads(groups)] = other_values[...]


def query_kernel(
    own, back_one, back_two, two_keys, attended_rows, two_grad, one_grad, own_grad,
    out_mine, query_mine, first_third, second_third, last_third, query_send,
):
    sends = (first_third, second_third, last_third)
    groups = own.shape[1]
    chunks = own_grad.shape[0]
    heads, length, width = out_mine.shape
    count = heads // chunks
    for n in range(chunks):
        g = n * groups // chunks
        rows = pl.ds(n * count, count)
        keys = join(two_back(back_two, (two_keys,), 0, g), back_one[0, g], own[0, g])
        part = matmul(keys, join(two_grad[n], one_grad[n], own_grad[n]), (0, 0))
        part = (part * width ** (-0.5)).astype(jnp.bfloat16)
        for index, (columns, mine) in enumerate(((attended_rows[n], out_mine), (part, query_mine))):
            block = columns.T.reshape(count, 2 * length, width)
            mine[rows] = block[:, :length]
            query_send[index, rows] = block[:, length:]
    for index, row, piece, taken in placed(sends, heads):
        piece[...] = query_send[index, pl.ds(row, taken)]


def assemble_kernel(
    out_mine, query_mine, first_third, second_third, last_third, out, query_grad, token
):
    heads = out_mine.shape[0]
    start = (1 - lax.axis_index("head")) * heads
    out[my_heads(heads)] = out_mine[...]
    query_grad[my_heads(heads)] = query_mine[...]
    for index, row, piece, count in placed((first_third, second_third, last_third), heads):
        (out, query_grad)[index][pl.ds(start + row, count)] = piece[...]
    token[...] = jnp.zeros(token.shape, token.dtype)


def own_sum_kernel(own_part, one_total, sum_mine, sum_send):
    length = sum_mine.shape[2]
    total = own_part[...] + one_total[...].astype(jnp.float32)
    sum_mine[...] = total[:, :, :length]
    sum_send[...] = total[:, :, length:].astype(jnp.bfloat16)


def final_kernel(sum_mine, sum_other, two_total, after, key_grad, value_grad):
    groups = sum_mine.shape[1]
    mine, other = my_heads(groups), other_heads(groups)
    for index, result in enumerate((key_grad, value_grad)):
        total = sum_mine[index] + two_total[index, mine].astype(jnp.float32)
        result[mine] = total.astype(jnp.bfloat16)
        total = sum_other[index].astype(jnp.float32) + two_total[index, other].astype(jnp.float32)
        result[other] = total.astype(jnp.bfloat16)


def shards(query_matrix, key_matrix, value_matrix, output_gradient, query_head_spans, slab_offset):
    groups, length, width = key_matrix.shape
    heads = query_matrix.shape[0]
    cores = lax.axis_size("head")
    tokens = cores * length
    groups_here, heads_here = groups // cores, heads // cores
    count = max(1, min(heads // groups, 256 // tokens))
    chunks = heads_here // count
    lanes = count * tokens
    half, full = jnp.bfloat16, jnp.float32
    vmem = pl.BlockSpec(memory_space=pltpu.VMEM)
    smem = pl.BlockSpec(memory_space=pltpu.SMEM)

    def call(kernel, name, outs, arrays, scalars=0, scratch=()):
        return pl.pallas_call(
            kernel,
            out_shape=tuple(jax.ShapeDtypeStruct(shape, kind) for shape, kind in outs),
            in_specs=[smem] * scalars + [vmem] * (len(arrays) - scalars),
            out_specs=(vmem,) * len(outs),
            scratch_shapes=scratch,
            compiler_params=pltpu.CompilerParams(vmem_limit_bytes=40 * 1024 * 1024),
            cost_estimate=pl.CostEstimate(flops=1, bytes_accessed=0, transcendentals=0),
            name=name,
        )(*arrays)

    def rows_of(rows, kind):
        return ((chunks, rows, lanes), kind)

    stat = rows_of(1, full)
    whole_pair = ((2, groups, length, width), half)
    half_block = ((groups_here, length, width), half)
    half_pair = ((2, groups_here, length, width), half)
    chip_pair = ((2, groups_here, tokens, width), half)
    half_rows = ((heads_here, length, width), half)
    third_rows = [((rows, length, width), half) for rows in thirds(heads_here)]
    chip_rows = ((heads_here, tokens, width), half)

    own = jnp.stack([key_matrix, value_matrix])
    chips = lax.axis_size("seq")
    wraps = [(chips - 2, 1), (chips - 1, 0)]
    back_two = lax.ppermute(own, "seq", [(i, i + 2) for i in range(chips - 2)] + wraps)
    own_sends = call(split_kernel, "split_own", [half_block] * 2, (own,))
    (own_head,) = call(
        join_own_kernel, "join_own", [chip_pair], (own, *[swapped(send, "head") for send in own_sends])
    )
    back_one = shifted(own_head, "seq", 1, ring=False)
    sends = call(
        split_rows_kernel,
        "split_rows",
        third_rows,
        (query_matrix, output_gradient, own),
    )
    (
        query_head, grad_head, grad_rows, first, own_max, own_total, own_out, own_weights,
        own_prob_grad,
    ) = call(
        own_kernel,
        "own_block",
        [
            chip_rows, chip_rows, rows_of(width, half), rows_of(1, jnp.int32), stat, stat,
            rows_of(width, full), rows_of(tokens, full), rows_of(tokens, full),
        ],
        (
            query_head_spans, slab_offset, query_matrix, output_gradient,
            *[swapped(send, "head") for send in sends], own_head,
        ),
        scalars=2,
    )
    back_two, first = lax.optimization_barrier((back_two, first))
    two_sends = call(split_kernel, "split_two", [half_block] * 2, (back_two,))
    two_other = [swapped(send, "head") for send in two_sends]
    near_max, near_total, near_out, near_weights, near_prob_grad, own_factor = call(
        near_forward_kernel,
        "near_forward",
        [stat, stat, rows_of(width, full), rows_of(tokens, full), rows_of(tokens, full), stat],
        (first, query_head, grad_head, back_two, *two_other, own_max, own_total, own_out),
    )
    back_one, near_max = lax.optimization_barrier((back_one, near_max))
    attended_rows, row_delta, near_factor, one_grad, one_part = call(
        last_kernel,
        "last_forward_backward",
        [rows_of(width, half), stat, stat, rows_of(tokens, half), chip_pair],
        (first, query_head, grad_head, back_one, grad_rows, near_max, near_total, near_out),
    )
    one_total = shifted(one_part, "seq", -1)
    two_grad, part_mine, *part_sends = call(
        two_backward_kernel,
        "two_backward",
        [rows_of(tokens, half), half_pair, half_block, half_block],
        (query_head, grad_head, near_weights, near_prob_grad, near_factor, row_delta),
    )
    (two_part,) = call(
        join_two_kernel,
        "join_two",
        [whole_pair],
        (part_mine, *[swapped(send, "head") for send in part_sends]),
    )
    two_total = shifted(two_part, "seq", -2)
    own_grad, own_part = call(
        own_backward_kernel,
        "own_backward",
        [rows_of(tokens, half), (chip_pair[0], full)],
        (
            query_head, grad_head, own_weights, own_prob_grad, near_factor, own_factor, row_delta,
            two_part,
        ),
    )
    out_mine, query_mine, *sends = call(
        query_kernel,
        "query_grad",
        [half_rows] * 2 + third_rows,
        (own_head, back_one, back_two, two_other[0], attended_rows, two_grad, one_grad, own_grad),
        scratch=[pltpu.VMEM((2,) + half_rows[0], half)],
    )
    attn_out, query_grad, token = call(
        assemble_kernel,
        "assemble",
        [(query_matrix.shape, half)] * 2 + [((8, 128), full)],
        (out_mine, query_mine, *[swapped(send, "head") for send in sends]),
    )
    sum_mine, sum_send = call(
        own_sum_kernel, "own_sum", [(half_pair[0], full), half_pair], (own_part, one_total)
    )
    key_grad, value_grad = call(
        final_kernel,
        "total",
        [(key_matrix.shape, half)] * 2,
        (sum_mine, swapped(sum_send, "head"), two_total, token),
    )
    return (attn_out, query_grad, key_grad, value_grad)


def solution(mesh):
    tokens = P(None, ("seq", "head"), None)
    return jax.shard_map(
        shards,
        mesh=mesh,
        in_specs=(tokens, tokens, tokens, tokens, P(), P()),
        out_specs=(tokens, tokens, tokens, tokens),
        check_vma=False,
    )
```

```python
import math

import jax
import jax.numpy as jnp
from jax import lax
from jax.experimental import pallas as pl
from jax.experimental.pallas import tpu as pltpu
from jax.sharding import PartitionSpec as P

REACH = 2
SEGMENT = 512

masked_score = -1e30


def shifted(block, axis, distance, ring=True):
    count = lax.axis_size(axis)
    route = [(i, (i + distance) % count) for i in range(count) if ring or i + distance < count]
    return lax.ppermute(block, axis, route)


def swapped(block, axis):
    count = lax.axis_size(axis)
    return lax.ppermute(block, axis, [(i, count - 1 - i) for i in range(count)])


def matmul(left, right, contract):
    return lax.dot_general(
        left, right, ((contract[:1], contract[1:]), ((), ())), preferred_element_type=jnp.float32
    )


def grouped(ref, n, count):
    _, length, width = ref.shape
    return ref[pl.ds(n * count, count)].reshape(count * length, width)


def join(*blocks):
    return jnp.concatenate(blocks, axis=0)


def core_offsets(length):
    core = lax.axis_index("head")
    return core * length, (1 - core) * length


def my_heads(count):
    return pl.ds(lax.axis_index("head") * count, count)


def other_heads(count):
    return pl.ds((1 - lax.axis_index("head")) * count, count)


def lane_tokens(count, length):
    lane = lax.broadcasted_iota(jnp.int32, (1, count * 2 * length), 1)
    token = lane - lane // (2 * length) * (2 * length)
    mine, other = core_offsets(length)
    return jnp.where(token < length, token + mine, token - length + other)


def first_visible(spans, offset, chunks, count, length):
    token = lane_tokens(count, length)
    lane_head = lax.broadcasted_iota(jnp.int32, token.shape, 1) // (2 * length)
    start = lax.axis_index("seq") * 2 * length
    segment_start = token - lax.bitwise_and(offset[0] + start + token, SEGMENT - 1)
    floor = jnp.maximum(segment_start, -start)
    base = lax.axis_index("head") * chunks * count
    result = []
    for n in range(chunks):
        span = jnp.full(token.shape, spans[base + n * count], jnp.int32)
        for a in range(1, count):
            span = jnp.where(lane_head == a, spans[base + n * count + a], span)
        result.append(jnp.maximum(floor, token - span + 1))
    return result


def masked(scores, first, chips_back, token=None):
    length = scores.shape[0] // 2
    row = lax.broadcasted_iota(jnp.int32, (length, scores.shape[1]), 0)
    pieces = []
    for part, offset in enumerate(core_offsets(length)):
        visible = row >= first + (chips_back * 2 * length - offset)
        if token is not None:
            visible &= row <= token - offset
        pieces.append(
            jnp.where(visible, scores[part * length : (part + 1) * length], masked_score)
        )
    return join(*pieces)


def split_kernel(block, *sends):
    for index, send in enumerate(sends):
        send[...] = block[index, other_heads(send.shape[0])]


def thirds(rows):
    return [2 * rows * (i + 1) // 3 - 2 * rows * i // 3 for i in range(3)]


def placed(pieces, rows):
    taken = 0
    for piece in pieces:
        count = piece.shape[0]
        for index in range(2):
            low = max(taken, index * rows)
            high = min(taken + count, (index + 1) * rows)
            if low < high:
                yield index, low - index * rows, piece.at[pl.ds(low - taken, high - low)], high - low
        taken += count


def split_rows_kernel(queries, grads, after, *sends):
    heads = queries.shape[0] // 2
    start = (1 - lax.axis_index("head")) * heads
    for index, row, piece, count in placed(sends, heads):
        piece[...] = (queries, grads)[index][pl.ds(start + row, count)]


def join_own_kernel(own, other_keys, other_values, own_head):
    groups, length = other_keys.shape[:2]
    own_head[:, :, pl.ds(0, length)] = own[:, my_heads(groups)]
    own_head[0, :, pl.ds(length, length)] = other_keys[...]
    own_head[1, :, pl.ds(length, length)] = other_values[...]


def own_kernel(
    spans, offset, queries, grads, first_third, second_third, last_third, own,
    query_head, grad_head, grad_rows, first, own_max, own_total, own_out, own_weights,
    own_prob_grad,
):
    heads, _, width = query_head.shape
    length = queries.shape[1]
    groups = own.shape[1]
    chunks = first.shape[0]
    count = heads // chunks
    query_head[:, pl.ds(0, length)] = queries[my_heads(heads)]
    grad_head[:, pl.ds(0, length)] = grads[my_heads(heads)]
    for index, row, piece, rows in placed((first_third, second_third, last_third), heads):
        (query_head, grad_head)[index][pl.ds(row, rows), pl.ds(length, length)] = piece[...]
    factor = width ** (-0.5) * math.log2(math.e)
    token = lane_tokens(count, length)
    for n, rows in enumerate(first_visible(spans, offset, chunks, count, length)):
        first[n] = rows

    def products(n):
        g = n * groups // chunks
        own_prob_grad[n] = matmul(own[1, g], grouped(grad_head, n, count), (1, 1))
        return (matmul(own[0, g], grouped(query_head, n, count), (1, 1)),)

    def softmax(n, scores):
        scores = masked(scores * factor, first[n], 0, token)
        row_max = jnp.max(scores, axis=0, keepdims=True)
        weights = jnp.exp2(scores - row_max)
        own_max[n] = row_max
        own_total[n] = jnp.sum(weights, axis=0, keepdims=True)
        own_weights[n] = weights
        return (weights.astype(jnp.bfloat16),)

    def weigh(n, halves):
        own_out[n] = matmul(own[1, n * groups // chunks], halves, (0, 0))
        grad_rows[n] = grouped(grad_head, n, count).T

    pipelined(chunks, products, softmax, weigh)


def two_back(back_two, two_other, index, g):
    base = lax.axis_index("head") * two_other[index].shape[0]
    return join(back_two[index, base + g], two_other[index][g])


def near_forward_kernel(
    first, query_head, grad_head, back_two, two_keys, two_values, own_max, own_total, own_out,
    near_max, near_total, near_out, near_weights, near_prob_grad, own_factor,
):
    groups = two_keys.shape[0]
    two_other = (two_keys, two_values)
    chunks = first.shape[0]
    heads, _, width = query_head.shape
    count = heads // chunks
    factor = width ** (-0.5) * math.log2(math.e)

    def products(n):
        g = n * groups // chunks
        keys = two_back(back_two, two_other, 0, g)
        values = two_back(back_two, two_other, 1, g)
        near_prob_grad[n] = matmul(values, grouped(grad_head, n, count), (1, 1))
        return (matmul(keys, grouped(query_head, n, count), (1, 1)),)

    def softmax(n, scores):
        scores = masked(scores * factor, first[n], 2)
        row_max = jnp.maximum(own_max[n], jnp.max(scores, axis=0, keepdims=True))
        weights = jnp.exp2(scores - row_max)
        rescale = jnp.exp2(own_max[n] - row_max)
        own_factor[n] = rescale
        near_max[n] = row_max
        near_total[n] = own_total[n] * rescale + jnp.sum(weights, axis=0, keepdims=True)
        near_weights[n] = weights
        return rescale, weights.astype(jnp.bfloat16)

    def weigh(n, rescale, halves):
        values = two_back(back_two, two_other, 1, n * groups // chunks)
        near_out[n] = own_out[n] * rescale + matmul(values, halves, (0, 0))

    pipelined(chunks, products, softmax, weigh)


def last_kernel(
    first, query_head, grad_head, back_one, grad_rows, near_max, near_total, near_out,
    attended_rows, row_delta, near_factor, one_grad, one_part,
):
    groups = back_one.shape[1]
    chunks = first.shape[0]
    heads, _, width = query_head.shape
    count = heads // chunks
    scale = width ** (-0.5)

    def products(n):
        g = n * groups // chunks
        scores = matmul(back_one[0, g], grouped(query_head, n, count), (1, 1))
        prob_grad = matmul(back_one[1, g], grouped(grad_head, n, count), (1, 1))
        return scores, prob_grad

    def softmax(n, scores, prob_grad):
        scores = masked(scores * (scale * math.log2(math.e)), first[n], 1)
        row_max = jnp.maximum(near_max[n], jnp.max(scores, axis=0, keepdims=True))
        weights = jnp.exp2(scores - row_max)
        rescale = jnp.exp2(near_max[n] - row_max)
        inverse = 1.0 / (near_total[n] * rescale + jnp.sum(weights, axis=0, keepdims=True))
        weighted = matmul(
            back_one[1, n * groups // chunks], weights.astype(jnp.bfloat16), (0, 0)
        )
        near_factor[n] = rescale * inverse
        return prob_grad, weights, weighted, rescale, inverse

    def differentiate(n, prob_grad, weights, weighted, rescale, inverse):
        attended = ((near_out[n] * rescale + weighted) * inverse).astype(jnp.bfloat16)
        delta = jnp.sum(
            grad_rows[n].astype(jnp.float32) * attended.astype(jnp.float32), axis=0, keepdims=True
        )
        prob = weights * inverse
        score_grad = (prob * (prob_grad - delta)).astype(jnp.bfloat16)
        attended_rows[n] = attended
        row_delta[n] = delta
        one_grad[n] = score_grad
        return score_grad, prob.astype(jnp.bfloat16)

    def store(g, key_part, value_part):
        one_part[0, g] = (key_part * scale).astype(jnp.bfloat16)
        one_part[1, g] = value_part.astype(jnp.bfloat16)

    accumulate = accumulator(query_head, grad_head, chunks, groups, store)
    pipelined(chunks, products, softmax, differentiate, accumulate)


def pipelined(chunks, *stages):
    ready = [{} for _ in range(len(stages) + 1)]
    for step in range(chunks + len(stages) - 1):
        for depth, stage in enumerate(stages):
            n = step - depth
            if 0 <= n < chunks:
                ready[depth + 1][n] = stage(n, *ready[depth].pop(n, ())) or ()


def accumulator(query_head, grad_head, chunks, groups, store):
    count = query_head.shape[0] // chunks
    parts = {}

    def accumulate(n, score_grad, half):
        g = n * groups // chunks
        key_part = matmul(score_grad, grouped(query_head, n, count), (1, 0))
        value_part = matmul(half, grouped(grad_head, n, count), (1, 0))
        if g in parts:
            key_part, value_part = parts[g][0] + key_part, parts[g][1] + value_part
        parts[g] = (key_part, value_part)
        if (n + 1) * groups // chunks != g:
            store(g, key_part, value_part)

    return accumulate


def two_backward_kernel(
    query_head, grad_head, near_weights, near_prob_grad, near_factor, row_delta,
    two_grad, two_mine, send_keys, send_values,
):
    chunks = near_weights.shape[0]
    groups, length, width = two_mine.shape[1:]

    def differentiate(n):
        prob = near_weights[n] * near_factor[n]
        score_grad = (prob * (near_prob_grad[n] - row_delta[n])).astype(jnp.bfloat16)
        two_grad[n] = score_grad
        return score_grad, prob.astype(jnp.bfloat16)

    def store(g, key_part, value_part):
        for index, (part, send) in enumerate(
            ((key_part * width ** (-0.5), send_keys), (value_part, send_values))
        ):
            two_mine[index, g] = part[:length].astype(jnp.bfloat16)
            send[g] = part[length:].astype(jnp.bfloat16)

    accumulate = accumulator(query_head, grad_head, chunks, groups, store)
    pipelined(chunks, differentiate, accumulate)


def own_backward_kernel(
    query_head, grad_head, own_weights, own_prob_grad, near_factor, own_factor, row_delta,
    after, own_grad, own_part,
):
    chunks = own_weights.shape[0]
    groups, _, width = own_part.shape[1:]

    def differentiate(n):
        prob = own_weights[n] * (own_factor[n] * near_factor[n])
        score_grad = (prob * (own_prob_grad[n] - row_delta[n])).astype(jnp.bfloat16)
        own_grad[n] = score_grad
        return score_grad, prob.astype(jnp.bfloat16)

    def store(g, key_part, value_part):
        own_part[0, g] = key_part * width ** (-0.5)
        own_part[1, g] = value_part

    accumulate = accumulator(query_head, grad_head, chunks, groups, store)
    pipelined(chunks, differentiate, accumulate)


def join_two_kernel(two_mine, other_keys, other_values, two_part):
    groups = two_mine.shape[1]
    two_part[:, my_heads(groups)] = two_mine[...]
    two_part[0, other_heads(groups)] = other_keys[...]
    two_part[1, other_heads(groups)] = other_values[...]


def query_kernel(
    own, back_one, back_two, two_keys, attended_rows, two_grad, one_grad, own_grad,
    out_mine, query_mine, first_third, second_third, last_third, query_send,
):
    sends = (first_third, second_third, last_third)
    groups = own.shape[1]
    chunks = own_grad.shape[0]
    heads, length, width = out_mine.shape
    count = heads // chunks
    for n in range(chunks):
        g = n * groups // chunks
        rows = pl.ds(n * count, count)
        keys = join(two_back(back_two, (two_keys,), 0, g), back_one[0, g], own[0, g])
        part = matmul(keys, join(two_grad[n], one_grad[n], own_grad[n]), (0, 0))
        part = (part * width ** (-0.5)).astype(jnp.bfloat16)
        for index, (columns, mine) in enumerate(((attended_rows[n], out_mine), (part, query_mine))):
            block = columns.T.reshape(count, 2 * length, width)
            mine[rows] = block[:, :length]
            query_send[index, rows] = block[:, length:]
    for index, row, piece, taken in placed(sends, heads):
        piece[...] = query_send[index, pl.ds(row, taken)]


def assemble_kernel(
    out_mine, query_mine, first_third, second_third, last_third, out, query_grad, token
):
    heads = out_mine.shape[0]
    start = (1 - lax.axis_index("head")) * heads
    out[my_heads(heads)] = out_mine[...]
    query_grad[my_heads(heads)] = query_mine[...]
    for index, row, piece, count in placed((first_third, second_third, last_third), heads):
        (out, query_grad)[index][pl.ds(start + row, count)] = piece[...]
    token[...] = jnp.zeros(token.shape, token.dtype)


def own_sum_kernel(own_part, one_total, sum_mine, sum_send):
    length = sum_mine.shape[2]
    total = own_part[...] + one_total[...].astype(jnp.float32)
    sum_mine[...] = total[:, :, :length]
    sum_send[...] = total[:, :, length:].astype(jnp.bfloat16)


def final_kernel(sum_mine, sum_other, two_total, after, key_grad, value_grad):
    groups = sum_mine.shape[1]
    mine, other = my_heads(groups), other_heads(groups)
    for index, result in enumerate((key_grad, value_grad)):
        total = sum_mine[index] + two_total[index, mine].astype(jnp.float32)
        result[mine] = total.astype(jnp.bfloat16)
        total = sum_other[index].astype(jnp.float32) + two_total[index, other].astype(jnp.float32)
        result[other] = total.astype(jnp.bfloat16)


def shards(query_matrix, key_matrix, value_matrix, output_gradient, query_head_spans, slab_offset):
    groups, length, width = key_matrix.shape
    heads = query_matrix.shape[0]
    cores = lax.axis_size("head")
    tokens = cores * length
    groups_here, heads_here = groups // cores, heads // cores
    count = max(1, min(heads // groups, 256 // tokens))
    chunks = heads_here // count
    lanes = count * tokens
    half, full = jnp.bfloat16, jnp.float32
    vmem = pl.BlockSpec(memory_space=pltpu.VMEM)
    smem = pl.BlockSpec(memory_space=pltpu.SMEM)

    def call(kernel, name, outs, arrays, scalars=0, scratch=()):
        return pl.pallas_call(
            kernel,
            out_shape=tuple(jax.ShapeDtypeStruct(shape, kind) for shape, kind in outs),
            in_specs=[smem] * scalars + [vmem] * (len(arrays) - scalars),
            out_specs=(vmem,) * len(outs),
            scratch_shapes=scratch,
            compiler_params=pltpu.CompilerParams(vmem_limit_bytes=40 * 1024 * 1024),
            cost_estimate=pl.CostEstimate(flops=1, bytes_accessed=0, transcendentals=0),
            name=name,
        )(*arrays)

    def rows_of(rows, kind):
        return ((chunks, rows, lanes), kind)

    stat = rows_of(1, full)
    whole_pair = ((2, groups, length, width), half)
    half_block = ((groups_here, length, width), half)
    half_pair = ((2, groups_here, length, width), half)
    chip_pair = ((2, groups_here, tokens, width), half)
    half_rows = ((heads_here, length, width), half)
    third_rows = [((rows, length, width), half) for rows in thirds(heads_here)]
    chip_rows = ((heads_here, tokens, width), half)

    own = jnp.stack([key_matrix, value_matrix])
    chips = lax.axis_size("seq")
    route = []
    for core in range(cores):
        route += [(core * chips + i, core * chips + i + 2) for i in range(chips - 2)]
        route += [
            (core * chips + chips - 2 + i, (cores - 1 - core) * chips + i) for i in range(2)
        ]
    back_two = lax.ppermute(own, ("head", "seq"), route)
    own_sends = call(split_kernel, "split_own", [half_block] * 2, (own,))
    (own_head,) = call(
        join_own_kernel, "join_own", [chip_pair], (own, *[swapped(send, "head") for send in own_sends])
    )
    back_one = shifted(own_head, "seq", 1, ring=False)
    sends = call(
        split_rows_kernel,
        "split_rows",
        third_rows,
        (query_matrix, output_gradient, own),
    )
    (
        query_head, grad_head, grad_rows, first, own_max, own_total, own_out, own_weights,
        own_prob_grad,
    ) = call(
        own_kernel,
        "own_block",
        [
            chip_rows, chip_rows, rows_of(width, half), rows_of(1, jnp.int32), stat, stat,
            rows_of(width, full), rows_of(tokens, full), rows_of(tokens, full),
        ],
        (
            query_head_spans, slab_offset, query_matrix, output_gradient,
            *[swapped(send, "head") for send in sends], own_head,
        ),
        scalars=2,
    )
    back_two, first = lax.optimization_barrier((back_two, first))
    two_sends = call(split_kernel, "split_two", [half_block] * 2, (back_two,))
    two_other = [swapped(send, "head") for send in two_sends]
    near_max, near_total, near_out, near_weights, near_prob_grad, own_factor = call(
        near_forward_kernel,
        "near_forward",
        [stat, stat, rows_of(width, full), rows_of(tokens, full), rows_of(tokens, full), stat],
        (first, query_head, grad_head, back_two, *two_other, own_max, own_total, own_out),
    )
    back_one, near_max = lax.optimization_barrier((back_one, near_max))
    attended_rows, row_delta, near_factor, one_grad, one_part = call(
        last_kernel,
        "last_forward_backward",
        [rows_of(width, half), stat, stat, rows_of(tokens, half), chip_pair],
        (first, query_head, grad_head, back_one, grad_rows, near_max, near_total, near_out),
    )
    one_total = shifted(one_part, "seq", -1)
    two_grad, part_mine, *part_sends = call(
        two_backward_kernel,
        "two_backward",
        [rows_of(tokens, half), half_pair, half_block, half_block],
        (query_head, grad_head, near_weights, near_prob_grad, near_factor, row_delta),
    )
    (two_part,) = call(
        join_two_kernel,
        "join_two",
        [whole_pair],
        (part_mine, *[swapped(send, "head") for send in part_sends]),
    )
    two_total = shifted(two_part, "seq", -2)
    own_grad, own_part = call(
        own_backward_kernel,
        "own_backward",
        [rows_of(tokens, half), (chip_pair[0], full)],
        (
            query_head, grad_head, own_weights, own_prob_grad, near_factor, own_factor, row_delta,
            two_part,
        ),
    )
    out_mine, query_mine, *sends = call(
        query_kernel,
        "query_grad",
        [half_rows] * 2 + third_rows,
        (own_head, back_one, back_two, two_other[0], attended_rows, two_grad, one_grad, own_grad),
        scratch=[pltpu.VMEM((2,) + half_rows[0], half)],
    )
    attn_out, query_grad, token = call(
        assemble_kernel,
        "assemble",
        [(query_matrix.shape, half)] * 2 + [((8, 128), full)],
        (out_mine, query_mine, *[swapped(send, "head") for send in sends]),
    )
    sum_mine, sum_send = call(
        own_sum_kernel, "own_sum", [(half_pair[0], full), half_pair], (own_part, one_total)
    )
    key_grad, value_grad = call(
        final_kernel,
        "total",
        [(key_matrix.shape, half)] * 2,
        (sum_mine, swapped(sum_send, "head"), two_total, token),
    )
    return (attn_out, query_grad, key_grad, value_grad)


def solution(mesh):
    tokens = P(None, ("seq", "head"), None)
    return jax.shard_map(
        shards,
        mesh=mesh,
        in_specs=(tokens, tokens, tokens, tokens, P(), P()),
        out_specs=(tokens, tokens, tokens, tokens),
        check_vma=False,
    )
```

```python
import math

import jax
import jax.numpy as jnp
from jax import lax
from jax.experimental import pallas as pl
from jax.experimental.pallas import tpu as pltpu
from jax.sharding import PartitionSpec as P

REACH = 2
SEGMENT = 512

masked_score = -1e30


def shifted(block, axis, distance, ring=True):
    count = lax.axis_size(axis)
    route = [(i, (i + distance) % count) for i in range(count) if ring or i + distance < count]
    return lax.ppermute(block, axis, route)


def swapped(block, axis):
    count = lax.axis_size(axis)
    return lax.ppermute(block, axis, [(i, count - 1 - i) for i in range(count)])


def matmul(left, right, contract):
    return lax.dot_general(
        left, right, ((contract[:1], contract[1:]), ((), ())), preferred_element_type=jnp.float32
    )


def grouped(ref, n, count):
    _, length, width = ref.shape
    return ref[pl.ds(n * count, count)].reshape(count * length, width)


def join(*blocks):
    return jnp.concatenate(blocks, axis=0)


def core_offsets(length):
    core = lax.axis_index("head")
    return core * length, (1 - core) * length


def my_heads(count):
    return pl.ds(lax.axis_index("head") * count, count)


def other_heads(count):
    return pl.ds((1 - lax.axis_index("head")) * count, count)


def lane_tokens(count, length):
    lane = lax.broadcasted_iota(jnp.int32, (1, count * 2 * length), 1)
    token = lane - lane // (2 * length) * (2 * length)
    mine, other = core_offsets(length)
    return jnp.where(token < length, token + mine, token - length + other)


def first_visible(spans, offset, chunks, count, length):
    token = lane_tokens(count, length)
    lane_head = lax.broadcasted_iota(jnp.int32, token.shape, 1) // (2 * length)
    start = lax.axis_index("seq") * 2 * length
    segment_start = token - lax.bitwise_and(offset[0] + start + token, SEGMENT - 1)
    floor = jnp.maximum(segment_start, -start)
    base = lax.axis_index("head") * chunks * count
    result = []
    for n in range(chunks):
        span = jnp.full(token.shape, spans[base + n * count], jnp.int32)
        for a in range(1, count):
            span = jnp.where(lane_head == a, spans[base + n * count + a], span)
        result.append(jnp.maximum(floor, token - span + 1))
    return result


def masked(scores, first, chips_back, token=None):
    length = scores.shape[0] // 2
    row = lax.broadcasted_iota(jnp.int32, (length, scores.shape[1]), 0)
    pieces = []
    for part, offset in enumerate(core_offsets(length)):
        visible = row >= first + (chips_back * 2 * length - offset)
        if token is not None:
            visible &= row <= token - offset
        pieces.append(
            jnp.where(visible, scores[part * length : (part + 1) * length], masked_score)
        )
    return join(*pieces)


def split_kernel(block, *sends):
    for index, send in enumerate(sends):
        send[...] = block[index, other_heads(send.shape[0])]


def thirds(rows):
    return [2 * rows * (i + 1) // 3 - 2 * rows * i // 3 for i in range(3)]


def placed(pieces, rows):
    taken = 0
    for piece in pieces:
        count = piece.shape[0]
        for index in range(2):
            low = max(taken, index * rows)
            high = min(taken + count, (index + 1) * rows)
            if low < high:
                yield index, low - index * rows, piece.at[pl.ds(low - taken, high - low)], high - low
        taken += count


def split_rows_kernel(queries, grads, after, *sends):
    heads = queries.shape[0] // 2
    start = (1 - lax.axis_index("head")) * heads
    for index, row, piece, count in placed(sends, heads):
        piece[...] = (queries, grads)[index][pl.ds(start + row, count)]


def join_own_kernel(own, other_keys, other_values, own_head):
    groups, length = other_keys.shape[:2]
    own_head[:, :, pl.ds(0, length)] = own[:, my_heads(groups)]
    own_head[0, :, pl.ds(length, length)] = other_keys[...]
    own_head[1, :, pl.ds(length, length)] = other_values[...]


def own_kernel(
    spans, offset, queries, grads, first_third, second_third, last_third, own,
    query_head, grad_head, grad_rows, first, own_max, own_total, own_out, own_weights,
    own_prob_grad,
):
    heads, _, width = query_head.shape
    length = queries.shape[1]
    groups = own.shape[1]
    chunks = first.shape[0]
    count = heads // chunks
    query_head[:, pl.ds(0, length)] = queries[my_heads(heads)]
    grad_head[:, pl.ds(0, length)] = grads[my_heads(heads)]
    for index, row, piece, rows in placed((first_third, second_third, last_third), heads):
        (query_head, grad_head)[index][pl.ds(row, rows), pl.ds(length, length)] = piece[...]
    factor = width ** (-0.5) * math.log2(math.e)
    token = lane_tokens(count, length)
    for n, rows in enumerate(first_visible(spans, offset, chunks, count, length)):
        first[n] = rows

    def products(n):
        g = n * groups // chunks
        own_prob_grad[n] = matmul(own[1, g], grouped(grad_head, n, count), (1, 1))
        return (matmul(own[0, g], grouped(query_head, n, count), (1, 1)),)

    def softmax(n, scores):
        scores = masked(scores * factor, first[n], 0, token)
        row_max = jnp.max(scores, axis=0, keepdims=True)
        weights = jnp.exp2(scores - row_max)
        own_max[n] = row_max
        own_total[n] = jnp.sum(weights, axis=0, keepdims=True)
        own_weights[n] = weights
        return (weights.astype(jnp.bfloat16),)

    def weigh(n, halves):
        own_out[n] = matmul(own[1, n * groups // chunks], halves, (0, 0))
        grad_rows[n] = grouped(grad_head, n, count).T

    pipelined(chunks, products, softmax, weigh)


def two_back(back_two, two_other, index, g):
    base = lax.axis_index("head") * two_other[index].shape[0]
    return join(back_two[index, base + g], two_other[index][g])


def near_forward_kernel(
    first, query_head, grad_head, back_two, two_keys, two_values, own_max, own_total, own_out,
    near_max, near_total, near_out, near_weights, near_prob_grad, own_factor,
):
    groups = two_keys.shape[0]
    two_other = (two_keys, two_values)
    chunks = first.shape[0]
    heads, _, width = query_head.shape
    count = heads // chunks
    factor = width ** (-0.5) * math.log2(math.e)

    def products(n):
        g = n * groups // chunks
        keys = two_back(back_two, two_other, 0, g)
        values = two_back(back_two, two_other, 1, g)
        near_prob_grad[n] = matmul(values, grouped(grad_head, n, count), (1, 1))
        return (matmul(keys, grouped(query_head, n, count), (1, 1)),)

    def softmax(n, scores):
        scores = masked(scores * factor, first[n], 2)
        row_max = jnp.maximum(own_max[n], jnp.max(scores, axis=0, keepdims=True))
        weights = jnp.exp2(scores - row_max)
        rescale = jnp.exp2(own_max[n] - row_max)
        own_factor[n] = rescale
        near_max[n] = row_max
        near_total[n] = own_total[n] * rescale + jnp.sum(weights, axis=0, keepdims=True)
        near_weights[n] = weights
        return rescale, weights.astype(jnp.bfloat16)

    def weigh(n, rescale, halves):
        values = two_back(back_two, two_other, 1, n * groups // chunks)
        near_out[n] = own_out[n] * rescale + matmul(values, halves, (0, 0))

    pipelined(chunks, products, softmax, weigh)


def last_kernel(
    first, query_head, grad_head, back_one, grad_rows, near_max, near_total, near_out,
    attended_rows, row_delta, near_factor, one_grad, one_part,
):
    groups = back_one.shape[1]
    chunks = first.shape[0]
    heads, _, width = query_head.shape
    count = heads // chunks
    scale = width ** (-0.5)

    def products(n):
        g = n * groups // chunks
        scores = matmul(back_one[0, g], grouped(query_head, n, count), (1, 1))
        prob_grad = matmul(back_one[1, g], grouped(grad_head, n, count), (1, 1))
        return scores, prob_grad

    def softmax(n, scores, prob_grad):
        scores = masked(scores * (scale * math.log2(math.e)), first[n], 1)
        row_max = jnp.maximum(near_max[n], jnp.max(scores, axis=0, keepdims=True))
        weights = jnp.exp2(scores - row_max)
        rescale = jnp.exp2(near_max[n] - row_max)
        inverse = 1.0 / (near_total[n] * rescale + jnp.sum(weights, axis=0, keepdims=True))
        weighted = matmul(
            back_one[1, n * groups // chunks], weights.astype(jnp.bfloat16), (0, 0)
        )
        near_factor[n] = rescale * inverse
        return prob_grad, weights, weighted, rescale, inverse

    def differentiate(n, prob_grad, weights, weighted, rescale, inverse):
        attended = ((near_out[n] * rescale + weighted) * inverse).astype(jnp.bfloat16)
        delta = jnp.sum(
            grad_rows[n].astype(jnp.float32) * attended.astype(jnp.float32), axis=0, keepdims=True
        )
        prob = weights * inverse
        score_grad = (prob * (prob_grad - delta)).astype(jnp.bfloat16)
        attended_rows[n] = attended
        row_delta[n] = delta
        one_grad[n] = score_grad
        return score_grad, prob.astype(jnp.bfloat16)

    def store(g, key_part, value_part):
        one_part[0, g] = (key_part * scale).astype(jnp.bfloat16)
        one_part[1, g] = value_part.astype(jnp.bfloat16)

    accumulate = accumulator(query_head, grad_head, chunks, groups, store)
    pipelined(chunks, products, softmax, differentiate, accumulate)


def pipelined(chunks, *stages):
    ready = [{} for _ in range(len(stages) + 1)]
    for step in range(chunks + len(stages) - 1):
        for depth, stage in enumerate(stages):
            n = step - depth
            if 0 <= n < chunks:
                ready[depth + 1][n] = stage(n, *ready[depth].pop(n, ())) or ()


def accumulator(query_head, grad_head, chunks, groups, store):
    count = query_head.shape[0] // chunks
    parts = {}

    def accumulate(n, score_grad, half):
        g = n * groups // chunks
        key_part = matmul(score_grad, grouped(query_head, n, count), (1, 0))
        value_part = matmul(half, grouped(grad_head, n, count), (1, 0))
        if g in parts:
            key_part, value_part = parts[g][0] + key_part, parts[g][1] + value_part
        parts[g] = (key_part, value_part)
        if (n + 1) * groups // chunks != g:
            store(g, key_part, value_part)

    return accumulate


def two_backward_kernel(
    query_head, grad_head, near_weights, near_prob_grad, near_factor, row_delta,
    two_grad, two_mine, two_send,
):
    chunks = near_weights.shape[0]
    groups, length, width = two_mine.shape[1:]

    def differentiate(n):
        prob = near_weights[n] * near_factor[n]
        score_grad = (prob * (near_prob_grad[n] - row_delta[n])).astype(jnp.bfloat16)
        two_grad[n] = score_grad
        return score_grad, prob.astype(jnp.bfloat16)

    def store(g, key_part, value_part):
        for index, part in enumerate((key_part * width ** (-0.5), value_part)):
            two_mine[index, g] = part[:length].astype(jnp.bfloat16)
            two_send[index, g] = part[length:].astype(jnp.bfloat16)

    accumulate = accumulator(query_head, grad_head, chunks, groups, store)
    pipelined(chunks, differentiate, accumulate)


def own_backward_kernel(
    query_head, grad_head, own_weights, own_prob_grad, near_factor, own_factor, row_delta,
    after, own_grad, own_part,
):
    chunks = own_weights.shape[0]
    groups, _, width = own_part.shape[1:]

    def differentiate(n):
        prob = own_weights[n] * (own_factor[n] * near_factor[n])
        score_grad = (prob * (own_prob_grad[n] - row_delta[n])).astype(jnp.bfloat16)
        own_grad[n] = score_grad
        return score_grad, prob.astype(jnp.bfloat16)

    def store(g, key_part, value_part):
        own_part[0, g] = key_part * width ** (-0.5)
        own_part[1, g] = value_part

    accumulate = accumulator(query_head, grad_head, chunks, groups, store)
    pipelined(chunks, differentiate, accumulate)


def join_two_kernel(two_mine, two_other, two_part):
    groups = two_mine.shape[1]
    two_part[:, my_heads(groups)] = two_mine[...]
    two_part[:, other_heads(groups)] = two_other[...]


def query_kernel(
    own, back_one, back_two, two_keys, attended_rows, two_grad, one_grad, own_grad,
    out_mine, query_mine, first_third, second_third, last_third, query_send,
):
    sends = (first_third, second_third, last_third)
    groups = own.shape[1]
    chunks = own_grad.shape[0]
    heads, length, width = out_mine.shape
    count = heads // chunks
    for n in range(chunks):
        g = n * groups // chunks
        rows = pl.ds(n * count, count)
        keys = join(two_back(back_two, (two_keys,), 0, g), back_one[0, g], own[0, g])
        part = matmul(keys, join(two_grad[n], one_grad[n], own_grad[n]), (0, 0))
        part = (part * width ** (-0.5)).astype(jnp.bfloat16)
        for index, (columns, mine) in enumerate(((attended_rows[n], out_mine), (part, query_mine))):
            block = columns.T.reshape(count, 2 * length, width)
            mine[rows] = block[:, :length]
            query_send[index, rows] = block[:, length:]
    for index, row, piece, taken in placed(sends, heads):
        piece[...] = query_send[index, pl.ds(row, taken)]


def assemble_kernel(
    out_mine, query_mine, first_third, second_third, last_third, out, query_grad, token
):
    heads = out_mine.shape[0]
    start = (1 - lax.axis_index("head")) * heads
    out[my_heads(heads)] = out_mine[...]
    query_grad[my_heads(heads)] = query_mine[...]
    for index, row, piece, count in placed((first_third, second_third, last_third), heads):
        (out, query_grad)[index][pl.ds(start + row, count)] = piece[...]
    token[...] = jnp.zeros(token.shape, token.dtype)


def own_sum_kernel(own_part, one_total, sum_mine, sum_send):
    length = sum_mine.shape[2]
    total = own_part[...] + one_total[...].astype(jnp.float32)
    sum_mine[...] = total[:, :, :length]
    sum_send[...] = total[:, :, length:].astype(jnp.bfloat16)


def final_kernel(sum_mine, sum_other, two_total, after, key_grad, value_grad):
    groups = sum_mine.shape[1]
    mine, other = my_heads(groups), other_heads(groups)
    for index, result in enumerate((key_grad, value_grad)):
        total = sum_mine[index] + two_total[index, mine].astype(jnp.float32)
        result[mine] = total.astype(jnp.bfloat16)
        total = sum_other[index].astype(jnp.float32) + two_total[index, other].astype(jnp.float32)
        result[other] = total.astype(jnp.bfloat16)


def shards(query_matrix, key_matrix, value_matrix, output_gradient, query_head_spans, slab_offset):
    groups, length, width = key_matrix.shape
    heads = query_matrix.shape[0]
    cores = lax.axis_size("head")
    tokens = cores * length
    groups_here, heads_here = groups // cores, heads // cores
    count = max(1, min(heads // groups, 256 // tokens))
    chunks = heads_here // count
    lanes = count * tokens
    half, full = jnp.bfloat16, jnp.float32
    vmem = pl.BlockSpec(memory_space=pltpu.VMEM)
    smem = pl.BlockSpec(memory_space=pltpu.SMEM)

    def call(kernel, name, outs, arrays, scalars=0, scratch=()):
        return pl.pallas_call(
            kernel,
            out_shape=tuple(jax.ShapeDtypeStruct(shape, kind) for shape, kind in outs),
            in_specs=[smem] * scalars + [vmem] * (len(arrays) - scalars),
            out_specs=(vmem,) * len(outs),
            scratch_shapes=scratch,
            compiler_params=pltpu.CompilerParams(vmem_limit_bytes=40 * 1024 * 1024),
            cost_estimate=pl.CostEstimate(flops=1, bytes_accessed=0, transcendentals=0),
            name=name,
        )(*arrays)

    def rows_of(rows, kind):
        return ((chunks, rows, lanes), kind)

    stat = rows_of(1, full)
    whole_pair = ((2, groups, length, width), half)
    half_block = ((groups_here, length, width), half)
    half_pair = ((2, groups_here, length, width), half)
    chip_pair = ((2, groups_here, tokens, width), half)
    half_rows = ((heads_here, length, width), half)
    third_rows = [((rows, length, width), half) for rows in thirds(heads_here)]
    chip_rows = ((heads_here, tokens, width), half)

    own = jnp.stack([key_matrix, value_matrix])
    back_two = shifted(own, "seq", 2)
    own_sends = call(split_kernel, "split_own", [half_block] * 2, (own,))
    (own_head,) = call(
        join_own_kernel, "join_own", [chip_pair], (own, *[swapped(send, "head") for send in own_sends])
    )
    back_one = shifted(own_head, "seq", 1, ring=False)
    sends = call(
        split_rows_kernel,
        "split_rows",
        third_rows,
        (query_matrix, output_gradient, own),
    )
    (
        query_head, grad_head, grad_rows, first, own_max, own_total, own_out, own_weights,
        own_prob_grad,
    ) = call(
        own_kernel,
        "own_block",
        [
            chip_rows, chip_rows, rows_of(width, half), rows_of(1, jnp.int32), stat, stat,
            rows_of(width, full), rows_of(tokens, full), rows_of(tokens, full),
        ],
        (
            query_head_spans, slab_offset, query_matrix, output_gradient,
            *[swapped(send, "head") for send in sends], own_head,
        ),
        scalars=2,
    )
    back_two, first = lax.optimization_barrier((back_two, first))
    two_sends = call(split_kernel, "split_two", [half_block] * 2, (back_two,))
    two_other = [swapped(send, "head") for send in two_sends]
    near_max, near_total, near_out, near_weights, near_prob_grad, own_factor = call(
        near_forward_kernel,
        "near_forward",
        [stat, stat, rows_of(width, full), rows_of(tokens, full), rows_of(tokens, full), stat],
        (first, query_head, grad_head, back_two, *two_other, own_max, own_total, own_out),
    )
    back_one, near_max = lax.optimization_barrier((back_one, near_max))
    attended_rows, row_delta, near_factor, one_grad, one_part = call(
        last_kernel,
        "last_forward_backward",
        [rows_of(width, half), stat, stat, rows_of(tokens, half), chip_pair],
        (first, query_head, grad_head, back_one, grad_rows, near_max, near_total, near_out),
    )
    one_total = shifted(one_part, "seq", -1)
    two_grad, part_mine, part_send = call(
        two_backward_kernel,
        "two_backward",
        [rows_of(tokens, half), half_pair, half_pair],
        (query_head, grad_head, near_weights, near_prob_grad, near_factor, row_delta),
    )
    (two_part,) = call(
        join_two_kernel,
        "join_two",
        [whole_pair],
        (part_mine, swapped(part_send, "head")),
    )
    two_total = shifted(two_part, "seq", -2)
    own_grad, own_part = call(
        own_backward_kernel,
        "own_backward",
        [rows_of(tokens, half), (chip_pair[0], full)],
        (
            query_head, grad_head, own_weights, own_prob_grad, near_factor, own_factor, row_delta,
            two_part,
        ),
    )
    out_mine, query_mine, *sends = call(
        query_kernel,
        "query_grad",
        [half_rows] * 2 + third_rows,
        (own_head, back_one, back_two, two_other[0], attended_rows, two_grad, one_grad, own_grad),
        scratch=[pltpu.VMEM((2,) + half_rows[0], half)],
    )
    attn_out, query_grad, token = call(
        assemble_kernel,
        "assemble",
        [(query_matrix.shape, half)] * 2 + [((8, 128), full)],
        (out_mine, query_mine, *[swapped(send, "head") for send in sends]),
    )
    sum_mine, sum_send = call(
        own_sum_kernel, "own_sum", [(half_pair[0], full), half_pair], (own_part, one_total)
    )
    key_grad, value_grad = call(
        final_kernel,
        "total",
        [(key_matrix.shape, half)] * 2,
        (sum_mine, swapped(sum_send, "head"), two_total, token),
    )
    return (attn_out, query_grad, key_grad, value_grad)


def solution(mesh):
    tokens = P(None, ("seq", "head"), None)
    return jax.shard_map(
        shards,
        mesh=mesh,
        in_specs=(tokens, tokens, tokens, tokens, P(), P()),
        out_specs=(tokens, tokens, tokens, tokens),
        check_vma=False,
    )
```

```python
import math

import jax
import jax.numpy as jnp
from jax import lax
from jax.experimental import pallas as pl
from jax.experimental.pallas import tpu as pltpu
from jax.sharding import PartitionSpec as P

REACH = 2
SEGMENT = 512

masked_score = -1e30


def shifted(block, axis, distance, ring=True):
    count = lax.axis_size(axis)
    route = [(i, (i + distance) % count) for i in range(count) if ring or i + distance < count]
    return lax.ppermute(block, axis, route)


def swapped(block, axis):
    count = lax.axis_size(axis)
    return lax.ppermute(block, axis, [(i, count - 1 - i) for i in range(count)])


def matmul(left, right, contract):
    return lax.dot_general(
        left, right, ((contract[:1], contract[1:]), ((), ())), preferred_element_type=jnp.float32
    )


def grouped(ref, n, count):
    _, length, width = ref.shape
    return ref[pl.ds(n * count, count)].reshape(count * length, width)


def join(*blocks):
    return jnp.concatenate(blocks, axis=0)


def core_offsets(length):
    core = lax.axis_index("head")
    return core * length, (1 - core) * length


def my_heads(count):
    return pl.ds(lax.axis_index("head") * count, count)


def other_heads(count):
    return pl.ds((1 - lax.axis_index("head")) * count, count)


def lane_tokens(count, length):
    lane = lax.broadcasted_iota(jnp.int32, (1, count * 2 * length), 1)
    token = lane - lane // (2 * length) * (2 * length)
    mine, other = core_offsets(length)
    return jnp.where(token < length, token + mine, token - length + other)


def first_visible(spans, offset, chunks, count, length):
    token = lane_tokens(count, length)
    lane_head = lax.broadcasted_iota(jnp.int32, token.shape, 1) // (2 * length)
    start = lax.axis_index("seq") * 2 * length
    segment_start = token - lax.bitwise_and(offset[0] + start + token, SEGMENT - 1)
    floor = jnp.maximum(segment_start, -start)
    base = lax.axis_index("head") * chunks * count
    result = []
    for n in range(chunks):
        span = jnp.full(token.shape, spans[base + n * count], jnp.int32)
        for a in range(1, count):
            span = jnp.where(lane_head == a, spans[base + n * count + a], span)
        result.append(jnp.maximum(floor, token - span + 1))
    return result


def masked(scores, first, chips_back, token=None):
    length = scores.shape[0] // 2
    row = lax.broadcasted_iota(jnp.int32, (length, scores.shape[1]), 0)
    pieces = []
    for part, offset in enumerate(core_offsets(length)):
        visible = row >= first + (chips_back * 2 * length - offset)
        if token is not None:
            visible &= row <= token - offset
        pieces.append(
            jnp.where(visible, scores[part * length : (part + 1) * length], masked_score)
        )
    return join(*pieces)


def split_kernel(block, *sends):
    for index, send in enumerate(sends):
        send[...] = block[index, other_heads(send.shape[0])]


def thirds(rows):
    return [2 * rows * (i + 1) // 3 - 2 * rows * i // 3 for i in range(3)]


def placed(pieces, rows):
    taken = 0
    for piece in pieces:
        count = piece.shape[0]
        for index in range(2):
            low = max(taken, index * rows)
            high = min(taken + count, (index + 1) * rows)
            if low < high:
                yield index, low - index * rows, piece.at[pl.ds(low - taken, high - low)], high - low
        taken += count


def split_rows_kernel(queries, grads, after, *sends):
    heads = queries.shape[0] // 2
    start = (1 - lax.axis_index("head")) * heads
    for index, row, piece, count in placed(sends, heads):
        piece[...] = (queries, grads)[index][pl.ds(start + row, count)]


def join_own_kernel(own, other_keys, other_values, own_head):
    groups, length = other_keys.shape[:2]
    own_head[:, :, pl.ds(0, length)] = own[:, my_heads(groups)]
    own_head[0, :, pl.ds(length, length)] = other_keys[...]
    own_head[1, :, pl.ds(length, length)] = other_values[...]


def own_kernel(
    spans, offset, queries, grads, first_third, second_third, last_third, own,
    query_head, grad_head, grad_rows, first, own_max, own_total, own_out, own_weights,
    own_prob_grad,
):
    heads, _, width = query_head.shape
    length = queries.shape[1]
    groups = own.shape[1]
    chunks = first.shape[0]
    count = heads // chunks
    query_head[:, pl.ds(0, length)] = queries[my_heads(heads)]
    grad_head[:, pl.ds(0, length)] = grads[my_heads(heads)]
    for index, row, piece, rows in placed((first_third, second_third, last_third), heads):
        (query_head, grad_head)[index][pl.ds(row, rows), pl.ds(length, length)] = piece[...]
    factor = width ** (-0.5) * math.log2(math.e)
    token = lane_tokens(count, length)
    for n, rows in enumerate(first_visible(spans, offset, chunks, count, length)):
        first[n] = rows

    def products(n):
        g = n * groups // chunks
        own_prob_grad[n] = matmul(own[1, g], grouped(grad_head, n, count), (1, 1))
        return (matmul(own[0, g], grouped(query_head, n, count), (1, 1)),)

    def softmax(n, scores):
        scores = masked(scores * factor, first[n], 0, token)
        row_max = jnp.max(scores, axis=0, keepdims=True)
        weights = jnp.exp2(scores - row_max)
        own_max[n] = row_max
        own_total[n] = jnp.sum(weights, axis=0, keepdims=True)
        own_weights[n] = weights
        return (weights.astype(jnp.bfloat16),)

    def weigh(n, halves):
        own_out[n] = matmul(own[1, n * groups // chunks], halves, (0, 0))
        grad_rows[n] = grouped(grad_head, n, count).T

    pipelined(chunks, products, softmax, weigh)


def two_back(back_two, two_other, index, g):
    base = lax.axis_index("head") * two_other[index].shape[0]
    return join(back_two[index, base + g], two_other[index][g])


def near_forward_kernel(
    first, query_head, grad_head, back_two, two_keys, two_values, own_max, own_total, own_out,
    near_max, near_total, near_out, near_weights, near_prob_grad, own_factor,
):
    groups = two_keys.shape[0]
    two_other = (two_keys, two_values)
    chunks = first.shape[0]
    heads, _, width = query_head.shape
    count = heads // chunks
    factor = width ** (-0.5) * math.log2(math.e)

    def products(n):
        g = n * groups // chunks
        keys = two_back(back_two, two_other, 0, g)
        values = two_back(back_two, two_other, 1, g)
        near_prob_grad[n] = matmul(values, grouped(grad_head, n, count), (1, 1))
        return (matmul(keys, grouped(query_head, n, count), (1, 1)),)

    def softmax(n, scores):
        scores = masked(scores * factor, first[n], 2)
        row_max = jnp.maximum(own_max[n], jnp.max(scores, axis=0, keepdims=True))
        weights = jnp.exp2(scores - row_max)
        rescale = jnp.exp2(own_max[n] - row_max)
        own_factor[n] = rescale
        near_max[n] = row_max
        near_total[n] = own_total[n] * rescale + jnp.sum(weights, axis=0, keepdims=True)
        near_weights[n] = weights
        return rescale, weights.astype(jnp.bfloat16)

    def weigh(n, rescale, halves):
        values = two_back(back_two, two_other, 1, n * groups // chunks)
        near_out[n] = own_out[n] * rescale + matmul(values, halves, (0, 0))

    pipelined(chunks, products, softmax, weigh)


def last_kernel(
    first, query_head, grad_head, back_one, grad_rows, near_max, near_total, near_out,
    attended_rows, row_delta, near_factor, one_grad, one_part,
):
    groups = back_one.shape[1]
    chunks = first.shape[0]
    heads, _, width = query_head.shape
    count = heads // chunks
    scale = width ** (-0.5)

    def products(n):
        g = n * groups // chunks
        scores = matmul(back_one[0, g], grouped(query_head, n, count), (1, 1))
        prob_grad = matmul(back_one[1, g], grouped(grad_head, n, count), (1, 1))
        return scores, prob_grad

    def softmax(n, scores, prob_grad):
        scores = masked(scores * (scale * math.log2(math.e)), first[n], 1)
        row_max = jnp.maximum(near_max[n], jnp.max(scores, axis=0, keepdims=True))
        weights = jnp.exp2(scores - row_max)
        rescale = jnp.exp2(near_max[n] - row_max)
        inverse = 1.0 / (near_total[n] * rescale + jnp.sum(weights, axis=0, keepdims=True))
        weighted = matmul(
            back_one[1, n * groups // chunks], weights.astype(jnp.bfloat16), (0, 0)
        )
        near_factor[n] = rescale * inverse
        return prob_grad, weights, weighted, rescale, inverse

    def differentiate(n, prob_grad, weights, weighted, rescale, inverse):
        attended = ((near_out[n] * rescale + weighted) * inverse).astype(jnp.bfloat16)
        delta = jnp.sum(
            grad_rows[n].astype(jnp.float32) * attended.astype(jnp.float32), axis=0, keepdims=True
        )
        prob = weights * inverse
        score_grad = (prob * (prob_grad - delta)).astype(jnp.bfloat16)
        attended_rows[n] = attended
        row_delta[n] = delta
        one_grad[n] = score_grad
        return score_grad, prob.astype(jnp.bfloat16)

    def store(g, key_part, value_part):
        one_part[0, g] = (key_part * scale).astype(jnp.bfloat16)
        one_part[1, g] = value_part.astype(jnp.bfloat16)

    accumulate = accumulator(query_head, grad_head, chunks, groups, store)
    pipelined(chunks, products, softmax, differentiate, accumulate)


def pipelined(chunks, *stages):
    ready = [{} for _ in range(len(stages) + 1)]
    for step in range(chunks + len(stages) - 1):
        for depth, stage in reversed(list(enumerate(stages))):
            n = step - depth
            if 0 <= n < chunks:
                ready[depth + 1][n] = stage(n, *ready[depth].pop(n, ())) or ()


def accumulator(query_head, grad_head, chunks, groups, store):
    count = query_head.shape[0] // chunks
    parts = {}

    def accumulate(n, score_grad, half):
        g = n * groups // chunks
        key_part = matmul(score_grad, grouped(query_head, n, count), (1, 0))
        value_part = matmul(half, grouped(grad_head, n, count), (1, 0))
        if g in parts:
            key_part, value_part = parts[g][0] + key_part, parts[g][1] + value_part
        parts[g] = (key_part, value_part)
        if (n + 1) * groups // chunks != g:
            store(g, key_part, value_part)

    return accumulate


def two_backward_kernel(
    query_head, grad_head, near_weights, near_prob_grad, near_factor, row_delta,
    two_grad, two_mine, send_keys, send_values,
):
    chunks = near_weights.shape[0]
    groups, length, width = two_mine.shape[1:]

    def differentiate(n):
        prob = near_weights[n] * near_factor[n]
        score_grad = (prob * (near_prob_grad[n] - row_delta[n])).astype(jnp.bfloat16)
        two_grad[n] = score_grad
        return score_grad, prob.astype(jnp.bfloat16)

    def store(g, key_part, value_part):
        for index, (part, send) in enumerate(
            ((key_part * width ** (-0.5), send_keys), (value_part, send_values))
        ):
            two_mine[index, g] = part[:length].astype(jnp.bfloat16)
            send[g] = part[length:].astype(jnp.bfloat16)

    accumulate = accumulator(query_head, grad_head, chunks, groups, store)
    pipelined(chunks, differentiate, accumulate)


def own_backward_kernel(
    query_head, grad_head, own_weights, own_prob_grad, near_factor, own_factor, row_delta,
    after, own_grad, own_part,
):
    chunks = own_weights.shape[0]
    groups, _, width = own_part.shape[1:]

    def differentiate(n):
        prob = own_weights[n] * (own_factor[n] * near_factor[n])
        score_grad = (prob * (own_prob_grad[n] - row_delta[n])).astype(jnp.bfloat16)
        own_grad[n] = score_grad
        return score_grad, prob.astype(jnp.bfloat16)

    def store(g, key_part, value_part):
        own_part[0, g] = key_part * width ** (-0.5)
        own_part[1, g] = value_part

    accumulate = accumulator(query_head, grad_head, chunks, groups, store)
    pipelined(chunks, differentiate, accumulate)


def join_two_kernel(two_mine, other_keys, other_values, two_part):
    groups = two_mine.shape[1]
    two_part[:, my_heads(groups)] = two_mine[...]
    two_part[0, other_heads(groups)] = other_keys[...]
    two_part[1, other_heads(groups)] = other_values[...]


def query_kernel(
    own, back_one, back_two, two_keys, attended_rows, two_grad, one_grad, own_grad,
    out_mine, query_mine, first_third, second_third, last_third, query_send,
):
    sends = (first_third, second_third, last_third)
    groups = own.shape[1]
    chunks = own_grad.shape[0]
    heads, length, width = out_mine.shape
    count = heads // chunks
    for n in range(chunks):
        g = n * groups // chunks
        rows = pl.ds(n * count, count)
        keys = join(two_back(back_two, (two_keys,), 0, g), back_one[0, g], own[0, g])
        part = matmul(keys, join(two_grad[n], one_grad[n], own_grad[n]), (0, 0))
        part = (part * width ** (-0.5)).astype(jnp.bfloat16)
        for index, (columns, mine) in enumerate(((attended_rows[n], out_mine), (part, query_mine))):
            block = columns.T.reshape(count, 2 * length, width)
            mine[rows] = block[:, :length]
            query_send[index, rows] = block[:, length:]
    for index, row, piece, taken in placed(sends, heads):
        piece[...] = query_send[index, pl.ds(row, taken)]


def assemble_kernel(
    out_mine, query_mine, first_third, second_third, last_third, out, query_grad, token
):
    heads = out_mine.shape[0]
    start = (1 - lax.axis_index("head")) * heads
    out[my_heads(heads)] = out_mine[...]
    query_grad[my_heads(heads)] = query_mine[...]
    for index, row, piece, count in placed((first_third, second_third, last_third), heads):
        (out, query_grad)[index][pl.ds(start + row, count)] = piece[...]
    token[...] = jnp.zeros(token.shape, token.dtype)


def own_sum_kernel(own_part, one_total, sum_mine, sum_send):
    length = sum_mine.shape[2]
    total = own_part[...] + one_total[...].astype(jnp.float32)
    sum_mine[...] = total[:, :, :length]
    sum_send[...] = total[:, :, length:].astype(jnp.bfloat16)


def final_kernel(sum_mine, sum_other, two_total, after, key_grad, value_grad):
    groups = sum_mine.shape[1]
    mine, other = my_heads(groups), other_heads(groups)
    for index, result in enumerate((key_grad, value_grad)):
        total = sum_mine[index] + two_total[index, mine].astype(jnp.float32)
        result[mine] = total.astype(jnp.bfloat16)
        total = sum_other[index].astype(jnp.float32) + two_total[index, other].astype(jnp.float32)
        result[other] = total.astype(jnp.bfloat16)


def shards(query_matrix, key_matrix, value_matrix, output_gradient, query_head_spans, slab_offset):
    groups, length, width = key_matrix.shape
    heads = query_matrix.shape[0]
    cores = lax.axis_size("head")
    tokens = cores * length
    groups_here, heads_here = groups // cores, heads // cores
    count = max(1, min(heads // groups, 256 // tokens))
    chunks = heads_here // count
    lanes = count * tokens
    half, full = jnp.bfloat16, jnp.float32
    vmem = pl.BlockSpec(memory_space=pltpu.VMEM)
    smem = pl.BlockSpec(memory_space=pltpu.SMEM)

    def call(kernel, name, outs, arrays, scalars=0, scratch=()):
        return pl.pallas_call(
            kernel,
            out_shape=tuple(jax.ShapeDtypeStruct(shape, kind) for shape, kind in outs),
            in_specs=[smem] * scalars + [vmem] * (len(arrays) - scalars),
            out_specs=(vmem,) * len(outs),
            scratch_shapes=scratch,
            compiler_params=pltpu.CompilerParams(vmem_limit_bytes=40 * 1024 * 1024),
            cost_estimate=pl.CostEstimate(flops=1, bytes_accessed=0, transcendentals=0),
            name=name,
        )(*arrays)

    def rows_of(rows, kind):
        return ((chunks, rows, lanes), kind)

    stat = rows_of(1, full)
    whole_pair = ((2, groups, length, width), half)
    half_block = ((groups_here, length, width), half)
    half_pair = ((2, groups_here, length, width), half)
    chip_pair = ((2, groups_here, tokens, width), half)
    half_rows = ((heads_here, length, width), half)
    third_rows = [((rows, length, width), half) for rows in thirds(heads_here)]
    chip_rows = ((heads_here, tokens, width), half)

    own = jnp.stack([key_matrix, value_matrix])
    back_two = shifted(own, "seq", 2)
    own_sends = call(split_kernel, "split_own", [half_block] * 2, (own,))
    (own_head,) = call(
        join_own_kernel, "join_own", [chip_pair], (own, *[swapped(send, "head") for send in own_sends])
    )
    back_one = shifted(own_head, "seq", 1, ring=False)
    sends = call(
        split_rows_kernel,
        "split_rows",
        third_rows,
        (query_matrix, output_gradient, own),
    )
    (
        query_head, grad_head, grad_rows, first, own_max, own_total, own_out, own_weights,
        own_prob_grad,
    ) = call(
        own_kernel,
        "own_block",
        [
            chip_rows, chip_rows, rows_of(width, half), rows_of(1, jnp.int32), stat, stat,
            rows_of(width, full), rows_of(tokens, full), rows_of(tokens, full),
        ],
        (
            query_head_spans, slab_offset, query_matrix, output_gradient,
            *[swapped(send, "head") for send in sends], own_head,
        ),
        scalars=2,
    )
    back_two, first = lax.optimization_barrier((back_two, first))
    two_sends = call(split_kernel, "split_two", [half_block] * 2, (back_two,))
    two_other = [swapped(send, "head") for send in two_sends]
    near_max, near_total, near_out, near_weights, near_prob_grad, own_factor = call(
        near_forward_kernel,
        "near_forward",
        [stat, stat, rows_of(width, full), rows_of(tokens, full), rows_of(tokens, full), stat],
        (first, query_head, grad_head, back_two, *two_other, own_max, own_total, own_out),
    )
    back_one, near_max = lax.optimization_barrier((back_one, near_max))
    attended_rows, row_delta, near_factor, one_grad, one_part = call(
        last_kernel,
        "last_forward_backward",
        [rows_of(width, half), stat, stat, rows_of(tokens, half), chip_pair],
        (first, query_head, grad_head, back_one, grad_rows, near_max, near_total, near_out),
    )
    one_total = shifted(one_part, "seq", -1)
    two_grad, part_mine, *part_sends = call(
        two_backward_kernel,
        "two_backward",
        [rows_of(tokens, half), half_pair, half_block, half_block],
        (query_head, grad_head, near_weights, near_prob_grad, near_factor, row_delta),
    )
    (two_part,) = call(
        join_two_kernel,
        "join_two",
        [whole_pair],
        (part_mine, *[swapped(send, "head") for send in part_sends]),
    )
    two_total = shifted(two_part, "seq", -2)
    own_grad, own_part = call(
        own_backward_kernel,
        "own_backward",
        [rows_of(tokens, half), (chip_pair[0], full)],
        (
            query_head, grad_head, own_weights, own_prob_grad, near_factor, own_factor, row_delta,
            two_part,
        ),
    )
    out_mine, query_mine, *sends = call(
        query_kernel,
        "query_grad",
        [half_rows] * 2 + third_rows,
        (own_head, back_one, back_two, two_other[0], attended_rows, two_grad, one_grad, own_grad),
        scratch=[pltpu.VMEM((2,) + half_rows[0], half)],
    )
    attn_out, query_grad, token = call(
        assemble_kernel,
        "assemble",
        [(query_matrix.shape, half)] * 2 + [((8, 128), full)],
        (out_mine, query_mine, *[swapped(send, "head") for send in sends]),
    )
    sum_mine, sum_send = call(
        own_sum_kernel, "own_sum", [(half_pair[0], full), half_pair], (own_part, one_total)
    )
    key_grad, value_grad = call(
        final_kernel,
        "total",
        [(key_matrix.shape, half)] * 2,
        (sum_mine, swapped(sum_send, "head"), two_total, token),
    )
    return (attn_out, query_grad, key_grad, value_grad)


def solution(mesh):
    tokens = P(None, ("seq", "head"), None)
    return jax.shard_map(
        shards,
        mesh=mesh,
        in_specs=(tokens, tokens, tokens, tokens, P(), P()),
        out_specs=(tokens, tokens, tokens, tokens),
        check_vma=False,
    )
```

```python
import math

import jax
import jax.numpy as jnp
from jax import lax
from jax.experimental import pallas as pl
from jax.experimental.pallas import tpu as pltpu
from jax.sharding import PartitionSpec as P

REACH = 2
SEGMENT = 512

masked_score = -1e30


def shifted(block, axis, distance, ring=True):
    count = lax.axis_size(axis)
    route = [(i, (i + distance) % count) for i in range(count) if ring or i + distance < count]
    return lax.ppermute(block, axis, route)


def swapped(block, axis):
    count = lax.axis_size(axis)
    return lax.ppermute(block, axis, [(i, count - 1 - i) for i in range(count)])


def matmul(left, right, contract):
    return lax.dot_general(
        left, right, ((contract[:1], contract[1:]), ((), ())), preferred_element_type=jnp.float32
    )


def grouped(ref, n, count):
    _, length, width = ref.shape
    return ref[pl.ds(n * count, count)].reshape(count * length, width)


def join(*blocks):
    return jnp.concatenate(blocks, axis=0)


def core_offsets(length):
    core = lax.axis_index("head")
    return core * length, (1 - core) * length


def my_heads(count):
    return pl.ds(lax.axis_index("head") * count, count)


def other_heads(count):
    return pl.ds((1 - lax.axis_index("head")) * count, count)


def lane_tokens(count, length):
    lane = lax.broadcasted_iota(jnp.int32, (1, count * 2 * length), 1)
    token = lane - lane // (2 * length) * (2 * length)
    mine, other = core_offsets(length)
    return jnp.where(token < length, token + mine, token - length + other)


def first_visible(spans, offset, chunks, count, length):
    token = lane_tokens(count, length)
    lane_head = lax.broadcasted_iota(jnp.int32, token.shape, 1) // (2 * length)
    start = lax.axis_index("seq") * 2 * length
    segment_start = token - lax.bitwise_and(offset[0] + start + token, SEGMENT - 1)
    floor = jnp.maximum(segment_start, -start)
    base = lax.axis_index("head") * chunks * count
    result = []
    for n in range(chunks):
        span = jnp.full(token.shape, spans[base + n * count], jnp.int32)
        for a in range(1, count):
            span = jnp.where(lane_head == a, spans[base + n * count + a], span)
        result.append(jnp.maximum(floor, token - span + 1))
    return result


def masked(scores, first, chips_back, token=None):
    length = scores.shape[0] // 2
    row = lax.broadcasted_iota(jnp.int32, (length, scores.shape[1]), 0)
    pieces = []
    for part, offset in enumerate(core_offsets(length)):
        visible = row >= first + (chips_back * 2 * length - offset)
        if token is not None:
            visible &= row <= token - offset
        pieces.append(
            jnp.where(visible, scores[part * length : (part + 1) * length], masked_score)
        )
    return join(*pieces)


def split_kernel(block, *sends):
    for index, send in enumerate(sends):
        send[...] = block[index, other_heads(send.shape[0])]


def thirds(rows):
    return [2 * rows * (i + 1) // 3 - 2 * rows * i // 3 for i in range(3)]


def placed(pieces, rows):
    taken = 0
    for piece in pieces:
        count = piece.shape[0]
        for index in range(2):
            low = max(taken, index * rows)
            high = min(taken + count, (index + 1) * rows)
            if low < high:
                yield index, low - index * rows, piece.at[pl.ds(low - taken, high - low)], high - low
        taken += count


def split_rows_kernel(queries, grads, after, *sends):
    heads = queries.shape[0] // 2
    start = (1 - lax.axis_index("head")) * heads
    for index, row, piece, count in placed(sends, heads):
        piece[...] = (queries, grads)[index][pl.ds(start + row, count)]


def join_own_kernel(own, other_keys, other_values, own_head):
    groups, length = other_keys.shape[:2]
    own_head[:, :, pl.ds(0, length)] = own[:, my_heads(groups)]
    own_head[0, :, pl.ds(length, length)] = other_keys[...]
    own_head[1, :, pl.ds(length, length)] = other_values[...]


def own_kernel(
    spans, offset, queries, grads, first_third, second_third, last_third, own,
    query_head, grad_head, grad_rows, first, own_max, own_total, own_out, own_weights,
    own_prob_grad,
):
    heads, _, width = query_head.shape
    length = queries.shape[1]
    groups = own.shape[1]
    chunks = first.shape[0]
    count = heads // chunks
    query_head[:, pl.ds(0, length)] = queries[my_heads(heads)]
    grad_head[:, pl.ds(0, length)] = grads[my_heads(heads)]
    for index, row, piece, rows in placed((first_third, second_third, last_third), heads):
        (query_head, grad_head)[index][pl.ds(row, rows), pl.ds(length, length)] = piece[...]
    factor = width ** (-0.5) * math.log2(math.e)
    token = lane_tokens(count, length)
    for n, rows in enumerate(first_visible(spans, offset, chunks, count, length)):
        first[n] = rows

    def products(n):
        g = n * groups // chunks
        own_prob_grad[n] = matmul(own[1, g], grouped(grad_head, n, count), (1, 1))
        return (matmul(own[0, g], grouped(query_head, n, count), (1, 1)),)

    def softmax(n, scores):
        scores = masked(scores * factor, first[n], 0, token)
        row_max = jnp.max(scores, axis=0, keepdims=True)
        weights = jnp.exp2(scores - row_max)
        own_max[n] = row_max
        own_total[n] = jnp.sum(weights, axis=0, keepdims=True)
        own_weights[n] = weights
        return (weights.astype(jnp.bfloat16),)

    def weigh(n, halves):
        own_out[n] = matmul(own[1, n * groups // chunks], halves, (0, 0))
        grad_rows[n] = grouped(grad_head, n, count).T

    pipelined(chunks, products, softmax, weigh)


def two_back(back_two, two_other, index, g):
    base = lax.axis_index("head") * two_other[index].shape[0]
    return join(back_two[index, base + g], two_other[index][g])


def near_forward_kernel(
    first, query_head, grad_head, back_two, two_keys, two_values, own_max, own_total, own_out,
    near_max, near_total, near_out, near_weights, near_prob_grad, own_factor,
):
    groups = two_keys.shape[0]
    two_other = (two_keys, two_values)
    chunks = first.shape[0]
    heads, _, width = query_head.shape
    count = heads // chunks
    factor = width ** (-0.5) * math.log2(math.e)

    def products(n):
        g = n * groups // chunks
        keys = two_back(back_two, two_other, 0, g)
        values = two_back(back_two, two_other, 1, g)
        near_prob_grad[n] = matmul(values, grouped(grad_head, n, count), (1, 1))
        return (matmul(keys, grouped(query_head, n, count), (1, 1)),)

    def softmax(n, scores):
        scores = masked(scores * factor, first[n], 2)
        row_max = jnp.maximum(own_max[n], jnp.max(scores, axis=0, keepdims=True))
        weights = jnp.exp2(scores - row_max)
        rescale = jnp.exp2(own_max[n] - row_max)
        own_factor[n] = rescale
        near_max[n] = row_max
        near_total[n] = own_total[n] * rescale + jnp.sum(weights, axis=0, keepdims=True)
        near_weights[n] = weights
        return rescale, weights.astype(jnp.bfloat16)

    def weigh(n, rescale, halves):
        values = two_back(back_two, two_other, 1, n * groups // chunks)
        near_out[n] = own_out[n] * rescale + matmul(values, halves, (0, 0))

    pipelined(chunks, products, softmax, weigh)


def last_kernel(
    first, query_head, grad_head, back_one, grad_rows, near_max, near_total, near_out,
    attended_rows, row_delta, near_factor, one_grad, one_part,
):
    groups = back_one.shape[1]
    chunks = first.shape[0]
    heads, _, width = query_head.shape
    count = heads // chunks
    scale = width ** (-0.5)

    def products(n):
        g = n * groups // chunks
        scores = matmul(back_one[0, g], grouped(query_head, n, count), (1, 1))
        prob_grad = matmul(back_one[1, g], grouped(grad_head, n, count), (1, 1))
        return scores, prob_grad

    def softmax(n, scores, prob_grad):
        scores = masked(scores * (scale * math.log2(math.e)), first[n], 1)
        row_max = jnp.maximum(near_max[n], jnp.max(scores, axis=0, keepdims=True))
        weights = jnp.exp2(scores - row_max)
        rescale = jnp.exp2(near_max[n] - row_max)
        inverse = 1.0 / (near_total[n] * rescale + jnp.sum(weights, axis=0, keepdims=True))
        weighted = matmul(
            back_one[1, n * groups // chunks], weights.astype(jnp.bfloat16), (0, 0)
        )
        near_factor[n] = rescale * inverse
        return prob_grad, weights, weighted, rescale, inverse

    def differentiate(n, prob_grad, weights, weighted, rescale, inverse):
        attended = ((near_out[n] * rescale + weighted) * inverse).astype(jnp.bfloat16)
        delta = jnp.sum(
            grad_rows[n].astype(jnp.float32) * attended.astype(jnp.float32), axis=0, keepdims=True
        )
        prob = weights * inverse
        score_grad = (prob * (prob_grad - delta)).astype(jnp.bfloat16)
        attended_rows[n] = attended
        row_delta[n] = delta
        one_grad[n] = score_grad
        return score_grad, prob.astype(jnp.bfloat16)

    def store(g, key_part, value_part):
        one_part[0, g] = (key_part * scale).astype(jnp.bfloat16)
        one_part[1, g] = value_part.astype(jnp.bfloat16)

    accumulate = accumulator(query_head, grad_head, chunks, groups, store)
    pipelined(chunks, products, wait, softmax, differentiate, accumulate)


def wait(n, *values):
    return values


def pipelined(chunks, *stages):
    ready = [{} for _ in range(len(stages) + 1)]
    for step in range(chunks + len(stages) - 1):
        for depth, stage in enumerate(stages):
            n = step - depth
            if 0 <= n < chunks:
                ready[depth + 1][n] = stage(n, *ready[depth].pop(n, ())) or ()


def accumulator(query_head, grad_head, chunks, groups, store):
    count = query_head.shape[0] // chunks
    parts = {}

    def accumulate(n, score_grad, half):
        g = n * groups // chunks
        key_part = matmul(score_grad, grouped(query_head, n, count), (1, 0))
        value_part = matmul(half, grouped(grad_head, n, count), (1, 0))
        if g in parts:
            key_part, value_part = parts[g][0] + key_part, parts[g][1] + value_part
        parts[g] = (key_part, value_part)
        if (n + 1) * groups // chunks != g:
            store(g, key_part, value_part)

    return accumulate


def two_backward_kernel(
    query_head, grad_head, near_weights, near_prob_grad, near_factor, row_delta,
    two_grad, two_mine, send_keys, send_values,
):
    chunks = near_weights.shape[0]
    groups, length, width = two_mine.shape[1:]

    def differentiate(n):
        prob = near_weights[n] * near_factor[n]
        score_grad = (prob * (near_prob_grad[n] - row_delta[n])).astype(jnp.bfloat16)
        two_grad[n] = score_grad
        return score_grad, prob.astype(jnp.bfloat16)

    def store(g, key_part, value_part):
        for index, (part, send) in enumerate(
            ((key_part * width ** (-0.5), send_keys), (value_part, send_values))
        ):
            two_mine[index, g] = part[:length].astype(jnp.bfloat16)
            send[g] = part[length:].astype(jnp.bfloat16)

    accumulate = accumulator(query_head, grad_head, chunks, groups, store)
    pipelined(chunks, differentiate, accumulate)


def own_backward_kernel(
    query_head, grad_head, own_weights, own_prob_grad, near_factor, own_factor, row_delta,
    after, own_grad, own_part,
):
    chunks = own_weights.shape[0]
    groups, _, width = own_part.shape[1:]

    def differentiate(n):
        prob = own_weights[n] * (own_factor[n] * near_factor[n])
        score_grad = (prob * (own_prob_grad[n] - row_delta[n])).astype(jnp.bfloat16)
        own_grad[n] = score_grad
        return score_grad, prob.astype(jnp.bfloat16)

    def store(g, key_part, value_part):
        own_part[0, g] = key_part * width ** (-0.5)
        own_part[1, g] = value_part

    accumulate = accumulator(query_head, grad_head, chunks, groups, store)
    pipelined(chunks, differentiate, accumulate)


def join_two_kernel(two_mine, other_keys, other_values, two_part):
    groups = two_mine.shape[1]
    two_part[:, my_heads(groups)] = two_mine[...]
    two_part[0, other_heads(groups)] = other_keys[...]
    two_part[1, other_heads(groups)] = other_values[...]


def query_kernel(
    own, back_one, back_two, two_keys, attended_rows, two_grad, one_grad, own_grad,
    out_mine, query_mine, first_third, second_third, last_third, query_send,
):
    sends = (first_third, second_third, last_third)
    groups = own.shape[1]
    chunks = own_grad.shape[0]
    heads, length, width = out_mine.shape
    count = heads // chunks
    for n in range(chunks):
        g = n * groups // chunks
        rows = pl.ds(n * count, count)
        keys = join(two_back(back_two, (two_keys,), 0, g), back_one[0, g], own[0, g])
        part = matmul(keys, join(two_grad[n], one_grad[n], own_grad[n]), (0, 0))
        part = (part * width ** (-0.5)).astype(jnp.bfloat16)
        for index, (columns, mine) in enumerate(((attended_rows[n], out_mine), (part, query_mine))):
            block = columns.T.reshape(count, 2 * length, width)
            mine[rows] = block[:, :length]
            query_send[index, rows] = block[:, length:]
    for index, row, piece, taken in placed(sends, heads):
        piece[...] = query_send[index, pl.ds(row, taken)]


def assemble_kernel(
    out_mine, query_mine, first_third, second_third, last_third, out, query_grad, token
):
    heads = out_mine.shape[0]
    start = (1 - lax.axis_index("head")) * heads
    out[my_heads(heads)] = out_mine[...]
    query_grad[my_heads(heads)] = query_mine[...]
    for index, row, piece, count in placed((first_third, second_third, last_third), heads):
        (out, query_grad)[index][pl.ds(start + row, count)] = piece[...]
    token[...] = jnp.zeros(token.shape, token.dtype)


def own_sum_kernel(own_part, one_total, sum_mine, sum_send):
    length = sum_mine.shape[2]
    total = own_part[...] + one_total[...].astype(jnp.float32)
    sum_mine[...] = total[:, :, :length]
    sum_send[...] = total[:, :, length:].astype(jnp.bfloat16)


def final_kernel(sum_mine, sum_other, two_total, after, key_grad, value_grad):
    groups = sum_mine.shape[1]
    mine, other = my_heads(groups), other_heads(groups)
    for index, result in enumerate((key_grad, value_grad)):
        total = sum_mine[index] + two_total[index, mine].astype(jnp.float32)
        result[mine] = total.astype(jnp.bfloat16)
        total = sum_other[index].astype(jnp.float32) + two_total[index, other].astype(jnp.float32)
        result[other] = total.astype(jnp.bfloat16)


def shards(query_matrix, key_matrix, value_matrix, output_gradient, query_head_spans, slab_offset):
    groups, length, width = key_matrix.shape
    heads = query_matrix.shape[0]
    cores = lax.axis_size("head")
    tokens = cores * length
    groups_here, heads_here = groups // cores, heads // cores
    count = max(1, min(heads // groups, 256 // tokens))
    chunks = heads_here // count
    lanes = count * tokens
    half, full = jnp.bfloat16, jnp.float32
    vmem = pl.BlockSpec(memory_space=pltpu.VMEM)
    smem = pl.BlockSpec(memory_space=pltpu.SMEM)

    def call(kernel, name, outs, arrays, scalars=0, scratch=()):
        return pl.pallas_call(
            kernel,
            out_shape=tuple(jax.ShapeDtypeStruct(shape, kind) for shape, kind in outs),
            in_specs=[smem] * scalars + [vmem] * (len(arrays) - scalars),
            out_specs=(vmem,) * len(outs),
            scratch_shapes=scratch,
            compiler_params=pltpu.CompilerParams(vmem_limit_bytes=40 * 1024 * 1024),
            cost_estimate=pl.CostEstimate(flops=1, bytes_accessed=0, transcendentals=0),
            name=name,
        )(*arrays)

    def rows_of(rows, kind):
        return ((chunks, rows, lanes), kind)

    stat = rows_of(1, full)
    whole_pair = ((2, groups, length, width), half)
    half_block = ((groups_here, length, width), half)
    half_pair = ((2, groups_here, length, width), half)
    chip_pair = ((2, groups_here, tokens, width), half)
    half_rows = ((heads_here, length, width), half)
    third_rows = [((rows, length, width), half) for rows in thirds(heads_here)]
    chip_rows = ((heads_here, tokens, width), half)

    own = jnp.stack([key_matrix, value_matrix])
    back_two = shifted(own, "seq", 2)
    own_sends = call(split_kernel, "split_own", [half_block] * 2, (own,))
    (own_head,) = call(
        join_own_kernel, "join_own", [chip_pair], (own, *[swapped(send, "head") for send in own_sends])
    )
    back_one = shifted(own_head, "seq", 1, ring=False)
    sends = call(
        split_rows_kernel,
        "split_rows",
        third_rows,
        (query_matrix, output_gradient, own),
    )
    (
        query_head, grad_head, grad_rows, first, own_max, own_total, own_out, own_weights,
        own_prob_grad,
    ) = call(
        own_kernel,
        "own_block",
        [
            chip_rows, chip_rows, rows_of(width, half), rows_of(1, jnp.int32), stat, stat,
            rows_of(width, full), rows_of(tokens, full), rows_of(tokens, full),
        ],
        (
            query_head_spans, slab_offset, query_matrix, output_gradient,
            *[swapped(send, "head") for send in sends], own_head,
        ),
        scalars=2,
    )
    back_two, first = lax.optimization_barrier((back_two, first))
    two_sends = call(split_kernel, "split_two", [half_block] * 2, (back_two,))
    two_other = [swapped(send, "head") for send in two_sends]
    near_max, near_total, near_out, near_weights, near_prob_grad, own_factor = call(
        near_forward_kernel,
        "near_forward",
        [stat, stat, rows_of(width, full), rows_of(tokens, full), rows_of(tokens, full), stat],
        (first, query_head, grad_head, back_two, *two_other, own_max, own_total, own_out),
    )
    back_one, near_max = lax.optimization_barrier((back_one, near_max))
    attended_rows, row_delta, near_factor, one_grad, one_part = call(
        last_kernel,
        "last_forward_backward",
        [rows_of(width, half), stat, stat, rows_of(tokens, half), chip_pair],
        (first, query_head, grad_head, back_one, grad_rows, near_max, near_total, near_out),
    )
    one_total = shifted(one_part, "seq", -1)
    two_grad, part_mine, *part_sends = call(
        two_backward_kernel,
        "two_backward",
        [rows_of(tokens, half), half_pair, half_block, half_block],
        (query_head, grad_head, near_weights, near_prob_grad, near_factor, row_delta),
    )
    (two_part,) = call(
        join_two_kernel,
        "join_two",
        [whole_pair],
        (part_mine, *[swapped(send, "head") for send in part_sends]),
    )
    two_total = shifted(two_part, "seq", -2)
    own_grad, own_part = call(
        own_backward_kernel,
        "own_backward",
        [rows_of(tokens, half), (chip_pair[0], full)],
        (
            query_head, grad_head, own_weights, own_prob_grad, near_factor, own_factor, row_delta,
            two_part,
        ),
    )
    out_mine, query_mine, *sends = call(
        query_kernel,
        "query_grad",
        [half_rows] * 2 + third_rows,
        (own_head, back_one, back_two, two_other[0], attended_rows, two_grad, one_grad, own_grad),
        scratch=[pltpu.VMEM((2,) + half_rows[0], half)],
    )
    attn_out, query_grad, token = call(
        assemble_kernel,
        "assemble",
        [(query_matrix.shape, half)] * 2 + [((8, 128), full)],
        (out_mine, query_mine, *[swapped(send, "head") for send in sends]),
    )
    sum_mine, sum_send = call(
        own_sum_kernel, "own_sum", [(half_pair[0], full), half_pair], (own_part, one_total)
    )
    key_grad, value_grad = call(
        final_kernel,
        "total",
        [(key_matrix.shape, half)] * 2,
        (sum_mine, swapped(sum_send, "head"), two_total, token),
    )
    return (attn_out, query_grad, key_grad, value_grad)


def solution(mesh):
    tokens = P(None, ("seq", "head"), None)
    return jax.shard_map(
        shards,
        mesh=mesh,
        in_specs=(tokens, tokens, tokens, tokens, P(), P()),
        out_specs=(tokens, tokens, tokens, tokens),
        check_vma=False,
    )
```

```python
import math

import jax
import jax.numpy as jnp
from jax import lax
from jax.experimental import pallas as pl
from jax.experimental.pallas import tpu as pltpu
from jax.sharding import PartitionSpec as P

REACH = 2
SEGMENT = 512

masked_score = -1e30


def shifted(block, axis, distance, ring=True):
    count = lax.axis_size(axis)
    route = [(i, (i + distance) % count) for i in range(count) if ring or i + distance < count]
    return lax.ppermute(block, axis, route)


def swapped(block, axis):
    count = lax.axis_size(axis)
    return lax.ppermute(block, axis, [(i, count - 1 - i) for i in range(count)])


def matmul(left, right, contract):
    return lax.dot_general(
        left, right, ((contract[:1], contract[1:]), ((), ())), preferred_element_type=jnp.float32
    )


def grouped(ref, n, count):
    _, length, width = ref.shape
    return ref[pl.ds(n * count, count)].reshape(count * length, width)


def join(*blocks):
    return jnp.concatenate(blocks, axis=0)


def core_offsets(length):
    core = lax.axis_index("head")
    return core * length, (1 - core) * length


def my_heads(count):
    return pl.ds(lax.axis_index("head") * count, count)


def other_heads(count):
    return pl.ds((1 - lax.axis_index("head")) * count, count)


def lane_tokens(count, length):
    lane = lax.broadcasted_iota(jnp.int32, (1, count * 2 * length), 1)
    token = lane - lane // (2 * length) * (2 * length)
    mine, other = core_offsets(length)
    return jnp.where(token < length, token + mine, token - length + other)


def first_visible(spans, offset, chunks, count, length):
    token = lane_tokens(count, length)
    lane_head = lax.broadcasted_iota(jnp.int32, token.shape, 1) // (2 * length)
    start = lax.axis_index("seq") * 2 * length
    segment_start = token - lax.bitwise_and(offset[0] + start + token, SEGMENT - 1)
    floor = jnp.maximum(segment_start, -start)
    base = lax.axis_index("head") * chunks * count
    result = []
    for n in range(chunks):
        span = jnp.full(token.shape, spans[base + n * count], jnp.int32)
        for a in range(1, count):
            span = jnp.where(lane_head == a, spans[base + n * count + a], span)
        result.append(jnp.maximum(floor, token - span + 1))
    return result


def masked(scores, first, chips_back, token=None):
    length = scores.shape[0] // 2
    row = lax.broadcasted_iota(jnp.int32, (length, scores.shape[1]), 0)
    pieces = []
    for part, offset in enumerate(core_offsets(length)):
        visible = row >= first + (chips_back * 2 * length - offset)
        if token is not None:
            visible &= row <= token - offset
        pieces.append(
            jnp.where(visible, scores[part * length : (part + 1) * length], masked_score)
        )
    return join(*pieces)


def split_kernel(block, *sends):
    for index, send in enumerate(sends):
        send[...] = block[index, other_heads(send.shape[0])]


def thirds(rows):
    return [2 * rows * (i + 1) // 3 - 2 * rows * i // 3 for i in range(3)]


def placed(pieces, rows):
    taken = 0
    for piece in pieces:
        count = piece.shape[0]
        for index in range(2):
            low = max(taken, index * rows)
            high = min(taken + count, (index + 1) * rows)
            if low < high:
                yield index, low - index * rows, piece.at[pl.ds(low - taken, high - low)], high - low
        taken += count


def split_rows_kernel(queries, grads, after, *sends):
    heads = queries.shape[0] // 2
    start = (1 - lax.axis_index("head")) * heads
    for index, row, piece, count in placed(sends, heads):
        piece[...] = (queries, grads)[index][pl.ds(start + row, count)]


def join_own_kernel(own, other_keys, other_values, own_head):
    groups, length = other_keys.shape[:2]
    own_head[:, :, pl.ds(0, length)] = own[:, my_heads(groups)]
    own_head[0, :, pl.ds(length, length)] = other_keys[...]
    own_head[1, :, pl.ds(length, length)] = other_values[...]


def own_kernel(
    spans, offset, queries, grads, first_third, second_third, last_third, own,
    query_head, grad_head, grad_rows, first, own_max, own_total, own_out, own_weights,
    own_prob_grad,
):
    heads, _, width = query_head.shape
    length = queries.shape[1]
    groups = own.shape[1]
    chunks = first.shape[0]
    count = heads // chunks
    query_head[:, pl.ds(0, length)] = queries[my_heads(heads)]
    grad_head[:, pl.ds(0, length)] = grads[my_heads(heads)]
    for index, row, piece, rows in placed((first_third, second_third, last_third), heads):
        (query_head, grad_head)[index][pl.ds(row, rows), pl.ds(length, length)] = piece[...]
    factor = width ** (-0.5) * math.log2(math.e)
    token = lane_tokens(count, length)
    for n, rows in enumerate(first_visible(spans, offset, chunks, count, length)):
        first[n] = rows

    def products(n):
        g = n * groups // chunks
        own_prob_grad[n] = matmul(own[1, g], grouped(grad_head, n, count), (1, 1))
        return (matmul(own[0, g], grouped(query_head, n, count), (1, 1)),)

    def softmax(n, scores):
        scores = masked(scores * factor, first[n], 0, token)
        row_max = jnp.max(scores, axis=0, keepdims=True)
        weights = jnp.exp2(scores - row_max)
        own_max[n] = row_max
        own_total[n] = jnp.sum(weights, axis=0, keepdims=True)
        own_weights[n] = weights
        return (weights.astype(jnp.bfloat16),)

    def weigh(n, halves):
        own_out[n] = matmul(own[1, n * groups // chunks], halves, (0, 0))
        grad_rows[n] = grouped(grad_head, n, count).T

    pipelined(chunks, products, wait, softmax, weigh)


def two_back(back_two, two_other, index, g):
    base = lax.axis_index("head") * two_other[index].shape[0]
    return join(back_two[index, base + g], two_other[index][g])


def near_forward_kernel(
    first, query_head, grad_head, back_two, two_keys, two_values, own_max, own_total, own_out,
    near_max, near_total, near_out, near_weights, near_prob_grad, own_factor,
):
    groups = two_keys.shape[0]
    two_other = (two_keys, two_values)
    chunks = first.shape[0]
    heads, _, width = query_head.shape
    count = heads // chunks
    factor = width ** (-0.5) * math.log2(math.e)

    def products(n):
        g = n * groups // chunks
        keys = two_back(back_two, two_other, 0, g)
        values = two_back(back_two, two_other, 1, g)
        near_prob_grad[n] = matmul(values, grouped(grad_head, n, count), (1, 1))
        return (matmul(keys, grouped(query_head, n, count), (1, 1)),)

    def softmax(n, scores):
        scores = masked(scores * factor, first[n], 2)
        row_max = jnp.maximum(own_max[n], jnp.max(scores, axis=0, keepdims=True))
        weights = jnp.exp2(scores - row_max)
        rescale = jnp.exp2(own_max[n] - row_max)
        own_factor[n] = rescale
        near_max[n] = row_max
        near_total[n] = own_total[n] * rescale + jnp.sum(weights, axis=0, keepdims=True)
        near_weights[n] = weights
        return rescale, weights.astype(jnp.bfloat16)

    def weigh(n, rescale, halves):
        values = two_back(back_two, two_other, 1, n * groups // chunks)
        near_out[n] = own_out[n] * rescale + matmul(values, halves, (0, 0))

    pipelined(chunks, products, wait, softmax, weigh)


def last_kernel(
    first, query_head, grad_head, back_one, grad_rows, near_max, near_total, near_out,
    attended_rows, row_delta, near_factor, one_grad, one_part,
):
    groups = back_one.shape[1]
    chunks = first.shape[0]
    heads, _, width = query_head.shape
    count = heads // chunks
    scale = width ** (-0.5)

    def products(n):
        g = n * groups // chunks
        scores = matmul(back_one[0, g], grouped(query_head, n, count), (1, 1))
        prob_grad = matmul(back_one[1, g], grouped(grad_head, n, count), (1, 1))
        return scores, prob_grad

    def softmax(n, scores, prob_grad):
        scores = masked(scores * (scale * math.log2(math.e)), first[n], 1)
        row_max = jnp.maximum(near_max[n], jnp.max(scores, axis=0, keepdims=True))
        weights = jnp.exp2(scores - row_max)
        rescale = jnp.exp2(near_max[n] - row_max)
        inverse = 1.0 / (near_total[n] * rescale + jnp.sum(weights, axis=0, keepdims=True))
        weighted = matmul(
            back_one[1, n * groups // chunks], weights.astype(jnp.bfloat16), (0, 0)
        )
        near_factor[n] = rescale * inverse
        return prob_grad, weights, weighted, rescale, inverse

    def differentiate(n, prob_grad, weights, weighted, rescale, inverse):
        attended = ((near_out[n] * rescale + weighted) * inverse).astype(jnp.bfloat16)
        delta = jnp.sum(
            grad_rows[n].astype(jnp.float32) * attended.astype(jnp.float32), axis=0, keepdims=True
        )
        prob = weights * inverse
        score_grad = (prob * (prob_grad - delta)).astype(jnp.bfloat16)
        attended_rows[n] = attended
        row_delta[n] = delta
        one_grad[n] = score_grad
        return score_grad, prob.astype(jnp.bfloat16)

    def store(g, key_part, value_part):
        one_part[0, g] = (key_part * scale).astype(jnp.bfloat16)
        one_part[1, g] = value_part.astype(jnp.bfloat16)

    accumulate = accumulator(query_head, grad_head, chunks, groups, store)
    pipelined(chunks, products, wait, softmax, wait, differentiate, accumulate)


def wait(n, *values):
    return values


def pipelined(chunks, *stages):
    ready = [{} for _ in range(len(stages) + 1)]
    for step in range(chunks + len(stages) - 1):
        for depth, stage in enumerate(stages):
            n = step - depth
            if 0 <= n < chunks:
                ready[depth + 1][n] = stage(n, *ready[depth].pop(n, ())) or ()


def accumulator(query_head, grad_head, chunks, groups, store):
    count = query_head.shape[0] // chunks
    parts = {}

    def accumulate(n, score_grad, half):
        g = n * groups // chunks
        key_part = matmul(score_grad, grouped(query_head, n, count), (1, 0))
        value_part = matmul(half, grouped(grad_head, n, count), (1, 0))
        if g in parts:
            key_part, value_part = parts[g][0] + key_part, parts[g][1] + value_part
        parts[g] = (key_part, value_part)
        if (n + 1) * groups // chunks != g:
            store(g, key_part, value_part)

    return accumulate


def two_backward_kernel(
    query_head, grad_head, near_weights, near_prob_grad, near_factor, row_delta,
    two_grad, two_mine, send_keys, send_values,
):
    chunks = near_weights.shape[0]
    groups, length, width = two_mine.shape[1:]

    def differentiate(n):
        prob = near_weights[n] * near_factor[n]
        score_grad = (prob * (near_prob_grad[n] - row_delta[n])).astype(jnp.bfloat16)
        two_grad[n] = score_grad
        return score_grad, prob.astype(jnp.bfloat16)

    def store(g, key_part, value_part):
        for index, (part, send) in enumerate(
            ((key_part * width ** (-0.5), send_keys), (value_part, send_values))
        ):
            two_mine[index, g] = part[:length].astype(jnp.bfloat16)
            send[g] = part[length:].astype(jnp.bfloat16)

    accumulate = accumulator(query_head, grad_head, chunks, groups, store)
    pipelined(chunks, differentiate, accumulate)


def own_backward_kernel(
    query_head, grad_head, own_weights, own_prob_grad, near_factor, own_factor, row_delta,
    after, own_grad, own_part,
):
    chunks = own_weights.shape[0]
    groups, _, width = own_part.shape[1:]

    def differentiate(n):
        prob = own_weights[n] * (own_factor[n] * near_factor[n])
        score_grad = (prob * (own_prob_grad[n] - row_delta[n])).astype(jnp.bfloat16)
        own_grad[n] = score_grad
        return score_grad, prob.astype(jnp.bfloat16)

    def store(g, key_part, value_part):
        own_part[0, g] = key_part * width ** (-0.5)
        own_part[1, g] = value_part

    accumulate = accumulator(query_head, grad_head, chunks, groups, store)
    pipelined(chunks, differentiate, accumulate)


def join_two_kernel(two_mine, other_keys, other_values, two_part):
    groups = two_mine.shape[1]
    two_part[:, my_heads(groups)] = two_mine[...]
    two_part[0, other_heads(groups)] = other_keys[...]
    two_part[1, other_heads(groups)] = other_values[...]


def query_kernel(
    own, back_one, back_two, two_keys, attended_rows, two_grad, one_grad, own_grad,
    out_mine, query_mine, first_third, second_third, last_third, query_send,
):
    sends = (first_third, second_third, last_third)
    groups = own.shape[1]
    chunks = own_grad.shape[0]
    heads, length, width = out_mine.shape
    count = heads // chunks
    for n in range(chunks):
        g = n * groups // chunks
        rows = pl.ds(n * count, count)
        keys = join(two_back(back_two, (two_keys,), 0, g), back_one[0, g], own[0, g])
        part = matmul(keys, join(two_grad[n], one_grad[n], own_grad[n]), (0, 0))
        part = (part * width ** (-0.5)).astype(jnp.bfloat16)
        for index, (columns, mine) in enumerate(((attended_rows[n], out_mine), (part, query_mine))):
            block = columns.T.reshape(count, 2 * length, width)
            mine[rows] = block[:, :length]
            query_send[index, rows] = block[:, length:]
    for index, row, piece, taken in placed(sends, heads):
        piece[...] = query_send[index, pl.ds(row, taken)]


def assemble_kernel(
    out_mine, query_mine, first_third, second_third, last_third, out, query_grad, token
):
    heads = out_mine.shape[0]
    start = (1 - lax.axis_index("head")) * heads
    out[my_heads(heads)] = out_mine[...]
    query_grad[my_heads(heads)] = query_mine[...]
    for index, row, piece, count in placed((first_third, second_third, last_third), heads):
        (out, query_grad)[index][pl.ds(start + row, count)] = piece[...]
    token[...] = jnp.zeros(token.shape, token.dtype)


def own_sum_kernel(own_part, one_total, sum_mine, sum_send):
    length = sum_mine.shape[2]
    total = own_part[...] + one_total[...].astype(jnp.float32)
    sum_mine[...] = total[:, :, :length]
    sum_send[...] = total[:, :, length:].astype(jnp.bfloat16)


def final_kernel(sum_mine, sum_other, two_total, after, key_grad, value_grad):
    groups = sum_mine.shape[1]
    mine, other = my_heads(groups), other_heads(groups)
    for index, result in enumerate((key_grad, value_grad)):
        total = sum_mine[index] + two_total[index, mine].astype(jnp.float32)
        result[mine] = total.astype(jnp.bfloat16)
        total = sum_other[index].astype(jnp.float32) + two_total[index, other].astype(jnp.float32)
        result[other] = total.astype(jnp.bfloat16)


def shards(query_matrix, key_matrix, value_matrix, output_gradient, query_head_spans, slab_offset):
    groups, length, width = key_matrix.shape
    heads = query_matrix.shape[0]
    cores = lax.axis_size("head")
    tokens = cores * length
    groups_here, heads_here = groups // cores, heads // cores
    count = max(1, min(heads // groups, 256 // tokens))
    chunks = heads_here // count
    lanes = count * tokens
    half, full = jnp.bfloat16, jnp.float32
    vmem = pl.BlockSpec(memory_space=pltpu.VMEM)
    smem = pl.BlockSpec(memory_space=pltpu.SMEM)

    def call(kernel, name, outs, arrays, scalars=0, scratch=()):
        return pl.pallas_call(
            kernel,
            out_shape=tuple(jax.ShapeDtypeStruct(shape, kind) for shape, kind in outs),
            in_specs=[smem] * scalars + [vmem] * (len(arrays) - scalars),
            out_specs=(vmem,) * len(outs),
            scratch_shapes=scratch,
            compiler_params=pltpu.CompilerParams(vmem_limit_bytes=40 * 1024 * 1024),
            cost_estimate=pl.CostEstimate(flops=1, bytes_accessed=0, transcendentals=0),
            name=name,
        )(*arrays)

    def rows_of(rows, kind):
        return ((chunks, rows, lanes), kind)

    stat = rows_of(1, full)
    whole_pair = ((2, groups, length, width), half)
    half_block = ((groups_here, length, width), half)
    half_pair = ((2, groups_here, length, width), half)
    chip_pair = ((2, groups_here, tokens, width), half)
    half_rows = ((heads_here, length, width), half)
    third_rows = [((rows, length, width), half) for rows in thirds(heads_here)]
    chip_rows = ((heads_here, tokens, width), half)

    own = jnp.stack([key_matrix, value_matrix])
    back_two = shifted(own, "seq", 2)
    own_sends = call(split_kernel, "split_own", [half_block] * 2, (own,))
    (own_head,) = call(
        join_own_kernel, "join_own", [chip_pair], (own, *[swapped(send, "head") for send in own_sends])
    )
    back_one = shifted(own_head, "seq", 1, ring=False)
    sends = call(
        split_rows_kernel,
        "split_rows",
        third_rows,
        (query_matrix, output_gradient, own),
    )
    (
        query_head, grad_head, grad_rows, first, own_max, own_total, own_out, own_weights,
        own_prob_grad,
    ) = call(
        own_kernel,
        "own_block",
        [
            chip_rows, chip_rows, rows_of(width, half), rows_of(1, jnp.int32), stat, stat,
            rows_of(width, full), rows_of(tokens, full), rows_of(tokens, full),
        ],
        (
            query_head_spans, slab_offset, query_matrix, output_gradient,
            *[swapped(send, "head") for send in sends], own_head,
        ),
        scalars=2,
    )
    back_two, first = lax.optimization_barrier((back_two, first))
    two_sends = call(split_kernel, "split_two", [half_block] * 2, (back_two,))
    two_other = [swapped(send, "head") for send in two_sends]
    near_max, near_total, near_out, near_weights, near_prob_grad, own_factor = call(
        near_forward_kernel,
        "near_forward",
        [stat, stat, rows_of(width, full), rows_of(tokens, full), rows_of(tokens, full), stat],
        (first, query_head, grad_head, back_two, *two_other, own_max, own_total, own_out),
    )
    back_one, near_max = lax.optimization_barrier((back_one, near_max))
    attended_rows, row_delta, near_factor, one_grad, one_part = call(
        last_kernel,
        "last_forward_backward",
        [rows_of(width, half), stat, stat, rows_of(tokens, half), chip_pair],
        (first, query_head, grad_head, back_one, grad_rows, near_max, near_total, near_out),
    )
    one_total = shifted(one_part, "seq", -1)
    two_grad, part_mine, *part_sends = call(
        two_backward_kernel,
        "two_backward",
        [rows_of(tokens, half), half_pair, half_block, half_block],
        (query_head, grad_head, near_weights, near_prob_grad, near_factor, row_delta),
    )
    (two_part,) = call(
        join_two_kernel,
        "join_two",
        [whole_pair],
        (part_mine, *[swapped(send, "head") for send in part_sends]),
    )
    two_total = shifted(two_part, "seq", -2)
    own_grad, own_part = call(
        own_backward_kernel,
        "own_backward",
        [rows_of(tokens, half), (chip_pair[0], full)],
        (
            query_head, grad_head, own_weights, own_prob_grad, near_factor, own_factor, row_delta,
            two_part,
        ),
    )
    out_mine, query_mine, *sends = call(
        query_kernel,
        "query_grad",
        [half_rows] * 2 + third_rows,
        (own_head, back_one, back_two, two_other[0], attended_rows, two_grad, one_grad, own_grad),
        scratch=[pltpu.VMEM((2,) + half_rows[0], half)],
    )
    attn_out, query_grad, token = call(
        assemble_kernel,
        "assemble",
        [(query_matrix.shape, half)] * 2 + [((8, 128), full)],
        (out_mine, query_mine, *[swapped(send, "head") for send in sends]),
    )
    sum_mine, sum_send = call(
        own_sum_kernel, "own_sum", [(half_pair[0], full), half_pair], (own_part, one_total)
    )
    key_grad, value_grad = call(
        final_kernel,
        "total",
        [(key_matrix.shape, half)] * 2,
        (sum_mine, swapped(sum_send, "head"), two_total, token),
    )
    return (attn_out, query_grad, key_grad, value_grad)


def solution(mesh):
    tokens = P(None, ("seq", "head"), None)
    return jax.shard_map(
        shards,
        mesh=mesh,
        in_specs=(tokens, tokens, tokens, tokens, P(), P()),
        out_specs=(tokens, tokens, tokens, tokens),
        check_vma=False,
    )
```

```python
import math

import jax
import jax.numpy as jnp
from jax import lax
from jax.experimental import pallas as pl
from jax.experimental.pallas import tpu as pltpu
from jax.sharding import PartitionSpec as P

REACH = 2
SEGMENT = 512

masked_score = -1e30


def shifted(block, axis, distance, ring=True):
    count = lax.axis_size(axis)
    route = [(i, (i + distance) % count) for i in range(count) if ring or i + distance < count]
    return lax.ppermute(block, axis, route)


def swapped(block, axis):
    count = lax.axis_size(axis)
    return lax.ppermute(block, axis, [(i, count - 1 - i) for i in range(count)])


def matmul(left, right, contract):
    return lax.dot_general(
        left, right, ((contract[:1], contract[1:]), ((), ())), preferred_element_type=jnp.float32
    )


def grouped(ref, n, count):
    _, length, width = ref.shape
    return ref[pl.ds(n * count, count)].reshape(count * length, width)


def join(*blocks):
    return jnp.concatenate(blocks, axis=0)


def core_offsets(length):
    core = lax.axis_index("head")
    return core * length, (1 - core) * length


def my_heads(count):
    return pl.ds(lax.axis_index("head") * count, count)


def other_heads(count):
    return pl.ds((1 - lax.axis_index("head")) * count, count)


def lane_tokens(count, length):
    lane = lax.broadcasted_iota(jnp.int32, (1, count * 2 * length), 1)
    token = lane - lane // (2 * length) * (2 * length)
    mine, other = core_offsets(length)
    return jnp.where(token < length, token + mine, token - length + other)


def first_visible(spans, offset, chunks, count, length):
    token = lane_tokens(count, length)
    lane_head = lax.broadcasted_iota(jnp.int32, token.shape, 1) // (2 * length)
    start = lax.axis_index("seq") * 2 * length
    segment_start = token - lax.bitwise_and(offset[0] + start + token, SEGMENT - 1)
    floor = jnp.maximum(segment_start, -start)
    base = lax.axis_index("head") * chunks * count
    result = []
    for n in range(chunks):
        span = jnp.full(token.shape, spans[base + n * count], jnp.int32)
        for a in range(1, count):
            span = jnp.where(lane_head == a, spans[base + n * count + a], span)
        result.append(jnp.maximum(floor, token - span + 1))
    return result


def masked(scores, first, chips_back, token=None):
    length = scores.shape[0] // 2
    row = lax.broadcasted_iota(jnp.int32, (length, scores.shape[1]), 0)
    pieces = []
    for part, offset in enumerate(core_offsets(length)):
        visible = row >= first + (chips_back * 2 * length - offset)
        if token is not None:
            visible &= row <= token - offset
        pieces.append(
            jnp.where(visible, scores[part * length : (part + 1) * length], masked_score)
        )
    return join(*pieces)


def split_kernel(block, *sends):
    for index, send in enumerate(sends):
        send[...] = block[index, other_heads(send.shape[0])]


def thirds(rows):
    return [2 * rows * (i + 1) // 3 - 2 * rows * i // 3 for i in range(3)]


def placed(pieces, rows):
    taken = 0
    for piece in pieces:
        count = piece.shape[0]
        for index in range(2):
            low = max(taken, index * rows)
            high = min(taken + count, (index + 1) * rows)
            if low < high:
                yield index, low - index * rows, piece.at[pl.ds(low - taken, high - low)], high - low
        taken += count


def split_rows_kernel(queries, grads, after, *sends):
    heads = queries.shape[0] // 2
    start = (1 - lax.axis_index("head")) * heads
    for index, row, piece, count in placed(sends, heads):
        piece[...] = (queries, grads)[index][pl.ds(start + row, count)]


def join_own_kernel(own, other_keys, other_values, own_head):
    groups, length = other_keys.shape[:2]
    own_head[:, :, pl.ds(0, length)] = own[:, my_heads(groups)]
    own_head[0, :, pl.ds(length, length)] = other_keys[...]
    own_head[1, :, pl.ds(length, length)] = other_values[...]


def own_kernel(
    spans, offset, queries, grads, first_third, second_third, last_third, own,
    query_head, grad_head, grad_rows, first, own_max, own_total, own_out, own_weights,
    own_prob_grad,
):
    heads, _, width = query_head.shape
    length = queries.shape[1]
    groups = own.shape[1]
    chunks = first.shape[0]
    count = heads // chunks
    query_head[:, pl.ds(0, length)] = queries[my_heads(heads)]
    grad_head[:, pl.ds(0, length)] = grads[my_heads(heads)]
    for index, row, piece, rows in placed((first_third, second_third, last_third), heads):
        (query_head, grad_head)[index][pl.ds(row, rows), pl.ds(length, length)] = piece[...]
    factor = width ** (-0.5) * math.log2(math.e)
    token = lane_tokens(count, length)
    for n, rows in enumerate(first_visible(spans, offset, chunks, count, length)):
        first[n] = rows

    def products(n):
        g = n * groups // chunks
        own_prob_grad[n] = matmul(own[1, g], grouped(grad_head, n, count), (1, 1))
        return (matmul(own[0, g], grouped(query_head, n, count), (1, 1)),)

    def softmax(n, scores):
        scores = masked(scores * factor, first[n], 0, token)
        row_max = jnp.max(scores, axis=0, keepdims=True)
        weights = jnp.exp2(scores - row_max)
        own_max[n] = row_max
        own_total[n] = jnp.sum(weights, axis=0, keepdims=True)
        own_weights[n] = weights
        return (weights.astype(jnp.bfloat16),)

    def weigh(n, halves):
        own_out[n] = matmul(own[1, n * groups // chunks], halves, (0, 0))
        grad_rows[n] = grouped(grad_head, n, count).T

    pipelined(chunks, products, wait, softmax, weigh)


def two_back(back_two, two_other, index, g):
    base = lax.axis_index("head") * two_other[index].shape[0]
    return join(back_two[index, base + g], two_other[index][g])


def near_forward_kernel(
    first, query_head, grad_head, back_two, two_keys, two_values, own_max, own_total, own_out,
    near_max, near_total, near_out, near_weights, near_prob_grad, own_factor,
):
    groups = two_keys.shape[0]
    two_other = (two_keys, two_values)
    chunks = first.shape[0]
    heads, _, width = query_head.shape
    count = heads // chunks
    factor = width ** (-0.5) * math.log2(math.e)

    def products(n):
        g = n * groups // chunks
        keys = two_back(back_two, two_other, 0, g)
        values = two_back(back_two, two_other, 1, g)
        near_prob_grad[n] = matmul(values, grouped(grad_head, n, count), (1, 1))
        return (matmul(keys, grouped(query_head, n, count), (1, 1)),)

    def softmax(n, scores):
        scores = masked(scores * factor, first[n], 2)
        row_max = jnp.maximum(own_max[n], jnp.max(scores, axis=0, keepdims=True))
        weights = jnp.exp2(scores - row_max)
        rescale = jnp.exp2(own_max[n] - row_max)
        own_factor[n] = rescale
        near_max[n] = row_max
        near_total[n] = own_total[n] * rescale + jnp.sum(weights, axis=0, keepdims=True)
        near_weights[n] = weights
        return rescale, weights.astype(jnp.bfloat16)

    def weigh(n, rescale, halves):
        values = two_back(back_two, two_other, 1, n * groups // chunks)
        near_out[n] = own_out[n] * rescale + matmul(values, halves, (0, 0))

    pipelined(chunks, products, wait, softmax, weigh)


def last_kernel(
    first, query_head, grad_head, back_one, grad_rows, near_max, near_total, near_out,
    attended_rows, row_delta, near_factor, one_grad, one_part,
):
    groups = back_one.shape[1]
    chunks = first.shape[0]
    heads, _, width = query_head.shape
    count = heads // chunks
    scale = width ** (-0.5)

    def products(n):
        g = n * groups // chunks
        scores = matmul(back_one[0, g], grouped(query_head, n, count), (1, 1))
        prob_grad = matmul(back_one[1, g], grouped(grad_head, n, count), (1, 1))
        return scores, prob_grad

    def softmax(n, scores, prob_grad):
        scores = masked(scores * (scale * math.log2(math.e)), first[n], 1)
        row_max = jnp.maximum(near_max[n], jnp.max(scores, axis=0, keepdims=True))
        weights = jnp.exp2(scores - row_max)
        rescale = jnp.exp2(near_max[n] - row_max)
        inverse = 1.0 / (near_total[n] * rescale + jnp.sum(weights, axis=0, keepdims=True))
        weighted = matmul(
            back_one[1, n * groups // chunks], weights.astype(jnp.bfloat16), (0, 0)
        )
        near_factor[n] = rescale * inverse
        return prob_grad, weights, weighted, rescale, inverse

    def differentiate(n, prob_grad, weights, weighted, rescale, inverse):
        attended = ((near_out[n] * rescale + weighted) * inverse).astype(jnp.bfloat16)
        delta = jnp.sum(
            grad_rows[n].astype(jnp.float32) * attended.astype(jnp.float32), axis=0, keepdims=True
        )
        prob = weights * inverse
        score_grad = (prob * (prob_grad - delta)).astype(jnp.bfloat16)
        attended_rows[n] = attended
        row_delta[n] = delta
        one_grad[n] = score_grad
        return score_grad, prob.astype(jnp.bfloat16)

    def store(g, key_part, value_part):
        one_part[0, g] = (key_part * scale).astype(jnp.bfloat16)
        one_part[1, g] = value_part.astype(jnp.bfloat16)

    accumulate = accumulator(query_head, grad_head, chunks, groups, store)
    pipelined(chunks, products, wait, softmax, differentiate, wait, accumulate)


def wait(n, *values):
    return values


def pipelined(chunks, *stages):
    ready = [{} for _ in range(len(stages) + 1)]
    for step in range(chunks + len(stages) - 1):
        for depth, stage in enumerate(stages):
            n = step - depth
            if 0 <= n < chunks:
                ready[depth + 1][n] = stage(n, *ready[depth].pop(n, ())) or ()


def accumulator(query_head, grad_head, chunks, groups, store):
    count = query_head.shape[0] // chunks
    parts = {}

    def accumulate(n, score_grad, half):
        g = n * groups // chunks
        key_part = matmul(score_grad, grouped(query_head, n, count), (1, 0))
        value_part = matmul(half, grouped(grad_head, n, count), (1, 0))
        if g in parts:
            key_part, value_part = parts[g][0] + key_part, parts[g][1] + value_part
        parts[g] = (key_part, value_part)
        if (n + 1) * groups // chunks != g:
            store(g, key_part, value_part)

    return accumulate


def two_backward_kernel(
    query_head, grad_head, near_weights, near_prob_grad, near_factor, row_delta,
    two_grad, two_mine, send_keys, send_values,
):
    chunks = near_weights.shape[0]
    groups, length, width = two_mine.shape[1:]

    def differentiate(n):
        prob = near_weights[n] * near_factor[n]
        score_grad = (prob * (near_prob_grad[n] - row_delta[n])).astype(jnp.bfloat16)
        two_grad[n] = score_grad
        return score_grad, prob.astype(jnp.bfloat16)

    def store(g, key_part, value_part):
        for index, (part, send) in enumerate(
            ((key_part * width ** (-0.5), send_keys), (value_part, send_values))
        ):
            two_mine[index, g] = part[:length].astype(jnp.bfloat16)
            send[g] = part[length:].astype(jnp.bfloat16)

    accumulate = accumulator(query_head, grad_head, chunks, groups, store)
    pipelined(chunks, differentiate, accumulate)


def own_backward_kernel(
    query_head, grad_head, own_weights, own_prob_grad, near_factor, own_factor, row_delta,
    after, own_grad, own_part,
):
    chunks = own_weights.shape[0]
    groups, _, width = own_part.shape[1:]

    def differentiate(n):
        prob = own_weights[n] * (own_factor[n] * near_factor[n])
        score_grad = (prob * (own_prob_grad[n] - row_delta[n])).astype(jnp.bfloat16)
        own_grad[n] = score_grad
        return score_grad, prob.astype(jnp.bfloat16)

    def store(g, key_part, value_part):
        own_part[0, g] = key_part * width ** (-0.5)
        own_part[1, g] = value_part

    accumulate = accumulator(query_head, grad_head, chunks, groups, store)
    pipelined(chunks, differentiate, accumulate)


def join_two_kernel(two_mine, other_keys, other_values, two_part):
    groups = two_mine.shape[1]
    two_part[:, my_heads(groups)] = two_mine[...]
    two_part[0, other_heads(groups)] = other_keys[...]
    two_part[1, other_heads(groups)] = other_values[...]


def query_kernel(
    own, back_one, back_two, two_keys, attended_rows, two_grad, one_grad, own_grad,
    out_mine, query_mine, first_third, second_third, last_third, query_send,
):
    sends = (first_third, second_third, last_third)
    groups = own.shape[1]
    chunks = own_grad.shape[0]
    heads, length, width = out_mine.shape
    count = heads // chunks
    for n in range(chunks):
        g = n * groups // chunks
        rows = pl.ds(n * count, count)
        keys = join(two_back(back_two, (two_keys,), 0, g), back_one[0, g], own[0, g])
        part = matmul(keys, join(two_grad[n], one_grad[n], own_grad[n]), (0, 0))
        part = (part * width ** (-0.5)).astype(jnp.bfloat16)
        for index, (columns, mine) in enumerate(((attended_rows[n], out_mine), (part, query_mine))):
            block = columns.T.reshape(count, 2 * length, width)
            mine[rows] = block[:, :length]
            query_send[index, rows] = block[:, length:]
    for index, row, piece, taken in placed(sends, heads):
        piece[...] = query_send[index, pl.ds(row, taken)]


def assemble_kernel(
    out_mine, query_mine, first_third, second_third, last_third, out, query_grad, token
):
    heads = out_mine.shape[0]
    start = (1 - lax.axis_index("head")) * heads
    out[my_heads(heads)] = out_mine[...]
    query_grad[my_heads(heads)] = query_mine[...]
    for index, row, piece, count in placed((first_third, second_third, last_third), heads):
        (out, query_grad)[index][pl.ds(start + row, count)] = piece[...]
    token[...] = jnp.zeros(token.shape, token.dtype)


def own_sum_kernel(own_part, one_total, sum_mine, sum_send):
    length = sum_mine.shape[2]
    total = own_part[...] + one_total[...].astype(jnp.float32)
    sum_mine[...] = total[:, :, :length]
    sum_send[...] = total[:, :, length:].astype(jnp.bfloat16)


def final_kernel(sum_mine, sum_other, two_total, after, key_grad, value_grad):
    groups = sum_mine.shape[1]
    mine, other = my_heads(groups), other_heads(groups)
    for index, result in enumerate((key_grad, value_grad)):
        total = sum_mine[index] + two_total[index, mine].astype(jnp.float32)
        result[mine] = total.astype(jnp.bfloat16)
        total = sum_other[index].astype(jnp.float32) + two_total[index, other].astype(jnp.float32)
        result[other] = total.astype(jnp.bfloat16)


def shards(query_matrix, key_matrix, value_matrix, output_gradient, query_head_spans, slab_offset):
    groups, length, width = key_matrix.shape
    heads = query_matrix.shape[0]
    cores = lax.axis_size("head")
    tokens = cores * length
    groups_here, heads_here = groups // cores, heads // cores
    count = max(1, min(heads // groups, 256 // tokens))
    chunks = heads_here // count
    lanes = count * tokens
    half, full = jnp.bfloat16, jnp.float32
    vmem = pl.BlockSpec(memory_space=pltpu.VMEM)
    smem = pl.BlockSpec(memory_space=pltpu.SMEM)

    def call(kernel, name, outs, arrays, scalars=0, scratch=()):
        return pl.pallas_call(
            kernel,
            out_shape=tuple(jax.ShapeDtypeStruct(shape, kind) for shape, kind in outs),
            in_specs=[smem] * scalars + [vmem] * (len(arrays) - scalars),
            out_specs=(vmem,) * len(outs),
            scratch_shapes=scratch,
            compiler_params=pltpu.CompilerParams(vmem_limit_bytes=40 * 1024 * 1024),
            cost_estimate=pl.CostEstimate(flops=1, bytes_accessed=0, transcendentals=0),
            name=name,
        )(*arrays)

    def rows_of(rows, kind):
        return ((chunks, rows, lanes), kind)

    stat = rows_of(1, full)
    whole_pair = ((2, groups, length, width), half)
    half_block = ((groups_here, length, width), half)
    half_pair = ((2, groups_here, length, width), half)
    chip_pair = ((2, groups_here, tokens, width), half)
    half_rows = ((heads_here, length, width), half)
    third_rows = [((rows, length, width), half) for rows in thirds(heads_here)]
    chip_rows = ((heads_here, tokens, width), half)

    own = jnp.stack([key_matrix, value_matrix])
    back_two = shifted(own, "seq", 2)
    own_sends = call(split_kernel, "split_own", [half_block] * 2, (own,))
    (own_head,) = call(
        join_own_kernel, "join_own", [chip_pair], (own, *[swapped(send, "head") for send in own_sends])
    )
    back_one = shifted(own_head, "seq", 1, ring=False)
    sends = call(
        split_rows_kernel,
        "split_rows",
        third_rows,
        (query_matrix, output_gradient, own),
    )
    (
        query_head, grad_head, grad_rows, first, own_max, own_total, own_out, own_weights,
        own_prob_grad,
    ) = call(
        own_kernel,
        "own_block",
        [
            chip_rows, chip_rows, rows_of(width, half), rows_of(1, jnp.int32), stat, stat,
            rows_of(width, full), rows_of(tokens, full), rows_of(tokens, full),
        ],
        (
            query_head_spans, slab_offset, query_matrix, output_gradient,
            *[swapped(send, "head") for send in sends], own_head,
        ),
        scalars=2,
    )
    back_two, first = lax.optimization_barrier((back_two, first))
    two_sends = call(split_kernel, "split_two", [half_block] * 2, (back_two,))
    two_other = [swapped(send, "head") for send in two_sends]
    near_max, near_total, near_out, near_weights, near_prob_grad, own_factor = call(
        near_forward_kernel,
        "near_forward",
        [stat, stat, rows_of(width, full), rows_of(tokens, full), rows_of(tokens, full), stat],
        (first, query_head, grad_head, back_two, *two_other, own_max, own_total, own_out),
    )
    back_one, near_max = lax.optimization_barrier((back_one, near_max))
    attended_rows, row_delta, near_factor, one_grad, one_part = call(
        last_kernel,
        "last_forward_backward",
        [rows_of(width, half), stat, stat, rows_of(tokens, half), chip_pair],
        (first, query_head, grad_head, back_one, grad_rows, near_max, near_total, near_out),
    )
    one_total = shifted(one_part, "seq", -1)
    two_grad, part_mine, *part_sends = call(
        two_backward_kernel,
        "two_backward",
        [rows_of(tokens, half), half_pair, half_block, half_block],
        (query_head, grad_head, near_weights, near_prob_grad, near_factor, row_delta),
    )
    (two_part,) = call(
        join_two_kernel,
        "join_two",
        [whole_pair],
        (part_mine, *[swapped(send, "head") for send in part_sends]),
    )
    two_total = shifted(two_part, "seq", -2)
    own_grad, own_part = call(
        own_backward_kernel,
        "own_backward",
        [rows_of(tokens, half), (chip_pair[0], full)],
        (
            query_head, grad_head, own_weights, own_prob_grad, near_factor, own_factor, row_delta,
            two_part,
        ),
    )
    out_mine, query_mine, *sends = call(
        query_kernel,
        "query_grad",
        [half_rows] * 2 + third_rows,
        (own_head, back_one, back_two, two_other[0], attended_rows, two_grad, one_grad, own_grad),
        scratch=[pltpu.VMEM((2,) + half_rows[0], half)],
    )
    attn_out, query_grad, token = call(
        assemble_kernel,
        "assemble",
        [(query_matrix.shape, half)] * 2 + [((8, 128), full)],
        (out_mine, query_mine, *[swapped(send, "head") for send in sends]),
    )
    sum_mine, sum_send = call(
        own_sum_kernel, "own_sum", [(half_pair[0], full), half_pair], (own_part, one_total)
    )
    key_grad, value_grad = call(
        final_kernel,
        "total",
        [(key_matrix.shape, half)] * 2,
        (sum_mine, swapped(sum_send, "head"), two_total, token),
    )
    return (attn_out, query_grad, key_grad, value_grad)


def solution(mesh):
    tokens = P(None, ("seq", "head"), None)
    return jax.shard_map(
        shards,
        mesh=mesh,
        in_specs=(tokens, tokens, tokens, tokens, P(), P()),
        out_specs=(tokens, tokens, tokens, tokens),
        check_vma=False,
    )
```
